32 devices in a mesh: seq: 8 (over z, x), batch: 4 (over y, core).
Axes of the slice: x: 2, y: 2, z: 4, core: 2. Of those that a mesh axis runs over, the one named last changes fastest.
Arguments:
- hidden_in: bfloat16 [4, 2048, 1024], P('batch', 'seq'), may hold values from -6 to 6
- out_grad: bfloat16 [4, 2048, 1024], P('batch', 'seq'), may hold values from -6 to 6
- norm_gain_pair: float32 [2, 1024], replicated, may hold values from 0.5 to 1.5
- norm_bias_pair: float32 [2, 1024], replicated, may hold values from -1.2 to 1.2
- w_qkv: bfloat16 [1024, 3072], replicated, may hold values from -0.1875 to 0.1875
- qv_bias: float32 [2, 1024], replicated, may hold values from -1.2 to 1.2
- w_out: bfloat16 [1024, 1024], replicated, may hold values from -1.5 to 1.5
- out_bias: float32 [1024], replicated, may hold values from -1.2 to 1.2
- w_in_exp: bfloat16 [16, 1024, 4096], P('seq', None, 'batch'), may hold values from -0.1875 to 0.1875
- b_in_exp: float32 [16, 4096], P('seq', 'batch'), may hold values from -0.9 to 0.9
- w_out_exp: bfloat16 [16, 4096, 1024], P('seq', 'batch'), may hold values from -0.125 to 0.125
- b_out_exp: float32 [16, 1024], P('seq'), may hold values from -0.6 to 0.6
- expert_ids: int32 [4, 2048, 1], P('batch', 'seq'), may hold values from 0 to 15; in each aligned block of 256 rows (0 to 255, 256 to 511, ..., all dimensions but the last counted through in order) at most 24 rows name the same one
- doc_lengths: int32 [4, 8], P('batch'), may hold values from 1 to 1794, 2048 in all within a row
- pad_mask: int32 [4, 2048], P('batch', 'seq'), may hold values 0 or 1
Outputs:
- output: bfloat16 [4, 2048, 1024], P('batch', 'seq')
- input_grad: bfloat16 [4, 2048, 1024], P('batch', 'seq')
- grad_norm_gains: float32 [2, 1024], P(None, ('seq', 'batch'))
- grad_norm_biases: float32 [2, 1024], P(None, ('seq', 'batch'))
- grad_w_qkv: float32 [1024, 3072], P(('seq', 'batch'))
- grad_qv_bias: float32 [2, 1024], P(None, ('seq', 'batch'))
- grad_w_out: float32 [1024, 1024], P(('seq', 'batch'))
- grad_out_bias: float32 [1024], P(('seq', 'batch'))
- grad_w_in_exp: float32 [16, 1024, 4096], P('seq', None, 'batch')
- grad_b_in_exp: float32 [16, 4096], P('seq', 'batch')
- grad_w_out_exp: float32 [16, 4096, 1024], P('seq', 'batch')
- grad_b_out_exp: float32 [16, 1024], P('seq')
The draws below stay inside these ranges and needn't reach their ends.
Inputs may be any that keep to these rules, and one draw needn't show every extreme that they name: `expert_ids`: among the 256 tokens of one device no expert is named more than 24 times, and in some devices one expert is named exactly 24 times. `doc_lengths`: each row's 8 lengths sum to 2048, and its longest dialogue has exactly 1794 positions.
All inputs are finite; a program needn't handle non-finite values. No bound on the sum of `pad_mask` on one device may be relied on, other than what follows from the above.
Results may differ from the reference program's by a relative error of at most 0.015.
Values may be sent and summed in bfloat16 or wider, within the bound.
No kernel may reach another device: no remote copies, remote signals or barrier semaphores. Data moves between devices by JAX's collectives and lax.ppermute only.
A program may use at most 256 MiB of HBM per device.

```python
import math
import jax
import jax.numpy as jnp
import numpy as np
from jax import lax

D = 1024
HEADS = 16
HEAD_DIM = 64
FF = 4096
TOK_DEV = 256
DOCS = 8
EXPERTS = 16
ROW = 2048
BATCH = 4
CAP = 24
N_SEQ = 8
N_BATCH = 4


def plant(values, stream_key, least, high):
    longest = values.shape.index(max(values.shape))
    spots = []
    for shift in (0, 1):
        where = [jax.random.randint(jax.random.fold_in(stream_key, axis), (), 0, length) for axis, length in enumerate(values.shape)]
        where[longest] = (where[longest] + shift) % values.shape[longest]
        spots.append(tuple(where))
    return values.at[spots[0]].set(least).at[spots[1]].set(high)


def block_levels(stream_key, extent, shards, least, top_value):
    def one(axis_at, blocks):
        steps = jax.random.uniform(jax.random.fold_in(jax.random.fold_in(stream_key, 6), axis_at), (blocks,), jnp.float32, least / len(shards), top_value / len(shards))
        return jnp.repeat(jnp.exp(steps), extent[axis_at] // blocks).reshape((-1,) + (1,) * (len(extent) - axis_at - 1))

    level = one(*shards[0])
    for cut in shards[1:]:
        level = level * one(*cut)
    return level


def split_up(number_of, total, most, skew):
    weights = [(1 << 20) // math.isqrt(grade ** skew) + 1 for grade in range(2, number_of + 1)]
    rest, holding = total - most - (number_of - 1), [1] * (number_of - 1)
    while rest > 0:
        free = [i for i in range(number_of - 1) if holding[i] < most]
        pool, remaining = sum([weights[i] for i in free]), rest
        for i in free:
            more = min(most - holding[i], max(1, remaining * weights[i] // pool), rest)
            holding[i] = holding[i] + more
            rest = rest - more
    return np.array([most] + holding)


def ragged_sizes(stream_key, count, total, bound, skew):
    if count == 2:
        one = jax.random.randint(stream_key, (), max(1, total - bound), min(bound, total - 1) + 1)
        return jnp.stack([one, total - one])
    tallies = jnp.asarray(split_up(count, total, bound, skew), jnp.int32)
    pairs = (count - 1) // 2
    source_of, taker = tallies[1:1 + 2 * pairs:2], tallies[2:2 + 2 * pairs:2]
    margin = jnp.minimum(source_of - 1, bound - taker)
    moved = jax.random.randint(jax.random.fold_in(stream_key, 1), (pairs,), 0, 1 << 20) % (margin + 1)
    tallies = tallies.at[1:1 + 2 * pairs:2].set(source_of - moved).at[2:2 + 2 * pairs:2].set(taker + moved)
    return tallies[jax.random.permutation(jax.random.fold_in(stream_key, 2), count)]


def assign_block(rng, own, number, rows, number_of, top, most, skew):
    sequence = jax.random.permutation(rng, number_of)
    crowded, usual = portions_of(number_of, rows * top, most, skew, True), portions_of(number_of, rows * top, most, skew, False)
    places = jnp.arange(number_of)

    def named(lengths, offset_by):
        used = int((lengths > 0).sum())
        fixed = max(1, used // 4)
        moved = fixed + (places - fixed + offset_by * (used - fixed)) % max(1, number_of - fixed)
        return jnp.zeros((number_of,), jnp.int32).at[sequence[jnp.where(places < fixed, places, moved)]].set(jnp.asarray(lengths, jnp.int32))

    lengths = jnp.where(number % 4 == 0, named(crowded, number // 4), named(usual, number - number // 4 - 1))
    mixed = jax.random.permutation(jax.random.fold_in(own, 3), number_of)
    donor, sink = mixed[0:number_of // 2 * 2:2], mixed[1:number_of // 2 * 2:2]
    margin = jnp.minimum(lengths[donor] - 1, most - lengths[sink]) // 2
    margin = jnp.where((donor == sequence[0]) | (sink == sequence[0]) | (lengths[sink] == 0), 0, jnp.maximum(margin, 0))
    moved = jax.random.randint(jax.random.fold_in(own, 4), (number_of // 2,), 0, 1 << 20) % (margin + 1)
    lengths = lengths.at[donor].add(-moved).at[sink].add(moved)
    labels = jnp.searchsorted(jnp.cumsum(lengths), jnp.arange(rows * top), side="right").astype(jnp.int32)
    listing = labels.reshape(top, rows).T
    listing = listing[jax.random.permutation(jax.random.fold_in(own, 1), rows)]
    offset_by = jax.random.randint(jax.random.fold_in(own, 2), (rows, 1), 0, top)
    return jnp.take_along_axis(listing, (jnp.arange(top)[None, :] + offset_by) % top, axis=1)


def portions_of(amount, total, bound, slope, full):
    portions = [(1 << 20) // math.isqrt(grade ** slope) + 1 for grade in range(1, amount + 1)]
    largest = bound if full else min(bound, max(-(-total // amount), total * portions[0] // sum(portions)))
    least = 1 if total - largest >= amount - 1 else 0
    given, rest = [largest] + [least] * (amount - 1), total - largest - least * (amount - 1)
    while rest > 0:
        candidates = [i for i in range(1, amount) if given[i] < largest] or [i for i in range(1, amount) if given[i] < bound]
        mass, left = sum([portions[i] for i in candidates]), rest
        for i in candidates:
            extra = min(bound - given[i], max(1, left * portions[i] // mass), rest)
            given[i] = given[i] + extra
            rest = rest - extra
    return np.array(given)


def gaussian(own_key, extent, scale, reach, split=(), kind=jnp.bfloat16):
    array = scale * jax.random.normal(own_key, extent, jnp.float32)
    if split:
        array = array * block_levels(own_key, extent, split, -0.22, 0.18)
    return jnp.clip(array, -reach, reach).astype(kind)


def setup_inputs(seed: int = 0) -> dict:
    arg_keys = jax.random.split(jax.random.key(seed), 16)
    hidden_in = gaussian(arg_keys[0], (BATCH, ROW, D), 1.0, 6.0, ((0, 4), (1, 8)))
    out_grad = gaussian(arg_keys[1], (BATCH, ROW, D), 1.0, 6.0, ((0, 4), (1, 8)))
    norm_gain_pair = jnp.clip(1.0 + 0.1 * jax.random.normal(arg_keys[2], (2, D), jnp.float32), 0.5, 1.5)
    norm_bias_pair = gaussian(arg_keys[3], (2, D), 0.2, 1.2, (), jnp.float32)
    w_qkv = gaussian(arg_keys[4], (D, 3 * D), D ** -0.5, 0.1875)
    qv_bias = gaussian(arg_keys[5], (2, D), 0.2, 1.2, (), jnp.float32)
    w_out = gaussian(arg_keys[6], (D, D), (D // 64) ** -0.5, 1.5)
    out_bias = gaussian(arg_keys[7], (D,), 0.2, 1.2, (), jnp.float32)
    w_in_exp = gaussian(arg_keys[8], (EXPERTS, D, FF), D ** -0.5, 0.1875, ((0, 8), (2, 4)))
    b_in_exp = gaussian(arg_keys[9], (EXPERTS, FF), 0.15, 0.9, ((0, 8), (1, 4)), jnp.float32)
    w_out_exp = gaussian(arg_keys[10], (EXPERTS, FF, D), (FF // 2) ** -0.5, 0.125, ((0, 8), (1, 4)))
    b_out_exp = gaussian(arg_keys[11], (EXPERTS, D), 0.1, 0.6, ((0, 8),), jnp.float32)
    expert_ids_keys = jax.random.split(jax.random.fold_in(arg_keys[12], 1), BATCH * ROW // TOK_DEV)
    expert_ids_turns = jax.random.permutation(jax.random.fold_in(arg_keys[12], 3), BATCH * ROW // TOK_DEV)
    expert_ids = jax.vmap(lambda own, number: assign_block(jax.random.fold_in(arg_keys[12], 2), own, number, TOK_DEV, EXPERTS, 1, CAP, 1))(expert_ids_keys, expert_ids_turns).reshape((BATCH, ROW, 1))
    doc_lengths = jax.vmap(lambda own: ragged_sizes(own, DOCS, ROW, ROW - TOK_DEV + 2, 2))(jax.random.split(arg_keys[13], BATCH)).reshape((BATCH, DOCS)).astype(jnp.int32)
    pad_mask = plant((jax.random.randint(arg_keys[14], (BATCH, ROW), 0, 8) < 7).astype(jnp.int32), jax.random.fold_in(arg_keys[14], 1), 0, 1)
    return {"hidden_in": hidden_in, "out_grad": out_grad, "norm_gain_pair": norm_gain_pair, "norm_bias_pair": norm_bias_pair, "w_qkv": w_qkv, "qv_bias": qv_bias, "w_out": w_out, "out_bias": out_bias, "w_in_exp": w_in_exp, "b_in_exp": b_in_exp, "w_out_exp": w_out_exp, "b_out_exp": b_out_exp, "expert_ids": expert_ids, "doc_lengths": doc_lengths, "pad_mask": pad_mask}


EPS = 1e-05
NEG = -1e+30
HIGH = lax.Precision.HIGHEST

@jax.custom_vjp
def low(v):
    return lax.optimization_barrier(v.astype(jnp.bfloat16)).astype(jnp.float32)

@jax.custom_vjp
def low_back(v):
    return v

def low_keep(v):
    return (low(v), None)

def low_pass(kept, grad):
    return (grad,)

def back_keep(v):
    return (v, None)

def back_low(kept, grad):
    return (low(grad),)
low.defvjp(low_keep, low_pass)
low_back.defvjp(back_keep, back_low)

def layer_normalize(values, gain, shift):
    centre = values - lax.optimization_barrier(jnp.mean(values, axis=-1, keepdims=True))
    spread = lax.optimization_barrier(jnp.mean(centre * centre, axis=-1, keepdims=True))
    return centre * lax.rsqrt(spread + EPS) * gain + shift

def attend_row(packed):
    queries, keys, values_in, doc_ids, pad_row = packed
    row_len = queries.shape[0]
    block_rows = math.gcd(row_len, 512)
    positions = jnp.arange(row_len, dtype=jnp.int32)

    def one_block(block_index):
        first_row = (block_index * block_rows).astype(jnp.int32)
        query_part = lax.dynamic_slice_in_dim(queries, first_row, block_rows, 0)
        query_pos = first_row + jnp.arange(block_rows, dtype=jnp.int32)
        query_doc = lax.dynamic_slice_in_dim(doc_ids, first_row, block_rows, 0)
        scores = jnp.einsum('qhd,khd->hqk', query_part, keys, precision=HIGH)
        scores = low_back(scores)
        allowed = (query_doc[:, None] == doc_ids[None, :]) & (positions[None, :] <= query_pos[:, None]) & ((pad_row[None, :] == 1) | (positions[None, :] == query_pos[:, None]))
        scores = jnp.where(allowed[None], scores, NEG)
        top = lax.optimization_barrier(jnp.max(scores, axis=-1, keepdims=True))
        weights = jnp.where(allowed[None], jnp.exp(scores - top), 0.0)
        probs = weights / lax.optimization_barrier(jnp.sum(weights, axis=-1, keepdims=True))
        mixed = jnp.einsum('hqk,khd->qhd', low(probs), values_in, precision=HIGH)
        return mixed.reshape(block_rows, -1)
    blocks = lax.map(jax.checkpoint(one_block), jnp.arange(row_len // block_rows, dtype=jnp.int32))
    return blocks.reshape(row_len, -1)

def forward(input_tokens, gains, shifts, w_qkv, qv_bias, w_out, out_bias, w_in, b_in, w_down, b_down, doc_ids, pad_mask, table):
    batch_rows = input_tokens.shape[0]
    h_one = low(layer_normalize(input_tokens, gains[0], shifts[0]))
    mixed = jnp.dot(h_one, w_qkv, precision=HIGH)
    scale = HEAD_DIM ** (-0.5)
    queries = low_back(low((mixed[..., :D] + qv_bias[0]) * scale))
    keys = low_back(low(mixed[..., D:2 * D]))
    values_in = low_back(low(mixed[..., 2 * D:] + qv_bias[1]))
    shape_four = (batch_rows, ROW, HEADS, HEAD_DIM)
    attended = lax.map(attend_row, (queries.reshape(shape_four), keys.reshape(shape_four), values_in.reshape(shape_four), doc_ids, pad_mask))
    attended = low_back(low(attended))
    branch = low_back(jnp.dot(attended, w_out, precision=HIGH)) + out_bias
    first_residual_input = input_tokens + branch
    x_two = low_back(low(layer_normalize(first_residual_input, gains[1], shifts[1])))
    flat = x_two.reshape(-1, D)
    total = flat.shape[0]
    padded = jnp.concatenate([flat, jnp.zeros((1, D), flat.dtype)], axis=0)
    picked = padded[table]
    pre = low_back(jnp.einsum('ecd,edf->ecf', picked, w_in, precision=HIGH) + b_in[:, None, :])
    hidden = low_back(low(jax.nn.gelu(pre, approximate=False)))
    expert_out = jnp.einsum('ecf,efd->ecd', hidden, w_down, precision=HIGH) + b_down[:, None, :]
    expert_out = low_back(low(expert_out))
    returned = jnp.zeros((total + 1, D), expert_out.dtype).at[table.reshape(-1)].add(expert_out.reshape(-1, D))
    return first_residual_input + returned[:total].reshape(input_tokens.shape)

def reference(hidden_in, out_grad, norm_gain_pair, norm_bias_pair, w_qkv, qv_bias, w_out, out_bias, w_in_exp, b_in_exp, w_out_exp, b_out_exp, expert_ids, doc_lengths, pad_mask):
    doc_ends = jnp.cumsum(doc_lengths, axis=1).astype(jnp.int32)
    positions = jnp.arange(ROW, dtype=jnp.int32)
    doc_ids = lax.optimization_barrier(jnp.sum((positions[None, :, None] >= doc_ends[:, None, :]).astype(jnp.int32), axis=2)).astype(jnp.int32)
    flat_ids = expert_ids.reshape(-1).astype(jnp.int32)
    total = flat_ids.shape[0]
    capacity = N_SEQ * N_BATCH * CAP
    expert_range = jnp.arange(EXPERTS, dtype=jnp.int32)
    counts = lax.optimization_barrier(jnp.sum((flat_ids[None, :] == expert_range[:, None]).astype(jnp.int32), axis=1)).astype(jnp.int32)
    starts = (jnp.cumsum(counts) - counts).astype(jnp.int32)
    order = jnp.argsort(flat_ids, stable=True).astype(jnp.int32)
    slots = jnp.arange(capacity, dtype=jnp.int32)
    spots = jnp.clip(starts[:, None] + slots[None, :], 0, total - 1).astype(jnp.int32)
    table = jnp.where(slots[None, :] < counts[:, None], order[spots], total).astype(jnp.int32)
    floats = (hidden_in.astype(jnp.float32), norm_gain_pair, norm_bias_pair, w_qkv.astype(jnp.float32), qv_bias, w_out.astype(jnp.float32), out_bias, w_in_exp.astype(jnp.float32), b_in_exp, w_out_exp.astype(jnp.float32), b_out_exp)

    def closed(*params):
        return forward(*params, doc_ids, pad_mask, table)
    result, pullback = jax.vjp(closed, *floats)
    grads = pullback(out_grad.astype(jnp.float32))
    return (result.astype(jnp.bfloat16), grads[0].astype(jnp.bfloat16), grads[1], grads[2], grads[3], grads[4], grads[5], grads[6], grads[7], grads[8], grads[9], grads[10])
```

```python
import math

import jax
import jax.numpy as jnp
import numpy as np
from jax import lax
from jax.experimental import pallas as pl
from jax.experimental.pallas import tpu as pltpu
from jax.sharding import PartitionSpec as P

D = 1024
HEADS = 16
HEAD_DIM = 64
EXP_DEV = 2


EPS = 1e-05
NEG = -1e30
BIG = 1e30
F32 = jnp.float32
BF16 = jnp.bfloat16
VMEM_LIMIT = 56 * 1024 * 1024


def dot_nn(a, b):
    return lax.dot_general(a, b, (((1,), (0,)), ((), ())), preferred_element_type=F32)


def dot_nt(a, b):
    return lax.dot_general(a, b, (((1,), (1,)), ((), ())), preferred_element_type=F32)


def dot_tn(a, b):
    return lax.dot_general(a, b, (((0,), (0,)), ((), ())), preferred_element_type=F32)


def normed_rows(values):
    centre = values - jnp.mean(values, axis=-1, keepdims=True)
    spread = jnp.mean(centre * centre, axis=-1, keepdims=True)
    inv_std = lax.rsqrt(spread + EPS)
    return centre * inv_std, inv_std


def whole(shape):
    return pl.BlockSpec(shape, lambda *_: (0,) * len(shape))


def params(**more):
    return pltpu.CompilerParams(vmem_limit_bytes=VMEM_LIMIT, **more)


def iota(shape, axis):
    return lax.broadcasted_iota(jnp.int32, shape, axis)


def running_sums(values):
    upto = jnp.arange(values.shape[0])[:, None] >= jnp.arange(values.shape[0])[None, :]
    return jnp.sum(jnp.where(upto, values[None, :], 0), axis=1)


def layer_normalize(values, gain, shift):
    centre = values - jnp.mean(values, axis=-1, keepdims=True)
    spread = jnp.mean(centre * centre, axis=-1, keepdims=True)
    inv_std = lax.rsqrt(spread + EPS)
    normed = centre * inv_std
    return (normed * gain + shift, normed, inv_std)


def norm_backward_pass(grads, normed, inv_std, gain):
    scaled = grads * gain
    first_mean = jnp.mean(scaled, axis=-1, keepdims=True)
    second_mean = jnp.mean(scaled * normed, axis=-1, keepdims=True)
    return (
        inv_std * (scaled - first_mean - normed * second_mean),
        jnp.sum(grads * normed, axis=0),
        jnp.sum(grads, axis=0),
    )


def doc_of(positions, doc_ends):
    return jnp.sum((positions[:, None] >= doc_ends[None, :]).astype(jnp.int32), axis=1)


def allowed_pairs(q_pos, q_doc, k_pos, k_doc, k_pad):
    same_doc = q_doc[:, None] == k_doc[None, :]
    before = k_pos[None, :] <= q_pos[:, None]
    usable = (k_pad[None, :] == 1) | (k_pos[None, :] == q_pos[:, None])
    return same_doc & before & usable


def over_blocks(step_fn, totals, arrays, first_row):
    row_count = arrays[0].shape[0]
    block_rows = math.gcd(row_count, 512)

    def advance(current, block_index):
        pieces = tuple(
            (
                lax.dynamic_slice_in_dim(member, block_index * block_rows, block_rows, 0)
                for member in arrays
            )
        )
        return (step_fn(current, pieces, first_row + block_index * block_rows), None)

    result, _ = lax.scan(advance, totals, jnp.arange(row_count // block_rows, dtype=jnp.int32))
    return result


def key_grads(
    query_h, dout_h, lse_rows, delta_rows, q_pos, q_doc, key_h, value_h, k_pos, k_doc, k_pad
):
    allowed = allowed_pairs(q_pos, q_doc, k_pos, k_doc, k_pad)
    scores = jnp.einsum("qhd,khd->hqk", query_h, key_h, preferred_element_type=jnp.float32)
    probs = jnp.where(allowed[None], jnp.exp(scores - lse_rows.T[:, :, None]), 0.0)
    dprobs = jnp.einsum("qhd,khd->hqk", dout_h, value_h, preferred_element_type=jnp.float32)
    dscores = (probs * (dprobs - delta_rows.T[:, :, None])).astype(jnp.bfloat16)
    grad_keys = jnp.einsum("hqk,qhd->khd", dscores, query_h, preferred_element_type=jnp.float32)
    grad_values = jnp.einsum(
        "hqk,qhd->khd", probs.astype(jnp.bfloat16), dout_h, preferred_element_type=jnp.float32
    )
    return (grad_keys, grad_values)


def gelu_exact(values):
    return jax.nn.gelu(values, approximate=False)


def local(
    hidden_in,
    out_grad,
    norm_gain_pair,
    norm_bias_pair,
    w_qkv,
    qv_bias,
    w_out,
    out_bias,
    w_in_exp,
    b_in_exp,
    w_out_exp,
    b_out_exp,
    expert_ids,
    doc_lengths,
    pad_mask,
):
    tok_rows = hidden_in.shape[1]
    seq_count = lax.axis_size("seq")
    experts_all = EXP_DEV * seq_count
    capacity = max(2, 3 * tok_rows // (2 * experts_all))
    scale = HEAD_DIM ** (-0.5)
    input_tokens = hidden_in[0].astype(jnp.float32)
    first_normalized, first_centred_scaled, first_inverse_deviation = layer_normalize(
        input_tokens, norm_gain_pair[0], norm_bias_pair[0]
    )
    h_one = first_normalized.astype(jnp.bfloat16)
    mixed = jnp.dot(h_one, w_qkv, preferred_element_type=jnp.float32)
    queries = ((mixed[:, :D] + qv_bias[0]) * scale).astype(jnp.bfloat16)
    keys_vals = jnp.concatenate(
        [mixed[:, D : 2 * D], mixed[:, 2 * D :] + qv_bias[1][None, :]], axis=1
    ).astype(jnp.bfloat16)
    query_h = queries.reshape(tok_rows, HEADS, HEAD_DIM)
    q_pos = lax.axis_index("seq") * tok_rows + jnp.arange(tok_rows, dtype=jnp.int32)
    doc_ends = running_sums(doc_lengths[0])
    q_doc = doc_of(q_pos, doc_ends)
    key_pad = pad_mask[0]

    def split_keys(pieces, first_row):
        block_kv, block_pad = pieces
        row_count = block_kv.shape[0]
        key_h = block_kv[:, :D].reshape(row_count, HEADS, HEAD_DIM)
        value_h = block_kv[:, D:].reshape(row_count, HEADS, HEAD_DIM)
        k_pos = first_row + jnp.arange(row_count, dtype=jnp.int32)
        allowed = allowed_pairs(q_pos, q_doc, k_pos, doc_of(k_pos, doc_ends), block_pad)
        scores = jnp.einsum("thd,khd->htk", query_h, key_h, preferred_element_type=jnp.float32)
        return (key_h, value_h, allowed, jnp.where(allowed[None], scores, NEG))

    def stats_step(current, pieces, first_row):
        _, _, allowed, scores = split_keys(pieces, first_row)
        top_now, mass_now = current
        new_top = jnp.maximum(top_now, jnp.max(scores, axis=-1))
        weights = jnp.where(allowed[None], jnp.exp(scores - new_top[:, :, None]), 0.0)
        return (new_top, mass_now * jnp.exp(top_now - new_top) + jnp.sum(weights, axis=-1))

    def output_step(current, pieces, first_row):
        _, value_h, allowed, scores = split_keys(pieces, first_row)
        probs = jnp.where(allowed[None], jnp.exp(scores - log_mass[:, :, None]), 0.0).astype(
            jnp.bfloat16
        )
        return current + jnp.einsum(
            "htk,khd->thd", probs, value_h, preferred_element_type=jnp.float32
        )

    def dquery_step(current, pieces, first_row):
        key_h, value_h, allowed, scores = split_keys(pieces, first_row)
        probs = jnp.where(allowed[None], jnp.exp(scores - log_mass[:, :, None]), 0.0)
        dprobs = jnp.einsum("thd,khd->htk", dout_h, value_h, preferred_element_type=jnp.float32)
        dscores = (probs * (dprobs - delta[:, :, None])).astype(jnp.bfloat16)
        return current + jnp.einsum(
            "htk,khd->thd", dscores, key_h, preferred_element_type=jnp.float32
        )

    head_zeros = jnp.zeros((tok_rows, HEADS, HEAD_DIM), jnp.float32)
    init_stats = (
        jnp.full((HEADS, tok_rows), NEG, jnp.float32),
        jnp.zeros((HEADS, tok_rows), jnp.float32),
    )
    all_kv, all_pad = (
        lax.all_gather(keys_vals, "seq", axis=0, tiled=True),
        lax.all_gather(key_pad, "seq", axis=0, tiled=True),
    )

    def run_keys(step_fn, totals):
        return over_blocks(step_fn, totals, (all_kv, all_pad), 0)

    top_all, mass_all = run_keys(stats_step, init_stats)
    log_mass = top_all + jnp.log(mass_all)
    attended = run_keys(output_step, head_zeros)
    attended_b = attended.reshape(tok_rows, D).astype(jnp.bfloat16)
    branch = jnp.dot(attended_b, w_out, preferred_element_type=jnp.float32) + out_bias
    first_residual_input = input_tokens + branch
    second_normalized, second_centred_scaled, second_inverse_deviation = layer_normalize(
        first_residual_input, norm_gain_pair[1], norm_bias_pair[1]
    )
    x_two = second_normalized.astype(jnp.bfloat16)
    token_ids = expert_ids[0, :, 0]
    earlier = jnp.arange(tok_rows)[None, :] < jnp.arange(tok_rows)[:, None]
    ranks = jnp.sum(((token_ids[:, None] == token_ids[None, :]) & earlier).astype(jnp.int32), axis=1)
    target = token_ids * capacity + ranks
    dispatch = (
        jnp.arange(experts_all * capacity, dtype=jnp.int32)[:, None] == target[None, :]
    ).astype(jnp.bfloat16)
    sent_rows = (
        jnp.dot(dispatch, x_two, preferred_element_type=jnp.float32)
        .astype(jnp.bfloat16)
        .reshape(seq_count, EXP_DEV, capacity, D)
    )
    rows_all = lax.all_gather(
        lax.all_to_all(sent_rows, "seq", split_axis=0, concat_axis=0, tiled=True),
        "batch",
        axis=0,
        tiled=True,
    )
    pre_act = (
        jnp.einsum("recd,edf->recf", rows_all, w_in_exp, preferred_element_type=jnp.float32)
        + b_in_exp[None, :, None, :]
    )
    hidden = gelu_exact(pre_act).astype(jnp.bfloat16)
    part_sums = jnp.einsum("recf,efd->recd", hidden, w_out_exp, preferred_element_type=jnp.float32)
    summed = lax.psum_scatter(
        part_sums.astype(jnp.bfloat16), "batch", scatter_dimension=0, tiled=True
    ).astype(jnp.float32)
    produced = (summed + b_out_exp[None, :, None, :]).astype(jnp.bfloat16)
    returned = lax.all_to_all(produced, "seq", split_axis=0, concat_axis=0, tiled=True)
    expert_rows = jnp.einsum(
        "st,sd->td",
        dispatch,
        returned.reshape(experts_all * capacity, D),
        preferred_element_type=jnp.float32,
    )
    output = (first_residual_input + expert_rows).astype(jnp.bfloat16)
    dout = out_grad[0].astype(jnp.float32)
    sent_grads = (
        jnp.dot(dispatch, out_grad[0], preferred_element_type=jnp.float32)
        .astype(jnp.bfloat16)
        .reshape(seq_count, EXP_DEV, capacity, D)
    )
    arrived_rows, arrived_grads = (
        lax.all_to_all(sent_rows, "seq", split_axis=0, concat_axis=0, tiled=True),
        lax.all_to_all(sent_grads, "seq", split_axis=0, concat_axis=0, tiled=True),
    )
    rows_all, grads_all = (
        lax.all_gather(arrived_rows, "batch", axis=0, tiled=True),
        lax.all_gather(arrived_grads, "batch", axis=0, tiled=True),
    )
    pre_act = (
        jnp.einsum("recd,edf->recf", rows_all, w_in_exp, preferred_element_type=jnp.float32)
        + b_in_exp[None, :, None, :]
    )
    hidden_f, gelu_back = jax.vjp(gelu_exact, pre_act)
    hidden_b = hidden_f.astype(jnp.bfloat16)
    dhidden = jnp.einsum(
        "recd,efd->recf", grads_all, w_out_exp, preferred_element_type=jnp.float32
    ).astype(jnp.bfloat16)
    dpre = gelu_back(dhidden.astype(jnp.float32))[0].astype(jnp.bfloat16)
    grad_w_out_exp = jnp.einsum(
        "recf,recd->efd", hidden_b, grads_all, preferred_element_type=jnp.float32
    )
    grad_b_out_exp = jnp.sum(grads_all, axis=(0, 2), dtype=jnp.float32)
    grad_w_in_exp = jnp.einsum("recd,recf->edf", rows_all, dpre, preferred_element_type=jnp.float32)
    grad_b_in_exp = jnp.sum(dpre, axis=(0, 2), dtype=jnp.float32)
    drows = jnp.einsum("recf,edf->recd", dpre, w_in_exp, preferred_element_type=jnp.float32)
    drows_sum = lax.psum_scatter(
        drows.astype(jnp.bfloat16), "batch", scatter_dimension=0, tiled=True
    )
    drows_home = lax.all_to_all(drows_sum, "seq", split_axis=0, concat_axis=0, tiled=True)
    second_residual_gradient = jnp.einsum(
        "st,sd->td",
        dispatch,
        drows_home.reshape(experts_all * capacity, D),
        preferred_element_type=jnp.float32,
    )
    second_norm_gradient, second_gain_gradient, second_shift_gradient = norm_backward_pass(
        second_residual_gradient, second_centred_scaled, second_inverse_deviation, norm_gain_pair[1]
    )
    d_one = dout + second_norm_gradient
    d_one_b = d_one.astype(jnp.bfloat16)
    grad_w_out = jnp.einsum("td,te->de", attended_b, d_one_b, preferred_element_type=jnp.float32)
    grad_out_bias = jnp.sum(d_one, axis=0)
    dout_b = jnp.einsum("te,de->td", d_one_b, w_out, preferred_element_type=jnp.float32).astype(
        jnp.bfloat16
    )
    dout_h = dout_b.reshape(tok_rows, HEADS, HEAD_DIM)
    delta = jnp.einsum("thd,thd->ht", dout_h.astype(jnp.float32), attended)
    dquery = run_keys(dquery_step, head_zeros)
    lse_rows = log_mass.T
    delta_rows = delta.T
    block_rows = math.gcd(tok_rows * lax.axis_size("seq"), 512)

    def one_block(block_index):
        first_key = block_index * block_rows
        block_kv = lax.dynamic_slice_in_dim(all_kv, first_key, block_rows, 0)
        block_pad = lax.dynamic_slice_in_dim(all_pad, first_key, block_rows, 0)
        k_pos = first_key + jnp.arange(block_rows, dtype=jnp.int32)
        grad_k, grad_v = key_grads(
            query_h,
            dout_h,
            lse_rows,
            delta_rows,
            q_pos,
            q_doc,
            block_kv[:, :D].reshape(block_rows, HEADS, HEAD_DIM),
            block_kv[:, D:].reshape(block_rows, HEADS, HEAD_DIM),
            k_pos,
            doc_of(k_pos, doc_ends),
            block_pad,
        )
        return jnp.concatenate(
            [grad_k.reshape(block_rows, D), grad_v.reshape(block_rows, D)], axis=1
        )

    blocks = lax.map(
        one_block, jnp.arange(tok_rows * lax.axis_size("seq") // block_rows, dtype=jnp.int32)
    )
    key_terms = lax.psum_scatter(
        blocks.reshape(tok_rows * lax.axis_size("seq"), 2 * D).astype(jnp.bfloat16),
        "seq",
        scatter_dimension=0,
        tiled=True,
    )
    dq_b = dquery.reshape(tok_rows, D).astype(jnp.bfloat16)
    dmixed = jnp.concatenate([dq_b * scale, key_terms], axis=1)
    grad_w_qkv = jnp.einsum("td,te->de", h_one, dmixed, preferred_element_type=jnp.float32)
    first_hidden_gradient = jnp.einsum(
        "te,de->td", dmixed, w_qkv, preferred_element_type=jnp.float32
    )
    first_norm_gradient, first_gain_gradient, first_shift_gradient = norm_backward_pass(
        first_hidden_gradient, first_centred_scaled, first_inverse_deviation, norm_gain_pair[0]
    )
    input_grad = (d_one + first_norm_gradient).astype(jnp.bfloat16)
    grad_q_bias = jnp.sum(dmixed[:, :D], axis=0, dtype=jnp.float32)
    grad_v_bias = jnp.sum(key_terms[:, D:], axis=0, dtype=jnp.float32)
    small_grads = jnp.stack(
        [
            first_gain_gradient,
            second_gain_gradient,
            first_shift_gradient,
            second_shift_gradient,
            grad_q_bias,
            grad_v_bias,
            grad_out_bias,
        ]
    )
    shared_qkv, shared_out, shared_small = (
        lax.psum_scatter(grad_w_qkv, ("seq", "batch"), scatter_dimension=0, tiled=True),
        lax.psum_scatter(grad_w_out, ("seq", "batch"), scatter_dimension=0, tiled=True),
        lax.psum_scatter(small_grads, ("seq", "batch"), scatter_dimension=1, tiled=True),
    )
    return (
        output[None],
        input_grad[None],
        shared_small[0:2],
        shared_small[2:4],
        shared_qkv,
        shared_small[4:6],
        shared_out,
        shared_small[6],
        grad_w_in_exp,
        grad_b_in_exp,
        grad_w_out_exp,
        grad_b_out_exp,
    )


def qkv_kernel(n, T, cap, sc, *refs):
    chunks = refs[: n - 1]
    last_a, last_b = refs[n - 1 : n + 1]
    wq, wk, wv, qvb, gain, bias, docs = refs[n + 1 : n + 8]
    h_out, qkv_out, kaug_out, code_out, sel_out = refs[n + 8 : n + 13]
    buf, w, sems = refs[n + 13 :]
    split = last_a.shape[0]
    copies = [
        pltpu.make_async_copy(ref, buf.at[c], sems.at[c]) for c, ref in enumerate(chunks)
    ]
    copies.append(
        pltpu.make_async_copy(last_a, buf.at[n - 1, pl.ds(0, split)], sems.at[n - 1])
    )
    copies.append(
        pltpu.make_async_copy(
            last_b, buf.at[n - 1, pl.ds(split, last_b.shape[0])], sems.at[n]
        )
    )
    for copy in copies:
        copy.start()
    w[:, 0:128] = wq[...]
    w[:, 128:256] = wk[...]
    w[:, 256:384] = wv[...]
    for copy in copies:
        copy.wait()
    me = sc[n]
    g_row, b_row = gain[...], bias[...]

    def one_chunk(c, carry):
        src = sc[c]

        def norm_part(r, carry2):
            rows = pl.ds(pl.multiple_of(r * 64, 64), 64)
            vhat, _ = normed_rows(buf[c, rows, :].astype(F32))
            h_out[c, rows, :] = (vhat * g_row + b_row).astype(BF16)
            return carry2

        lax.fori_loop(0, T // 64, norm_part, 0)
        rows = pl.ds(pl.multiple_of(src * T, T), T)
        mixed = dot_nn(h_out[c], w[...])
        q = (mixed[:, 0:128] + qvb[0:1, :]) * (HEAD_DIM**-0.5)
        qkv_out[rows, 0:128] = q.astype(BF16)
        qkv_out[rows, 128:256] = mixed[:, 128:256].astype(BF16)
        qkv_out[rows, 256:384] = (mixed[:, 256:384] + qvb[1:2, :]).astype(BF16)
        codes = buf[c, pl.ds(T, 16), :].astype(F32)
        id_row = codes[0:1, 0:T]
        pad_row = codes[0:1, T : 2 * T]
        id_col = jnp.transpose(jnp.broadcast_to(id_row, (128, T)))
        pad_col = jnp.transpose(jnp.broadcast_to(pad_row, (128, T)))
        same = jnp.where(
            (id_col[:, 0:1] == id_row) & (iota((T, T), 0) < iota((T, T), 1)), 1.0, 0.0
        )
        rank_row = jnp.sum(same, axis=0, keepdims=True)
        rank_col = jnp.transpose(jnp.broadcast_to(rank_row, (128, T)))
        lane = iota((T, 128), 1)
        pos = (iota((T, 128), 0) + src * T).astype(F32)
        doc = jnp.where((pos >= docs[0:1, :]) & (pos < docs[1:2, :]), 1.0, 0.0)
        aug = jnp.where(lane < 8, doc, 0.0)
        aug = jnp.where(lane == 8, 1.0 - pad_col, aug)
        aug = jnp.where(lane == 16, id_col, aug)
        aug = jnp.where(lane == 17, rank_col, aug)
        kaug_out[rows, :] = aug.astype(BF16)
        slot = (id_row * cap + rank_row).astype(jnp.int32)
        half = lax.rem(src, 2) * cap
        code_out[src] = (id_row * (2 * cap) + rank_row).astype(jnp.int32) + half
        pick = jnp.where(
            slot == iota((EXP_DEV * cap, T), 0) + me * (EXP_DEV * cap), 1.0, 0.0
        ).astype(BF16)
        chosen = dot_nn(pick, buf[c, pl.ds(0, T), :])
        for e in range(EXP_DEV):
            at = pl.multiple_of(e * n * cap + src * cap, 8)
            sel_out[pl.ds(at, cap), :] = chosen[e * cap : (e + 1) * cap]
        return carry

    lax.fori_loop(0, n, one_chunk, 0)


def qkv_call(n, T, cap, sc, chunks, w_qkv, qv_bias, gain, bias, docs):
    rows = T + 16
    anywhere = pl.BlockSpec(memory_space=pl.ANY)
    in_specs = [anywhere] * (n + 1) + [
        pl.BlockSpec((D, 128), lambda i, sc: (0, sc[n])),
        pl.BlockSpec((D, 128), lambda i, sc: (0, n + sc[n])),
        pl.BlockSpec((D, 128), lambda i, sc: (0, 2 * n + sc[n])),
        pl.BlockSpec((2, 128), lambda i, sc: (0, sc[n])),
        whole((1, D)),
        whole((1, D)),
        whole((2, 128)),
    ]
    shapes = [
        ((n, T, D), BF16),
        ((n * T, 384), BF16),
        ((n * T, 128), BF16),
        ((n, 1, T), jnp.int32),
        ((EXP_DEV * n * cap, D), F32),
    ]
    return pl.pallas_call(
        lambda *a: qkv_kernel(n, T, cap, *a),
        grid_spec=pltpu.PrefetchScalarGridSpec(
            num_scalar_prefetch=1,
            grid=(1,),
            in_specs=in_specs,
            out_specs=[whole(s) for s, _ in shapes],
            scratch_shapes=[
                pltpu.VMEM((n, rows, D), BF16),
                pltpu.VMEM((D, 384), BF16),
                pltpu.SemaphoreType.DMA((n + 1,)),
            ],
        ),
        out_shape=[jax.ShapeDtypeStruct(s, t) for s, t in shapes],
        compiler_params=params(),
        name="qkv",
    )(sc, *chunks, w_qkv, w_qkv, w_qkv, qv_bias, gain, bias, docs)


def head_split(n, T, qkv, kaug, qa, ka):
    def part(r, carry):
        rows = pl.ds(pl.multiple_of(r * T, T), T)
        lane = iota((T, 128), 1)
        q = qkv[rows, 0:128].astype(F32)
        feature = kaug[rows, :].astype(F32)
        extra = jnp.where(
            lane < 8, (feature - 1.0) * BIG, jnp.where(lane == 8, -BIG, 0.0)
        ).astype(BF16)
        qa[0, rows, 0:128] = jnp.where(lane < HEAD_DIM, q, 0.0).astype(BF16)
        qa[1, rows, 0:128] = jnp.where(lane >= HEAD_DIM, q, 0.0).astype(BF16)
        qa[0, rows, 128:256] = extra
        qa[1, rows, 128:256] = extra
        ka[rows, 0:128] = qkv[rows, 128:256]
        ka[rows, 128:256] = kaug[rows, :]
        return carry

    lax.fori_loop(0, n, part, 0)


def diag_parts(T, kaug_rows):
    lane = iota((T, 128), 1)
    feature = kaug_rows.astype(F32)
    unpadded = jnp.where(lane == 8, 0.0, feature).astype(BF16)
    k_at, q_at = iota((T, T), 0), iota((T, T), 1)
    padded = feature[:, 8:9] > 0.5
    allowed = ((k_at < q_at) & jnp.logical_not(padded)) | (k_at == q_at)
    return unpadded, allowed


def attn_fwd_kernel(
    n, T, cap, qkv, kaug, code, att_out, o_out, lse_out, qa, ka, vt, att, acc
):
    head_split(n, T, qkv, kaug, qa, ka)

    def turn(r, carry):
        rows = pl.ds(pl.multiple_of(r * T, T), T)
        vt[r] = jnp.transpose(qkv[rows, 256:384].astype(F32)).astype(BF16)
        return carry

    lax.fori_loop(0, n, turn, 0)
    halves = [slice(h * HEAD_DIM, (h + 1) * HEAD_DIM) for h in range(2)]

    def query_block(i, carry):
        rows = pl.ds(pl.multiple_of(i * T, T), T)
        unpadded, allowed = diag_parts(T, kaug[rows, :])
        kd = jnp.concatenate([qkv[rows, 128:256], unpadded], axis=1)
        state = []
        for h in range(2):
            s = jnp.where(allowed, dot_nt(kd, qa[h, rows, :]), NEG)
            top = jnp.max(s, axis=0, keepdims=True)
            p = jnp.exp(s - top)
            state += [top, jnp.sum(p, axis=0, keepdims=True)]
            acc[halves[h], :] = dot_nn(vt[i, halves[h], :], p.astype(BF16))

        def key_block(j, state):
            cols = pl.ds(pl.multiple_of(j * T, T), T)
            out = []
            for h in range(2):
                top, mass = state[2 * h : 2 * h + 2]
                s = dot_nt(ka[cols, :], qa[h, rows, :])
                new_top = jnp.maximum(top, jnp.max(s, axis=0, keepdims=True))
                fade = jnp.exp(top - new_top)
                p = jnp.exp(s - new_top)
                out += [new_top, mass * fade + jnp.sum(p, axis=0, keepdims=True)]
                acc[halves[h], :] = acc[halves[h], :] * fade + dot_nn(
                    vt[j, halves[h], :], p.astype(BF16)
                )
            return tuple(out)

        top0, mass0, top1, mass1 = lax.fori_loop(0, i, key_block, tuple(state))
        lse_out[0, i] = top0 + jnp.log(mass0)
        lse_out[1, i] = top1 + jnp.log(mass1)
        o = jnp.transpose(
            jnp.concatenate([acc[halves[0], :] / mass0, acc[halves[1], :] / mass1], axis=0)
        )
        o_out[rows, :] = o
        att[rows, :] = o.astype(BF16)
        return carry

    lax.fori_loop(0, n, query_block, 0)
    slots = n * EXP_DEV * 2 * cap

    def pair(p, carry):
        codes = jnp.concatenate([code[2 * p], code[2 * p + 1]], axis=1)
        pick = jnp.where(codes == iota((slots, 2 * T), 0), 1.0, 0.0).astype(BF16)
        chosen = dot_nn(pick, att[pl.ds(pl.multiple_of(p * 2 * T, 2 * T), 2 * T), :]).astype(
            BF16
        )
        for k in range(n):
            for e in range(EXP_DEV):
                first = (k * EXP_DEV + e) * 2 * cap
                at = pl.multiple_of(e * n * cap + p * 2 * cap, 16)
                att_out[k, pl.ds(at, 2 * cap), :] = chosen[first : first + 2 * cap]
        return carry

    lax.fori_loop(0, n // 2, pair, 0)


def attn_fwd_call(n, T, cap, qkv, kaug, code):
    row = n * T
    shapes = [
        ((n, EXP_DEV * n * cap, 128), BF16),
        ((row, 128), F32),
        ((2, n, 1, T), F32),
    ]
    return pl.pallas_call(
        lambda *a: attn_fwd_kernel(n, T, cap, *a),
        out_shape=[jax.ShapeDtypeStruct(s, t) for s, t in shapes],
        in_specs=[pl.BlockSpec(memory_space=pltpu.VMEM)] * 3,
        out_specs=[pl.BlockSpec(memory_space=pltpu.VMEM)] * 3,
        scratch_shapes=[
            pltpu.VMEM((2, row, 256), BF16),
            pltpu.VMEM((row, 256), BF16),
            pltpu.VMEM((n, 128, T), BF16),
            pltpu.VMEM((row, 128), BF16),
            pltpu.VMEM((128, T), F32),
        ],
        compiler_params=params(),
        name="attn_fwd",
    )(qkv, kaug, code)


def attn_bwd_kernel(
    n, T, cap, qkv, kaug, lse, o_ref, datt, dm_out, ka_h, qa, v_h, kt, do, delta, dqt, dka, dva
):
    halves = [slice(h * HEAD_DIM, (h + 1) * HEAD_DIM) for h in range(2)]
    slots = n * EXP_DEV * 2 * cap

    def pair(p, carry):
        rows = pl.ds(pl.multiple_of(p * 2 * T, 2 * T), 2 * T)
        feature = kaug[rows, :].astype(F32)
        at_row = iota((2 * T, 1), 0)
        half = jnp.where(at_row >= T, float(cap), 0.0)
        code = (feature[:, 16:17] * (2 * cap) + feature[:, 17:18] + half).astype(jnp.int32)
        pick = jnp.where(code == iota((2 * T, slots), 1), 1.0, 0.0).astype(BF16)
        parts = []
        for k in range(n):
            for e in range(EXP_DEV):
                at = pl.multiple_of(e * n * cap + p * 2 * cap, 16)
                parts.append(datt[k, pl.ds(at, 2 * cap), :])
        got = dot_nn(pick, jnp.concatenate(parts, axis=0))
        do[rows, :] = got.astype(BF16)
        prod = jnp.transpose(got * o_ref[rows, :])
        for h in range(2):
            total = jnp.sum(prod[halves[h], :], axis=0, keepdims=True)
            delta[h, 2 * p] = total[:, 0:T]
            delta[h, 2 * p + 1] = total[:, T : 2 * T]
        return carry

    lax.fori_loop(0, n // 2, pair, 0)

    def prepare(r, carry):
        rows = pl.ds(pl.multiple_of(r * T, T), T)
        lane = iota((T, 128), 1)
        feature = kaug[rows, :].astype(F32)
        extra = jnp.where(
            lane < 8, (feature - 1.0) * BIG, jnp.where(lane == 8, -BIG, 0.0)
        ).astype(BF16)
        qa[rows, 0:128] = qkv[rows, 0:128]
        qa[rows, 128:256] = extra
        k = qkv[rows, 128:256].astype(F32)
        v = qkv[rows, 256:384].astype(F32)
        for h in range(2):
            mine = (lane < HEAD_DIM) == (h == 0)
            ka_h[h, rows, 0:128] = jnp.where(mine, k, 0.0).astype(BF16)
            ka_h[h, rows, 128:256] = kaug[rows, :]
            v_h[h, rows, :] = jnp.where(mine, v, 0.0).astype(BF16)
        kt[r] = jnp.transpose(k).astype(BF16)
        dqt[r] = jnp.zeros((128, T), F32)
        return carry

    lax.fori_loop(0, n, prepare, 0)

    def tile(h, i, j, rows, key_rows, mask):
        s = dot_nt(key_rows, qa[rows, :])
        if mask is not None:
            s = jnp.where(mask, s, NEG)
        p = jnp.exp(s - lse[h, i])
        dp = dot_nt(v_h[h, pl.ds(pl.multiple_of(j * T, T), T), :], do[rows, :])
        ds = (p * (dp - delta[h, i])).astype(BF16)
        dv = dot_nn(p.astype(BF16), do[rows, :])
        dk = dot_nn(ds, qa[rows, 0:128])
        dqt[i, halves[h], :] += dot_nn(kt[j, halves[h], :], ds)
        return dk, dv

    def key_block(j, carry):
        cols = pl.ds(pl.multiple_of(j * T, T), T)
        unpadded, allowed = diag_parts(T, kaug[cols, :])
        for h in range(2):
            kd = jnp.concatenate([ka_h[h, cols, 0:128], unpadded], axis=1)
            dka[h], dva[h] = tile(h, j, j, cols, kd, allowed)

        def query_block(i, carry2):
            rows = pl.ds(pl.multiple_of(i * T, T), T)
            for h in range(2):
                dk, dv = tile(h, i, j, rows, ka_h[h, cols, :], None)
                dka[h] += dk
                dva[h] += dv
            return carry2

        lax.fori_loop(j + 1, n, query_block, 0)
        lane = iota((T, 128), 1)
        dm_out[j, :, 128:256] = jnp.where(lane < HEAD_DIM, dka[0], dka[1]).astype(BF16)
        dm_out[j, :, 256:384] = jnp.where(lane < HEAD_DIM, dva[0], dva[1]).astype(BF16)
        return carry

    lax.fori_loop(0, n, key_block, 0)

    def finish(i, carry):
        dq = jnp.transpose(dqt[i]).astype(BF16).astype(F32)
        dm_out[i, :, 0:128] = (dq * (HEAD_DIM**-0.5)).astype(BF16)
        return carry

    lax.fori_loop(0, n, finish, 0)


def attn_bwd_call(n, T, cap, qkv, kaug, lse, o, datt):
    row = n * T
    return pl.pallas_call(
        lambda *a: attn_bwd_kernel(n, T, cap, *a),
        out_shape=jax.ShapeDtypeStruct((n, T, 384), BF16),
        in_specs=[pl.BlockSpec(memory_space=pltpu.VMEM)] * 5,
        out_specs=pl.BlockSpec(memory_space=pltpu.VMEM),
        scratch_shapes=[
            pltpu.VMEM((2, row, 256), BF16),
            pltpu.VMEM((row, 256), BF16),
            pltpu.VMEM((2, row, 128), BF16),
            pltpu.VMEM((n, 128, T), BF16),
            pltpu.VMEM((row, 128), BF16),
            pltpu.VMEM((2, n, 1, T), F32),
            pltpu.VMEM((n, 128, T), F32),
            pltpu.VMEM((2, T, 128), F32),
            pltpu.VMEM((2, T, 128), F32),
        ],
        compiler_params=params(),
        name="attn_bwd",
    )(qkv, kaug, lse, o, datt)


def owner_fwd_kernel(n, att_in, w_out, sel, out_bias, gain, bias, x_two, x_one, att_b):
    for k in range(n):
        att_b[:, k * 128 : (k + 1) * 128] = att_in[k]
    branch = dot_nn(att_b[...], w_out[...]) + out_bias[...]
    x = sel[...] + branch
    x_one[...] = x
    vhat, _ = normed_rows(x)
    x_two[...] = (vhat * gain[...] + bias[...]).astype(BF16)


def owner_fwd_call(n, att_in, w_out, sel, out_bias, gain, bias):
    slots = sel.shape[0]
    block = 128
    rows = pl.BlockSpec((block, D), lambda i: (i, 0))
    return pl.pallas_call(
        lambda *a: owner_fwd_kernel(n, *a),
        grid=(slots // block,),
        in_specs=[
            pl.BlockSpec((n, block, 128), lambda i: (0, i, 0)),
            whole((D, D)),
            rows,
            whole((1, D)),
            whole((1, D)),
            whole((1, D)),
        ],
        out_specs=[rows, rows, rows],
        out_shape=[
            jax.ShapeDtypeStruct((slots, D), BF16),
            jax.ShapeDtypeStruct((slots, D), F32),
            jax.ShapeDtypeStruct((slots, D), BF16),
        ],
        compiler_params=params(),
        name="owner_fwd",
    )(att_in, w_out, sel, out_bias, gain, bias)


def owner_bwd_kernel(n, part_a, part_b, x_one, og, gain, w_out, datt, d_one_b, small):
    u = (part_a[...].astype(F32) + part_b[...].astype(F32)).astype(BF16).astype(F32)
    vhat, inv_std = normed_rows(x_one[...])
    scaled = u * gain[...]
    first = jnp.mean(scaled, axis=-1, keepdims=True)
    second = jnp.mean(scaled * vhat, axis=-1, keepdims=True)
    d_one = og[...].astype(F32) + inv_std * (scaled - first - vhat * second)
    d_b = d_one.astype(BF16)
    d_one_b[...] = d_b
    back = dot_nt(d_b, w_out[...]).astype(BF16)
    for k in range(n):
        datt[k] = back[:, k * 128 : (k + 1) * 128]

    @pl.when(pl.program_id(0) == 0)
    def _():
        small[...] = jnp.zeros_like(small)

    small[0:1, :] += jnp.sum(u * vhat, axis=0, keepdims=True)
    small[1:2, :] += jnp.sum(u, axis=0, keepdims=True)
    small[2:3, :] += jnp.sum(d_one, axis=0, keepdims=True)


def owner_bwd_call(n, part_a, part_b, x_one, og, gain, w_out):
    slots = x_one.shape[0]
    block = 128
    rows = pl.BlockSpec((block, D), lambda i: (i, 0))
    return pl.pallas_call(
        lambda *a: owner_bwd_kernel(n, *a),
        grid=(slots // block,),
        in_specs=[rows, rows, rows, rows, whole((1, D)), whole((D, D))],
        out_specs=[
            pl.BlockSpec((n, block, 128), lambda i: (0, i, 0)),
            rows,
            whole((8, D)),
        ],
        out_shape=[
            jax.ShapeDtypeStruct((n, slots, 128), BF16),
            jax.ShapeDtypeStruct((slots, D), BF16),
            jax.ShapeDtypeStruct((8, D), F32),
        ],
        compiler_params=params(),
        name="owner_bwd",
    )(part_a, part_b, x_one, og, gain, w_out)


def expert_kernel(
    nb, rows, steps, sc, *refs
):
    x_parts, g_parts = refs[:nb], refs[nb : 2 * nb]
    w_in, b_in, w_out = refs[2 * nb : 2 * nb + 3]
    hidden_out, dpre_out, keep, send, grad_b = refs[2 * nb + 3 : 2 * nb + 8]
    xs, gs, total = refs[2 * nb + 8 :]
    f = pl.program_id(1)

    @pl.when(f == 0)
    def _():
        for k in range(nb):
            xs[k * rows : (k + 1) * rows, :] = x_parts[k][...]
            gs[k * rows : (k + 1) * rows, :] = g_parts[k][0]
        total[...] = jnp.zeros_like(total)

    pre = dot_nn(xs[...], w_in[0]) + b_in[0]
    cdf = 0.5 * (1.0 + lax.erf(pre * (0.5**0.5)))
    slope = cdf + pre * jnp.exp(-0.5 * pre * pre) * ((2.0 * math.pi) ** -0.5)
    hidden_out[0] = (pre * cdf).astype(BF16)
    dhidden = dot_nt(gs[...], w_out[0]).astype(BF16).astype(F32)
    dpre = (dhidden * slope).astype(BF16)
    dpre_out[0] = dpre
    grad_b[0] = jnp.sum(dpre.astype(F32), axis=0, keepdims=True)
    total[...] += dot_nt(dpre, w_in[0])

    @pl.when(f == steps - 1)
    def _():
        for y in range(2):
            keep[y] = total[2 * y * rows : (2 * y + 1) * rows, :].astype(BF16)
            send[y] = total[(2 * y + 1) * rows : (2 * y + 2) * rows, :].astype(BF16)


def expert_call(sc, x_parts, g_all, w_in, b_in, w_out):
    nb = len(x_parts)
    rows = x_parts[0].shape[0] // EXP_DEV
    ff = w_in.shape[2]
    width = min(256, ff)
    steps = ff // width
    g_specs = [
        pl.BlockSpec((1, rows, D), lambda e, f, sc, k=k: (sc[0] ^ k, e, 0)) for k in range(nb)
    ]
    two = pl.BlockSpec((2, rows, D), lambda e, f, sc: (0, e, 0))
    act = pl.BlockSpec((1, nb * rows, width), lambda e, f, sc: (e, 0, f))
    return pl.pallas_call(
        lambda *a: expert_kernel(nb, rows, steps, *a),
        grid_spec=pltpu.PrefetchScalarGridSpec(
            num_scalar_prefetch=1,
            grid=(EXP_DEV, steps),
            in_specs=[pl.BlockSpec((rows, D), lambda e, f, sc: (e, 0))] * nb
            + g_specs
            + [
                pl.BlockSpec((1, D, width), lambda e, f, sc: (e, 0, f)),
                pl.BlockSpec((1, 1, width), lambda e, f, sc: (e, 0, f)),
                pl.BlockSpec((1, width, D), lambda e, f, sc: (e, f, 0)),
            ],
            out_specs=[act, act, two, two, pl.BlockSpec((1, 1, width), lambda e, f, sc: (e, 0, f))],
            scratch_shapes=[
                pltpu.VMEM((nb * rows, D), BF16),
                pltpu.VMEM((nb * rows, D), BF16),
                pltpu.VMEM((nb * rows, D), F32),
            ],
        ),
        out_shape=[
            jax.ShapeDtypeStruct((EXP_DEV, nb * rows, ff), BF16),
            jax.ShapeDtypeStruct((EXP_DEV, nb * rows, ff), BF16),
            jax.ShapeDtypeStruct((2, EXP_DEV * rows, D), BF16),
            jax.ShapeDtypeStruct((2, EXP_DEV * rows, D), BF16),
            jax.ShapeDtypeStruct((EXP_DEV, 1, ff), F32),
        ],
        compiler_params=params(),
        name="expert_main",
    )(sc, *x_parts, *([g_all] * nb), w_in, b_in[:, None, :], w_out)


def expert_out_kernel(rows, hidden, w_out, keep, send):
    total = dot_nn(hidden[0], w_out[0]).astype(BF16)
    for y in range(2):
        keep[y] = total[2 * y * rows : (2 * y + 1) * rows, :]
        send[y] = total[(2 * y + 1) * rows : (2 * y + 2) * rows, :]


def expert_out_call(hidden, w_out, nb):
    rows = hidden.shape[1] // nb
    ff = hidden.shape[2]
    two = pl.BlockSpec((2, rows, D), lambda e: (0, e, 0))
    return pl.pallas_call(
        lambda *a: expert_out_kernel(rows, *a),
        grid=(EXP_DEV,),
        in_specs=[
            pl.BlockSpec((1, nb * rows, ff), lambda e: (e, 0, 0)),
            pl.BlockSpec((1, ff, D), lambda e: (e, 0, 0)),
        ],
        out_specs=[two, two],
        out_shape=[jax.ShapeDtypeStruct((2, EXP_DEV * rows, D), BF16)] * 2,
        compiler_params=params(),
        name="expert_out",
    )(hidden, w_out)


def expert_grad_kernel(nb, rows, sc, *refs):
    x_parts, g_parts = refs[:nb], refs[nb : 2 * nb]
    hidden, dpre = refs[2 * nb : 2 * nb + 2]
    grad_in, grad_out, grad_b = refs[2 * nb + 2 : 2 * nb + 5]
    xs, gs = refs[2 * nb + 5 :]

    @pl.when(pl.program_id(1) == 0)
    def _():
        sums = []
        for k in range(nb):
            xs[k * rows : (k + 1) * rows, :] = x_parts[k][...]
            gs[k * rows : (k + 1) * rows, :] = g_parts[k][0]
            sums.append(jnp.sum(g_parts[k][0].astype(F32), axis=0, keepdims=True))
        grad_b[0] = (sums[0] + sums[1]) + (sums[2] + sums[3])

    grad_in[0] = dot_tn(xs[...], dpre[0])
    grad_out[0] = dot_tn(hidden[0], gs[...])


def expert_grad_call(sc, x_parts, g_all, hidden, dpre):
    nb = len(x_parts)
    rows = x_parts[0].shape[0] // EXP_DEV
    ff = hidden.shape[2]
    width = min(256, ff)
    g_specs = [
        pl.BlockSpec((1, rows, D), lambda e, f, sc, k=k: (sc[0] ^ k, e, 0)) for k in range(nb)
    ]
    act = pl.BlockSpec((1, nb * rows, width), lambda e, f, sc: (e, 0, f))
    return pl.pallas_call(
        lambda *a: expert_grad_kernel(nb, rows, *a),
        grid_spec=pltpu.PrefetchScalarGridSpec(
            num_scalar_prefetch=1,
            grid=(EXP_DEV, ff // width),
            in_specs=[pl.BlockSpec((rows, D), lambda e, f, sc: (e, 0))] * nb
            + g_specs
            + [act, act],
            out_specs=[
                pl.BlockSpec((1, D, width), lambda e, f, sc: (e, 0, f)),
                pl.BlockSpec((1, width, D), lambda e, f, sc: (e, f, 0)),
                pl.BlockSpec((1, 1, D), lambda e, f, sc: (e, 0, 0)),
            ],
            scratch_shapes=[pltpu.VMEM((nb * rows, D), BF16)] * 2,
        ),
        out_shape=[
            jax.ShapeDtypeStruct((EXP_DEV, D, ff), F32),
            jax.ShapeDtypeStruct((EXP_DEV, ff, D), F32),
            jax.ShapeDtypeStruct((EXP_DEV, 1, D), F32),
        ],
        compiler_params=params(),
        name="expert_grads",
    )(sc, *x_parts, *([g_all] * nb), hidden, dpre)


def qkv_grad_kernel(n, nb, T, sc, h, dm, aux, keep, send, total):
    me_b = sc[n + 1]

    def add(c, carry):
        total[...] += dot_tn(dm[sc[c]], h[c])
        return carry

    total[...] = jnp.zeros_like(total)
    lax.fori_loop(0, n, add, 0)
    col_sum = jnp.zeros((1, 384), F32)
    for r in range(n):
        col_sum = col_sum + jnp.sum(dm[r].astype(F32), axis=0, keepdims=True)
    width = D // n
    size = width // nb
    top = iota((16, 384), 0)
    for r in range(n):
        part = jnp.transpose(total[:, r * width : (r + 1) * width])
        for k in range(nb):
            bb = me_b ^ k
            rows = jnp.zeros((size, 384), F32)
            for c in range(nb):
                rows = jnp.where(bb == c, part[c * size : (c + 1) * size, :], rows)
            extra = jnp.where(
                top == 0, col_sum, jnp.where(top == 1, aux[r * nb + bb], 0.0)
            )
            to = keep if k % 2 == 0 else send
            to[k // 2, r, 0:size, :] = rows.astype(BF16)
            to[k // 2, r, size : size + 16, :] = extra.astype(BF16)


def qkv_grad_call(n, nb, T, sc, h, dm, aux):
    size = D // (n * nb)
    shape = (2, n, size + 16, 384)
    return pl.pallas_call(
        lambda *a: qkv_grad_kernel(n, nb, T, *a),
        grid_spec=pltpu.PrefetchScalarGridSpec(
            num_scalar_prefetch=1,
            grid=(1,),
            in_specs=[whole((n, T, D)), whole((n, T, 384)), whole((n * nb, 1, 384))],
            out_specs=[whole(shape), whole(shape)],
            scratch_shapes=[pltpu.VMEM((384, D), F32)],
        ),
        out_shape=[jax.ShapeDtypeStruct(shape, BF16)] * 2,
        compiler_params=params(),
        name="qkv_grad",
    )(sc, h, dm, aux)


def scatter_rows(cap, slots, kaug, values):
    feature = kaug.astype(F32)
    code = (feature[:, 16:17] * cap + feature[:, 17:18]).astype(jnp.int32)
    pick = jnp.where(code == iota((feature.shape[0], slots), 1), 1.0, 0.0).astype(BF16)
    return dot_nn(pick, values)


def input_grad_kernel(n, T, cap, sc, dm, w_qkv, hidden, d_ret, kaug, gain, out, full):
    for k in range(n):
        for part in range(3):
            full[:, part * D + k * 128 : part * D + (k + 1) * 128] = dm[
                k, :, part * 128 : (part + 1) * 128
            ]
    u = dot_nt(full[...], w_qkv[...])
    vhat, inv_std = normed_rows(hidden[...].astype(F32))
    scaled = u * gain[...]
    first = jnp.mean(scaled, axis=-1, keepdims=True)
    second = jnp.mean(scaled * vhat, axis=-1, keepdims=True)
    d_one = scatter_rows(cap, d_ret.shape[0], kaug[...], d_ret[...])
    out[...] = (d_one + inv_std * (scaled - first - vhat * second)).astype(BF16)


def input_grad_call(n, T, cap, sc, dm, w_qkv, hidden, d_ret, kaug, gain):
    slots = d_ret.shape[0]
    return pl.pallas_call(
        lambda *a: input_grad_kernel(n, T, cap, *a),
        grid_spec=pltpu.PrefetchScalarGridSpec(
            num_scalar_prefetch=1,
            grid=(1,),
            in_specs=[
                whole((n, T, 384)),
                whole((D, 3 * D)),
                whole((T, D)),
                whole((slots, D)),
                pl.BlockSpec((T, 128), lambda i, sc: (sc[n], 0)),
                whole((1, D)),
            ],
            out_specs=whole((T, D)),
            scratch_shapes=[pltpu.VMEM((T, 3 * D), BF16)],
        ),
        out_shape=jax.ShapeDtypeStruct((T, D), BF16),
        compiler_params=params(),
        name="input_grad",
    )(sc, dm, w_qkv, hidden, d_ret, kaug, gain)


def output_kernel(cap, sc, ret, kaug, out):
    out[...] = scatter_rows(cap, ret.shape[0], kaug[...], ret[...]).astype(BF16)


def output_call(n, T, cap, sc, ret, kaug):
    return pl.pallas_call(
        lambda *a: output_kernel(cap, *a),
        grid_spec=pltpu.PrefetchScalarGridSpec(
            num_scalar_prefetch=1,
            grid=(1,),
            in_specs=[
                whole(ret.shape),
                pl.BlockSpec((T, 128), lambda i, sc: (sc[n], 0)),
            ],
            out_specs=whole((T, D)),
        ),
        out_shape=jax.ShapeDtypeStruct((T, D), BF16),
        compiler_params=params(),
        name="output_rows",
    )(sc, ret, kaug)


def final_kernel(n, nb, sc, got, w_rows, gb, gw, gains, biases, qvb, outb, s_rows, w_full):
    size = D // (n * nb)
    me, me_b = sc[n], sc[n + 1]
    smalls = jnp.zeros((1, 384), F32)
    s_rows[...] = jnp.zeros_like(s_rows)
    for k in range(n):
        tile = got[k].astype(F32)
        for part in range(3):
            cols = slice(part * D + k * 128, part * D + (k + 1) * 128)
            w_full[:, cols] = tile[0:size, part * 128 : (part + 1) * 128]
            s_rows[0:1, cols] = tile[size : size + 1, part * 128 : (part + 1) * 128]
        smalls = smalls + tile[size + 1 : size + 2, :]
    gw[...] = w_full[...]
    weights = w_rows[...].astype(F32)
    high = lax.Precision.HIGHEST
    nt = (((1,), (1,)), ((), ()))
    bias_one = lax.dot_general(s_rows[...], weights, nt, precision=high, preferred_element_type=F32)[0:1]
    both = lax.dot_general(
        jnp.ones((8, 3 * D), F32), weights * w_full[...], nt, precision=high, preferred_element_type=F32
    )[0:1]
    gains[0:1, :] = (both - gb[1:2, :] * bias_one) / gb[0:1, :]
    gains[1:2, :] = smalls[:, 0:size]
    biases[0:1, :] = bias_one
    biases[1:2, :] = smalls[:, size : 2 * size]
    outb[...] = smalls[:, 2 * size : 3 * size]
    own = got[me, size : size + 16, :].astype(F32)[0:1]
    for row, first in ((0, 0), (1, 256)):
        value = jnp.zeros((1, size), F32)
        for c in range(nb):
            value = jnp.where(me_b == c, own[:, first + c * size : first + (c + 1) * size], value)
        qvb[row : row + 1, :] = value


def final_call(n, nb, sc, got, w_qkv, gb):
    size = D // (n * nb)
    shapes = [(size, 3 * D), (2, size), (2, size), (2, size), (1, size)]
    return pl.pallas_call(
        lambda *a: final_kernel(n, nb, *a),
        grid_spec=pltpu.PrefetchScalarGridSpec(
            num_scalar_prefetch=1,
            grid=(1,),
            in_specs=[
                whole((n, size + 16, 384)),
                pl.BlockSpec((size, 3 * D), lambda i, sc: (nb * sc[n] + sc[n + 1], 0)),
                whole((2, size)),
            ],
            out_specs=[whole(s) for s in shapes],
            scratch_shapes=[pltpu.VMEM((8, 3 * D), F32), pltpu.VMEM((size, 3 * D), F32)],
        ),
        out_shape=[jax.ShapeDtypeStruct(s, F32) for s in shapes],
        compiler_params=params(),
        name="final_rows",
    )(sc, got, w_qkv, gb)


def exchange(values, axis, bit):
    size = lax.axis_size(axis)
    return lax.ppermute(values, axis, [(i, i ^ bit) for i in range(size)])


def gather_ring(payload, ring):
    n = len(ring)
    ahead = [(ring[i], ring[(i + 1) % n]) for i in range(n)]
    back = [(ring[i], ring[i - 1]) for i in range(n)]
    split = -(-payload.shape[0] // 32) * 16
    chunks = [payload]
    left = right = payload
    for _ in range(n // 2 - 1):
        left = lax.ppermute(left, "seq", ahead)
        right = lax.ppermute(right, "seq", back)
        chunks += [left, right]
    return chunks + [
        lax.ppermute(left[:split], "seq", ahead),
        lax.ppermute(right[split:], "seq", back),
    ]


def reduce_batch(keep, send):
    got = exchange(send, "batch", 1)
    both = (keep.astype(F32) + got.astype(F32)).astype(BF16)
    return both[0], exchange(both[1], "batch", 2)


def local_by_heads(
    hidden_in,
    out_grad,
    norm_gain_pair,
    norm_bias_pair,
    w_qkv,
    qv_bias,
    w_out,
    out_bias,
    w_in_exp,
    b_in_exp,
    w_out_exp,
    b_out_exp,
    expert_ids,
    doc_lengths,
    pad_mask,
):
    T = hidden_in.shape[1]
    n, nb = lax.axis_size("seq"), lax.axis_size("batch")
    experts = EXP_DEV * n
    cap = max(2, 3 * T // (2 * experts))
    s, b = lax.axis_index("seq"), lax.axis_index("batch")
    ring = [*range(0, n, 2), *range(n - 1, 0, -2)]
    place = [ring.index(i) for i in range(n)]
    order = [0]
    for step in range(1, n // 2):
        order += [-step, step]
    order += [n // 2]
    table = np.array(
        [[ring[(place[i] + o) % n] for o in order] + [i] for i in range(n)], np.int32
    )
    sc = jnp.concatenate(
        [lax.dynamic_index_in_dim(jnp.asarray(table), s, 0, keepdims=False), b[None].astype(jnp.int32)]
    )
    sc_b = b[None].astype(jnp.int32)
    hidden = hidden_in[0]
    ids = expert_ids[0, :, 0]
    codes = jnp.concatenate([ids, pad_mask[0], jnp.zeros((D - 2 * T,), jnp.int32)]).astype(BF16)
    codes = jnp.where(jnp.arange(16)[:, None] == 0, codes[None, :], jnp.zeros((), BF16))
    payload = jnp.concatenate([hidden, codes], axis=0)
    chunks = gather_ring(payload, ring)

    count = doc_lengths.shape[1]
    at = jnp.arange(128)
    ends = jnp.sum(
        jnp.where(jnp.arange(count)[:, None] <= at[None, :], doc_lengths[0][:, None], 0), axis=0
    )
    starts = jnp.sum(
        jnp.where(jnp.arange(count)[:, None] < at[None, :], doc_lengths[0][:, None], 0), axis=0
    )
    docs = jnp.stack([starts, ends]).astype(F32)
    gain_rows = [norm_gain_pair[i : i + 1] for i in range(2)]
    bias_rows = [norm_bias_pair[i : i + 1] for i in range(2)]

    h_one, qkv, kaug, code, sel = qkv_call(
        n, T, cap, sc, chunks, w_qkv, qv_bias, gain_rows[0], bias_rows[0], docs
    )
    same = (ids[:, None] == ids[None, :]) & (jnp.arange(T)[:, None] < jnp.arange(T)[None, :])
    ranks = jnp.sum(same.astype(jnp.int32), axis=0)
    slot = ids * cap + ranks
    dispatch = (jnp.arange(experts * cap)[:, None] == slot[None, :]).astype(BF16)
    sent_grads = dot_nn(dispatch, out_grad[0]).astype(BF16).reshape(n, EXP_DEV * cap, D)
    grads = lax.all_to_all(sent_grads, "seq", split_axis=0, concat_axis=0, tiled=True)
    grads = grads.reshape(n, EXP_DEV, cap, D).transpose(1, 0, 2, 3).reshape(experts * cap, D)
    g_all = lax.all_gather(grads, "batch", axis=0, tiled=False)

    att_out, o, lse = attn_fwd_call(n, T, cap, qkv, kaug, code)
    att_in = lax.all_to_all(att_out, "seq", split_axis=0, concat_axis=0, tiled=True)
    x_two, x_one, att_b = owner_fwd_call(
        n, att_in, w_out, sel, out_bias[None], gain_rows[1], bias_rows[1]
    )
    x_core = exchange(x_two, "batch", 1)
    x_y = exchange(x_two, "batch", 2)
    x_far = exchange(x_y, "batch", 1)
    x_parts = [x_two, x_core, x_y, x_far]
    hidden_act, dpre, keep, send, grad_b_in = expert_call(
        sc_b, x_parts, g_all, w_in_exp, b_in_exp, w_out_exp
    )
    part_a, part_b = reduce_batch(keep, send)
    datt_out, d_one_b, small = owner_bwd_call(
        n, part_a, part_b, x_one, grads, gain_rows[1], w_out
    )
    datt = lax.all_to_all(datt_out, "seq", split_axis=0, concat_axis=0, tiled=True)

    keep_f, send_f = expert_out_call(hidden_act, w_out_exp, nb)
    out_a, out_b = reduce_batch(keep_f, send_f)
    expert_rows = (
        (out_a.astype(F32) + out_b.astype(F32)).reshape(EXP_DEV, n * cap, D) + b_out_exp[:, None, :]
    ).astype(BF16)
    out_rows = (x_one.reshape(EXP_DEV, n * cap, D) + expert_rows.astype(F32)).astype(BF16)

    def homeward(rows):
        rows = rows.reshape(EXP_DEV, n, cap, D).transpose(1, 0, 2, 3)
        rows = lax.all_to_all(rows, "seq", split_axis=0, concat_axis=0, tiled=True)
        return rows.reshape(experts * cap, D)

    d_ret = homeward(d_one_b)
    out_ret = homeward(out_rows)
    output = output_call(n, T, cap, sc, out_ret, kaug)

    grad_w_in, grad_w_out_exp, grad_b_out = expert_grad_call(sc_b, x_parts, g_all, hidden_act, dpre)
    size = D // (n * nb)
    grad_w_out = dot_tn(att_b, d_one_b).astype(BF16).reshape(n, nb, size, D)
    grad_w_out = lax.psum_scatter(grad_w_out, "batch", scatter_dimension=1, tiled=False)
    grad_w_out = lax.psum_scatter(grad_w_out, "seq", scatter_dimension=0, tiled=False).astype(F32)

    dm = attn_bwd_call(n, T, cap, qkv, kaug, lse, o, datt)
    dm_own = lax.all_to_all(dm, "seq", split_axis=0, concat_axis=0, tiled=True)
    aux = small[:3].reshape(3, n * nb, size).transpose(1, 0, 2).reshape(n * nb, 1, 3 * size)
    aux = jnp.pad(aux, ((0, 0), (0, 0), (0, 384 - 3 * size)))
    keep_w, send_w = qkv_grad_call(n, nb, T, sc, h_one, dm, aux)
    w_a, w_b = reduce_batch(keep_w, send_w)
    w_sum = (w_a.astype(F32) + w_b.astype(F32)).astype(BF16)
    w_got = lax.all_to_all(w_sum, "seq", split_axis=0, concat_axis=0, tiled=True)
    own = (s * nb + b) * size
    gb = jnp.stack(
        [
            lax.dynamic_slice_in_dim(norm_gain_pair[0], own, size, 0),
            lax.dynamic_slice_in_dim(norm_bias_pair[0], own, size, 0),
        ]
    )
    gw_qkv, g_gains, g_biases, g_qvb, g_outb = final_call(n, nb, sc, w_got, w_qkv, gb)
    input_grad = input_grad_call(n, T, cap, sc, dm_own, w_qkv, hidden, d_ret, kaug, gain_rows[0])
    return (
        output[None],
        input_grad[None],
        g_gains,
        g_biases,
        gw_qkv,
        g_qvb,
        grad_w_out,
        g_outb[0],
        grad_w_in,
        grad_b_in[:, 0],
        grad_w_out_exp,
        grad_b_out[:, 0],
    )


def solution(mesh):
    n, nb = mesh.shape["seq"], mesh.shape["batch"]
    by_heads = HEADS * HEAD_DIM == 128 * n and nb == 4
    return jax.shard_map(
        local_by_heads if by_heads else local,
        mesh=mesh,
        in_specs=(
            P("batch", "seq", None),
            P("batch", "seq", None),
            P(),
            P(),
            P(),
            P(),
            P(),
            P(),
            P("seq", None, "batch"),
            P("seq", "batch"),
            P("seq", "batch", None),
            P("seq", None),
            P("batch", "seq", None),
            P("batch", None),
            P("batch", "seq"),
        ),
        out_specs=(
            P("batch", "seq", None),
            P("batch", "seq", None),
            P(None, ("seq", "batch")),
            P(None, ("seq", "batch")),
            P(("seq", "batch"), None),
            P(None, ("seq", "batch")),
            P(("seq", "batch"), None),
            P(("seq", "batch")),
            P("seq", None, "batch"),
            P("seq", "batch"),
            P("seq", "batch", None),
            P("seq", None),
        ),
        check_vma=False,
    )
```

```python
import math

import jax
import jax.numpy as jnp
import numpy as np
from jax import lax
from jax.experimental import pallas as pl
from jax.experimental.pallas import tpu as pltpu
from jax.sharding import PartitionSpec as P

D = 1024
HEADS = 16
HEAD_DIM = 64
EXP_DEV = 2


EPS = 1e-05
NEG = -1e30
BIG = 1e30
F32 = jnp.float32
BF16 = jnp.bfloat16
VMEM_LIMIT = 56 * 1024 * 1024


def dot_nn(a, b):
    return lax.dot_general(a, b, (((1,), (0,)), ((), ())), preferred_element_type=F32)


def dot_nt(a, b):
    return lax.dot_general(a, b, (((1,), (1,)), ((), ())), preferred_element_type=F32)


def dot_tn(a, b):
    return lax.dot_general(a, b, (((0,), (0,)), ((), ())), preferred_element_type=F32)


def normed_rows(values):
    centre = values - jnp.mean(values, axis=-1, keepdims=True)
    spread = jnp.mean(centre * centre, axis=-1, keepdims=True)
    inv_std = lax.rsqrt(spread + EPS)
    return centre * inv_std, inv_std


def whole(shape):
    return pl.BlockSpec(shape, lambda *_: (0,) * len(shape))


def params(**more):
    return pltpu.CompilerParams(vmem_limit_bytes=VMEM_LIMIT, **more)


def iota(shape, axis):
    return lax.broadcasted_iota(jnp.int32, shape, axis)


def running_sums(values):
    upto = jnp.arange(values.shape[0])[:, None] >= jnp.arange(values.shape[0])[None, :]
    return jnp.sum(jnp.where(upto, values[None, :], 0), axis=1)


def layer_normalize(values, gain, shift):
    centre = values - jnp.mean(values, axis=-1, keepdims=True)
    spread = jnp.mean(centre * centre, axis=-1, keepdims=True)
    inv_std = lax.rsqrt(spread + EPS)
    normed = centre * inv_std
    return (normed * gain + shift, normed, inv_std)


def norm_backward_pass(grads, normed, inv_std, gain):
    scaled = grads * gain
    first_mean = jnp.mean(scaled, axis=-1, keepdims=True)
    second_mean = jnp.mean(scaled * normed, axis=-1, keepdims=True)
    return (
        inv_std * (scaled - first_mean - normed * second_mean),
        jnp.sum(grads * normed, axis=0),
        jnp.sum(grads, axis=0),
    )


def doc_of(positions, doc_ends):
    return jnp.sum((positions[:, None] >= doc_ends[None, :]).astype(jnp.int32), axis=1)


def allowed_pairs(q_pos, q_doc, k_pos, k_doc, k_pad):
    same_doc = q_doc[:, None] == k_doc[None, :]
    before = k_pos[None, :] <= q_pos[:, None]
    usable = (k_pad[None, :] == 1) | (k_pos[None, :] == q_pos[:, None])
    return same_doc & before & usable


def over_blocks(step_fn, totals, arrays, first_row):
    row_count = arrays[0].shape[0]
    block_rows = math.gcd(row_count, 512)

    def advance(current, block_index):
        pieces = tuple(
            (
                lax.dynamic_slice_in_dim(member, block_index * block_rows, block_rows, 0)
                for member in arrays
            )
        )
        return (step_fn(current, pieces, first_row + block_index * block_rows), None)

    result, _ = lax.scan(advance, totals, jnp.arange(row_count // block_rows, dtype=jnp.int32))
    return result


def key_grads(
    query_h, dout_h, lse_rows, delta_rows, q_pos, q_doc, key_h, value_h, k_pos, k_doc, k_pad
):
    allowed = allowed_pairs(q_pos, q_doc, k_pos, k_doc, k_pad)
    scores = jnp.einsum("qhd,khd->hqk", query_h, key_h, preferred_element_type=jnp.float32)
    probs = jnp.where(allowed[None], jnp.exp(scores - lse_rows.T[:, :, None]), 0.0)
    dprobs = jnp.einsum("qhd,khd->hqk", dout_h, value_h, preferred_element_type=jnp.float32)
    dscores = (probs * (dprobs - delta_rows.T[:, :, None])).astype(jnp.bfloat16)
    grad_keys = jnp.einsum("hqk,qhd->khd", dscores, query_h, preferred_element_type=jnp.float32)
    grad_values = jnp.einsum(
        "hqk,qhd->khd", probs.astype(jnp.bfloat16), dout_h, preferred_element_type=jnp.float32
    )
    return (grad_keys, grad_values)


def gelu_exact(values):
    return jax.nn.gelu(values, approximate=False)


def local(
    hidden_in,
    out_grad,
    norm_gain_pair,
    norm_bias_pair,
    w_qkv,
    qv_bias,
    w_out,
    out_bias,
    w_in_exp,
    b_in_exp,
    w_out_exp,
    b_out_exp,
    expert_ids,
    doc_lengths,
    pad_mask,
):
    tok_rows = hidden_in.shape[1]
    seq_count = lax.axis_size("seq")
    experts_all = EXP_DEV * seq_count
    capacity = max(2, 3 * tok_rows // (2 * experts_all))
    scale = HEAD_DIM ** (-0.5)
    input_tokens = hidden_in[0].astype(jnp.float32)
    first_normalized, first_centred_scaled, first_inverse_deviation = layer_normalize(
        input_tokens, norm_gain_pair[0], norm_bias_pair[0]
    )
    h_one = first_normalized.astype(jnp.bfloat16)
    mixed = jnp.dot(h_one, w_qkv, preferred_element_type=jnp.float32)
    queries = ((mixed[:, :D] + qv_bias[0]) * scale).astype(jnp.bfloat16)
    keys_vals = jnp.concatenate(
        [mixed[:, D : 2 * D], mixed[:, 2 * D :] + qv_bias[1][None, :]], axis=1
    ).astype(jnp.bfloat16)
    query_h = queries.reshape(tok_rows, HEADS, HEAD_DIM)
    q_pos = lax.axis_index("seq") * tok_rows + jnp.arange(tok_rows, dtype=jnp.int32)
    doc_ends = running_sums(doc_lengths[0])
    q_doc = doc_of(q_pos, doc_ends)
    key_pad = pad_mask[0]

    def split_keys(pieces, first_row):
        block_kv, block_pad = pieces
        row_count = block_kv.shape[0]
        key_h = block_kv[:, :D].reshape(row_count, HEADS, HEAD_DIM)
        value_h = block_kv[:, D:].reshape(row_count, HEADS, HEAD_DIM)
        k_pos = first_row + jnp.arange(row_count, dtype=jnp.int32)
        allowed = allowed_pairs(q_pos, q_doc, k_pos, doc_of(k_pos, doc_ends), block_pad)
        scores = jnp.einsum("thd,khd->htk", query_h, key_h, preferred_element_type=jnp.float32)
        return (key_h, value_h, allowed, jnp.where(allowed[None], scores, NEG))

    def stats_step(current, pieces, first_row):
        _, _, allowed, scores = split_keys(pieces, first_row)
        top_now, mass_now = current
        new_top = jnp.maximum(top_now, jnp.max(scores, axis=-1))
        weights = jnp.where(allowed[None], jnp.exp(scores - new_top[:, :, None]), 0.0)
        return (new_top, mass_now * jnp.exp(top_now - new_top) + jnp.sum(weights, axis=-1))

    def output_step(current, pieces, first_row):
        _, value_h, allowed, scores = split_keys(pieces, first_row)
        probs = jnp.where(allowed[None], jnp.exp(scores - log_mass[:, :, None]), 0.0).astype(
            jnp.bfloat16
        )
        return current + jnp.einsum(
            "htk,khd->thd", probs, value_h, preferred_element_type=jnp.float32
        )

    def dquery_step(current, pieces, first_row):
        key_h, value_h, allowed, scores = split_keys(pieces, first_row)
        probs = jnp.where(allowed[None], jnp.exp(scores - log_mass[:, :, None]), 0.0)
        dprobs = jnp.einsum("thd,khd->htk", dout_h, value_h, preferred_element_type=jnp.float32)
        dscores = (probs * (dprobs - delta[:, :, None])).astype(jnp.bfloat16)
        return current + jnp.einsum(
            "htk,khd->thd", dscores, key_h, preferred_element_type=jnp.float32
        )

    head_zeros = jnp.zeros((tok_rows, HEADS, HEAD_DIM), jnp.float32)
    init_stats = (
        jnp.full((HEADS, tok_rows), NEG, jnp.float32),
        jnp.zeros((HEADS, tok_rows), jnp.float32),
    )
    all_kv, all_pad = (
        lax.all_gather(keys_vals, "seq", axis=0, tiled=True),
        lax.all_gather(key_pad, "seq", axis=0, tiled=True),
    )

    def run_keys(step_fn, totals):
        return over_blocks(step_fn, totals, (all_kv, all_pad), 0)

    top_all, mass_all = run_keys(stats_step, init_stats)
    log_mass = top_all + jnp.log(mass_all)
    attended = run_keys(output_step, head_zeros)
    attended_b = attended.reshape(tok_rows, D).astype(jnp.bfloat16)
    branch = jnp.dot(attended_b, w_out, preferred_element_type=jnp.float32) + out_bias
    first_residual_input = input_tokens + branch
    second_normalized, second_centred_scaled, second_inverse_deviation = layer_normalize(
        first_residual_input, norm_gain_pair[1], norm_bias_pair[1]
    )
    x_two = second_normalized.astype(jnp.bfloat16)
    token_ids = expert_ids[0, :, 0]
    earlier = jnp.arange(tok_rows)[None, :] < jnp.arange(tok_rows)[:, None]
    ranks = jnp.sum(((token_ids[:, None] == token_ids[None, :]) & earlier).astype(jnp.int32), axis=1)
    target = token_ids * capacity + ranks
    dispatch = (
        jnp.arange(experts_all * capacity, dtype=jnp.int32)[:, None] == target[None, :]
    ).astype(jnp.bfloat16)
    sent_rows = (
        jnp.dot(dispatch, x_two, preferred_element_type=jnp.float32)
        .astype(jnp.bfloat16)
        .reshape(seq_count, EXP_DEV, capacity, D)
    )
    rows_all = lax.all_gather(
        lax.all_to_all(sent_rows, "seq", split_axis=0, concat_axis=0, tiled=True),
        "batch",
        axis=0,
        tiled=True,
    )
    pre_act = (
        jnp.einsum("recd,edf->recf", rows_all, w_in_exp, preferred_element_type=jnp.float32)
        + b_in_exp[None, :, None, :]
    )
    hidden = gelu_exact(pre_act).astype(jnp.bfloat16)
    part_sums = jnp.einsum("recf,efd->recd", hidden, w_out_exp, preferred_element_type=jnp.float32)
    summed = lax.psum_scatter(
        part_sums.astype(jnp.bfloat16), "batch", scatter_dimension=0, tiled=True
    ).astype(jnp.float32)
    produced = (summed + b_out_exp[None, :, None, :]).astype(jnp.bfloat16)
    returned = lax.all_to_all(produced, "seq", split_axis=0, concat_axis=0, tiled=True)
    expert_rows = jnp.einsum(
        "st,sd->td",
        dispatch,
        returned.reshape(experts_all * capacity, D),
        preferred_element_type=jnp.float32,
    )
    output = (first_residual_input + expert_rows).astype(jnp.bfloat16)
    dout = out_grad[0].astype(jnp.float32)
    sent_grads = (
        jnp.dot(dispatch, out_grad[0], preferred_element_type=jnp.float32)
        .astype(jnp.bfloat16)
        .reshape(seq_count, EXP_DEV, capacity, D)
    )
    arrived_rows, arrived_grads = (
        lax.all_to_all(sent_rows, "seq", split_axis=0, concat_axis=0, tiled=True),
        lax.all_to_all(sent_grads, "seq", split_axis=0, concat_axis=0, tiled=True),
    )
    rows_all, grads_all = (
        lax.all_gather(arrived_rows, "batch", axis=0, tiled=True),
        lax.all_gather(arrived_grads, "batch", axis=0, tiled=True),
    )
    pre_act = (
        jnp.einsum("recd,edf->recf", rows_all, w_in_exp, preferred_element_type=jnp.float32)
        + b_in_exp[None, :, None, :]
    )
    hidden_f, gelu_back = jax.vjp(gelu_exact, pre_act)
    hidden_b = hidden_f.astype(jnp.bfloat16)
    dhidden = jnp.einsum(
        "recd,efd->recf", grads_all, w_out_exp, preferred_element_type=jnp.float32
    ).astype(jnp.bfloat16)
    dpre = gelu_back(dhidden.astype(jnp.float32))[0].astype(jnp.bfloat16)
    grad_w_out_exp = jnp.einsum(
        "recf,recd->efd", hidden_b, grads_all, preferred_element_type=jnp.float32
    )
    grad_b_out_exp = jnp.sum(grads_all, axis=(0, 2), dtype=jnp.float32)
    grad_w_in_exp = jnp.einsum("recd,recf->edf", rows_all, dpre, preferred_element_type=jnp.float32)
    grad_b_in_exp = jnp.sum(dpre, axis=(0, 2), dtype=jnp.float32)
    drows = jnp.einsum("recf,edf->recd", dpre, w_in_exp, preferred_element_type=jnp.float32)
    drows_sum = lax.psum_scatter(
        drows.astype(jnp.bfloat16), "batch", scatter_dimension=0, tiled=True
    )
    drows_home = lax.all_to_all(drows_sum, "seq", split_axis=0, concat_axis=0, tiled=True)
    second_residual_gradient = jnp.einsum(
        "st,sd->td",
        dispatch,
        drows_home.reshape(experts_all * capacity, D),
        preferred_element_type=jnp.float32,
    )
    second_norm_gradient, second_gain_gradient, second_shift_gradient = norm_backward_pass(
        second_residual_gradient, second_centred_scaled, second_inverse_deviation, norm_gain_pair[1]
    )
    d_one = dout + second_norm_gradient
    d_one_b = d_one.astype(jnp.bfloat16)
    grad_w_out = jnp.einsum("td,te->de", attended_b, d_one_b, preferred_element_type=jnp.float32)
    grad_out_bias = jnp.sum(d_one, axis=0)
    dout_b = jnp.einsum("te,de->td", d_one_b, w_out, preferred_element_type=jnp.float32).astype(
        jnp.bfloat16
    )
    dout_h = dout_b.reshape(tok_rows, HEADS, HEAD_DIM)
    delta = jnp.einsum("thd,thd->ht", dout_h.astype(jnp.float32), attended)
    dquery = run_keys(dquery_step, head_zeros)
    lse_rows = log_mass.T
    delta_rows = delta.T
    block_rows = math.gcd(tok_rows * lax.axis_size("seq"), 512)

    def one_block(block_index):
        first_key = block_index * block_rows
        block_kv = lax.dynamic_slice_in_dim(all_kv, first_key, block_rows, 0)
        block_pad = lax.dynamic_slice_in_dim(all_pad, first_key, block_rows, 0)
        k_pos = first_key + jnp.arange(block_rows, dtype=jnp.int32)
        grad_k, grad_v = key_grads(
            query_h,
            dout_h,
            lse_rows,
            delta_rows,
            q_pos,
            q_doc,
            block_kv[:, :D].reshape(block_rows, HEADS, HEAD_DIM),
            block_kv[:, D:].reshape(block_rows, HEADS, HEAD_DIM),
            k_pos,
            doc_of(k_pos, doc_ends),
            block_pad,
        )
        return jnp.concatenate(
            [grad_k.reshape(block_rows, D), grad_v.reshape(block_rows, D)], axis=1
        )

    blocks = lax.map(
        one_block, jnp.arange(tok_rows * lax.axis_size("seq") // block_rows, dtype=jnp.int32)
    )
    key_terms = lax.psum_scatter(
        blocks.reshape(tok_rows * lax.axis_size("seq"), 2 * D).astype(jnp.bfloat16),
        "seq",
        scatter_dimension=0,
        tiled=True,
    )
    dq_b = dquery.reshape(tok_rows, D).astype(jnp.bfloat16)
    dmixed = jnp.concatenate([dq_b * scale, key_terms], axis=1)
    grad_w_qkv = jnp.einsum("td,te->de", h_one, dmixed, preferred_element_type=jnp.float32)
    first_hidden_gradient = jnp.einsum(
        "te,de->td", dmixed, w_qkv, preferred_element_type=jnp.float32
    )
    first_norm_gradient, first_gain_gradient, first_shift_gradient = norm_backward_pass(
        first_hidden_gradient, first_centred_scaled, first_inverse_deviation, norm_gain_pair[0]
    )
    input_grad = (d_one + first_norm_gradient).astype(jnp.bfloat16)
    grad_q_bias = jnp.sum(dmixed[:, :D], axis=0, dtype=jnp.float32)
    grad_v_bias = jnp.sum(key_terms[:, D:], axis=0, dtype=jnp.float32)
    small_grads = jnp.stack(
        [
            first_gain_gradient,
            second_gain_gradient,
            first_shift_gradient,
            second_shift_gradient,
            grad_q_bias,
            grad_v_bias,
            grad_out_bias,
        ]
    )
    shared_qkv, shared_out, shared_small = (
        lax.psum_scatter(grad_w_qkv, ("seq", "batch"), scatter_dimension=0, tiled=True),
        lax.psum_scatter(grad_w_out, ("seq", "batch"), scatter_dimension=0, tiled=True),
        lax.psum_scatter(small_grads, ("seq", "batch"), scatter_dimension=1, tiled=True),
    )
    return (
        output[None],
        input_grad[None],
        shared_small[0:2],
        shared_small[2:4],
        shared_qkv,
        shared_small[4:6],
        shared_out,
        shared_small[6],
        grad_w_in_exp,
        grad_b_in_exp,
        grad_w_out_exp,
        grad_b_out_exp,
    )


MICROSECOND = 1 << 30


def cost(us):
    return pl.CostEstimate(flops=us * MICROSECOND, bytes_accessed=1 << 20, transcendentals=0)


def qkv_kernel(n, T, cap, block, halves, sc, *refs):
    chunk = refs[:halves]
    wq, wk, wv, qvb, gain, bias, docs = refs[halves : halves + 7]
    h_out, qa_out, ka_out, vt_out, kt_out, v_out, code_out, sel_out = refs[-10:-2]
    buf, w = refs[-2:]
    src, me = sc[block], sc[n]
    first = 0
    for ref in chunk:
        buf[first : first + ref.shape[0], :] = ref[...]
        first += ref.shape[0]
    w[:, 0:128] = wq[...]
    w[:, 128:256] = wk[...]
    w[:, 256:384] = wv[...]
    g_row, b_row = gain[...], bias[...]

    def norm_part(r, carry):
        rows = pl.ds(pl.multiple_of(r * 64, 64), 64)
        vhat, _ = normed_rows(buf[rows, :].astype(F32))
        h_out[0, rows, :] = (vhat * g_row + b_row).astype(BF16)
        return carry

    lax.fori_loop(0, T // 64, norm_part, 0)
    mixed = dot_nn(h_out[0], w[...])
    q = ((mixed[:, 0:128] + qvb[0:1, :]) * (HEAD_DIM**-0.5)).astype(BF16).astype(F32)
    k = mixed[:, 128:256].astype(BF16)
    v = (mixed[:, 256:384] + qvb[1:2, :]).astype(BF16)
    codes = buf[T : T + 16, :].astype(F32)
    id_row = codes[0:1, 0:T]
    pad_row = codes[0:1, T : 2 * T]
    id_col = jnp.transpose(jnp.broadcast_to(id_row, (128, T)))
    pad_col = jnp.transpose(jnp.broadcast_to(pad_row, (128, T)))
    same = jnp.where(
        (id_col[:, 0:1] == id_row) & (iota((T, T), 0) < iota((T, T), 1)), 1.0, 0.0
    )
    rank_row = jnp.sum(same, axis=0, keepdims=True)
    rank_col = jnp.transpose(jnp.broadcast_to(rank_row, (128, T)))
    lane = iota((T, 128), 1)
    pos = (iota((T, 128), 0) + src * T).astype(F32)
    doc = jnp.where((pos >= docs[0:1, :]) & (pos < docs[1:2, :]), 1.0, 0.0)
    aug = jnp.where(lane < 8, doc, 0.0)
    aug = jnp.where(lane == 8, 1.0 - pad_col, aug)
    aug = jnp.where(lane == 16, id_col, aug)
    aug = jnp.where(lane == 17, rank_col, aug)
    extra = jnp.where(lane < 8, (doc - 1.0) * BIG, jnp.where(lane == 8, -BIG, 0.0)).astype(BF16)
    for h in range(2):
        mine = (lane < HEAD_DIM) == (h == 0)
        qa_out[h, :, 0:128] = jnp.where(mine, q, 0.0).astype(BF16)
        qa_out[h, :, 128:256] = extra
    ka_out[:, 0:128] = k
    ka_out[:, 128:256] = aug.astype(BF16)
    v_out[...] = v
    vt_out[0] = jnp.transpose(v.astype(F32)).astype(BF16)
    kt_out[0] = jnp.transpose(k.astype(F32)).astype(BF16)
    slot = (id_row * cap + rank_row).astype(jnp.int32)
    half = lax.rem(src, 2) * cap
    code_out[0] = (id_row * (2 * cap) + rank_row).astype(jnp.int32) + half
    pick = jnp.where(
        slot == iota((EXP_DEV * cap, T), 0) + me * (EXP_DEV * cap), 1.0, 0.0
    ).astype(BF16)
    chosen = dot_nn(pick, buf[0:T, :])
    for e in range(EXP_DEV):
        sel_out[e, 0] = chosen[e * cap : (e + 1) * cap]


def qkv_call(n, T, cap, block, sc, chunk, held, w_qkv, qv_bias, gain, bias, docs):
    rows = T + 16
    in_specs = [whole(part.shape) for part in chunk] + [
        pl.BlockSpec((D, 128), lambda i, sc: (0, sc[n])),
        pl.BlockSpec((D, 128), lambda i, sc: (0, n + sc[n])),
        pl.BlockSpec((D, 128), lambda i, sc: (0, 2 * n + sc[n])),
        pl.BlockSpec((2, 128), lambda i, sc: (0, sc[n])),
        whole((1, D)),
        whole((1, D)),
        whole((2, 128)),
    ]
    shapes = [
        ((n, T, D), BF16),
        ((2, n * T, 256), BF16),
        ((n * T, 256), BF16),
        ((n, 128, T), BF16),
        ((n, 128, T), BF16),
        ((n * T, 128), BF16),
        ((n, 1, T), jnp.int32),
        ((EXP_DEV, n, cap, D), F32),
    ]
    out_specs = [
        pl.BlockSpec((1, T, D), lambda i, sc: (sc[block], 0, 0)),
        pl.BlockSpec((2, T, 256), lambda i, sc: (0, sc[block], 0)),
        pl.BlockSpec((T, 256), lambda i, sc: (sc[block], 0)),
        pl.BlockSpec((1, 128, T), lambda i, sc: (sc[block], 0, 0)),
        pl.BlockSpec((1, 128, T), lambda i, sc: (sc[block], 0, 0)),
        pl.BlockSpec((T, 128), lambda i, sc: (sc[block], 0)),
        pl.BlockSpec((1, 1, T), lambda i, sc: (sc[block], 0, 0)),
        pl.BlockSpec((EXP_DEV, 1, cap, D), lambda i, sc: (0, sc[block], 0, 0)),
    ]
    aliases = {}
    if held is not None:
        aliases = {1 + len(in_specs) + i: i for i in range(len(shapes))}
        in_specs = in_specs + [pl.BlockSpec(memory_space=pl.ANY)] * len(shapes)
    return pl.pallas_call(
        lambda *a: qkv_kernel(n, T, cap, block, len(chunk), *a),
        grid_spec=pltpu.PrefetchScalarGridSpec(
            num_scalar_prefetch=1,
            grid=(1,),
            in_specs=in_specs,
            out_specs=out_specs,
            scratch_shapes=[pltpu.VMEM((rows, D), BF16), pltpu.VMEM((D, 384), BF16)],
        ),
        out_shape=[jax.ShapeDtypeStruct(s, t) for s, t in shapes],
        input_output_aliases=aliases,
        compiler_params=params(),
        cost_estimate=pl.CostEstimate(
            flops=4 * MICROSECOND, bytes_accessed=6 * T * D * 2, transcendentals=0
        ),
        name="qkv",
    )(sc, *chunk, w_qkv, w_qkv, w_qkv, qv_bias, gain, bias, docs, *(held or ()))


HALVES = [slice(h * HEAD_DIM, (h + 1) * HEAD_DIM) for h in range(2)]


def block_rows(i, T):
    return pl.ds(pl.multiple_of(i * T, T), T)


def diag_parts(T, key_rows):
    lane = iota((T, 256), 1)
    values = key_rows.astype(F32)
    unpadded = jnp.where(lane == 136, 0.0, values).astype(BF16)
    k_at, q_at = iota((T, T), 0), iota((T, T), 1)
    padded = values[:, 136:137] > 0.5
    allowed = ((k_at < q_at) & jnp.logical_not(padded)) | (k_at == q_at)
    return unpadded, allowed


def attn_fwd_kernel(n, T, cap, at_tile, diags, pairs, first, last, tiles, qa, ka, vt, *refs):
    if last:
        code, refs = refs[0], refs[1:]
    if first:
        top, mass, acc = refs[:3]
        rest = refs[3:]
    else:
        for old, new in zip(refs[:3], refs[3:6]):
            new[...] = old[...]
        top, mass, acc = refs[3:6]
        rest = refs[6:]

    def diag_tile(i):
        rows = block_rows(i, T)
        kd, allowed = diag_parts(T, ka[rows, :])
        for h in range(2):
            s = jnp.where(allowed, dot_nt(kd, qa[h, rows, :]), NEG)
            best = jnp.max(s, axis=0, keepdims=True)
            p = jnp.exp(s - best)
            top[h, i] = best
            mass[h, i] = jnp.sum(p, axis=0, keepdims=True)
            acc[i, HALVES[h], :] = dot_nn(vt[i, HALVES[h], :], p.astype(BF16))

    def pair_tile(at):
        i, j = tiles[at_tile + 2 * at], tiles[at_tile + 2 * at + 1]
        rows, cols = block_rows(i, T), block_rows(j, T)
        for h in range(2):
            s = dot_nt(ka[cols, :], qa[h, rows, :])
            old = top[h, i]
            best = jnp.maximum(old, jnp.max(s, axis=0, keepdims=True))
            fade = jnp.exp(old - best)
            p = jnp.exp(s - best)
            top[h, i] = best
            mass[h, i] = mass[h, i] * fade + jnp.sum(p, axis=0, keepdims=True)
            acc[i, HALVES[h], :] = acc[i, HALVES[h], :] * fade + dot_nn(
                vt[j, HALVES[h], :], p.astype(BF16)
            )

    def one_diag(r, carry):
        diag_tile(tiles[at_tile + 2 * r])
        return carry

    lax.fori_loop(0, diags, one_diag, 0)

    def two_pairs(r, carry):
        pair_tile(diags + 2 * r)
        pair_tile(diags + 2 * r + 1)
        return carry

    lax.fori_loop(0, pairs // 2, two_pairs, 0)
    if pairs % 2:
        pair_tile(diags + pairs - 1)
    if not last:
        return
    att_out, o_out, lse_out, att = rest

    def finish(i, carry):
        rows = block_rows(i, T)
        parts = []
        for h in range(2):
            lse_out[h, i] = top[h, i] + jnp.log(mass[h, i])
            parts.append(acc[i, HALVES[h], :] / mass[h, i])
        o = jnp.transpose(jnp.concatenate(parts, axis=0))
        o_out[rows, :] = o
        att[rows, :] = o.astype(BF16)
        return carry

    lax.fori_loop(0, n, finish, 0)
    slots = n * EXP_DEV * 2 * cap

    def pair(p, carry):
        codes = jnp.concatenate([code[2 * p], code[2 * p + 1]], axis=1)
        pick = jnp.where(codes == iota((slots, 2 * T), 0), 1.0, 0.0).astype(BF16)
        chosen = dot_nn(pick, att[block_rows(p, 2 * T), :]).astype(BF16)
        for k in range(n):
            for e in range(EXP_DEV):
                at = (k * EXP_DEV + e) * 2 * cap
                to = pl.multiple_of(e * n * cap + p * 2 * cap, 16)
                att_out[k, pl.ds(to, 2 * cap), :] = chosen[at : at + 2 * cap]
        return carry

    lax.fori_loop(0, n // 2, pair, 0)


def attn_fwd_call(n, T, cap, at_tile, diags, pairs, tiles, qa, ka, vt, state, code=None):
    row = n * T
    first, last = state is None, code is not None
    vmem = pl.BlockSpec(memory_space=pltpu.VMEM)
    shapes = [((2, n, 1, T), F32), ((2, n, 1, T), F32), ((n, 128, T), F32)]
    operands = [qa, ka, vt] + ([code] if last else []) + ([] if first else list(state))
    scratch = []
    if last:
        shapes += [
            ((n, EXP_DEV * n * cap, 128), BF16),
            ((row, 128), F32),
            ((2, n, 1, T), F32),
        ]
        scratch = [pltpu.VMEM((row, 128), BF16)]
    count = diags + pairs
    return pl.pallas_call(
        lambda *a: attn_fwd_kernel(n, T, cap, at_tile, diags, pairs, first, last, *a),
        out_shape=[jax.ShapeDtypeStruct(s, t) for s, t in shapes],
        in_specs=[pl.BlockSpec(memory_space=pltpu.SMEM)] + [vmem] * len(operands),
        out_specs=[vmem] * len(shapes),
        scratch_shapes=scratch,
        compiler_params=params(),
        cost_estimate=pl.CostEstimate(
            flops=count * MICROSECOND, bytes_accessed=6 << 20, transcendentals=0
        ),
        name="attn_fwd",
    )(tiles, *operands)


def attn_bwd_kernel(
    n, T, cap, at_tile, diags, pairs, tiles, qa, ka, kt, v, lse, o_ref, datt, *refs
):
    dm_out, do, delta, dqt, dka, dva = refs[-6:]
    slots = n * EXP_DEV * 2 * cap

    def pair(p, carry):
        rows = block_rows(p, 2 * T)
        feature = ka[rows, 128:256].astype(F32)
        half = jnp.where(iota((2 * T, 1), 0) >= T, float(cap), 0.0)
        code = (feature[:, 16:17] * (2 * cap) + feature[:, 17:18] + half).astype(jnp.int32)
        pick = jnp.where(code == iota((2 * T, slots), 1), 1.0, 0.0).astype(BF16)
        parts = []
        for k in range(n):
            for e in range(EXP_DEV):
                at = pl.multiple_of(e * n * cap + p * 2 * cap, 16)
                parts.append(datt[k, pl.ds(at, 2 * cap), :])
        got = dot_nn(pick, jnp.concatenate(parts, axis=0))
        lane = iota((2 * T, 128), 1)
        do[0, rows, :] = jnp.where(lane < HEAD_DIM, got, 0.0).astype(BF16)
        do[1, rows, :] = jnp.where(lane < HEAD_DIM, 0.0, got).astype(BF16)
        prod = jnp.transpose(got * o_ref[rows, :])
        for h in range(2):
            total = jnp.sum(prod[HALVES[h], :], axis=0, keepdims=True)
            delta[h, 2 * p] = total[:, 0:T]
            delta[h, 2 * p + 1] = total[:, T : 2 * T]
        return carry

    lax.fori_loop(0, n // 2, pair, 0)

    def tile(i, j, key_rows, mask):
        rows, cols = block_rows(i, T), block_rows(j, T)
        ps, dss, dqs = [], [], []
        for h in range(2):
            s = dot_nt(key_rows, qa[h, rows, :])
            dp = dot_nt(v[cols, :], do[h, rows, :])
            if mask is not None:
                s = jnp.where(mask, s, NEG)
            p = jnp.exp(s - lse[h, i])
            ds = (p * (dp - delta[h, i])).astype(BF16)
            ps.append(p.astype(BF16))
            dss.append(ds)
            dqs.append(dot_nn(kt[j, HALVES[h], :], ds))
        dv = dot_nn(
            jnp.concatenate(ps, axis=1), jnp.concatenate([do[0, rows, :], do[1, rows, :]], axis=0)
        )
        dk = dot_nn(
            jnp.concatenate(dss, axis=1),
            jnp.concatenate([qa[0, rows, 0:128], qa[1, rows, 0:128]], axis=0),
        )
        return jnp.concatenate(dqs, axis=0), dk, dv

    def diag_tile(j, carry):
        kd, allowed = diag_parts(T, ka[block_rows(j, T), :])
        dqt[j], dka[j], dva[j] = tile(j, j, kd, allowed)
        return carry

    lax.fori_loop(0, n, diag_tile, 0)

    def pair_tile(at):
        i, j = tiles[at_tile + 2 * at], tiles[at_tile + 2 * at + 1]
        dq, dk, dv = tile(i, j, ka[block_rows(j, T), :], None)
        dqt[i] += dq
        dka[j] += dk
        dva[j] += dv

    def two_pairs(r, carry):
        pair_tile(diags + 2 * r)
        pair_tile(diags + 2 * r + 1)
        return carry

    lax.fori_loop(0, pairs // 2, two_pairs, 0)
    if pairs % 2:
        pair_tile(diags + pairs - 1)

    def finish(i, carry):
        dq = jnp.transpose(dqt[i]).astype(BF16).astype(F32)
        dm_out[i, :, 0:128] = (dq * (HEAD_DIM**-0.5)).astype(BF16)
        dm_out[i, :, 128:256] = dka[i].astype(BF16)
        dm_out[i, :, 256:384] = dva[i].astype(BF16)
        return carry

    lax.fori_loop(0, n, finish, 0)


def attn_bwd_call(n, T, cap, at_tile, diags, pairs, tiles, qa, ka, kt, v, lse, o, datt, after):
    row = n * T
    vmem = pl.BlockSpec(memory_space=pltpu.VMEM)
    return pl.pallas_call(
        lambda *a: attn_bwd_kernel(n, T, cap, at_tile, diags, pairs, *a),
        out_shape=jax.ShapeDtypeStruct((n, T, 384), BF16),
        in_specs=[pl.BlockSpec(memory_space=pltpu.SMEM)]
        + [vmem] * 7
        + [pl.BlockSpec(memory_space=pl.ANY)] * len(after),
        out_specs=vmem,
        scratch_shapes=[
            pltpu.VMEM((2, row, 128), BF16),
            pltpu.VMEM((2, n, 1, T), F32),
            pltpu.VMEM((n, 128, T), F32),
            pltpu.VMEM((n, T, 128), F32),
            pltpu.VMEM((n, T, 128), F32),
        ],
        compiler_params=params(),
        cost_estimate=pl.CostEstimate(
            flops=(diags + pairs) * MICROSECOND, bytes_accessed=8 << 20, transcendentals=0
        ),
        name="attn_bwd",
    )(tiles, qa, ka, kt, v, lse, o, datt, *after)


def dispatch_kernel(cap, slots, after, ids, grads, out):
    id_row = ids[...].astype(F32)
    T = id_row.shape[1]
    id_col = jnp.transpose(jnp.broadcast_to(id_row, (128, T)))[:, 0:1]
    same = jnp.where((id_col == id_row) & (iota((T, T), 0) < iota((T, T), 1)), 1.0, 0.0)
    rank = jnp.sum(same, axis=0, keepdims=True)
    slot = (id_row * cap + rank).astype(jnp.int32)
    pick = jnp.where(slot == iota((slots, T), 0), 1.0, 0.0).astype(BF16)
    out[...] = dot_nn(pick, grads[...]).astype(BF16)


def dispatch_call(cap, slots, after, ids, grads):
    vmem = pl.BlockSpec(memory_space=pltpu.VMEM)
    return pl.pallas_call(
        lambda *a: dispatch_kernel(cap, slots, *a),
        out_shape=jax.ShapeDtypeStruct((slots, D), BF16),
        in_specs=[pl.BlockSpec(memory_space=pl.ANY), vmem, vmem],
        out_specs=vmem,
        compiler_params=params(),
        cost_estimate=cost(3),
        name="dispatch",
    )(after, ids, grads)


def owner_fwd_kernel(n, att_in, w_out, sel, out_bias, gain, bias, x_two, x_one, att_b):
    for k in range(n):
        att_b[:, k * 128 : (k + 1) * 128] = att_in[k]
    branch = dot_nn(att_b[...], w_out[...]) + out_bias[...]
    x = sel[...] + branch
    x_one[...] = x
    vhat, _ = normed_rows(x)
    x_two[...] = (vhat * gain[...] + bias[...]).astype(BF16)


def owner_fwd_call(n, e, att_in, w_out, sel, out_bias, gain, bias):
    slots = sel.shape[0] // EXP_DEV
    rows = pl.BlockSpec((slots, D), lambda i: (e, 0))
    mine = whole((slots, D))
    return pl.pallas_call(
        lambda *a: owner_fwd_kernel(n, *a),
        grid=(1,),
        in_specs=[
            pl.BlockSpec((n, slots, 128), lambda i: (0, e, 0)),
            whole((D, D)),
            rows,
            whole((1, D)),
            whole((1, D)),
            whole((1, D)),
        ],
        out_specs=[mine, mine, mine],
        out_shape=[
            jax.ShapeDtypeStruct((slots, D), BF16),
            jax.ShapeDtypeStruct((slots, D), F32),
            jax.ShapeDtypeStruct((slots, D), BF16),
        ],
        compiler_params=params(),
        cost_estimate=cost(3),
        name="owner_fwd",
    )(att_in, w_out, sel, out_bias, gain, bias)


def owner_bwd_kernel(n, part_a, part_b, x_one, og, gain, w_out, *refs):
    datt, d_one_b, small = refs[-3:]
    u = (part_a[...].astype(F32) + part_b[...].astype(F32)).astype(BF16).astype(F32)
    vhat, inv_std = normed_rows(x_one[...])
    scaled = u * gain[...]
    first = jnp.mean(scaled, axis=-1, keepdims=True)
    second = jnp.mean(scaled * vhat, axis=-1, keepdims=True)
    d_one = og[...].astype(F32) + inv_std * (scaled - first - vhat * second)
    d_b = d_one.astype(BF16)
    d_one_b[...] = d_b
    back = dot_nt(d_b, w_out[...]).astype(BF16)
    for k in range(n):
        datt[k] = back[:, k * 128 : (k + 1) * 128]
    small[0:1, :] = jnp.sum(u * vhat, axis=0, keepdims=True)
    small[1:2, :] = jnp.sum(u, axis=0, keepdims=True)
    small[2:3, :] = jnp.sum(d_one, axis=0, keepdims=True)


def owner_bwd_call(n, e, part_a, part_b, x_one, og, gain, w_out, held, after):
    slots = x_one.shape[0]
    mine = whole((slots, D))
    in_specs = [
        mine,
        mine,
        mine,
        pl.BlockSpec((slots, D), lambda i: (e, 0)),
        whole((1, D)),
        whole((D, D)),
    ]
    more = ([] if held is None else [held]) + after
    return pl.pallas_call(
        lambda *a: owner_bwd_kernel(n, *a),
        grid=(1,),
        in_specs=in_specs + [pl.BlockSpec(memory_space=pl.ANY)] * len(more),
        out_specs=[
            pl.BlockSpec((n, slots, 128), lambda i: (0, e, 0)),
            mine,
            whole((8, D)),
        ],
        out_shape=[
            jax.ShapeDtypeStruct((n, EXP_DEV * slots, 128), BF16),
            jax.ShapeDtypeStruct((slots, D), BF16),
            jax.ShapeDtypeStruct((8, D), F32),
        ],
        input_output_aliases={} if held is None else {len(in_specs): 0},
        compiler_params=params(),
        cost_estimate=cost(4),
        name="owner_bwd",
    )(part_a, part_b, x_one, og, gain, w_out, *more)


def gelu_parts(u):
    cdf = 0.5 * (1.0 + lax.erf(u * (0.5**0.5)))
    return cdf, cdf + u * jnp.exp(-0.5 * u * u) * ((2.0 * math.pi) ** -0.5)


def expert_kernel(nb, rows, steps, sc, *refs):
    x_parts, g_parts = refs[:nb], refs[nb : 2 * nb]
    w_in, b_in, w_out = refs[2 * nb : 2 * nb + 3]
    hidden_out, dpre_out, keep, send, grad_b, xs, gs, total = refs[-8:]
    f = pl.program_id(0)

    @pl.when(f == 0)
    def _():
        for k in range(nb):
            xs[k * rows : (k + 1) * rows, :] = x_parts[k][...]
            gs[k * rows : (k + 1) * rows, :] = g_parts[k][0]
        total[...] = jnp.zeros_like(total)

    pre = dot_nn(xs[...], w_in[0]) + b_in[0]
    cdf, slope = gelu_parts(pre)
    hidden_out[...] = (pre * cdf).astype(BF16)
    dhidden = dot_nt(gs[...], w_out[0]).astype(BF16).astype(F32)
    dpre = (dhidden * slope).astype(BF16)
    dpre_out[...] = dpre
    grad_b[0] = jnp.sum(dpre.astype(F32), axis=0, keepdims=True)
    total[...] += dot_nt(dpre, w_in[0])

    @pl.when(f == steps - 1)
    def _():
        for y in range(2):
            keep[y] = total[2 * y * rows : (2 * y + 1) * rows, :].astype(BF16)
            send[y] = total[(2 * y + 1) * rows : (2 * y + 2) * rows, :].astype(BF16)


def expert_call(e, at_b, sc, x_parts, g_all, w_in, b_in, w_out, after):
    nb = len(x_parts)
    rows = x_parts[0].shape[0]
    ff = w_in.shape[2]
    width = min(256, ff)
    steps = ff // width
    g_specs = [
        pl.BlockSpec((1, rows, D), lambda f, sc, k=k: (sc[at_b] ^ k, e, 0)) for k in range(nb)
    ]
    act = pl.BlockSpec((nb * rows, width), lambda f, sc: (0, f))
    return pl.pallas_call(
        lambda *a: expert_kernel(nb, rows, steps, *a),
        grid_spec=pltpu.PrefetchScalarGridSpec(
            num_scalar_prefetch=1,
            grid=(steps,),
            in_specs=[whole((rows, D))] * nb
            + g_specs
            + [
                pl.BlockSpec((1, D, width), lambda f, sc: (e, 0, f)),
                pl.BlockSpec((1, 1, width), lambda f, sc: (e, 0, f)),
                pl.BlockSpec((1, width, D), lambda f, sc: (e, f, 0)),
            ]
            + [pl.BlockSpec(memory_space=pl.ANY)] * len(after),
            out_specs=[
                act,
                act,
                whole((2, rows, D)),
                whole((2, rows, D)),
                pl.BlockSpec((1, 1, width), lambda f, sc: (0, 0, f)),
            ],
            scratch_shapes=[
                pltpu.VMEM((nb * rows, D), BF16),
                pltpu.VMEM((nb * rows, D), BF16),
                pltpu.VMEM((nb * rows, D), F32),
            ],
        ),
        out_shape=[
            jax.ShapeDtypeStruct((nb * rows, ff), BF16),
            jax.ShapeDtypeStruct((nb * rows, ff), BF16),
            jax.ShapeDtypeStruct((2, rows, D), BF16),
            jax.ShapeDtypeStruct((2, rows, D), BF16),
            jax.ShapeDtypeStruct((1, 1, ff), F32),
        ],
        compiler_params=params(),
        cost_estimate=cost(10),
        name="expert_main",
    )(sc, *x_parts, *([g_all] * nb), w_in, b_in[:, None, :], w_out, *after)


def expert_out_kernel(rows, hidden, w_out, keep, send):
    total = dot_nn(hidden[...], w_out[0]).astype(BF16)
    for y in range(2):
        keep[y] = total[2 * y * rows : (2 * y + 1) * rows, :]
        send[y] = total[(2 * y + 1) * rows : (2 * y + 2) * rows, :]


def expert_out_call(nb, e, hidden, w_out):
    rows = hidden.shape[0] // nb
    ff = hidden.shape[1]
    return pl.pallas_call(
        lambda *a: expert_out_kernel(rows, *a),
        grid=(1,),
        in_specs=[whole(hidden.shape), pl.BlockSpec((1, ff, D), lambda i: (e, 0, 0))],
        out_specs=[whole((2, rows, D))] * 2,
        out_shape=[jax.ShapeDtypeStruct((2, rows, D), BF16)] * 2,
        compiler_params=params(),
        cost_estimate=cost(4),
        name="expert_out",
    )(hidden, w_out)


def expert_grad_kernel(nb, rows, sc, *refs):
    x_parts, g_parts = refs[:nb], refs[nb : 2 * nb]
    hidden, dpre = refs[2 * nb : 2 * nb + 2]
    grad_in, grad_out, grad_b, xs, gs = refs[-5:]

    @pl.when(pl.program_id(0) == 0)
    def _():
        sums = []
        for k in range(nb):
            xs[k * rows : (k + 1) * rows, :] = x_parts[k][...]
            gs[k * rows : (k + 1) * rows, :] = g_parts[k][0]
            sums.append(jnp.sum(g_parts[k][0].astype(F32), axis=0, keepdims=True))
        grad_b[0] = (sums[0] + sums[1]) + (sums[2] + sums[3])

    grad_in[0] = dot_tn(xs[...], dpre[...])
    grad_out[0] = dot_tn(hidden[...], gs[...])


def expert_grad_call(e, at_b, sc, x_parts, g_all, hidden, dpre, held, after):
    nb = len(x_parts)
    rows = x_parts[0].shape[0]
    ff = hidden.shape[1]
    width = min(256, ff)
    g_specs = [
        pl.BlockSpec((1, rows, D), lambda f, sc, k=k: (sc[at_b] ^ k, e, 0)) for k in range(nb)
    ]
    act = pl.BlockSpec((nb * rows, width), lambda f, sc: (0, f))
    in_specs = [whole((rows, D))] * nb + g_specs + [act, act]
    more = [] if held is None else list(held)
    aliases = {1 + len(in_specs) + i: i for i in range(len(more))}
    more += after
    return pl.pallas_call(
        lambda *a: expert_grad_kernel(nb, rows, *a),
        grid_spec=pltpu.PrefetchScalarGridSpec(
            num_scalar_prefetch=1,
            grid=(ff // width,),
            in_specs=in_specs + [pl.BlockSpec(memory_space=pl.ANY)] * len(more),
            out_specs=[
                pl.BlockSpec((1, D, width), lambda f, sc: (e, 0, f)),
                pl.BlockSpec((1, width, D), lambda f, sc: (e, f, 0)),
                pl.BlockSpec((1, 1, D), lambda f, sc: (e, 0, 0)),
            ],
            scratch_shapes=[pltpu.VMEM((nb * rows, D), BF16)] * 2,
        ),
        out_shape=[
            jax.ShapeDtypeStruct((EXP_DEV, D, ff), F32),
            jax.ShapeDtypeStruct((EXP_DEV, ff, D), F32),
            jax.ShapeDtypeStruct((EXP_DEV, 1, D), F32),
        ],
        input_output_aliases=aliases,
        compiler_params=params(),
        cost_estimate=cost(8),
        name="expert_grads",
    )(sc, *x_parts, *([g_all] * nb), hidden, dpre, *more)


def w_out_grad_kernel(n, nb, sc, *refs):
    keep, send = refs[-2:]
    total = dot_tn(refs[0][...], refs[EXP_DEV][...])
    for e in range(1, EXP_DEV):
        total = total + dot_tn(refs[e][...], refs[EXP_DEV + e][...])
    size = D // (n * nb)
    core = lax.rem(sc[n + 1], 2)
    chip = lax.div(sc[n + 1], 2)
    for r in range(n):
        for y in range(nb // 2):
            first = (r * nb + 2 * y) * size
            pair = [total[first + c * size : first + (c + 1) * size].astype(BF16) for c in range(2)]
            place = y ^ chip
            at_keep = jnp.where(core == 0, pair[0].astype(F32), pair[1].astype(F32)).astype(BF16)
            at_send = jnp.where(core == 0, pair[1].astype(F32), pair[0].astype(F32)).astype(BF16)
            keep[place, r] = at_keep
            send[place, r] = at_send


def w_out_grad_call(n, nb, sc, att_b, d_one_b):
    size = D // (n * nb)
    shape = (nb // 2, n, size, D)
    return pl.pallas_call(
        lambda *a: w_out_grad_kernel(n, nb, *a),
        grid_spec=pltpu.PrefetchScalarGridSpec(
            num_scalar_prefetch=1,
            grid=(1,),
            in_specs=[whole(att_b[0].shape)] * (2 * EXP_DEV),
            out_specs=[whole(shape)] * 2,
        ),
        out_shape=[jax.ShapeDtypeStruct(shape, BF16)] * 2,
        compiler_params=params(),
        cost_estimate=cost(4),
        name="w_out_grad",
    )(sc, *att_b, *d_one_b)


def qkv_grad_kernel(n, nb, T, sc, h, dm, aux, after, keep, send, total):
    me_b = sc[n + 1]

    def add(c, carry):
        total[...] += dot_tn(dm[c], h[c])
        return carry

    total[...] = jnp.zeros_like(total)
    lax.fori_loop(0, n, add, 0)
    col_sum = jnp.zeros((1, 384), F32)
    for r in range(n):
        col_sum = col_sum + jnp.sum(dm[r].astype(F32), axis=0, keepdims=True)
    width = D // n
    size = width // nb
    top = iota((16, 384), 0)
    for r in range(n):
        part = jnp.transpose(total[:, r * width : (r + 1) * width])
        for k in range(nb):
            bb = me_b ^ k
            rows = jnp.zeros((size, 384), F32)
            for c in range(nb):
                rows = jnp.where(bb == c, part[c * size : (c + 1) * size, :], rows)
            extra = jnp.where(
                top == 0, col_sum, jnp.where(top == 1, aux[r * nb + bb], 0.0)
            )
            to = keep if k % 2 == 0 else send
            to[k // 2, r, 0:size, :] = rows.astype(BF16)
            to[k // 2, r, size : size + 16, :] = extra.astype(BF16)


def qkv_grad_call(n, nb, T, sc, h, dm, aux, after):
    size = D // (n * nb)
    shape = (2, n, size + 16, 384)
    return pl.pallas_call(
        lambda *a: qkv_grad_kernel(n, nb, T, *a),
        grid_spec=pltpu.PrefetchScalarGridSpec(
            num_scalar_prefetch=1,
            grid=(1,),
            in_specs=[
                whole((n, T, D)),
                whole((n, T, 384)),
                whole((n * nb, 1, 384)),
                pl.BlockSpec(memory_space=pl.ANY),
            ],
            out_specs=[whole(shape), whole(shape)],
            scratch_shapes=[pltpu.VMEM((384, D), F32)],
        ),
        out_shape=[jax.ShapeDtypeStruct(shape, BF16)] * 2,
        compiler_params=params(),
        cost_estimate=cost(8),
        name="qkv_grad",
    )(sc, h, dm, aux, after)


def scatter_rows(cap, slots, kaug, values):
    feature = kaug[:, 128:256].astype(F32)
    code = (feature[:, 16:17] * cap + feature[:, 17:18]).astype(jnp.int32)
    pick = jnp.where(code == iota((feature.shape[0], slots), 1), 1.0, 0.0).astype(BF16)
    return dot_nn(pick, values)


def input_grad_kernel(n, T, cap, sc, dm, w_qkv, hidden, d_ret, kaug, gain, out, full):
    for k in range(n):
        for part in range(3):
            full[:, part * D + k * 128 : part * D + (k + 1) * 128] = dm[
                k, :, part * 128 : (part + 1) * 128
            ]
    u = dot_nt(full[...], w_qkv[...])
    vhat, inv_std = normed_rows(hidden[...].astype(F32))
    scaled = u * gain[...]
    first = jnp.mean(scaled, axis=-1, keepdims=True)
    second = jnp.mean(scaled * vhat, axis=-1, keepdims=True)
    d_one = scatter_rows(cap, d_ret.shape[0], kaug[...], d_ret[...])
    out[...] = (d_one + inv_std * (scaled - first - vhat * second)).astype(BF16)


def input_grad_call(n, T, cap, sc, dm, w_qkv, hidden, d_ret, kaug, gain):
    slots = d_ret.shape[0]
    return pl.pallas_call(
        lambda *a: input_grad_kernel(n, T, cap, *a),
        grid_spec=pltpu.PrefetchScalarGridSpec(
            num_scalar_prefetch=1,
            grid=(1,),
            in_specs=[
                whole((n, T, 384)),
                whole((D, 3 * D)),
                whole((T, D)),
                whole((slots, D)),
                pl.BlockSpec((T, 256), lambda i, sc: (sc[n], 0)),
                whole((1, D)),
            ],
            out_specs=whole((T, D)),
            scratch_shapes=[pltpu.VMEM((T, 3 * D), BF16)],
        ),
        out_shape=jax.ShapeDtypeStruct((T, D), BF16),
        compiler_params=params(),
        cost_estimate=cost(60),
        name="input_grad",
    )(sc, dm, w_qkv, hidden, d_ret, kaug, gain)


def output_kernel(cap, sc, ret, kaug, out):
    out[...] = scatter_rows(cap, ret.shape[0], kaug[...], ret[...]).astype(BF16)


def output_call(n, T, cap, sc, ret, kaug):
    return pl.pallas_call(
        lambda *a: output_kernel(cap, *a),
        grid_spec=pltpu.PrefetchScalarGridSpec(
            num_scalar_prefetch=1,
            grid=(1,),
            in_specs=[
                whole(ret.shape),
                pl.BlockSpec((T, 256), lambda i, sc: (sc[n], 0)),
            ],
            out_specs=whole((T, D)),
        ),
        out_shape=jax.ShapeDtypeStruct((T, D), BF16),
        compiler_params=params(),
        cost_estimate=cost(3),
        name="output_rows",
    )(sc, ret, kaug)


def final_kernel(n, nb, sc, got, w_rows, gb, gw, gains, biases, qvb, outb, s_rows, w_full):
    size = D // (n * nb)
    me, me_b = sc[n], sc[n + 1]
    smalls = jnp.zeros((1, 384), F32)
    s_rows[...] = jnp.zeros_like(s_rows)
    for k in range(n):
        tile = got[k].astype(F32)
        for part in range(3):
            cols = slice(part * D + k * 128, part * D + (k + 1) * 128)
            w_full[:, cols] = tile[0:size, part * 128 : (part + 1) * 128]
            s_rows[0:1, cols] = tile[size : size + 1, part * 128 : (part + 1) * 128]
        smalls = smalls + tile[size + 1 : size + 2, :]
    gw[...] = w_full[...]
    weights = w_rows[...].astype(F32)
    high = lax.Precision.HIGHEST
    nt = (((1,), (1,)), ((), ()))
    bias_one = lax.dot_general(s_rows[...], weights, nt, precision=high, preferred_element_type=F32)[0:1]
    both = lax.dot_general(
        jnp.ones((8, 3 * D), F32), weights * w_full[...], nt, precision=high, preferred_element_type=F32
    )[0:1]
    gains[0:1, :] = (both - gb[1:2, :] * bias_one) / gb[0:1, :]
    gains[1:2, :] = smalls[:, 0:size]
    biases[0:1, :] = bias_one
    biases[1:2, :] = smalls[:, size : 2 * size]
    outb[...] = smalls[:, 2 * size : 3 * size]
    own = got[me, size : size + 16, :].astype(F32)[0:1]
    for row, first in ((0, 0), (1, 256)):
        value = jnp.zeros((1, size), F32)
        for c in range(nb):
            value = jnp.where(me_b == c, own[:, first + c * size : first + (c + 1) * size], value)
        qvb[row : row + 1, :] = value


def final_call(n, nb, sc, got, w_qkv, gb):
    size = D // (n * nb)
    shapes = [(size, 3 * D), (2, size), (2, size), (2, size), (1, size)]
    return pl.pallas_call(
        lambda *a: final_kernel(n, nb, *a),
        grid_spec=pltpu.PrefetchScalarGridSpec(
            num_scalar_prefetch=1,
            grid=(1,),
            in_specs=[
                whole((n, size + 16, 384)),
                pl.BlockSpec((size, 3 * D), lambda i, sc: (nb * sc[n] + sc[n + 1], 0)),
                whole((2, size)),
            ],
            out_specs=[whole(s) for s in shapes],
            scratch_shapes=[pltpu.VMEM((8, 3 * D), F32), pltpu.VMEM((size, 3 * D), F32)],
        ),
        out_shape=[jax.ShapeDtypeStruct(s, F32) for s in shapes],
        compiler_params=params(),
        cost_estimate=cost(3),
        name="final_rows",
    )(sc, got, w_qkv, gb)


def exchange(values, axis, bit):
    size = lax.axis_size(axis)
    return lax.ppermute(values, axis, [(i, i ^ bit) for i in range(size)])


def gather_ring(payload, ring):
    n = len(ring)
    ahead = [(ring[i], ring[(i + 1) % n]) for i in range(n)]
    back = [(ring[i], ring[i - 1]) for i in range(n)]
    split = -(-payload.shape[0] // 32) * 16
    steps = [[[payload]]]
    left = right = payload
    for _ in range(n // 2 - 1):
        left = lax.ppermute(left, "seq", ahead)
        right = lax.ppermute(right, "seq", back)
        steps.append([[left], [right]])
    steps.append(
        [[lax.ppermute(left[:split], "seq", ahead), lax.ppermute(right[split:], "seq", back)]]
    )
    return steps


def arrival_tables(n, ring):
    place = [ring.index(i) for i in range(n)]
    order = [[0]] + [[-o, o] for o in range(1, n // 2)] + [[n // 2]]
    sources, tiles, counts = [], [], None
    for i in range(n):
        blocks = [[ring[(place[i] + o) % n] for o in step] for step in order]
        arrived, listed, sizes = [], [], []
        for at, step in enumerate(blocks):
            arrived += step
            if at == 0:
                continue
            new = arrived if at == 1 else step
            diag = [(q, q) for q in sorted(new)]
            pairs = [
                (q, k)
                for k in range(n)
                for q in range(k + 1, n)
                if q in arrived and k in arrived and (q in new or k in new)
            ]
            listed.append([x for t in diag + pairs for x in t])
            sizes.append((len(diag), len(pairs)))
        sources.append([b for step in blocks for b in step])
        tiles.append(listed)
        counts = counts or sizes
    return np.array(sources, np.int32), tiles, counts


def reduce_cores(keep, send, after=None):
    got = exchange(send, "batch", 1)
    if after is not None:
        got = gate(got, after)
    return [(keep[y].astype(F32) + got[y].astype(F32)).astype(BF16) for y in range(2)]


def gate(value, after):
    def nothing(held, later, out):
        del held, later, out

    anywhere = pl.BlockSpec(memory_space=pl.ANY)
    return pl.pallas_call(
        nothing,
        in_specs=[anywhere, anywhere],
        out_specs=anywhere,
        out_shape=jax.ShapeDtypeStruct(value.shape, value.dtype),
        input_output_aliases={0: 0},
        name="gate",
    )(value, after)


def local_by_heads(
    hidden_in,
    out_grad,
    norm_gain_pair,
    norm_bias_pair,
    w_qkv,
    qv_bias,
    w_out,
    out_bias,
    w_in_exp,
    b_in_exp,
    w_out_exp,
    b_out_exp,
    expert_ids,
    doc_lengths,
    pad_mask,
):
    T = hidden_in.shape[1]
    n, nb = lax.axis_size("seq"), lax.axis_size("batch")
    experts = EXP_DEV * n
    cap = max(2, 3 * T // (2 * experts))
    s, b = lax.axis_index("seq"), lax.axis_index("batch")
    ring = [*range(0, n, 2), *range(n - 1, 0, -2)]
    sources, tiles, counts = arrival_tables(n, ring)

    every = [(i, i) for i in range(n)] + [(q, k) for k in range(n) for q in range(k + 1, n)]
    every = np.array(every, np.int32).reshape(-1)
    table = [
        np.concatenate([sources[i], [i, 0]] + tiles[i] + [every]).astype(np.int32) for i in range(n)
    ]
    firsts = n + 2 + np.cumsum([0] + [2 * (d + p) for d, p in counts])
    row = lax.dynamic_index_in_dim(jnp.asarray(np.stack(table)), s, 0, keepdims=False)
    sc = jnp.where(jnp.arange(row.shape[0]) == n + 1, b.astype(jnp.int32), row)
    hidden = hidden_in[0]
    ids = expert_ids[0, :, 0]
    codes = jnp.concatenate([ids, pad_mask[0], jnp.zeros((D - 2 * T,), jnp.int32)]).astype(BF16)
    codes = jnp.where(jnp.arange(16)[:, None] == 0, codes[None, :], jnp.zeros((), BF16))
    payload = jnp.concatenate([hidden, codes], axis=0)
    steps = gather_ring(payload, ring)

    count = doc_lengths.shape[1]
    at = jnp.arange(128)
    ends = jnp.sum(
        jnp.where(jnp.arange(count)[:, None] <= at[None, :], doc_lengths[0][:, None], 0), axis=0
    )
    starts = jnp.sum(
        jnp.where(jnp.arange(count)[:, None] < at[None, :], doc_lengths[0][:, None], 0), axis=0
    )
    docs = jnp.stack([starts, ends]).astype(F32)
    gain_rows = [norm_gain_pair[i : i + 1] for i in range(2)]
    bias_rows = [norm_bias_pair[i : i + 1] for i in range(2)]

    held = state = None
    block = 0
    for step, blocks in enumerate(steps):
        for chunk in blocks:
            held = qkv_call(
                n, T, cap, block, sc, chunk, held, w_qkv, qv_bias, gain_rows[0], bias_rows[0], docs
            )
            block += 1
        if step == 0:
            continue
        h_one, qa, ka, vt, kt, v, code, sel = held
        diags, pairs = counts[step - 1]
        at_tile = int(firsts[step - 1])
        done = attn_fwd_call(
            n, T, cap, at_tile, diags, pairs, sc, qa, ka, vt, state, code if step == n // 2 else None
        )
        state = done[:3]
    att_out, o, lse = done[3:]
    sel = sel.reshape(EXP_DEV * n * cap, D)

    sent_grads = dispatch_call(cap, experts * cap, steps[DISPATCH_STEP][0][0], ids[None], out_grad[0])
    sent_grads = sent_grads.reshape(n, EXP_DEV * cap, D)
    grads = lax.all_to_all(sent_grads, "seq", split_axis=0, concat_axis=0, tiled=True)
    grads = grads.reshape(n, EXP_DEV, cap, D).transpose(1, 0, 2, 3).reshape(experts * cap, D)
    g_all = lax.all_gather(grads, "batch", axis=0, tiled=False)

    att_in = lax.all_to_all(att_out, "seq", split_axis=0, concat_axis=0, tiled=True)
    x_two, x_one, att_b = [], [], []
    for e in range(EXP_DEV):
        rows, one, att_rows = owner_fwd_call(
            n, e, att_in, w_out, sel, out_bias[None], gain_rows[1], bias_rows[1]
        )
        x_two.append(rows)
        x_one.append(one)
        att_b.append(att_rows)
    x_core = [exchange(rows, "batch", 1) for rows in x_two]
    x_y = [exchange(rows, "batch", 2) for rows in x_two]
    x_parts, hidden_act, dpre, grad_b_in, sums, ahead = [], [], [], [], [], []
    after = [x_one[-1]]
    terms = None
    for e in range(EXP_DEV):
        if e:
            x_y[e] = gate(x_y[e], terms[0])
        x_parts.append([x_two[e], x_core[e], x_y[e], exchange(x_y[e], "batch", 1)])
        act, dact, *terms, grad_b = expert_call(
            e, n + 1, sc, x_parts[e], g_all, w_in_exp, b_in_exp, w_out_exp, after
        )
        ahead.append(expert_out_call(nb, e, act, w_out_exp))
        sums.append(reduce_cores(*terms, after=ahead[e][0]))
        after = [sums[e][0]]
        hidden_act.append(act)
        dpre.append(dact)
        grad_b_in.append(grad_b[0])
    from_y = [exchange(both[1], "batch", 2) for both in sums]
    d_one_b, small, outs = [], [], []
    datt_out = None
    for e in range(EXP_DEV):
        datt_out, rows, totals = owner_bwd_call(
            n, e, sums[e][0], from_y[e], x_one[e], grads, gain_rows[1], w_out, datt_out, after
        )
        d_one_b.append(rows)
        small.append(totals)
        if e + 1 < EXP_DEV:
            outs = [reduce_cores(*ahead[i], after=rows) for i in range(EXP_DEV)]
            after = [both[0] for both in outs]
    from_y = [exchange(gate(both[1], from_y[-1]), "batch", 2) for both in outs]
    from_y = [gate(rows, datt_out) for rows in from_y]
    datt = lax.all_to_all(datt_out, "seq", split_axis=0, concat_axis=0, tiled=True)

    size = D // (n * nb)
    both = reduce_cores(*w_out_grad_call(n, nb, sc, att_b, d_one_b))
    w_out_y = exchange(both[1], "batch", 2)
    weights = expert_grad_call(
        0, n + 1, sc, x_parts[0], g_all, hidden_act[0], dpre[0], None, [both[0]]
    )
    w_out_y = gate(w_out_y, weights[2])
    summed = (both[0].astype(F32) + w_out_y.astype(F32)).astype(BF16)
    home = []
    for e in range(EXP_DEV):
        expert_rows = (
            outs[e][0].astype(F32) + from_y[e].astype(F32) + b_out_exp[e][None, :]
        ).astype(BF16)
        home.append((x_one[e] + expert_rows.astype(F32)).astype(BF16))
    home = [rows.reshape(n, cap, D) for rows in d_one_b + home] + [summed]
    home = jnp.concatenate(home, axis=1)
    returned = lax.all_to_all(home, "seq", split_axis=0, concat_axis=0, tiled=True)
    at = EXP_DEV * cap
    d_ret = returned[:, :at].reshape(experts * cap, D)
    out_ret = returned[:, at : 2 * at].reshape(experts * cap, D)
    output = output_call(n, T, cap, sc, out_ret, ka)
    grad_w_out = jnp.sum(returned[:, 2 * at :].astype(F32), axis=0)

    dm = attn_bwd_call(
        n, T, cap, int(firsts[-1]), n, n * (n - 1) // 2, sc, qa, ka, kt, v, lse, o, datt, [home, weights[2]]
    )
    dm_own = lax.all_to_all(dm, "seq", split_axis=0, concat_axis=0, tiled=True)
    aux = sum(small)[:3].reshape(3, n * nb, size).transpose(1, 0, 2).reshape(n * nb, 1, 3 * size)
    aux = jnp.pad(aux, ((0, 0), (0, 0), (0, 384 - 3 * size)))
    keep_w, send_w = qkv_grad_call(n, nb, T, sc, h_one, dm, aux, returned)
    both = reduce_cores(keep_w, send_w)
    w_y = exchange(both[1], "batch", 2)
    for e in range(1, EXP_DEV):
        weights = expert_grad_call(
            e, n + 1, sc, x_parts[e], g_all, hidden_act[e], dpre[e], weights, [both[0]]
        )
    grad_w_in, grad_w_out_exp, grad_b_out = weights
    w_y = gate(w_y, grad_b_out)
    w_sum = (both[0].astype(F32) + w_y.astype(F32)).astype(BF16)
    w_sum = gate(w_sum, dm_own)
    w_got = lax.all_to_all(w_sum, "seq", split_axis=0, concat_axis=0, tiled=True)
    own = (s * nb + b) * size
    gb = jnp.stack(
        [
            lax.dynamic_slice_in_dim(norm_gain_pair[0], own, size, 0),
            lax.dynamic_slice_in_dim(norm_bias_pair[0], own, size, 0),
        ]
    )
    gw_qkv, g_gains, g_biases, g_qvb, g_outb = final_call(n, nb, sc, w_got, w_qkv, gb)
    input_grad = input_grad_call(n, T, cap, sc, dm_own, w_qkv, hidden, d_ret, ka, gain_rows[0])
    return (
        output[None],
        input_grad[None],
        g_gains,
        g_biases,
        gw_qkv,
        g_qvb,
        grad_w_out,
        g_outb[0],
        grad_w_in,
        jnp.concatenate(grad_b_in, axis=0),
        grad_w_out_exp,
        grad_b_out[:, 0],
    )


DISPATCH_STEP = 2


def solution(mesh):
    n, nb = mesh.shape["seq"], mesh.shape["batch"]
    by_heads = HEADS * HEAD_DIM == 128 * n and nb == 4
    return jax.shard_map(
        local_by_heads if by_heads else local,
        mesh=mesh,
        in_specs=(
            P("batch", "seq", None),
            P("batch", "seq", None),
            P(),
            P(),
            P(),
            P(),
            P(),
            P(),
            P("seq", None, "batch"),
            P("seq", "batch"),
            P("seq", "batch", None),
            P("seq", None),
            P("batch", "seq", None),
            P("batch", None),
            P("batch", "seq"),
        ),
        out_specs=(
            P("batch", "seq", None),
            P("batch", "seq", None),
            P(None, ("seq", "batch")),
            P(None, ("seq", "batch")),
            P(("seq", "batch"), None),
            P(None, ("seq", "batch")),
            P(("seq", "batch"), None),
            P(("seq", "batch")),
            P("seq", None, "batch"),
            P("seq", "batch"),
            P("seq", "batch", None),
            P("seq", None),
        ),
        check_vma=False,
    )
```

```python
import math

import jax
import jax.numpy as jnp
import numpy as np
from jax import lax
from jax.experimental import pallas as pl
from jax.experimental.pallas import tpu as pltpu
from jax.sharding import PartitionSpec as P

D = 1024
HEADS = 16
HEAD_DIM = 64
EXP_DEV = 2


EPS = 1e-05
NEG = -1e30
BIG = 1e30
F32 = jnp.float32
BF16 = jnp.bfloat16
VMEM_LIMIT = 56 * 1024 * 1024


def dot_nn(a, b):
    return lax.dot_general(a, b, (((1,), (0,)), ((), ())), preferred_element_type=F32)


def dot_nt(a, b):
    return lax.dot_general(a, b, (((1,), (1,)), ((), ())), preferred_element_type=F32)


def dot_tn(a, b):
    return lax.dot_general(a, b, (((0,), (0,)), ((), ())), preferred_element_type=F32)


def normed_rows(values):
    centre = values - jnp.mean(values, axis=-1, keepdims=True)
    spread = jnp.mean(centre * centre, axis=-1, keepdims=True)
    inv_std = lax.rsqrt(spread + EPS)
    return centre * inv_std, inv_std


def whole(shape):
    return pl.BlockSpec(shape, lambda *_: (0,) * len(shape))


def params(**more):
    return pltpu.CompilerParams(vmem_limit_bytes=VMEM_LIMIT, **more)


def iota(shape, axis):
    return lax.broadcasted_iota(jnp.int32, shape, axis)


def running_sums(values):
    upto = jnp.arange(values.shape[0])[:, None] >= jnp.arange(values.shape[0])[None, :]
    return jnp.sum(jnp.where(upto, values[None, :], 0), axis=1)


def layer_normalize(values, gain, shift):
    centre = values - jnp.mean(values, axis=-1, keepdims=True)
    spread = jnp.mean(centre * centre, axis=-1, keepdims=True)
    inv_std = lax.rsqrt(spread + EPS)
    normed = centre * inv_std
    return (normed * gain + shift, normed, inv_std)


def norm_backward_pass(grads, normed, inv_std, gain):
    scaled = grads * gain
    first_mean = jnp.mean(scaled, axis=-1, keepdims=True)
    second_mean = jnp.mean(scaled * normed, axis=-1, keepdims=True)
    return (
        inv_std * (scaled - first_mean - normed * second_mean),
        jnp.sum(grads * normed, axis=0),
        jnp.sum(grads, axis=0),
    )


def doc_of(positions, doc_ends):
    return jnp.sum((positions[:, None] >= doc_ends[None, :]).astype(jnp.int32), axis=1)


def allowed_pairs(q_pos, q_doc, k_pos, k_doc, k_pad):
    same_doc = q_doc[:, None] == k_doc[None, :]
    before = k_pos[None, :] <= q_pos[:, None]
    usable = (k_pad[None, :] == 1) | (k_pos[None, :] == q_pos[:, None])
    return same_doc & before & usable


def over_blocks(step_fn, totals, arrays, first_row):
    row_count = arrays[0].shape[0]
    block_rows = math.gcd(row_count, 512)

    def advance(current, block_index):
        pieces = tuple(
            (
                lax.dynamic_slice_in_dim(member, block_index * block_rows, block_rows, 0)
                for member in arrays
            )
        )
        return (step_fn(current, pieces, first_row + block_index * block_rows), None)

    result, _ = lax.scan(advance, totals, jnp.arange(row_count // block_rows, dtype=jnp.int32))
    return result


def key_grads(
    query_h, dout_h, lse_rows, delta_rows, q_pos, q_doc, key_h, value_h, k_pos, k_doc, k_pad
):
    allowed = allowed_pairs(q_pos, q_doc, k_pos, k_doc, k_pad)
    scores = jnp.einsum("qhd,khd->hqk", query_h, key_h, preferred_element_type=jnp.float32)
    probs = jnp.where(allowed[None], jnp.exp(scores - lse_rows.T[:, :, None]), 0.0)
    dprobs = jnp.einsum("qhd,khd->hqk", dout_h, value_h, preferred_element_type=jnp.float32)
    dscores = (probs * (dprobs - delta_rows.T[:, :, None])).astype(jnp.bfloat16)
    grad_keys = jnp.einsum("hqk,qhd->khd", dscores, query_h, preferred_element_type=jnp.float32)
    grad_values = jnp.einsum(
        "hqk,qhd->khd", probs.astype(jnp.bfloat16), dout_h, preferred_element_type=jnp.float32
    )
    return (grad_keys, grad_values)


def gelu_exact(values):
    return jax.nn.gelu(values, approximate=False)


def local(
    hidden_in,
    out_grad,
    norm_gain_pair,
    norm_bias_pair,
    w_qkv,
    qv_bias,
    w_out,
    out_bias,
    w_in_exp,
    b_in_exp,
    w_out_exp,
    b_out_exp,
    expert_ids,
    doc_lengths,
    pad_mask,
):
    tok_rows = hidden_in.shape[1]
    seq_count = lax.axis_size("seq")
    experts_all = EXP_DEV * seq_count
    capacity = max(2, 3 * tok_rows // (2 * experts_all))
    scale = HEAD_DIM ** (-0.5)
    input_tokens = hidden_in[0].astype(jnp.float32)
    first_normalized, first_centred_scaled, first_inverse_deviation = layer_normalize(
        input_tokens, norm_gain_pair[0], norm_bias_pair[0]
    )
    h_one = first_normalized.astype(jnp.bfloat16)
    mixed = jnp.dot(h_one, w_qkv, preferred_element_type=jnp.float32)
    queries = ((mixed[:, :D] + qv_bias[0]) * scale).astype(jnp.bfloat16)
    keys_vals = jnp.concatenate(
        [mixed[:, D : 2 * D], mixed[:, 2 * D :] + qv_bias[1][None, :]], axis=1
    ).astype(jnp.bfloat16)
    query_h = queries.reshape(tok_rows, HEADS, HEAD_DIM)
    q_pos = lax.axis_index("seq") * tok_rows + jnp.arange(tok_rows, dtype=jnp.int32)
    doc_ends = running_sums(doc_lengths[0])
    q_doc = doc_of(q_pos, doc_ends)
    key_pad = pad_mask[0]

    def split_keys(pieces, first_row):
        block_kv, block_pad = pieces
        row_count = block_kv.shape[0]
        key_h = block_kv[:, :D].reshape(row_count, HEADS, HEAD_DIM)
        value_h = block_kv[:, D:].reshape(row_count, HEADS, HEAD_DIM)
        k_pos = first_row + jnp.arange(row_count, dtype=jnp.int32)
        allowed = allowed_pairs(q_pos, q_doc, k_pos, doc_of(k_pos, doc_ends), block_pad)
        scores = jnp.einsum("thd,khd->htk", query_h, key_h, preferred_element_type=jnp.float32)
        return (key_h, value_h, allowed, jnp.where(allowed[None], scores, NEG))

    def stats_step(current, pieces, first_row):
        _, _, allowed, scores = split_keys(pieces, first_row)
        top_now, mass_now = current
        new_top = jnp.maximum(top_now, jnp.max(scores, axis=-1))
        weights = jnp.where(allowed[None], jnp.exp(scores - new_top[:, :, None]), 0.0)
        return (new_top, mass_now * jnp.exp(top_now - new_top) + jnp.sum(weights, axis=-1))

    def output_step(current, pieces, first_row):
        _, value_h, allowed, scores = split_keys(pieces, first_row)
        probs = jnp.where(allowed[None], jnp.exp(scores - log_mass[:, :, None]), 0.0).astype(
            jnp.bfloat16
        )
        return current + jnp.einsum(
            "htk,khd->thd", probs, value_h, preferred_element_type=jnp.float32
        )

    def dquery_step(current, pieces, first_row):
        key_h, value_h, allowed, scores = split_keys(pieces, first_row)
        probs = jnp.where(allowed[None], jnp.exp(scores - log_mass[:, :, None]), 0.0)
        dprobs = jnp.einsum("thd,khd->htk", dout_h, value_h, preferred_element_type=jnp.float32)
        dscores = (probs * (dprobs - delta[:, :, None])).astype(jnp.bfloat16)
        return current + jnp.einsum(
            "htk,khd->thd", dscores, key_h, preferred_element_type=jnp.float32
        )

    head_zeros = jnp.zeros((tok_rows, HEADS, HEAD_DIM), jnp.float32)
    init_stats = (
        jnp.full((HEADS, tok_rows), NEG, jnp.float32),
        jnp.zeros((HEADS, tok_rows), jnp.float32),
    )
    all_kv, all_pad = (
        lax.all_gather(keys_vals, "seq", axis=0, tiled=True),
        lax.all_gather(key_pad, "seq", axis=0, tiled=True),
    )

    def run_keys(step_fn, totals):
        return over_blocks(step_fn, totals, (all_kv, all_pad), 0)

    top_all, mass_all = run_keys(stats_step, init_stats)
    log_mass = top_all + jnp.log(mass_all)
    attended = run_keys(output_step, head_zeros)
    attended_b = attended.reshape(tok_rows, D).astype(jnp.bfloat16)
    branch = jnp.dot(attended_b, w_out, preferred_element_type=jnp.float32) + out_bias
    first_residual_input = input_tokens + branch
    second_normalized, second_centred_scaled, second_inverse_deviation = layer_normalize(
        first_residual_input, norm_gain_pair[1], norm_bias_pair[1]
    )
    x_two = second_normalized.astype(jnp.bfloat16)
    token_ids = expert_ids[0, :, 0]
    earlier = jnp.arange(tok_rows)[None, :] < jnp.arange(tok_rows)[:, None]
    ranks = jnp.sum(((token_ids[:, None] == token_ids[None, :]) & earlier).astype(jnp.int32), axis=1)
    target = token_ids * capacity + ranks
    dispatch = (
        jnp.arange(experts_all * capacity, dtype=jnp.int32)[:, None] == target[None, :]
    ).astype(jnp.bfloat16)
    sent_rows = (
        jnp.dot(dispatch, x_two, preferred_element_type=jnp.float32)
        .astype(jnp.bfloat16)
        .reshape(seq_count, EXP_DEV, capacity, D)
    )
    rows_all = lax.all_gather(
        lax.all_to_all(sent_rows, "seq", split_axis=0, concat_axis=0, tiled=True),
        "batch",
        axis=0,
        tiled=True,
    )
    pre_act = (
        jnp.einsum("recd,edf->recf", rows_all, w_in_exp, preferred_element_type=jnp.float32)
        + b_in_exp[None, :, None, :]
    )
    hidden = gelu_exact(pre_act).astype(jnp.bfloat16)
    part_sums = jnp.einsum("recf,efd->recd", hidden, w_out_exp, preferred_element_type=jnp.float32)
    summed = lax.psum_scatter(
        part_sums.astype(jnp.bfloat16), "batch", scatter_dimension=0, tiled=True
    ).astype(jnp.float32)
    produced = (summed + b_out_exp[None, :, None, :]).astype(jnp.bfloat16)
    returned = lax.all_to_all(produced, "seq", split_axis=0, concat_axis=0, tiled=True)
    expert_rows = jnp.einsum(
        "st,sd->td",
        dispatch,
        returned.reshape(experts_all * capacity, D),
        preferred_element_type=jnp.float32,
    )
    output = (first_residual_input + expert_rows).astype(jnp.bfloat16)
    dout = out_grad[0].astype(jnp.float32)
    sent_grads = (
        jnp.dot(dispatch, out_grad[0], preferred_element_type=jnp.float32)
        .astype(jnp.bfloat16)
        .reshape(seq_count, EXP_DEV, capacity, D)
    )
    arrived_rows, arrived_grads = (
        lax.all_to_all(sent_rows, "seq", split_axis=0, concat_axis=0, tiled=True),
        lax.all_to_all(sent_grads, "seq", split_axis=0, concat_axis=0, tiled=True),
    )
    rows_all, grads_all = (
        lax.all_gather(arrived_rows, "batch", axis=0, tiled=True),
        lax.all_gather(arrived_grads, "batch", axis=0, tiled=True),
    )
    pre_act = (
        jnp.einsum("recd,edf->recf", rows_all, w_in_exp, preferred_element_type=jnp.float32)
        + b_in_exp[None, :, None, :]
    )
    hidden_f, gelu_back = jax.vjp(gelu_exact, pre_act)
    hidden_b = hidden_f.astype(jnp.bfloat16)
    dhidden = jnp.einsum(
        "recd,efd->recf", grads_all, w_out_exp, preferred_element_type=jnp.float32
    ).astype(jnp.bfloat16)
    dpre = gelu_back(dhidden.astype(jnp.float32))[0].astype(jnp.bfloat16)
    grad_w_out_exp = jnp.einsum(
        "recf,recd->efd", hidden_b, grads_all, preferred_element_type=jnp.float32
    )
    grad_b_out_exp = jnp.sum(grads_all, axis=(0, 2), dtype=jnp.float32)
    grad_w_in_exp = jnp.einsum("recd,recf->edf", rows_all, dpre, preferred_element_type=jnp.float32)
    grad_b_in_exp = jnp.sum(dpre, axis=(0, 2), dtype=jnp.float32)
    drows = jnp.einsum("recf,edf->recd", dpre, w_in_exp, preferred_element_type=jnp.float32)
    drows_sum = lax.psum_scatter(
        drows.astype(jnp.bfloat16), "batch", scatter_dimension=0, tiled=True
    )
    drows_home = lax.all_to_all(drows_sum, "seq", split_axis=0, concat_axis=0, tiled=True)
    second_residual_gradient = jnp.einsum(
        "st,sd->td",
        dispatch,
        drows_home.reshape(experts_all * capacity, D),
        preferred_element_type=jnp.float32,
    )
    second_norm_gradient, second_gain_gradient, second_shift_gradient = norm_backward_pass(
        second_residual_gradient, second_centred_scaled, second_inverse_deviation, norm_gain_pair[1]
    )
    d_one = dout + second_norm_gradient
    d_one_b = d_one.astype(jnp.bfloat16)
    grad_w_out = jnp.einsum("td,te->de", attended_b, d_one_b, preferred_element_type=jnp.float32)
    grad_out_bias = jnp.sum(d_one, axis=0)
    dout_b = jnp.einsum("te,de->td", d_one_b, w_out, preferred_element_type=jnp.float32).astype(
        jnp.bfloat16
    )
    dout_h = dout_b.reshape(tok_rows, HEADS, HEAD_DIM)
    delta = jnp.einsum("thd,thd->ht", dout_h.astype(jnp.float32), attended)
    dquery = run_keys(dquery_step, head_zeros)
    lse_rows = log_mass.T
    delta_rows = delta.T
    block_rows = math.gcd(tok_rows * lax.axis_size("seq"), 512)

    def one_block(block_index):
        first_key = block_index * block_rows
        block_kv = lax.dynamic_slice_in_dim(all_kv, first_key, block_rows, 0)
        block_pad = lax.dynamic_slice_in_dim(all_pad, first_key, block_rows, 0)
        k_pos = first_key + jnp.arange(block_rows, dtype=jnp.int32)
        grad_k, grad_v = key_grads(
            query_h,
            dout_h,
            lse_rows,
            delta_rows,
            q_pos,
            q_doc,
            block_kv[:, :D].reshape(block_rows, HEADS, HEAD_DIM),
            block_kv[:, D:].reshape(block_rows, HEADS, HEAD_DIM),
            k_pos,
            doc_of(k_pos, doc_ends),
            block_pad,
        )
        return jnp.concatenate(
            [grad_k.reshape(block_rows, D), grad_v.reshape(block_rows, D)], axis=1
        )

    blocks = lax.map(
        one_block, jnp.arange(tok_rows * lax.axis_size("seq") // block_rows, dtype=jnp.int32)
    )
    key_terms = lax.psum_scatter(
        blocks.reshape(tok_rows * lax.axis_size("seq"), 2 * D).astype(jnp.bfloat16),
        "seq",
        scatter_dimension=0,
        tiled=True,
    )
    dq_b = dquery.reshape(tok_rows, D).astype(jnp.bfloat16)
    dmixed = jnp.concatenate([dq_b * scale, key_terms], axis=1)
    grad_w_qkv = jnp.einsum("td,te->de", h_one, dmixed, preferred_element_type=jnp.float32)
    first_hidden_gradient = jnp.einsum(
        "te,de->td", dmixed, w_qkv, preferred_element_type=jnp.float32
    )
    first_norm_gradient, first_gain_gradient, first_shift_gradient = norm_backward_pass(
        first_hidden_gradient, first_centred_scaled, first_inverse_deviation, norm_gain_pair[0]
    )
    input_grad = (d_one + first_norm_gradient).astype(jnp.bfloat16)
    grad_q_bias = jnp.sum(dmixed[:, :D], axis=0, dtype=jnp.float32)
    grad_v_bias = jnp.sum(key_terms[:, D:], axis=0, dtype=jnp.float32)
    small_grads = jnp.stack(
        [
            first_gain_gradient,
            second_gain_gradient,
            first_shift_gradient,
            second_shift_gradient,
            grad_q_bias,
            grad_v_bias,
            grad_out_bias,
        ]
    )
    shared_qkv, shared_out, shared_small = (
        lax.psum_scatter(grad_w_qkv, ("seq", "batch"), scatter_dimension=0, tiled=True),
        lax.psum_scatter(grad_w_out, ("seq", "batch"), scatter_dimension=0, tiled=True),
        lax.psum_scatter(small_grads, ("seq", "batch"), scatter_dimension=1, tiled=True),
    )
    return (
        output[None],
        input_grad[None],
        shared_small[0:2],
        shared_small[2:4],
        shared_qkv,
        shared_small[4:6],
        shared_out,
        shared_small[6],
        grad_w_in_exp,
        grad_b_in_exp,
        grad_w_out_exp,
        grad_b_out_exp,
    )


MICROSECOND = 1 << 30


def cost(us):
    return pl.CostEstimate(flops=us * MICROSECOND, bytes_accessed=1 << 20, transcendentals=0)


MICROSECOND = 1 << 30


def cost(us):
    return pl.CostEstimate(flops=us * MICROSECOND, bytes_accessed=1 << 20, transcendentals=0)


HALVES = [slice(h * HEAD_DIM, (h + 1) * HEAD_DIM) for h in range(2)]


def block_rows(i, T):
    return pl.ds(pl.multiple_of(i * T, T), T)


def diag_parts(T, key_rows):
    lane = iota((T, 256), 1)
    values = key_rows.astype(F32)
    unpadded = jnp.where(lane == 136, 0.0, values).astype(BF16)
    k_at, q_at = iota((T, T), 0), iota((T, T), 1)
    padded = values[:, 136:137] > 0.5
    allowed = ((k_at < q_at) & jnp.logical_not(padded)) | (k_at == q_at)
    return unpadded, allowed


def ring_kernel(n, T, cap, block, parts, at_tile, diags, pairs, first, last, extra, sc, *refs):
    refs = list(refs)

    def take(count):
        got = refs[:count]
        del refs[:count]
        return got

    count = len(parts)
    chunks = [take(p) for p in parts]
    wq, wk, wv, qvb, gain, bias, docs = take(7)
    old = [] if first else take(9)
    take(extra)
    outs = take(9)
    results = take(3) if last else None
    h_out, sel_out, qa_out, ka_out, vt_out, code_out = outs[:6]
    h_s, sel_s, qa, ka, vt, code, top, mass, acc, w, in_sems, out_sems = take(12)
    me = sc[n]
    loads = [
        pltpu.make_async_copy(ref, to, in_sems.at[i])
        for i, (ref, to) in enumerate(zip(old[2:], (qa, ka, vt, code, top, mass, acc)))
    ]
    for load in loads:
        load.start()
    w[:, 0:128] = wq[...]
    w[:, 128:256] = wk[...]
    w[:, 256:384] = wv[...]
    payloads = []
    for c in range(count):
        rows = [ref[...] for ref in chunks[c]]
        rows = rows[0] if len(rows) == 1 else jnp.concatenate(rows, axis=0)
        payloads.append(rows)
        vhat, _ = normed_rows(rows[0:T].astype(F32))
        h_s[c] = (vhat * gain[...] + bias[...]).astype(BF16)
    for load in loads:
        load.wait()
    stores = []

    def send(ref, to):
        store = pltpu.make_async_copy(ref, to, out_sems.at[len(stores)])
        store.start()
        stores.append(store)

    for c in range(count):
        src = sc[block + c]
        rows = block_rows(src, T)
        mixed = dot_nn(h_s[c], w[...])
        q = ((mixed[:, 0:128] + qvb[0:1, :]) * (HEAD_DIM**-0.5)).astype(BF16).astype(F32)
        v = (mixed[:, 256:384] + qvb[1:2, :]).astype(BF16)
        codes = payloads[c][T : T + 16].astype(F32)
        id_row = codes[0:1, 0:T]
        pad_row = codes[0:1, T : 2 * T]
        id_col = jnp.transpose(jnp.broadcast_to(id_row, (128, T)))
        pad_col = jnp.transpose(jnp.broadcast_to(pad_row, (128, T)))
        same = jnp.where(
            (id_col[:, 0:1] == id_row) & (iota((T, T), 0) < iota((T, T), 1)), 1.0, 0.0
        )
        rank_row = jnp.sum(same, axis=0, keepdims=True)
        rank_col = jnp.transpose(jnp.broadcast_to(rank_row, (128, T)))
        lane = iota((T, 128), 1)
        pos = (iota((T, 128), 0) + src * T).astype(F32)
        doc = jnp.where((pos >= docs[0:1, :]) & (pos < docs[1:2, :]), 1.0, 0.0)
        aug = jnp.where(lane < 8, doc, 0.0)
        aug = jnp.where(lane == 8, 1.0 - pad_col, aug)
        aug = jnp.where(lane == 16, id_col, aug)
        aug = jnp.where(lane == 17, rank_col, aug)
        masked = jnp.where(lane < 8, (doc - 1.0) * BIG, jnp.where(lane == 8, -BIG, 0.0)).astype(BF16)
        for h in range(2):
            mine = (lane < HEAD_DIM) == (h == 0)
            qa[h, rows, 0:128] = jnp.where(mine, q, 0.0).astype(BF16)
            qa[h, rows, 128:256] = masked
        ka[rows, 0:128] = mixed[:, 128:256].astype(BF16)
        ka[rows, 128:256] = aug.astype(BF16)
        ka[rows, 256:384] = v
        vt[src] = jnp.transpose(v.astype(F32)).astype(BF16)
        slot = (id_row * cap + rank_row).astype(jnp.int32)
        half = lax.rem(src, 2) * cap
        code[src] = (id_row * (2 * cap) + rank_row).astype(jnp.int32) + half
        pick = jnp.where(
            slot == iota((EXP_DEV * cap, T), 0) + me * (EXP_DEV * cap), 1.0, 0.0
        ).astype(BF16)
        chosen = dot_nn(pick, payloads[c][0:T])
        for e in range(EXP_DEV):
            sel_s[c, e] = chosen[e * cap : (e + 1) * cap]
            send(sel_s.at[c, e], sel_out.at[e, src])
        send(h_s.at[c], h_out.at[src])
        for h in range(2):
            send(qa.at[h, rows], qa_out.at[h, rows])
        send(ka.at[rows], ka_out.at[rows])
        if not last:
            send(vt.at[src], vt_out.at[src])
            send(code.at[src], code_out.at[src])

    def one_diag(r, carry):
        i = sc[at_tile + 2 * r]
        rows = block_rows(i, T)
        kd, allowed = diag_parts(T, ka[rows, 0:256])
        for h in range(2):
            s = jnp.where(allowed, dot_nt(kd, qa[h, rows, :]), NEG)
            best = jnp.max(s, axis=0, keepdims=True)
            p = jnp.exp(s - best)
            top[h, i] = best
            mass[h, i] = jnp.sum(p, axis=0, keepdims=True)
            acc[i, HALVES[h], :] = dot_nn(vt[i, HALVES[h], :], p.astype(BF16))
        return carry

    lax.fori_loop(0, diags, one_diag, 0)

    def pair_tile(at):
        i, j = sc[at_tile + 2 * at], sc[at_tile + 2 * at + 1]
        rows, cols = block_rows(i, T), block_rows(j, T)
        old_top = [top[h, i] for h in range(2)]
        old_mass = [mass[h, i] for h in range(2)]
        old_acc = [acc[i, HALVES[h], :] for h in range(2)]
        s = [dot_nt(ka[cols, 0:256], qa[h, rows, :]) for h in range(2)]
        best = [jnp.maximum(old_top[h], jnp.max(s[h], axis=0, keepdims=True)) for h in range(2)]
        p = [jnp.exp(s[h] - best[h]) for h in range(2)]
        more = [dot_nn(vt[j, HALVES[h], :], p[h].astype(BF16)) for h in range(2)]
        for h in range(2):
            fade = jnp.exp(old_top[h] - best[h])
            top[h, i] = best[h]
            mass[h, i] = old_mass[h] * fade + jnp.sum(p[h], axis=0, keepdims=True)
            acc[i, HALVES[h], :] = old_acc[h] * fade + more[h]

    def two_pairs(r, carry):
        pair_tile(diags + 2 * r)
        pair_tile(diags + 2 * r + 1)
        return carry

    lax.fori_loop(0, pairs // 2, two_pairs, 0)
    if pairs % 2:
        pair_tile(diags + pairs - 1)
    if not last:
        for ref, to in zip((top, mass, acc), outs[6:]):
            send(ref, to)
    else:
        att_out, o_out, lse_out = results

        def finish(i, carry):
            rows = block_rows(i, T)
            scaled = []
            for h in range(2):
                lse_out[h, i] = top[h, i] + jnp.log(mass[h, i])
                scaled.append(acc[i, HALVES[h], :] / mass[h, i])
            o_out[rows, :] = jnp.transpose(jnp.concatenate(scaled, axis=0))
            return carry

        lax.fori_loop(0, n, finish, 0)
        slots = n * EXP_DEV * 2 * cap

        def pair(p, carry):
            codes = jnp.concatenate([code[2 * p], code[2 * p + 1]], axis=1)
            pick = jnp.where(codes == iota((slots, 2 * T), 0), 1.0, 0.0).astype(BF16)
            chosen = dot_nn(pick, o_out[block_rows(p, 2 * T), :].astype(BF16)).astype(BF16)
            for k in range(n):
                for e in range(EXP_DEV):
                    at = (k * EXP_DEV + e) * 2 * cap
                    to = pl.multiple_of(e * n * cap + p * 2 * cap, 16)
                    att_out[k, pl.ds(to, 2 * cap), :] = chosen[at : at + 2 * cap]
            return carry

        lax.fori_loop(0, n // 2, pair, 0)
    for store in stores:
        store.wait()


def ring_call(
    n, T, cap, block, at_tile, diags, pairs, sc, chunks, held, last, w_qkv, qv_bias, gain, bias, docs, after
):
    row = n * T
    shapes = [
        ((n, T, D), BF16),
        ((EXP_DEV, n, cap, D), F32),
        ((2, row, 256), BF16),
        ((row, 384), BF16),
        ((n, 128, T), BF16),
        ((n, 1, T), jnp.int32),
        ((2, n, 1, T), F32),
        ((2, n, 1, T), F32),
        ((n, 128, T), F32),
    ]
    anywhere = pl.BlockSpec(memory_space=pl.ANY)
    operands = [part for chunk in chunks for part in chunk]
    in_specs = [whole(part.shape) for part in operands] + [
        pl.BlockSpec((D, 128), lambda i, sc: (0, sc[n])),
        pl.BlockSpec((D, 128), lambda i, sc: (0, n + sc[n])),
        pl.BlockSpec((D, 128), lambda i, sc: (0, 2 * n + sc[n])),
        pl.BlockSpec((2, 128), lambda i, sc: (0, sc[n])),
        whole((1, D)),
        whole((1, D)),
        whole((2, 128)),
    ]
    aliases = {}
    first = held is None
    if not first:
        aliases = {1 + len(in_specs) + i: i for i in range(len(shapes))}
        in_specs = in_specs + [anywhere] * len(shapes)
    in_specs = in_specs + [anywhere] * len(after)
    out_specs = [anywhere] * len(shapes)
    results = []
    if last:
        results = [((n, EXP_DEV * n * cap, 128), BF16), ((row, 128), F32), ((2, n, 1, T), F32)]
        out_specs = out_specs + [whole(s) for s, _ in results]
    count = len(chunks)
    parts = [len(chunk) for chunk in chunks]
    return pl.pallas_call(
        lambda *a: ring_kernel(
            n, T, cap, block, parts, at_tile, diags, pairs, first, last, len(after), *a
        ),
        grid_spec=pltpu.PrefetchScalarGridSpec(
            num_scalar_prefetch=1,
            grid=(1,),
            in_specs=in_specs,
            out_specs=out_specs,
            scratch_shapes=[
                pltpu.VMEM((count, T, D), BF16),
                pltpu.VMEM((count, EXP_DEV, cap, D), F32),
            ]
            + [pltpu.VMEM(s, t) for s, t in shapes[2:]]
            + [
                pltpu.VMEM((D, 384), BF16),
                pltpu.SemaphoreType.DMA((7,)),
                pltpu.SemaphoreType.DMA((8 * count + 3,)),
            ],
        ),
        out_shape=[jax.ShapeDtypeStruct(s, t) for s, t in shapes + results],
        input_output_aliases=aliases,
        compiler_params=params(),
        cost_estimate=cost(10),
        name="ring_step",
    )(sc, *operands, w_qkv, w_qkv, w_qkv, qv_bias, gain, bias, docs, *(held or ()), *after)


def attn_bwd_kernel(
    n, T, cap, at_tile, diags, pairs, tiles, qa, ka, lse, o_ref, datt, *refs
):
    dm_out, do, delta, kh, dqa, dka, dva = refs[-7:]
    slots = n * EXP_DEV * 2 * cap

    def pair(p, carry):
        rows = block_rows(p, 2 * T)
        feature = ka[rows, 128:256].astype(F32)
        half = jnp.where(iota((2 * T, 1), 0) >= T, float(cap), 0.0)
        code = (feature[:, 16:17] * (2 * cap) + feature[:, 17:18] + half).astype(jnp.int32)
        pick = jnp.where(code == iota((2 * T, slots), 1), 1.0, 0.0).astype(BF16)
        parts = []
        for k in range(n):
            for e in range(EXP_DEV):
                at = pl.multiple_of(e * n * cap + p * 2 * cap, 16)
                parts.append(datt[k, pl.ds(at, 2 * cap), :])
        got = dot_nn(pick, jnp.concatenate(parts, axis=0))
        lane = iota((2 * T, 128), 1)
        keys = ka[rows, 0:128].astype(F32)
        for h in range(2):
            mine = (lane < HEAD_DIM) == (h == 0)
            do[h, rows, :] = jnp.where(mine, got, 0.0).astype(BF16)
            kh[h, rows, :] = jnp.where(mine, keys, 0.0).astype(BF16)
        prod = jnp.transpose(got * o_ref[rows, :])
        for h in range(2):
            total = jnp.sum(prod[HALVES[h], :], axis=0, keepdims=True)
            delta[h, 2 * p] = total[:, 0:T]
            delta[h, 2 * p + 1] = total[:, T : 2 * T]
        return carry

    lax.fori_loop(0, n // 2, pair, 0)

    def tile(i, j, key_rows, mask):
        rows, cols = block_rows(i, T), block_rows(j, T)
        ps, dss = [], []
        for h in range(2):
            s = dot_nt(key_rows, qa[h, rows, :])
            dp = dot_nt(ka[cols, 256:384], do[h, rows, :])
            if mask is not None:
                s = jnp.where(mask, s, NEG)
            p = jnp.exp(s - lse[h, i])
            dss.append((p * (dp - delta[h, i])).astype(BF16))
            ps.append(p.astype(BF16))
        dv = dot_nn(
            jnp.concatenate(ps, axis=1), jnp.concatenate([do[0, rows, :], do[1, rows, :]], axis=0)
        )
        dk = dot_nn(
            jnp.concatenate(dss, axis=1),
            jnp.concatenate([qa[0, rows, 0:128], qa[1, rows, 0:128]], axis=0),
        )
        dq = dot_tn(
            jnp.concatenate(dss, axis=0), jnp.concatenate([kh[0, cols, :], kh[1, cols, :]], axis=0)
        )
        return dq, dk, dv

    def diag_tile(j, carry):
        kd, allowed = diag_parts(T, ka[block_rows(j, T), 0:256])
        dqa[j], dka[j], dva[j] = tile(j, j, kd, allowed)
        return carry

    lax.fori_loop(0, n, diag_tile, 0)

    def pair_tile(at):
        i, j = tiles[at_tile + 2 * at], tiles[at_tile + 2 * at + 1]
        dq, dk, dv = tile(i, j, ka[block_rows(j, T), 0:256], None)
        dqa[i] += dq
        dka[j] += dk
        dva[j] += dv

    width = next(w for w in (4, 2, 1) if pairs % w == 0)

    def some_pairs(r, carry):
        for w in range(width):
            pair_tile(diags + width * r + w)
        return carry

    lax.fori_loop(0, pairs // width, some_pairs, 0)

    def finish(i, carry):
        dq = dqa[i].astype(BF16).astype(F32)
        dm_out[i, :, 0:128] = (dq * (HEAD_DIM**-0.5)).astype(BF16)
        dm_out[i, :, 128:256] = dka[i].astype(BF16)
        dm_out[i, :, 256:384] = dva[i].astype(BF16)
        return carry

    lax.fori_loop(0, n, finish, 0)


def attn_bwd_call(n, T, cap, at_tile, diags, pairs, tiles, qa, ka, lse, o, datt, after):
    row = n * T
    vmem = pl.BlockSpec(memory_space=pltpu.VMEM)
    return pl.pallas_call(
        lambda *a: attn_bwd_kernel(n, T, cap, at_tile, diags, pairs, *a),
        out_shape=jax.ShapeDtypeStruct((n, T, 384), BF16),
        in_specs=[pl.BlockSpec(memory_space=pltpu.SMEM)]
        + [vmem] * 5
        + [pl.BlockSpec(memory_space=pl.ANY)] * len(after),
        out_specs=vmem,
        scratch_shapes=[
            pltpu.VMEM((2, row, 128), BF16),
            pltpu.VMEM((2, n, 1, T), F32),
            pltpu.VMEM((2, row, 128), BF16),
            pltpu.VMEM((n, T, 128), F32),
            pltpu.VMEM((n, T, 128), F32),
            pltpu.VMEM((n, T, 128), F32),
        ],
        compiler_params=params(),
        cost_estimate=cost(28),
        name="attn_bwd",
    )(tiles, qa, ka, lse, o, datt, *after)


def dispatch_kernel(cap, slots, ids, grads, *refs):
    out = refs[-1]
    id_row = ids[...].astype(F32)
    T = id_row.shape[1]
    id_col = jnp.transpose(jnp.broadcast_to(id_row, (128, T)))[:, 0:1]
    same = jnp.where((id_col == id_row) & (iota((T, T), 0) < iota((T, T), 1)), 1.0, 0.0)
    rank = jnp.sum(same, axis=0, keepdims=True)
    slot = (id_row * cap + rank).astype(jnp.int32)
    pick = jnp.where(slot == iota((slots, T), 0), 1.0, 0.0).astype(BF16)
    out[...] = dot_nn(pick, grads[...]).astype(BF16)


def dispatch_call(cap, slots, after, ids, grads):
    vmem = pl.BlockSpec(memory_space=pltpu.VMEM)
    return pl.pallas_call(
        lambda *a: dispatch_kernel(cap, slots, *a),
        out_shape=jax.ShapeDtypeStruct((slots, D), BF16),
        in_specs=[vmem, vmem] + [pl.BlockSpec(memory_space=pl.ANY)] * len(after),
        out_specs=vmem,
        compiler_params=params(),
        cost_estimate=cost(3),
        name="dispatch",
    )(ids, grads, *after)


def owner_fwd_kernel(n, att_in, w_out, sel, out_bias, gain, bias, x_two, x_one, att_b):
    for k in range(n):
        att_b[:, k * 128 : (k + 1) * 128] = att_in[k]
    branch = dot_nn(att_b[...], w_out[...]) + out_bias[...]
    x = sel[...] + branch
    x_one[...] = x
    vhat, _ = normed_rows(x)
    x_two[...] = (vhat * gain[...] + bias[...]).astype(BF16)


def owner_fwd_call(n, e, att_in, w_out, sel, out_bias, gain, bias):
    slots = sel.shape[0] // EXP_DEV
    rows = pl.BlockSpec((slots, D), lambda i: (e, 0))
    mine = whole((slots, D))
    return pl.pallas_call(
        lambda *a: owner_fwd_kernel(n, *a),
        grid=(1,),
        in_specs=[
            pl.BlockSpec((n, slots, 128), lambda i: (0, e, 0)),
            whole((D, D)),
            rows,
            whole((1, D)),
            whole((1, D)),
            whole((1, D)),
        ],
        out_specs=[mine, mine, mine],
        out_shape=[
            jax.ShapeDtypeStruct((slots, D), BF16),
            jax.ShapeDtypeStruct((slots, D), F32),
            jax.ShapeDtypeStruct((slots, D), BF16),
        ],
        compiler_params=params(),
        cost_estimate=cost(3),
        name="owner_fwd",
    )(att_in, w_out, sel, out_bias, gain, bias)


def owner_bwd_kernel(n, part_a, part_b, x_one, og, gain, w_out, *refs):
    datt, d_one_b, small = refs[-3:]
    u = (part_a[...].astype(F32) + part_b[...].astype(F32)).astype(BF16).astype(F32)
    vhat, inv_std = normed_rows(x_one[...])
    scaled = u * gain[...]
    first = jnp.mean(scaled, axis=-1, keepdims=True)
    second = jnp.mean(scaled * vhat, axis=-1, keepdims=True)
    d_one = og[...].astype(F32) + inv_std * (scaled - first - vhat * second)
    d_b = d_one.astype(BF16)
    d_one_b[...] = d_b
    back = dot_nt(d_b, w_out[...]).astype(BF16)
    for k in range(n):
        datt[k] = back[:, k * 128 : (k + 1) * 128]
    small[0:1, :] = jnp.sum(u * vhat, axis=0, keepdims=True)
    small[1:2, :] = jnp.sum(u, axis=0, keepdims=True)
    small[2:3, :] = jnp.sum(d_one, axis=0, keepdims=True)


def owner_bwd_call(n, e, part_a, part_b, x_one, og, gain, w_out, held, after):
    slots = x_one.shape[0]
    mine = whole((slots, D))
    in_specs = [
        mine,
        mine,
        mine,
        pl.BlockSpec((slots, D), lambda i: (e, 0)),
        whole((1, D)),
        whole((D, D)),
    ]
    more = ([] if held is None else [held]) + after
    return pl.pallas_call(
        lambda *a: owner_bwd_kernel(n, *a),
        grid=(1,),
        in_specs=in_specs + [pl.BlockSpec(memory_space=pl.ANY)] * len(more),
        out_specs=[
            pl.BlockSpec((n, slots, 128), lambda i: (0, e, 0)),
            mine,
            whole((8, D)),
        ],
        out_shape=[
            jax.ShapeDtypeStruct((n, EXP_DEV * slots, 128), BF16),
            jax.ShapeDtypeStruct((slots, D), BF16),
            jax.ShapeDtypeStruct((8, D), F32),
        ],
        input_output_aliases={} if held is None else {len(in_specs): 0},
        compiler_params=params(),
        cost_estimate=cost(4),
        name="owner_bwd",
    )(part_a, part_b, x_one, og, gain, w_out, *more)


def gelu_parts(u):
    cdf = 0.5 * (1.0 + lax.erf(u * (0.5**0.5)))
    return cdf, cdf + u * jnp.exp(-0.5 * u * u) * ((2.0 * math.pi) ** -0.5)


def expert_kernel(nb, rows, steps, sc, *refs):
    x_parts, g_parts = refs[:nb], refs[nb : 2 * nb]
    w_in, b_in, w_out = refs[2 * nb : 2 * nb + 3]
    hidden_out, dpre_out, keep, send, grad_b, xs, gs, total = refs[-8:]
    f = pl.program_id(0)

    @pl.when(f == 0)
    def _():
        for k in range(nb):
            xs[k * rows : (k + 1) * rows, :] = x_parts[k][...]
            gs[k * rows : (k + 1) * rows, :] = g_parts[k][...]
        total[...] = jnp.zeros_like(total)

    pre = dot_nn(xs[...], w_in[0]) + b_in[0]
    cdf, slope = gelu_parts(pre)
    hidden_out[...] = (pre * cdf).astype(BF16)
    dhidden = dot_nt(gs[...], w_out[0]).astype(BF16).astype(F32)
    dpre = (dhidden * slope).astype(BF16)
    dpre_out[...] = dpre
    grad_b[0] = jnp.sum(dpre.astype(F32), axis=0, keepdims=True)
    total[...] += dot_nt(dpre, w_in[0])

    @pl.when(f == steps - 1)
    def _():
        for y in range(2):
            keep[y] = total[2 * y * rows : (2 * y + 1) * rows, :].astype(BF16)
            send[y] = total[(2 * y + 1) * rows : (2 * y + 2) * rows, :].astype(BF16)


def expert_call(e, sc, x_parts, g_parts, w_in, b_in, w_out, after):
    nb = len(x_parts)
    rows = x_parts[0].shape[0]
    ff = w_in.shape[2]
    width = min(256, ff)
    steps = ff // width
    g_specs = [pl.BlockSpec((rows, D), lambda f, sc: (e, 0))] * nb
    act = pl.BlockSpec((nb * rows, width), lambda f, sc: (0, f))
    return pl.pallas_call(
        lambda *a: expert_kernel(nb, rows, steps, *a),
        grid_spec=pltpu.PrefetchScalarGridSpec(
            num_scalar_prefetch=1,
            grid=(steps,),
            in_specs=[whole((rows, D))] * nb
            + g_specs
            + [
                pl.BlockSpec((1, D, width), lambda f, sc: (e, 0, f)),
                pl.BlockSpec((1, 1, width), lambda f, sc: (e, 0, f)),
                pl.BlockSpec((1, width, D), lambda f, sc: (e, f, 0)),
            ]
            + [pl.BlockSpec(memory_space=pl.ANY)] * len(after),
            out_specs=[
                act,
                act,
                whole((2, rows, D)),
                whole((2, rows, D)),
                pl.BlockSpec((1, 1, width), lambda f, sc: (0, 0, f)),
            ],
            scratch_shapes=[
                pltpu.VMEM((nb * rows, D), BF16),
                pltpu.VMEM((nb * rows, D), BF16),
                pltpu.VMEM((nb * rows, D), F32),
            ],
        ),
        out_shape=[
            jax.ShapeDtypeStruct((nb * rows, ff), BF16),
            jax.ShapeDtypeStruct((nb * rows, ff), BF16),
            jax.ShapeDtypeStruct((2, rows, D), BF16),
            jax.ShapeDtypeStruct((2, rows, D), BF16),
            jax.ShapeDtypeStruct((1, 1, ff), F32),
        ],
        compiler_params=params(),
        cost_estimate=cost(10),
        name="expert_main",
    )(sc, *x_parts, *g_parts, w_in, b_in[:, None, :], w_out, *after)


def expert_out_kernel(rows, hidden, w_out, keep, send):
    total = dot_nn(hidden[...], w_out[0]).astype(BF16)
    for y in range(2):
        keep[y] = total[2 * y * rows : (2 * y + 1) * rows, :]
        send[y] = total[(2 * y + 1) * rows : (2 * y + 2) * rows, :]


def expert_out_call(nb, e, hidden, w_out):
    rows = hidden.shape[0] // nb
    ff = hidden.shape[1]
    return pl.pallas_call(
        lambda *a: expert_out_kernel(rows, *a),
        grid=(1,),
        in_specs=[whole(hidden.shape), pl.BlockSpec((1, ff, D), lambda i: (e, 0, 0))],
        out_specs=[whole((2, rows, D))] * 2,
        out_shape=[jax.ShapeDtypeStruct((2, rows, D), BF16)] * 2,
        compiler_params=params(),
        cost_estimate=cost(4),
        name="expert_out",
    )(hidden, w_out)


def expert_grad_kernel(nb, rows, sc, *refs):
    x_parts, g_parts = refs[:nb], refs[nb : 2 * nb]
    hidden, dpre = refs[2 * nb : 2 * nb + 2]
    grad_in, grad_out, grad_b, xs, gs = refs[-5:]

    @pl.when(pl.program_id(0) == 0)
    def _():
        sums = []
        for k in range(nb):
            xs[k * rows : (k + 1) * rows, :] = x_parts[k][...]
            gs[k * rows : (k + 1) * rows, :] = g_parts[k][...]
            sums.append(jnp.sum(g_parts[k][...].astype(F32), axis=0, keepdims=True))
        grad_b[0] = (sums[0] + sums[1]) + (sums[2] + sums[3])

    grad_in[0] = dot_tn(xs[...], dpre[...])
    grad_out[0] = dot_tn(hidden[...], gs[...])


def expert_grad_call(e, sc, x_parts, g_parts, hidden, dpre, held, after):
    nb = len(x_parts)
    rows = x_parts[0].shape[0]
    ff = hidden.shape[1]
    width = min(256, ff)
    g_specs = [pl.BlockSpec((rows, D), lambda f, sc: (e, 0))] * nb
    act = pl.BlockSpec((nb * rows, width), lambda f, sc: (0, f))
    in_specs = [whole((rows, D))] * nb + g_specs + [act, act]
    more = [] if held is None else list(held)
    aliases = {1 + len(in_specs) + i: i for i in range(len(more))}
    more += after
    return pl.pallas_call(
        lambda *a: expert_grad_kernel(nb, rows, *a),
        grid_spec=pltpu.PrefetchScalarGridSpec(
            num_scalar_prefetch=1,
            grid=(ff // width,),
            in_specs=in_specs + [pl.BlockSpec(memory_space=pl.ANY)] * len(more),
            out_specs=[
                pl.BlockSpec((1, D, width), lambda f, sc: (e, 0, f)),
                pl.BlockSpec((1, width, D), lambda f, sc: (e, f, 0)),
                pl.BlockSpec((1, 1, D), lambda f, sc: (e, 0, 0)),
            ],
            scratch_shapes=[pltpu.VMEM((nb * rows, D), BF16)] * 2,
        ),
        out_shape=[
            jax.ShapeDtypeStruct((EXP_DEV, D, ff), F32),
            jax.ShapeDtypeStruct((EXP_DEV, ff, D), F32),
            jax.ShapeDtypeStruct((EXP_DEV, 1, D), F32),
        ],
        input_output_aliases=aliases,
        compiler_params=params(),
        cost_estimate=cost(8),
        name="expert_grads",
    )(sc, *x_parts, *g_parts, hidden, dpre, *more)


def w_out_grad_kernel(n, nb, sc, *refs):
    keep, send = refs[-2:]
    total = dot_tn(refs[0][...], refs[EXP_DEV][...])
    for e in range(1, EXP_DEV):
        total = total + dot_tn(refs[e][...], refs[EXP_DEV + e][...])
    size = D // (n * nb)
    core = lax.rem(sc[n + 1], 2)
    chip = lax.div(sc[n + 1], 2)
    for r in range(n):
        for y in range(nb // 2):
            first = (r * nb + 2 * y) * size
            pair = [total[first + c * size : first + (c + 1) * size].astype(BF16) for c in range(2)]
            place = y ^ chip
            at_keep = jnp.where(core == 0, pair[0].astype(F32), pair[1].astype(F32)).astype(BF16)
            at_send = jnp.where(core == 0, pair[1].astype(F32), pair[0].astype(F32)).astype(BF16)
            keep[place, r] = at_keep
            send[place, r] = at_send


def w_out_grad_call(n, nb, sc, att_b, d_one_b):
    size = D // (n * nb)
    shape = (nb // 2, n, size, D)
    return pl.pallas_call(
        lambda *a: w_out_grad_kernel(n, nb, *a),
        grid_spec=pltpu.PrefetchScalarGridSpec(
            num_scalar_prefetch=1,
            grid=(1,),
            in_specs=[whole(att_b[0].shape)] * (2 * EXP_DEV),
            out_specs=[whole(shape)] * 2,
        ),
        out_shape=[jax.ShapeDtypeStruct(shape, BF16)] * 2,
        compiler_params=params(),
        cost_estimate=cost(4),
        name="w_out_grad",
    )(sc, *att_b, *d_one_b)


def qkv_grad_kernel(n, nb, T, sc, h, dm, aux, after, keep, send, total):
    me_b = sc[n + 1]

    def add(c, carry):
        total[...] += dot_tn(dm[c], h[c])
        return carry

    total[...] = jnp.zeros_like(total)
    lax.fori_loop(0, n, add, 0)
    col_sum = jnp.zeros((1, 384), F32)
    for r in range(n):
        col_sum = col_sum + jnp.sum(dm[r].astype(F32), axis=0, keepdims=True)
    width = D // n
    size = width // nb
    top = iota((16, 384), 0)
    for r in range(n):
        part = jnp.transpose(total[:, r * width : (r + 1) * width])
        for k in range(nb):
            bb = me_b ^ k
            rows = jnp.zeros((size, 384), F32)
            for c in range(nb):
                rows = jnp.where(bb == c, part[c * size : (c + 1) * size, :], rows)
            extra = jnp.where(
                top == 0, col_sum, jnp.where(top == 1, aux[r * nb + bb], 0.0)
            )
            to = keep if k % 2 == 0 else send
            to[k // 2, r, 0:size, :] = rows.astype(BF16)
            to[k // 2, r, size : size + 16, :] = extra.astype(BF16)


def qkv_grad_call(n, nb, T, sc, h, dm, aux, after):
    size = D // (n * nb)
    shape = (2, n, size + 16, 384)
    return pl.pallas_call(
        lambda *a: qkv_grad_kernel(n, nb, T, *a),
        grid_spec=pltpu.PrefetchScalarGridSpec(
            num_scalar_prefetch=1,
            grid=(1,),
            in_specs=[
                whole((n, T, D)),
                whole((n, T, 384)),
                whole((n * nb, 1, 384)),
                pl.BlockSpec(memory_space=pl.ANY),
            ],
            out_specs=[whole(shape), whole(shape)],
            scratch_shapes=[pltpu.VMEM((384, D), F32)],
        ),
        out_shape=[jax.ShapeDtypeStruct(shape, BF16)] * 2,
        compiler_params=params(),
        cost_estimate=cost(8),
        name="qkv_grad",
    )(sc, h, dm, aux, after)


def scatter_rows(cap, slots, kaug, values):
    feature = kaug[:, 128:256].astype(F32)
    code = (feature[:, 16:17] * cap + feature[:, 17:18]).astype(jnp.int32)
    pick = jnp.where(code == iota((feature.shape[0], slots), 1), 1.0, 0.0).astype(BF16)
    return dot_nn(pick, values)


def input_grad_kernel(n, T, cap, sc, dm, w_qkv, hidden, d_ret, kaug, gain, out, full):
    for k in range(n):
        for part in range(3):
            full[:, part * D + k * 128 : part * D + (k + 1) * 128] = dm[
                k, :, part * 128 : (part + 1) * 128
            ]
    u = dot_nt(full[...], w_qkv[...])
    vhat, inv_std = normed_rows(hidden[...].astype(F32))
    scaled = u * gain[...]
    first = jnp.mean(scaled, axis=-1, keepdims=True)
    second = jnp.mean(scaled * vhat, axis=-1, keepdims=True)
    d_one = scatter_rows(cap, d_ret.shape[0], kaug[...], d_ret[...])
    out[...] = (d_one + inv_std * (scaled - first - vhat * second)).astype(BF16)


def input_grad_call(n, T, cap, sc, dm, w_qkv, hidden, d_ret, kaug, gain):
    slots = d_ret.shape[0]
    return pl.pallas_call(
        lambda *a: input_grad_kernel(n, T, cap, *a),
        grid_spec=pltpu.PrefetchScalarGridSpec(
            num_scalar_prefetch=1,
            grid=(1,),
            in_specs=[
                whole((n, T, 384)),
                whole((D, 3 * D)),
                whole((T, D)),
                whole((slots, D)),
                pl.BlockSpec((T, 256), lambda i, sc: (sc[n], 0)),
                whole((1, D)),
            ],
            out_specs=whole((T, D)),
            scratch_shapes=[pltpu.VMEM((T, 3 * D), BF16)],
        ),
        out_shape=jax.ShapeDtypeStruct((T, D), BF16),
        compiler_params=params(),
        cost_estimate=cost(60),
        name="input_grad",
    )(sc, dm, w_qkv, hidden, d_ret, kaug, gain)


def output_kernel(cap, sc, ret, kaug, out):
    out[...] = scatter_rows(cap, ret.shape[0], kaug[...], ret[...]).astype(BF16)


def output_call(n, T, cap, sc, ret, kaug):
    return pl.pallas_call(
        lambda *a: output_kernel(cap, *a),
        grid_spec=pltpu.PrefetchScalarGridSpec(
            num_scalar_prefetch=1,
            grid=(1,),
            in_specs=[
                whole(ret.shape),
                pl.BlockSpec((T, 256), lambda i, sc: (sc[n], 0)),
            ],
            out_specs=whole((T, D)),
        ),
        out_shape=jax.ShapeDtypeStruct((T, D), BF16),
        compiler_params=params(),
        cost_estimate=cost(3),
        name="output_rows",
    )(sc, ret, kaug)


def final_kernel(n, nb, sc, got, w_rows, gb, gw, gains, biases, qvb, outb, s_rows, w_full):
    size = D // (n * nb)
    me, me_b = sc[n], sc[n + 1]
    smalls = jnp.zeros((1, 384), F32)
    s_rows[...] = jnp.zeros_like(s_rows)
    for k in range(n):
        tile = got[k].astype(F32)
        for part in range(3):
            cols = slice(part * D + k * 128, part * D + (k + 1) * 128)
            w_full[:, cols] = tile[0:size, part * 128 : (part + 1) * 128]
            s_rows[0:1, cols] = tile[size : size + 1, part * 128 : (part + 1) * 128]
        smalls = smalls + tile[size + 1 : size + 2, :]
    gw[...] = w_full[...]
    weights = w_rows[...].astype(F32)
    high = lax.Precision.HIGHEST
    nt = (((1,), (1,)), ((), ()))
    bias_one = lax.dot_general(s_rows[...], weights, nt, precision=high, preferred_element_type=F32)[0:1]
    both = lax.dot_general(
        jnp.ones((8, 3 * D), F32), weights * w_full[...], nt, precision=high, preferred_element_type=F32
    )[0:1]
    gains[0:1, :] = (both - gb[1:2, :] * bias_one) / gb[0:1, :]
    gains[1:2, :] = smalls[:, 0:size]
    biases[0:1, :] = bias_one
    biases[1:2, :] = smalls[:, size : 2 * size]
    outb[...] = smalls[:, 2 * size : 3 * size]
    own = got[me, size : size + 16, :].astype(F32)[0:1]
    for row, first in ((0, 0), (1, 256)):
        value = jnp.zeros((1, size), F32)
        for c in range(nb):
            value = jnp.where(me_b == c, own[:, first + c * size : first + (c + 1) * size], value)
        qvb[row : row + 1, :] = value


def final_call(n, nb, sc, got, w_qkv, gb):
    size = D // (n * nb)
    shapes = [(size, 3 * D), (2, size), (2, size), (2, size), (1, size)]
    return pl.pallas_call(
        lambda *a: final_kernel(n, nb, *a),
        grid_spec=pltpu.PrefetchScalarGridSpec(
            num_scalar_prefetch=1,
            grid=(1,),
            in_specs=[
                whole((n, size + 16, 384)),
                pl.BlockSpec((size, 3 * D), lambda i, sc: (nb * sc[n] + sc[n + 1], 0)),
                whole((2, size)),
            ],
            out_specs=[whole(s) for s in shapes],
            scratch_shapes=[pltpu.VMEM((8, 3 * D), F32), pltpu.VMEM((size, 3 * D), F32)],
        ),
        out_shape=[jax.ShapeDtypeStruct(s, F32) for s in shapes],
        compiler_params=params(),
        cost_estimate=cost(3),
        name="final_rows",
    )(sc, got, w_qkv, gb)


def exchange(values, axis, bit):
    size = lax.axis_size(axis)
    return lax.ppermute(values, axis, [(i, i ^ bit) for i in range(size)])


def arrival_tables(n, ring):
    place = [ring.index(i) for i in range(n)]
    order = [[0]] + [[-o, o] for o in range(1, n // 2)] + [[n // 2]]
    sources, tiles, counts = [], [], None
    for i in range(n):
        blocks = [[ring[(place[i] + o) % n] for o in step] for step in order]
        arrived, listed, sizes = [], [], []
        for at, step in enumerate(blocks):
            arrived += step
            if at == 0:
                continue
            new = arrived if at == 1 else step
            diag = [(q, q) for q in sorted(new)]
            pairs = [
                (q, k)
                for k in range(n)
                for q in range(k + 1, n)
                if q in arrived and k in arrived and (q in new or k in new)
            ]
            listed.append([x for t in diag + pairs for x in t])
            sizes.append((len(diag), len(pairs)))
        sources.append([b for step in blocks for b in step])
        tiles.append(listed)
        counts = counts or sizes
    return np.array(sources, np.int32), tiles, counts


def reduce_cores(keep, send, after=None):
    got = exchange(send, "batch", 1)
    if after is not None:
        got = gate(got, after)
    return [(keep[y].astype(F32) + got[y].astype(F32)).astype(BF16) for y in range(2)]


def gate(value, *after):
    def nothing(*refs):
        del refs

    anywhere = pl.BlockSpec(memory_space=pl.ANY)
    return pl.pallas_call(
        nothing,
        in_specs=[anywhere] * (1 + len(after)),
        out_specs=anywhere,
        out_shape=jax.ShapeDtypeStruct(value.shape, value.dtype),
        input_output_aliases={0: 0},
        name="gate",
    )(value, *after)


def local_by_heads(
    hidden_in,
    out_grad,
    norm_gain_pair,
    norm_bias_pair,
    w_qkv,
    qv_bias,
    w_out,
    out_bias,
    w_in_exp,
    b_in_exp,
    w_out_exp,
    b_out_exp,
    expert_ids,
    doc_lengths,
    pad_mask,
):
    T = hidden_in.shape[1]
    n, nb = lax.axis_size("seq"), lax.axis_size("batch")
    experts = EXP_DEV * n
    cap = max(2, 3 * T // (2 * experts))
    s, b = lax.axis_index("seq"), lax.axis_index("batch")
    ring = [*range(0, n, 2), *range(n - 1, 0, -2)]
    sources, tiles, counts = arrival_tables(n, ring)

    every = [(i, i) for i in range(n)] + [(q, k) for k in range(n) for q in range(k + 1, n)]
    every = np.array(every, np.int32).reshape(-1)
    table = [
        np.concatenate([sources[i], [i, 0]] + tiles[i] + [every]).astype(np.int32) for i in range(n)
    ]
    firsts = n + 2 + np.cumsum([0] + [2 * (d + p) for d, p in counts])
    row = lax.dynamic_index_in_dim(jnp.asarray(np.stack(table)), s, 0, keepdims=False)
    sc = jnp.where(jnp.arange(row.shape[0]) == n + 1, b.astype(jnp.int32), row)
    hidden = hidden_in[0]
    ids = expert_ids[0, :, 0]
    codes = jnp.concatenate([ids, pad_mask[0], jnp.zeros((D - 2 * T,), jnp.int32)]).astype(BF16)
    codes = jnp.where(jnp.arange(16)[:, None] == 0, codes[None, :], jnp.zeros((), BF16))
    payload = jnp.concatenate([hidden, codes], axis=0)

    count = doc_lengths.shape[1]
    at = jnp.arange(128)
    ends = jnp.sum(
        jnp.where(jnp.arange(count)[:, None] <= at[None, :], doc_lengths[0][:, None], 0), axis=0
    )
    starts = jnp.sum(
        jnp.where(jnp.arange(count)[:, None] < at[None, :], doc_lengths[0][:, None], 0), axis=0
    )
    docs = jnp.stack([starts, ends]).astype(F32)
    gain_rows = [norm_gain_pair[i : i + 1] for i in range(2)]
    bias_rows = [norm_bias_pair[i : i + 1] for i in range(2)]

    ahead = [(ring[i], ring[(i + 1) % n]) for i in range(n)]
    back = [(ring[i], ring[i - 1]) for i in range(n)]
    split = -(-payload.shape[0] // 32) * 16
    held, block = None, 0
    left = right = payload
    waiting = [[payload]]
    sent_grads = dispatch_call(cap, experts * cap, [], ids[None], out_grad[0])
    for step in range(1, n // 2 + 1):
        last = step == n // 2
        if last:
            left, right = left[:split], right[split:]
        left, right = lax.ppermute(left, "seq", ahead), lax.ppermute(right, "seq", back)
        if last:
            waiting.append([left, right])
        else:
            left = gate(left, right, *(held or ())[6:7])
            right = gate(right, left)
            waiting += [[left], [right]]
        if last:
            sent_grads = gate(sent_grads, left, right, held[6])
        diags, pairs = counts[step - 1]
        held = ring_call(
            n, T, cap, block, int(firsts[step - 1]), diags, pairs, sc, waiting, held, last,
            w_qkv, qv_bias, gain_rows[0], bias_rows[0], docs, [sent_grads] if last else [],
        )
        block += len(waiting)
        waiting = []
    h_one, sel, qa, ka = held[:4]
    att_out, o, lse = held[9:]
    sel = sel.reshape(EXP_DEV * n * cap, D)

    sent_grads = sent_grads.reshape(n, EXP_DEV * cap, D)
    grads = lax.all_to_all(sent_grads, "seq", split_axis=0, concat_axis=0, tiled=True)
    grads = grads.reshape(n, EXP_DEV, cap, D).transpose(1, 0, 2, 3).reshape(experts * cap, D)
    g_y = exchange(grads, "batch", 2)
    g_parts = [grads, exchange(grads, "batch", 1), g_y, exchange(g_y, "batch", 1)]

    att_in = lax.all_to_all(att_out, "seq", split_axis=0, concat_axis=0, tiled=True)
    x_two, x_one, att_b = [], [], []
    for e in range(EXP_DEV):
        rows, one, att_rows = owner_fwd_call(
            n, e, att_in, w_out, sel, out_bias[None], gain_rows[1], bias_rows[1]
        )
        x_two.append(rows)
        x_one.append(one)
        att_b.append(att_rows)
    x_core = [exchange(rows, "batch", 1) for rows in x_two]
    x_y = [exchange(rows, "batch", 2) for rows in x_two]
    x_parts, hidden_act, dpre, grad_b_in, sums, ahead = [], [], [], [], [], []
    after = [x_one[-1]]
    terms = None
    for e in range(EXP_DEV):
        if e:
            x_y[e] = gate(x_y[e], terms[0])
        x_parts.append([x_two[e], x_core[e], x_y[e], exchange(x_y[e], "batch", 1)])
        act, dact, *terms, grad_b = expert_call(
            e, sc, x_parts[e], g_parts, w_in_exp, b_in_exp, w_out_exp, after
        )
        ahead.append(expert_out_call(nb, e, act, w_out_exp))
        sums.append(reduce_cores(*terms, after=ahead[e][0]))
        after = [sums[e][0]]
        hidden_act.append(act)
        dpre.append(dact)
        grad_b_in.append(grad_b[0])
    from_y = [exchange(both[1], "batch", 2) for both in sums]
    d_one_b, small, outs = [], [], []
    datt_out = None
    for e in range(EXP_DEV):
        datt_out, rows, totals = owner_bwd_call(
            n, e, sums[e][0], from_y[e], x_one[e], grads, gain_rows[1], w_out, datt_out, after
        )
        d_one_b.append(rows)
        small.append(totals)
        if e + 1 < EXP_DEV:
            outs = [reduce_cores(*ahead[i], after=rows) for i in range(EXP_DEV)]
            after = [both[0] for both in outs]
    from_y = [exchange(gate(both[1], from_y[-1]), "batch", 2) for both in outs]
    from_y = [gate(rows, datt_out) for rows in from_y]
    datt = lax.all_to_all(datt_out, "seq", split_axis=0, concat_axis=0, tiled=True)

    size = D // (n * nb)
    both = reduce_cores(*w_out_grad_call(n, nb, sc, att_b, d_one_b))
    w_out_y = exchange(both[1], "batch", 2)
    weights = expert_grad_call(
        0, sc, x_parts[0], g_parts, hidden_act[0], dpre[0], None, [both[0]]
    )
    w_out_y = gate(w_out_y, weights[2])
    summed = (both[0].astype(F32) + w_out_y.astype(F32)).astype(BF16)
    home = []
    for e in range(EXP_DEV):
        expert_rows = (
            outs[e][0].astype(F32) + from_y[e].astype(F32) + b_out_exp[e][None, :]
        ).astype(BF16)
        home.append((x_one[e] + expert_rows.astype(F32)).astype(BF16))
    home = [rows.reshape(n, cap, D) for rows in d_one_b + home] + [summed]
    home = jnp.concatenate(home, axis=1)
    returned = lax.all_to_all(home, "seq", split_axis=0, concat_axis=0, tiled=True)
    at = EXP_DEV * cap
    d_ret = returned[:, :at].reshape(experts * cap, D)
    out_ret = returned[:, at : 2 * at].reshape(experts * cap, D)
    output = output_call(n, T, cap, sc, out_ret, ka)
    grad_w_out = jnp.sum(returned[:, 2 * at :].astype(F32), axis=0)

    dm = attn_bwd_call(
        n, T, cap, int(firsts[-1]), n, n * (n - 1) // 2, sc, qa, ka, lse, o, datt, [home, weights[2]]
    )
    dm_own = lax.all_to_all(dm, "seq", split_axis=0, concat_axis=0, tiled=True)
    aux = sum(small)[:3].reshape(3, n * nb, size).transpose(1, 0, 2).reshape(n * nb, 1, 3 * size)
    aux = jnp.pad(aux, ((0, 0), (0, 0), (0, 384 - 3 * size)))
    keep_w, send_w = qkv_grad_call(n, nb, T, sc, h_one, dm, aux, returned)
    both = reduce_cores(keep_w, send_w)
    w_y = exchange(both[1], "batch", 2)
    for e in range(1, EXP_DEV):
        weights = expert_grad_call(
            e, sc, x_parts[e], g_parts, hidden_act[e], dpre[e], weights, [both[0]]
        )
    grad_w_in, grad_w_out_exp, grad_b_out = weights
    w_y = gate(w_y, grad_b_out)
    w_sum = (both[0].astype(F32) + w_y.astype(F32)).astype(BF16)
    w_sum = gate(w_sum, dm_own)
    w_got = lax.all_to_all(w_sum, "seq", split_axis=0, concat_axis=0, tiled=True)
    own = (s * nb + b) * size
    gb = jnp.stack(
        [
            lax.dynamic_slice_in_dim(norm_gain_pair[0], own, size, 0),
            lax.dynamic_slice_in_dim(norm_bias_pair[0], own, size, 0),
        ]
    )
    gw_qkv, g_gains, g_biases, g_qvb, g_outb = final_call(n, nb, sc, w_got, w_qkv, gb)
    input_grad = input_grad_call(n, T, cap, sc, dm_own, w_qkv, hidden, d_ret, ka, gain_rows[0])
    return (
        output[None],
        input_grad[None],
        g_gains,
        g_biases,
        gw_qkv,
        g_qvb,
        grad_w_out,
        g_outb[0],
        grad_w_in,
        jnp.concatenate(grad_b_in, axis=0),
        grad_w_out_exp,
        grad_b_out[:, 0],
    )


def solution(mesh):
    n, nb = mesh.shape["seq"], mesh.shape["batch"]
    by_heads = HEADS * HEAD_DIM == 128 * n and nb == 4
    return jax.shard_map(
        local_by_heads if by_heads else local,
        mesh=mesh,
        in_specs=(
            P("batch", "seq", None),
            P("batch", "seq", None),
            P(),
            P(),
            P(),
            P(),
            P(),
            P(),
            P("seq", None, "batch"),
            P("seq", "batch"),
            P("seq", "batch", None),
            P("seq", None),
            P("batch", "seq", None),
            P("batch", None),
            P("batch", "seq"),
        ),
        out_specs=(
            P("batch", "seq", None),
            P("batch", "seq", None),
            P(None, ("seq", "batch")),
            P(None, ("seq", "batch")),
            P(("seq", "batch"), None),
            P(None, ("seq", "batch")),
            P(("seq", "batch"), None),
            P(("seq", "batch")),
            P("seq", None, "batch"),
            P("seq", "batch"),
            P("seq", "batch", None),
            P("seq", None),
        ),
        check_vma=False,
    )
```

```python
import math

import jax
import jax.numpy as jnp
import numpy as np
from jax import lax
from jax.experimental import pallas as pl
from jax.experimental.pallas import tpu as pltpu
from jax.sharding import PartitionSpec as P

D = 1024
HEADS = 16
HEAD_DIM = 64
EXP_DEV = 2


EPS = 1e-05
NEG = -1e30
BIG = 1e30
F32 = jnp.float32
BF16 = jnp.bfloat16
VMEM_LIMIT = 60 * 1024 * 1024


def dot_nn(a, b):
    return lax.dot_general(a, b, (((1,), (0,)), ((), ())), preferred_element_type=F32)


def dot_nt(a, b):
    return lax.dot_general(a, b, (((1,), (1,)), ((), ())), preferred_element_type=F32)


def dot_tn(a, b):
    return lax.dot_general(a, b, (((0,), (0,)), ((), ())), preferred_element_type=F32)


def normed_rows(values):
    centre = values - jnp.mean(values, axis=-1, keepdims=True)
    spread = jnp.mean(centre * centre, axis=-1, keepdims=True)
    inv_std = lax.rsqrt(spread + EPS)
    return centre * inv_std, inv_std


def whole(shape):
    return pl.BlockSpec(shape, lambda *_: (0,) * len(shape))


def params(**more):
    return pltpu.CompilerParams(vmem_limit_bytes=VMEM_LIMIT, **more)


def iota(shape, axis):
    return lax.broadcasted_iota(jnp.int32, shape, axis)


def running_sums(values):
    upto = jnp.arange(values.shape[0])[:, None] >= jnp.arange(values.shape[0])[None, :]
    return jnp.sum(jnp.where(upto, values[None, :], 0), axis=1)


def layer_normalize(values, gain, shift):
    centre = values - jnp.mean(values, axis=-1, keepdims=True)
    spread = jnp.mean(centre * centre, axis=-1, keepdims=True)
    inv_std = lax.rsqrt(spread + EPS)
    normed = centre * inv_std
    return (normed * gain + shift, normed, inv_std)


def norm_backward_pass(grads, normed, inv_std, gain):
    scaled = grads * gain
    first_mean = jnp.mean(scaled, axis=-1, keepdims=True)
    second_mean = jnp.mean(scaled * normed, axis=-1, keepdims=True)
    return (
        inv_std * (scaled - first_mean - normed * second_mean),
        jnp.sum(grads * normed, axis=0),
        jnp.sum(grads, axis=0),
    )


def doc_of(positions, doc_ends):
    return jnp.sum((positions[:, None] >= doc_ends[None, :]).astype(jnp.int32), axis=1)


def allowed_pairs(q_pos, q_doc, k_pos, k_doc, k_pad):
    same_doc = q_doc[:, None] == k_doc[None, :]
    before = k_pos[None, :] <= q_pos[:, None]
    usable = (k_pad[None, :] == 1) | (k_pos[None, :] == q_pos[:, None])
    return same_doc & before & usable


def over_blocks(step_fn, totals, arrays, first_row):
    row_count = arrays[0].shape[0]
    block_rows = math.gcd(row_count, 512)

    def advance(current, block_index):
        pieces = tuple(
            (
                lax.dynamic_slice_in_dim(member, block_index * block_rows, block_rows, 0)
                for member in arrays
            )
        )
        return (step_fn(current, pieces, first_row + block_index * block_rows), None)

    result, _ = lax.scan(advance, totals, jnp.arange(row_count // block_rows, dtype=jnp.int32))
    return result


def key_grads(
    query_h, dout_h, lse_rows, delta_rows, q_pos, q_doc, key_h, value_h, k_pos, k_doc, k_pad
):
    allowed = allowed_pairs(q_pos, q_doc, k_pos, k_doc, k_pad)
    scores = jnp.einsum("qhd,khd->hqk", query_h, key_h, preferred_element_type=jnp.float32)
    probs = jnp.where(allowed[None], jnp.exp(scores - lse_rows.T[:, :, None]), 0.0)
    dprobs = jnp.einsum("qhd,khd->hqk", dout_h, value_h, preferred_element_type=jnp.float32)
    dscores = (probs * (dprobs - delta_rows.T[:, :, None])).astype(jnp.bfloat16)
    grad_keys = jnp.einsum("hqk,qhd->khd", dscores, query_h, preferred_element_type=jnp.float32)
    grad_values = jnp.einsum(
        "hqk,qhd->khd", probs.astype(jnp.bfloat16), dout_h, preferred_element_type=jnp.float32
    )
    return (grad_keys, grad_values)


def gelu_exact(values):
    return jax.nn.gelu(values, approximate=False)


def local(
    hidden_in,
    out_grad,
    norm_gain_pair,
    norm_bias_pair,
    w_qkv,
    qv_bias,
    w_out,
    out_bias,
    w_in_exp,
    b_in_exp,
    w_out_exp,
    b_out_exp,
    expert_ids,
    doc_lengths,
    pad_mask,
):
    tok_rows = hidden_in.shape[1]
    seq_count = lax.axis_size("seq")
    experts_all = EXP_DEV * seq_count
    capacity = max(2, 3 * tok_rows // (2 * experts_all))
    scale = HEAD_DIM ** (-0.5)
    input_tokens = hidden_in[0].astype(jnp.float32)
    first_normalized, first_centred_scaled, first_inverse_deviation = layer_normalize(
        input_tokens, norm_gain_pair[0], norm_bias_pair[0]
    )
    h_one = first_normalized.astype(jnp.bfloat16)
    mixed = jnp.dot(h_one, w_qkv, preferred_element_type=jnp.float32)
    queries = ((mixed[:, :D] + qv_bias[0]) * scale).astype(jnp.bfloat16)
    keys_vals = jnp.concatenate(
        [mixed[:, D : 2 * D], mixed[:, 2 * D :] + qv_bias[1][None, :]], axis=1
    ).astype(jnp.bfloat16)
    query_h = queries.reshape(tok_rows, HEADS, HEAD_DIM)
    q_pos = lax.axis_index("seq") * tok_rows + jnp.arange(tok_rows, dtype=jnp.int32)
    doc_ends = running_sums(doc_lengths[0])
    q_doc = doc_of(q_pos, doc_ends)
    key_pad = pad_mask[0]

    def split_keys(pieces, first_row):
        block_kv, block_pad = pieces
        row_count = block_kv.shape[0]
        key_h = block_kv[:, :D].reshape(row_count, HEADS, HEAD_DIM)
        value_h = block_kv[:, D:].reshape(row_count, HEADS, HEAD_DIM)
        k_pos = first_row + jnp.arange(row_count, dtype=jnp.int32)
        allowed = allowed_pairs(q_pos, q_doc, k_pos, doc_of(k_pos, doc_ends), block_pad)
        scores = jnp.einsum("thd,khd->htk", query_h, key_h, preferred_element_type=jnp.float32)
        return (key_h, value_h, allowed, jnp.where(allowed[None], scores, NEG))

    def stats_step(current, pieces, first_row):
        _, _, allowed, scores = split_keys(pieces, first_row)
        top_now, mass_now = current
        new_top = jnp.maximum(top_now, jnp.max(scores, axis=-1))
        weights = jnp.where(allowed[None], jnp.exp(scores - new_top[:, :, None]), 0.0)
        return (new_top, mass_now * jnp.exp(top_now - new_top) + jnp.sum(weights, axis=-1))

    def output_step(current, pieces, first_row):
        _, value_h, allowed, scores = split_keys(pieces, first_row)
        probs = jnp.where(allowed[None], jnp.exp(scores - log_mass[:, :, None]), 0.0).astype(
            jnp.bfloat16
        )
        return current + jnp.einsum(
            "htk,khd->thd", probs, value_h, preferred_element_type=jnp.float32
        )

    def dquery_step(current, pieces, first_row):
        key_h, value_h, allowed, scores = split_keys(pieces, first_row)
        probs = jnp.where(allowed[None], jnp.exp(scores - log_mass[:, :, None]), 0.0)
        dprobs = jnp.einsum("thd,khd->htk", dout_h, value_h, preferred_element_type=jnp.float32)
        dscores = (probs * (dprobs - delta[:, :, None])).astype(jnp.bfloat16)
        return current + jnp.einsum(
            "htk,khd->thd", dscores, key_h, preferred_element_type=jnp.float32
        )

    head_zeros = jnp.zeros((tok_rows, HEADS, HEAD_DIM), jnp.float32)
    init_stats = (
        jnp.full((HEADS, tok_rows), NEG, jnp.float32),
        jnp.zeros((HEADS, tok_rows), jnp.float32),
    )
    all_kv, all_pad = (
        lax.all_gather(keys_vals, "seq", axis=0, tiled=True),
        lax.all_gather(key_pad, "seq", axis=0, tiled=True),
    )

    def run_keys(step_fn, totals):
        return over_blocks(step_fn, totals, (all_kv, all_pad), 0)

    top_all, mass_all = run_keys(stats_step, init_stats)
    log_mass = top_all + jnp.log(mass_all)
    attended = run_keys(output_step, head_zeros)
    attended_b = attended.reshape(tok_rows, D).astype(jnp.bfloat16)
    branch = jnp.dot(attended_b, w_out, preferred_element_type=jnp.float32) + out_bias
    first_residual_input = input_tokens + branch
    second_normalized, second_centred_scaled, second_inverse_deviation = layer_normalize(
        first_residual_input, norm_gain_pair[1], norm_bias_pair[1]
    )
    x_two = second_normalized.astype(jnp.bfloat16)
    token_ids = expert_ids[0, :, 0]
    earlier = jnp.arange(tok_rows)[None, :] < jnp.arange(tok_rows)[:, None]
    ranks = jnp.sum(((token_ids[:, None] == token_ids[None, :]) & earlier).astype(jnp.int32), axis=1)
    target = token_ids * capacity + ranks
    dispatch = (
        jnp.arange(experts_all * capacity, dtype=jnp.int32)[:, None] == target[None, :]
    ).astype(jnp.bfloat16)
    sent_rows = (
        jnp.dot(dispatch, x_two, preferred_element_type=jnp.float32)
        .astype(jnp.bfloat16)
        .reshape(seq_count, EXP_DEV, capacity, D)
    )
    rows_all = lax.all_gather(
        lax.all_to_all(sent_rows, "seq", split_axis=0, concat_axis=0, tiled=True),
        "batch",
        axis=0,
        tiled=True,
    )
    pre_act = (
        jnp.einsum("recd,edf->recf", rows_all, w_in_exp, preferred_element_type=jnp.float32)
        + b_in_exp[None, :, None, :]
    )
    hidden = gelu_exact(pre_act).astype(jnp.bfloat16)
    part_sums = jnp.einsum("recf,efd->recd", hidden, w_out_exp, preferred_element_type=jnp.float32)
    summed = lax.psum_scatter(
        part_sums.astype(jnp.bfloat16), "batch", scatter_dimension=0, tiled=True
    ).astype(jnp.float32)
    produced = (summed + b_out_exp[None, :, None, :]).astype(jnp.bfloat16)
    returned = lax.all_to_all(produced, "seq", split_axis=0, concat_axis=0, tiled=True)
    expert_rows = jnp.einsum(
        "st,sd->td",
        dispatch,
        returned.reshape(experts_all * capacity, D),
        preferred_element_type=jnp.float32,
    )
    output = (first_residual_input + expert_rows).astype(jnp.bfloat16)
    dout = out_grad[0].astype(jnp.float32)
    sent_grads = (
        jnp.dot(dispatch, out_grad[0], preferred_element_type=jnp.float32)
        .astype(jnp.bfloat16)
        .reshape(seq_count, EXP_DEV, capacity, D)
    )
    arrived_rows, arrived_grads = (
        lax.all_to_all(sent_rows, "seq", split_axis=0, concat_axis=0, tiled=True),
        lax.all_to_all(sent_grads, "seq", split_axis=0, concat_axis=0, tiled=True),
    )
    rows_all, grads_all = (
        lax.all_gather(arrived_rows, "batch", axis=0, tiled=True),
        lax.all_gather(arrived_grads, "batch", axis=0, tiled=True),
    )
    pre_act = (
        jnp.einsum("recd,edf->recf", rows_all, w_in_exp, preferred_element_type=jnp.float32)
        + b_in_exp[None, :, None, :]
    )
    hidden_f, gelu_back = jax.vjp(gelu_exact, pre_act)
    hidden_b = hidden_f.astype(jnp.bfloat16)
    dhidden = jnp.einsum(
        "recd,efd->recf", grads_all, w_out_exp, preferred_element_type=jnp.float32
    ).astype(jnp.bfloat16)
    dpre = gelu_back(dhidden.astype(jnp.float32))[0].astype(jnp.bfloat16)
    grad_w_out_exp = jnp.einsum(
        "recf,recd->efd", hidden_b, grads_all, preferred_element_type=jnp.float32
    )
    grad_b_out_exp = jnp.sum(grads_all, axis=(0, 2), dtype=jnp.float32)
    grad_w_in_exp = jnp.einsum("recd,recf->edf", rows_all, dpre, preferred_element_type=jnp.float32)
    grad_b_in_exp = jnp.sum(dpre, axis=(0, 2), dtype=jnp.float32)
    drows = jnp.einsum("recf,edf->recd", dpre, w_in_exp, preferred_element_type=jnp.float32)
    drows_sum = lax.psum_scatter(
        drows.astype(jnp.bfloat16), "batch", scatter_dimension=0, tiled=True
    )
    drows_home = lax.all_to_all(drows_sum, "seq", split_axis=0, concat_axis=0, tiled=True)
    second_residual_gradient = jnp.einsum(
        "st,sd->td",
        dispatch,
        drows_home.reshape(experts_all * capacity, D),
        preferred_element_type=jnp.float32,
    )
    second_norm_gradient, second_gain_gradient, second_shift_gradient = norm_backward_pass(
        second_residual_gradient, second_centred_scaled, second_inverse_deviation, norm_gain_pair[1]
    )
    d_one = dout + second_norm_gradient
    d_one_b = d_one.astype(jnp.bfloat16)
    grad_w_out = jnp.einsum("td,te->de", attended_b, d_one_b, preferred_element_type=jnp.float32)
    grad_out_bias = jnp.sum(d_one, axis=0)
    dout_b = jnp.einsum("te,de->td", d_one_b, w_out, preferred_element_type=jnp.float32).astype(
        jnp.bfloat16
    )
    dout_h = dout_b.reshape(tok_rows, HEADS, HEAD_DIM)
    delta = jnp.einsum("thd,thd->ht", dout_h.astype(jnp.float32), attended)
    dquery = run_keys(dquery_step, head_zeros)
    lse_rows = log_mass.T
    delta_rows = delta.T
    block_rows = math.gcd(tok_rows * lax.axis_size("seq"), 512)

    def one_block(block_index):
        first_key = block_index * block_rows
        block_kv = lax.dynamic_slice_in_dim(all_kv, first_key, block_rows, 0)
        block_pad = lax.dynamic_slice_in_dim(all_pad, first_key, block_rows, 0)
        k_pos = first_key + jnp.arange(block_rows, dtype=jnp.int32)
        grad_k, grad_v = key_grads(
            query_h,
            dout_h,
            lse_rows,
            delta_rows,
            q_pos,
            q_doc,
            block_kv[:, :D].reshape(block_rows, HEADS, HEAD_DIM),
            block_kv[:, D:].reshape(block_rows, HEADS, HEAD_DIM),
            k_pos,
            doc_of(k_pos, doc_ends),
            block_pad,
        )
        return jnp.concatenate(
            [grad_k.reshape(block_rows, D), grad_v.reshape(block_rows, D)], axis=1
        )

    blocks = lax.map(
        one_block, jnp.arange(tok_rows * lax.axis_size("seq") // block_rows, dtype=jnp.int32)
    )
    key_terms = lax.psum_scatter(
        blocks.reshape(tok_rows * lax.axis_size("seq"), 2 * D).astype(jnp.bfloat16),
        "seq",
        scatter_dimension=0,
        tiled=True,
    )
    dq_b = dquery.reshape(tok_rows, D).astype(jnp.bfloat16)
    dmixed = jnp.concatenate([dq_b * scale, key_terms], axis=1)
    grad_w_qkv = jnp.einsum("td,te->de", h_one, dmixed, preferred_element_type=jnp.float32)
    first_hidden_gradient = jnp.einsum(
        "te,de->td", dmixed, w_qkv, preferred_element_type=jnp.float32
    )
    first_norm_gradient, first_gain_gradient, first_shift_gradient = norm_backward_pass(
        first_hidden_gradient, first_centred_scaled, first_inverse_deviation, norm_gain_pair[0]
    )
    input_grad = (d_one + first_norm_gradient).astype(jnp.bfloat16)
    grad_q_bias = jnp.sum(dmixed[:, :D], axis=0, dtype=jnp.float32)
    grad_v_bias = jnp.sum(key_terms[:, D:], axis=0, dtype=jnp.float32)
    small_grads = jnp.stack(
        [
            first_gain_gradient,
            second_gain_gradient,
            first_shift_gradient,
            second_shift_gradient,
            grad_q_bias,
            grad_v_bias,
            grad_out_bias,
        ]
    )
    shared_qkv, shared_out, shared_small = (
        lax.psum_scatter(grad_w_qkv, ("seq", "batch"), scatter_dimension=0, tiled=True),
        lax.psum_scatter(grad_w_out, ("seq", "batch"), scatter_dimension=0, tiled=True),
        lax.psum_scatter(small_grads, ("seq", "batch"), scatter_dimension=1, tiled=True),
    )
    return (
        output[None],
        input_grad[None],
        shared_small[0:2],
        shared_small[2:4],
        shared_qkv,
        shared_small[4:6],
        shared_out,
        shared_small[6],
        grad_w_in_exp,
        grad_b_in_exp,
        grad_w_out_exp,
        grad_b_out_exp,
    )


MICROSECOND = 1 << 30


def cost(us):
    return pl.CostEstimate(flops=us * MICROSECOND, bytes_accessed=1 << 20, transcendentals=0)


MICROSECOND = 1 << 30


def cost(us):
    return pl.CostEstimate(flops=us * MICROSECOND, bytes_accessed=1 << 20, transcendentals=0)


SMALL = pl.CostEstimate(flops=1, bytes_accessed=1, transcendentals=0)
HALVES = [slice(h * HEAD_DIM, (h + 1) * HEAD_DIM) for h in range(2)]


def block_rows(i, T):
    return pl.ds(pl.multiple_of(i * T, T), T)


def diag_parts(T, key_rows):
    lane = iota((T, 256), 1)
    values = key_rows.astype(F32)
    unpadded = jnp.where(lane == 136, 0.0, values).astype(BF16)
    k_at, q_at = iota((T, T), 0), iota((T, T), 1)
    padded = values[:, 136:137] > 0.5
    allowed = ((k_at < q_at) & jnp.logical_not(padded)) | (k_at == q_at)
    return unpadded, allowed


def ring_kernel(n, T, cap, block, parts, at_tile, diags, pairs, first, last, extra, sc, *refs):
    refs = list(refs)

    def take(count):
        got = refs[:count]
        del refs[:count]
        return got

    count = len(parts)
    chunks = [take(p) for p in parts]
    wq, wk, wv, qvb, gain, bias, docs = take(7)
    old = [] if first else take(9)
    take(extra)
    outs = take(9)
    results = take(EXP_DEV + 2) if last else None
    h_out, sel_out, qa_out, ka_out, vt_out, code_out = outs[:6]
    h_s, sel_s, qa, ka, vt, code, top, mass, acc, w, in_sems, out_sems = take(12)
    me = sc[n]
    loads = [
        pltpu.make_async_copy(ref, to, in_sems.at[i])
        for i, (ref, to) in enumerate(zip(old[2:], (qa, ka, vt, code, top, mass, acc)))
    ]
    for load in loads:
        load.start()
    w[:, 0:128] = wq[...]
    w[:, 128:256] = wk[...]
    w[:, 256:384] = wv[...]
    payloads = []
    for c in range(count):
        rows = [ref[...] for ref in chunks[c]]
        rows = rows[0] if len(rows) == 1 else jnp.concatenate(rows, axis=0)
        payloads.append(rows)
        vhat, _ = normed_rows(rows[0:T].astype(F32))
        h_s[c] = (vhat * gain[...] + bias[...]).astype(BF16)
    for load in loads:
        load.wait()
    stores = []

    def send(ref, to):
        store = pltpu.make_async_copy(ref, to, out_sems.at[len(stores)])
        store.start()
        stores.append(store)

    for c in range(count):
        src = sc[block + c]
        rows = block_rows(src, T)
        mixed = dot_nn(h_s[c], w[...])
        q = ((mixed[:, 0:128] + qvb[0:1, :]) * (HEAD_DIM**-0.5)).astype(BF16).astype(F32)
        v = (mixed[:, 256:384] + qvb[1:2, :]).astype(BF16)
        codes = payloads[c][T : T + 16].astype(F32)
        id_row = codes[0:1, 0:T]
        pad_row = codes[0:1, T : 2 * T]
        id_col = jnp.transpose(jnp.broadcast_to(id_row, (128, T)))
        pad_col = jnp.transpose(jnp.broadcast_to(pad_row, (128, T)))
        same = jnp.where(
            (id_col[:, 0:1] == id_row) & (iota((T, T), 0) < iota((T, T), 1)), 1.0, 0.0
        )
        rank_row = jnp.sum(same, axis=0, keepdims=True)
        rank_col = jnp.transpose(jnp.broadcast_to(rank_row, (128, T)))
        lane = iota((T, 128), 1)
        pos = (iota((T, 128), 0) + src * T).astype(F32)
        doc = jnp.where((pos >= docs[0:1, :]) & (pos < docs[1:2, :]), 1.0, 0.0)
        aug = jnp.where(lane < 8, doc, 0.0)
        aug = jnp.where(lane == 8, 1.0 - pad_col, aug)
        aug = jnp.where(lane == 16, id_col, aug)
        aug = jnp.where(lane == 17, rank_col, aug)
        masked = jnp.where(lane < 8, (doc - 1.0) * BIG, jnp.where(lane == 8, -BIG, 0.0)).astype(BF16)
        for h in range(2):
            mine = (lane < HEAD_DIM) == (h == 0)
            qa[h, rows, 0:128] = jnp.where(mine, q, 0.0).astype(BF16)
            qa[h, rows, 128:256] = masked
        ka[rows, 0:128] = mixed[:, 128:256].astype(BF16)
        ka[rows, 128:256] = aug.astype(BF16)
        ka[rows, 256:384] = v
        vt[src] = jnp.transpose(v.astype(F32)).astype(BF16)
        slot = (id_row * cap + rank_row).astype(jnp.int32)
        half = lax.rem(src, 2) * cap
        code[src] = (id_row * (2 * cap) + rank_row).astype(jnp.int32) + half
        pick = jnp.where(
            slot == iota((EXP_DEV * cap, T), 0) + me * (EXP_DEV * cap), 1.0, 0.0
        ).astype(BF16)
        chosen = dot_nn(pick, payloads[c][0:T])
        for e in range(EXP_DEV):
            sel_s[c, e] = chosen[e * cap : (e + 1) * cap]
            send(sel_s.at[c, e], sel_out.at[e, src])
        send(h_s.at[c], h_out.at[src])
        for h in range(2):
            send(qa.at[h, rows], qa_out.at[h, rows])
        send(ka.at[rows], ka_out.at[rows])
        if not last:
            send(vt.at[src], vt_out.at[src])
            send(code.at[src], code_out.at[src])

    def one_diag(r, carry):
        i = sc[at_tile + 2 * r]
        rows = block_rows(i, T)
        kd, allowed = diag_parts(T, ka[rows, 0:256])
        for h in range(2):
            s = jnp.where(allowed, dot_nt(kd, qa[h, rows, :]), NEG)
            best = jnp.max(s, axis=0, keepdims=True)
            p = jnp.exp(s - best)
            top[h, i] = best
            mass[h, i] = jnp.sum(p, axis=0, keepdims=True)
            acc[i, HALVES[h], :] = dot_nn(vt[i, HALVES[h], :], p.astype(BF16))
        return carry

    lax.fori_loop(0, diags, one_diag, 0)

    def pair_tile(at):
        i, j = sc[at_tile + 2 * at], sc[at_tile + 2 * at + 1]
        rows, cols = block_rows(i, T), block_rows(j, T)
        old_top = [top[h, i] for h in range(2)]
        old_mass = [mass[h, i] for h in range(2)]
        old_acc = [acc[i, HALVES[h], :] for h in range(2)]
        s = [dot_nt(ka[cols, 0:256], qa[h, rows, :]) for h in range(2)]
        best = [jnp.maximum(old_top[h], jnp.max(s[h], axis=0, keepdims=True)) for h in range(2)]
        p = [jnp.exp(s[h] - best[h]) for h in range(2)]
        more = [dot_nn(vt[j, HALVES[h], :], p[h].astype(BF16)) for h in range(2)]
        for h in range(2):
            fade = jnp.exp(old_top[h] - best[h])
            top[h, i] = best[h]
            mass[h, i] = old_mass[h] * fade + jnp.sum(p[h], axis=0, keepdims=True)
            acc[i, HALVES[h], :] = old_acc[h] * fade + more[h]

    def two_pairs(r, carry):
        pair_tile(diags + 2 * r)
        pair_tile(diags + 2 * r + 1)
        return carry

    lax.fori_loop(0, pairs // 2, two_pairs, 0)
    if pairs % 2:
        pair_tile(diags + pairs - 1)
    if not last:
        for ref, to in zip((top, mass, acc), outs[6:]):
            send(ref, to)
    else:
        *att_out, o_out, lse_out = results

        def finish(i, carry):
            rows = block_rows(i, T)
            scaled = []
            for h in range(2):
                lse_out[h, i] = top[h, i] + jnp.log(mass[h, i])
                scaled.append(acc[i, HALVES[h], :] / mass[h, i])
            o_out[rows, :] = jnp.transpose(jnp.concatenate(scaled, axis=0))
            return carry

        lax.fori_loop(0, n, finish, 0)
        slots = n * EXP_DEV * 2 * cap

        def pair(p, carry):
            codes = jnp.concatenate([code[2 * p], code[2 * p + 1]], axis=1)
            pick = jnp.where(codes == iota((slots, 2 * T), 0), 1.0, 0.0).astype(BF16)
            chosen = dot_nn(pick, o_out[block_rows(p, 2 * T), :].astype(BF16)).astype(BF16)
            for k in range(n):
                for e in range(EXP_DEV):
                    at = (k * EXP_DEV + e) * 2 * cap
                    to = pl.multiple_of(p * 2 * cap, 16)
                    att_out[e][k, pl.ds(to, 2 * cap), :] = chosen[at : at + 2 * cap]
            return carry

        lax.fori_loop(0, n // 2, pair, 0)
    for store in stores:
        store.wait()


def ring_call(
    n, T, cap, block, at_tile, diags, pairs, sc, chunks, held, last, w_qkv, qv_bias, gain, bias, docs, after
):
    row = n * T
    shapes = [
        ((n, T, D), BF16),
        ((EXP_DEV, n, cap, D), F32),
        ((2, row, 256), BF16),
        ((row, 384), BF16),
        ((n, 128, T), BF16),
        ((n, 1, T), jnp.int32),
        ((2, n, 1, T), F32),
        ((2, n, 1, T), F32),
        ((n, 128, T), F32),
    ]
    anywhere = pl.BlockSpec(memory_space=pl.ANY)
    operands = [part for chunk in chunks for part in chunk]
    in_specs = [whole(part.shape) for part in operands] + [
        pl.BlockSpec((D, 128), lambda i, sc: (0, sc[n])),
        pl.BlockSpec((D, 128), lambda i, sc: (0, n + sc[n])),
        pl.BlockSpec((D, 128), lambda i, sc: (0, 2 * n + sc[n])),
        pl.BlockSpec((2, 128), lambda i, sc: (0, sc[n])),
        whole((1, D)),
        whole((1, D)),
        whole((2, 128)),
    ]
    aliases = {}
    first = held is None
    if not first:
        aliases = {1 + len(in_specs) + i: i for i in range(len(shapes))}
        in_specs = in_specs + [anywhere] * len(shapes)
    in_specs = in_specs + [anywhere] * len(after)
    out_specs = [anywhere] * len(shapes)
    results = []
    if last:
        results = [((n, n * cap, 128), BF16)] * EXP_DEV
        results = results + [((row, 128), F32), ((2, n, 1, T), F32)]
        out_specs = out_specs + [whole(s) for s, _ in results]
    count = len(chunks)
    parts = [len(chunk) for chunk in chunks]
    return pl.pallas_call(
        lambda *a: ring_kernel(
            n, T, cap, block, parts, at_tile, diags, pairs, first, last, len(after), *a
        ),
        grid_spec=pltpu.PrefetchScalarGridSpec(
            num_scalar_prefetch=1,
            grid=(1,),
            in_specs=in_specs,
            out_specs=out_specs,
            scratch_shapes=[
                pltpu.VMEM((count, T, D), BF16),
                pltpu.VMEM((count, EXP_DEV, cap, D), F32),
            ]
            + [pltpu.VMEM(s, t) for s, t in shapes[2:]]
            + [
                pltpu.VMEM((D, 384), BF16),
                pltpu.SemaphoreType.DMA((7,)),
                pltpu.SemaphoreType.DMA((8 * count + 3,)),
            ],
        ),
        out_shape=[jax.ShapeDtypeStruct(s, t) for s, t in shapes + results],
        input_output_aliases=aliases,
        compiler_params=params(),
        cost_estimate=cost(10),
        name="ring_step",
    )(sc, *operands, w_qkv, w_qkv, w_qkv, qv_bias, gain, bias, docs, *(held or ()), *after)


def attn_bwd_kernel(
    n, T, cap, at_tile, diags, pairs, tiles, qa, ka, lse, o_ref, *refs
):
    datt = refs[:EXP_DEV]
    dm_out, do, delta, kh, dqa, dka, dva = refs[-7:]
    slots = n * EXP_DEV * 2 * cap

    def pair(p, carry):
        rows = block_rows(p, 2 * T)
        feature = ka[rows, 128:256].astype(F32)
        half = jnp.where(iota((2 * T, 1), 0) >= T, float(cap), 0.0)
        code = (feature[:, 16:17] * (2 * cap) + feature[:, 17:18] + half).astype(jnp.int32)
        pick = jnp.where(code == iota((2 * T, slots), 1), 1.0, 0.0).astype(BF16)
        parts = []
        for k in range(n):
            for e in range(EXP_DEV):
                at = pl.multiple_of(p * 2 * cap, 16)
                parts.append(datt[e][k, pl.ds(at, 2 * cap), :])
        got = dot_nn(pick, jnp.concatenate(parts, axis=0))
        lane = iota((2 * T, 128), 1)
        keys = ka[rows, 0:128].astype(F32)
        for h in range(2):
            mine = (lane < HEAD_DIM) == (h == 0)
            do[h, rows, :] = jnp.where(mine, got, 0.0).astype(BF16)
            kh[h, rows, :] = jnp.where(mine, keys, 0.0).astype(BF16)
        prod = jnp.transpose(got * o_ref[rows, :])
        for h in range(2):
            total = jnp.sum(prod[HALVES[h], :], axis=0, keepdims=True)
            delta[h, 2 * p] = total[:, 0:T]
            delta[h, 2 * p + 1] = total[:, T : 2 * T]
        return carry

    lax.fori_loop(0, n // 2, pair, 0)

    def tile(i, j, key_rows, mask):
        rows, cols = block_rows(i, T), block_rows(j, T)
        ps, dss = [], []
        for h in range(2):
            s = dot_nt(key_rows, qa[h, rows, :])
            dp = dot_nt(ka[cols, 256:384], do[h, rows, :])
            if mask is not None:
                s = jnp.where(mask, s, NEG)
            p = jnp.exp(s - lse[h, i])
            dss.append((p * (dp - delta[h, i])).astype(BF16))
            ps.append(p.astype(BF16))
        dv = dot_nn(
            jnp.concatenate(ps, axis=1), jnp.concatenate([do[0, rows, :], do[1, rows, :]], axis=0)
        )
        dk = dot_nn(
            jnp.concatenate(dss, axis=1),
            jnp.concatenate([qa[0, rows, 0:128], qa[1, rows, 0:128]], axis=0),
        )
        dq = dot_tn(
            jnp.concatenate(dss, axis=0), jnp.concatenate([kh[0, cols, :], kh[1, cols, :]], axis=0)
        )
        return dq, dk, dv

    def diag_tile(j, carry):
        kd, allowed = diag_parts(T, ka[block_rows(j, T), 0:256])
        dqa[j], dka[j], dva[j] = tile(j, j, kd, allowed)
        return carry

    lax.fori_loop(0, n, diag_tile, 0)

    def pair_tile(at):
        i, j = tiles[at_tile + 2 * at], tiles[at_tile + 2 * at + 1]
        dq, dk, dv = tile(i, j, ka[block_rows(j, T), 0:256], None)
        dqa[i] += dq
        dka[j] += dk
        dva[j] += dv

    width = next(w for w in (4, 2, 1) if pairs % w == 0)

    def some_pairs(r, carry):
        for w in range(width):
            pair_tile(diags + width * r + w)
        return carry

    lax.fori_loop(0, pairs // width, some_pairs, 0)

    def finish(i, carry):
        dq = dqa[i].astype(BF16).astype(F32)
        dm_out[i, :, 0:128] = (dq * (HEAD_DIM**-0.5)).astype(BF16)
        dm_out[i, :, 128:256] = dka[i].astype(BF16)
        dm_out[i, :, 256:384] = dva[i].astype(BF16)
        return carry

    lax.fori_loop(0, n, finish, 0)


def attn_bwd_call(n, T, cap, at_tile, diags, pairs, tiles, qa, ka, lse, o, datt, after):
    row = n * T
    vmem = pl.BlockSpec(memory_space=pltpu.VMEM)
    return pl.pallas_call(
        lambda *a: attn_bwd_kernel(n, T, cap, at_tile, diags, pairs, *a),
        out_shape=jax.ShapeDtypeStruct((n, T, 384), BF16),
        in_specs=[pl.BlockSpec(memory_space=pltpu.SMEM)]
        + [vmem] * (4 + EXP_DEV)
        + [pl.BlockSpec(memory_space=pl.ANY)] * len(after),
        out_specs=vmem,
        scratch_shapes=[
            pltpu.VMEM((2, row, 128), BF16),
            pltpu.VMEM((2, n, 1, T), F32),
            pltpu.VMEM((2, row, 128), BF16),
            pltpu.VMEM((n, T, 128), F32),
            pltpu.VMEM((n, T, 128), F32),
            pltpu.VMEM((n, T, 128), F32),
        ],
        compiler_params=params(),
        cost_estimate=cost(28),
        name="attn_bwd",
    )(tiles, qa, ka, lse, o, *datt, *after)


def dispatch_kernel(cap, slots, ids, grads, *refs):
    out = refs[-1]
    id_row = ids[...].astype(F32)
    T = id_row.shape[1]
    id_col = jnp.transpose(jnp.broadcast_to(id_row, (128, T)))[:, 0:1]
    same = jnp.where((id_col == id_row) & (iota((T, T), 0) < iota((T, T), 1)), 1.0, 0.0)
    rank = jnp.sum(same, axis=0, keepdims=True)
    slot = (id_row * cap + rank).astype(jnp.int32)
    pick = jnp.where(slot == iota((slots, T), 0), 1.0, 0.0).astype(BF16)
    out[...] = dot_nn(pick, grads[...]).astype(BF16)


def dispatch_call(cap, slots, after, ids, grads):
    vmem = pl.BlockSpec(memory_space=pltpu.VMEM)
    return pl.pallas_call(
        lambda *a: dispatch_kernel(cap, slots, *a),
        out_shape=jax.ShapeDtypeStruct((slots, D), BF16),
        in_specs=[vmem, vmem] + [pl.BlockSpec(memory_space=pl.ANY)] * len(after),
        out_specs=vmem,
        compiler_params=params(),
        cost_estimate=cost(3),
        name="dispatch",
    )(ids, grads, *after)


def owner_fwd_kernel(n, att_in, w_out, sel, out_bias, gain, bias, x_two, x_one, att_b):
    for k in range(n):
        att_b[:, k * 128 : (k + 1) * 128] = att_in[k]
    branch = dot_nn(att_b[...], w_out[...]) + out_bias[...]
    x = sel[...] + branch
    x_one[...] = x
    vhat, _ = normed_rows(x)
    x_two[...] = (vhat * gain[...] + bias[...]).astype(BF16)


def owner_fwd_call(n, e, att_in, w_out, sel, out_bias, gain, bias):
    slots = sel.shape[0] // EXP_DEV
    rows = pl.BlockSpec((slots, D), lambda i: (e, 0))
    mine = whole((slots, D))
    return pl.pallas_call(
        lambda *a: owner_fwd_kernel(n, *a),
        grid=(1,),
        in_specs=[
            whole((n, slots, 128)),
            whole((D, D)),
            rows,
            whole((1, D)),
            whole((1, D)),
            whole((1, D)),
        ],
        out_specs=[mine, mine, mine],
        out_shape=[
            jax.ShapeDtypeStruct((slots, D), BF16),
            jax.ShapeDtypeStruct((slots, D), F32),
            jax.ShapeDtypeStruct((slots, D), BF16),
        ],
        compiler_params=params(),
        cost_estimate=cost(3),
        name="owner_fwd",
    )(att_in, w_out, sel, out_bias, gain, bias)


def owner_bwd_kernel(n, part_a, part_b, x_one, og, gain, w_out, *refs):
    datt, d_one_b, small = refs[-3:]
    u = (part_a[...].astype(F32) + part_b[...].astype(F32)).astype(BF16).astype(F32)
    vhat, inv_std = normed_rows(x_one[...])
    scaled = u * gain[...]
    first = jnp.mean(scaled, axis=-1, keepdims=True)
    second = jnp.mean(scaled * vhat, axis=-1, keepdims=True)
    d_one = og[...].astype(F32) + inv_std * (scaled - first - vhat * second)
    d_b = d_one.astype(BF16)
    d_one_b[...] = d_b
    back = dot_nt(d_b, w_out[...]).astype(BF16)
    for k in range(n):
        datt[k] = back[:, k * 128 : (k + 1) * 128]
    small[0:1, :] = jnp.sum(u * vhat, axis=0, keepdims=True)
    small[1:2, :] = jnp.sum(u, axis=0, keepdims=True)
    small[2:3, :] = jnp.sum(d_one, axis=0, keepdims=True)


def owner_bwd_call(n, e, part_a, part_b, x_one, og, gain, w_out, after):
    slots = x_one.shape[0]
    mine = whole((slots, D))
    in_specs = [
        mine,
        mine,
        mine,
        pl.BlockSpec((slots, D), lambda i: (e, 0)),
        whole((1, D)),
        whole((D, D)),
    ]
    return pl.pallas_call(
        lambda *a: owner_bwd_kernel(n, *a),
        grid=(1,),
        in_specs=in_specs + [pl.BlockSpec(memory_space=pl.ANY)] * len(after),
        out_specs=[
            whole((n, slots, 128)),
            mine,
            whole((8, D)),
        ],
        out_shape=[
            jax.ShapeDtypeStruct((n, slots, 128), BF16),
            jax.ShapeDtypeStruct((slots, D), BF16),
            jax.ShapeDtypeStruct((8, D), F32),
        ],
        compiler_params=params(),
        cost_estimate=cost(4),
        name="owner_bwd",
    )(part_a, part_b, x_one, og, gain, w_out, *after)


def gelu_parts(u):
    cdf = 0.5 * (1.0 + lax.erf(u * (0.5**0.5)))
    return cdf, cdf + u * jnp.exp(-0.5 * u * u) * ((2.0 * math.pi) ** -0.5)


ROW_ORDER = (1, 3, 0, 2)


def expert_kernel(e, nb, rows, ff, width, extra, *refs):
    x_parts, g_parts = refs[:nb], refs[nb : 2 * nb]
    w_in, b_in, w_out = refs[2 * nb : 2 * nb + 3]
    hidden_out, dpre_out, keep, send, grad_b = refs[2 * nb + 3 + extra : 2 * nb + 8 + extra]
    xs, gs, w1, w2, hidden, dpre, part, sems = refs[2 * nb + 8 + extra :]
    copies = []

    def copy(ref, to):
        made = pltpu.make_async_copy(ref, to, sems.at[len(copies)])
        made.start()
        copies.append(made)

    for at, k in enumerate(ROW_ORDER):
        copy(x_parts[k], xs.at[pl.ds(at * rows, rows)])
    copy(w_in.at[e], w1)
    for at, k in enumerate(ROW_ORDER):
        copy(g_parts[k].at[pl.ds(e * rows, rows)], gs.at[pl.ds(at * rows, rows)])
    copy(w_out.at[e], w2)
    for c in copies[: nb + 1]:
        c.wait()
    ready = len(copies)
    for f in range(ff // width):
        cols = slice(f * width, (f + 1) * width)
        pre = dot_nn(xs[...], w1[:, cols]) + b_in[e : e + 1, cols]
        if f == 0:
            for c in copies[nb + 1 : ready]:
                c.wait()
        dhidden = dot_nt(gs[...], w2[cols, :]).astype(BF16).astype(F32)
        cdf, slope = gelu_parts(pre)
        hidden[:, cols] = (pre * cdf).astype(BF16)
        value = (dhidden * slope).astype(BF16)
        dpre[:, cols] = value
        grad_b[0, :, cols] = jnp.sum(value.astype(F32), axis=0, keepdims=True)
    copy(hidden, hidden_out)
    copy(dpre, dpre_out)
    for half, to in enumerate((send, keep)):
        at = slice(2 * half * rows, 2 * (half + 1) * rows)
        value = dot_nt(dpre[at, :], w1[...]).astype(BF16)
        for y in range(2):
            part[2 * half + y] = value[y * rows : (y + 1) * rows]
            copy(part.at[2 * half + y], to.at[y])
    for c in copies[ready:]:
        c.wait()


def expert_call(e, sc, x_parts, g_parts, w_in, b_in, w_out, after):
    del sc
    nb = len(x_parts)
    rows = x_parts[0].shape[0]
    ff = w_in.shape[2]
    anywhere = pl.BlockSpec(memory_space=pl.ANY)
    return pl.pallas_call(
        lambda *a: expert_kernel(e, nb, rows, ff, min(256, ff), len(after), *a),
        in_specs=[anywhere] * (2 * nb + 1)
        + [pl.BlockSpec(memory_space=pltpu.VMEM), anywhere]
        + [anywhere] * len(after),
        out_specs=[anywhere] * 4 + [pl.BlockSpec(memory_space=pltpu.VMEM)],
        scratch_shapes=[
            pltpu.VMEM((nb * rows, D), BF16),
            pltpu.VMEM((nb * rows, D), BF16),
            pltpu.VMEM((D, ff), BF16),
            pltpu.VMEM((ff, D), BF16),
            pltpu.VMEM((nb * rows, ff), BF16),
            pltpu.VMEM((nb * rows, ff), BF16),
            pltpu.VMEM((nb, rows, D), BF16),
            pltpu.SemaphoreType.DMA((3 * nb + 4,)),
        ],
        out_shape=[
            jax.ShapeDtypeStruct((nb * rows, ff), BF16),
            jax.ShapeDtypeStruct((nb * rows, ff), BF16),
            jax.ShapeDtypeStruct((2, rows, D), BF16),
            jax.ShapeDtypeStruct((2, rows, D), BF16),
            jax.ShapeDtypeStruct((1, 1, ff), F32),
        ],
        compiler_params=params(),
        cost_estimate=cost(10),
        name="expert_main",
    )(*x_parts, *g_parts, w_in, b_in, w_out, *after)


def expert_out_kernel(rows, hidden, w_out, *refs):
    keep, send = refs[-2:]
    total = dot_nn(hidden[...], w_out[0]).astype(BF16)
    for y in range(2):
        send[y] = total[y * rows : (y + 1) * rows, :]
        keep[y] = total[(2 + y) * rows : (3 + y) * rows, :]


def expert_out_call(nb, e, hidden, w_out, after):
    rows = hidden.shape[0] // nb
    ff = hidden.shape[1]
    return pl.pallas_call(
        lambda *a: expert_out_kernel(rows, *a),
        grid=(1,),
        in_specs=[whole(hidden.shape), pl.BlockSpec((1, ff, D), lambda i: (e, 0, 0))]
        + [pl.BlockSpec(memory_space=pl.ANY)] * len(after),
        out_specs=[whole((2, rows, D))] * 2,
        out_shape=[jax.ShapeDtypeStruct((2, rows, D), BF16)] * 2,
        compiler_params=params(),
        cost_estimate=cost(4),
        name="expert_out",
    )(hidden, w_out, *after)


def expert_grad_kernel(nb, rows, sc, *refs):
    x_parts, g_parts = refs[:nb], refs[nb : 2 * nb]
    hidden, dpre = refs[2 * nb : 2 * nb + 2]
    grad_in, grad_out, grad_b, xs, gs = refs[-5:]

    @pl.when(pl.program_id(0) == 0)
    def _():
        sums = []
        for at, k in enumerate(ROW_ORDER):
            xs[at * rows : (at + 1) * rows, :] = x_parts[k][...]
            gs[at * rows : (at + 1) * rows, :] = g_parts[k][...]
        for k in range(nb):
            sums.append(jnp.sum(g_parts[k][...].astype(F32), axis=0, keepdims=True))
        grad_b[0] = (sums[0] + sums[1]) + (sums[2] + sums[3])

    grad_in[0] = dot_tn(xs[...], dpre[...])
    grad_out[0] = dot_tn(hidden[...], gs[...])


def expert_grad_call(e, sc, x_parts, g_parts, hidden, dpre, held, after):
    nb = len(x_parts)
    rows = x_parts[0].shape[0]
    ff = hidden.shape[1]
    width = min(256, ff)
    g_specs = [pl.BlockSpec((rows, D), lambda f, sc: (e, 0))] * nb
    act = pl.BlockSpec((nb * rows, width), lambda f, sc: (0, f))
    in_specs = [whole((rows, D))] * nb + g_specs + [act, act]
    more = [] if held is None else list(held)
    aliases = {1 + len(in_specs) + i: i for i in range(len(more))}
    more += after
    return pl.pallas_call(
        lambda *a: expert_grad_kernel(nb, rows, *a),
        grid_spec=pltpu.PrefetchScalarGridSpec(
            num_scalar_prefetch=1,
            grid=(ff // width,),
            in_specs=in_specs + [pl.BlockSpec(memory_space=pl.ANY)] * len(more),
            out_specs=[
                pl.BlockSpec((1, D, width), lambda f, sc: (e, 0, f)),
                pl.BlockSpec((1, width, D), lambda f, sc: (e, f, 0)),
                pl.BlockSpec((1, 1, D), lambda f, sc: (e, 0, 0)),
            ],
            scratch_shapes=[pltpu.VMEM((nb * rows, D), BF16)] * 2,
        ),
        out_shape=[
            jax.ShapeDtypeStruct((EXP_DEV, D, ff), F32),
            jax.ShapeDtypeStruct((EXP_DEV, ff, D), F32),
            jax.ShapeDtypeStruct((EXP_DEV, 1, D), F32),
        ],
        input_output_aliases=aliases,
        compiler_params=params(),
        cost_estimate=SMALL,
        name="expert_grads",
    )(sc, *x_parts, *g_parts, hidden, dpre, *more)


def w_out_grad_kernel(n, nb, sc, *refs):
    keep, send = refs[-2:]
    total = dot_tn(refs[0][...], refs[EXP_DEV][...])
    for e in range(1, EXP_DEV):
        total = total + dot_tn(refs[e][...], refs[EXP_DEV + e][...])
    size = D // (n * nb)
    core = lax.rem(sc[n + 1], 2)
    chip = lax.div(sc[n + 1], 2)
    for r in range(n):
        for y in range(nb // 2):
            first = (r * nb + 2 * y) * size
            place = y ^ chip
            for g in range(-(-D // 384)):
                cols = slice(g * 384, min(D, (g + 1) * 384))
                width = cols.stop - cols.start
                pair = [total[first + c * size : first + (c + 1) * size, cols] for c in range(2)]
                rows = slice(g * size, (g + 1) * size)
                keep[place, r, rows, 0:width] = jnp.where(core == 0, pair[0], pair[1]).astype(BF16)
                send[place, r, rows, 0:width] = jnp.where(core == 0, pair[1], pair[0]).astype(BF16)
                if width < 384:
                    keep[place, r, rows, width:384] = jnp.zeros((size, 384 - width), BF16)
                    send[place, r, rows, width:384] = jnp.zeros((size, 384 - width), BF16)


def w_out_grad_call(n, nb, sc, att_b, d_one_b, after):
    size = D // (n * nb)
    shape = (nb // 2, n, -(-D // 384) * size, 384)
    return pl.pallas_call(
        lambda *a: w_out_grad_kernel(n, nb, *a[: 1 + 2 * EXP_DEV], *a[-2:]),
        grid_spec=pltpu.PrefetchScalarGridSpec(
            num_scalar_prefetch=1,
            grid=(1,),
            in_specs=[whole(att_b[0].shape)] * (2 * EXP_DEV)
            + [pl.BlockSpec(memory_space=pl.ANY)] * len(after),
            out_specs=[whole(shape)] * 2,
        ),
        out_shape=[jax.ShapeDtypeStruct(shape, BF16)] * 2,
        compiler_params=params(),
        cost_estimate=cost(4),
        name="w_out_grad",
    )(sc, *att_b, *d_one_b, *after)


def qkv_grad_kernel(n, nb, T, sc, h, dm, aux, after, keep, send, total):
    me_b = sc[n + 1]

    def add(c, carry):
        total[...] += dot_tn(dm[c], h[c])
        return carry

    total[...] = jnp.zeros_like(total)
    lax.fori_loop(0, n, add, 0)
    col_sum = jnp.zeros((1, 384), F32)
    for r in range(n):
        col_sum = col_sum + jnp.sum(dm[r].astype(F32), axis=0, keepdims=True)
    width = D // n
    size = width // nb
    top = iota((16, 384), 0)
    for r in range(n):
        part = jnp.transpose(total[:, r * width : (r + 1) * width])
        for k in range(nb):
            bb = me_b ^ k
            rows = jnp.zeros((size, 384), F32)
            for c in range(nb):
                rows = jnp.where(bb == c, part[c * size : (c + 1) * size, :], rows)
            extra = jnp.where(
                top == 0, col_sum, jnp.where(top == 1, aux[r * nb + bb], 0.0)
            )
            to = keep if k % 2 == 0 else send
            to[k // 2, r, 0:size, :] = rows.astype(BF16)
            to[k // 2, r, size : size + 16, :] = extra.astype(BF16)


def qkv_grad_call(n, nb, T, sc, h, dm, aux, after):
    size = D // (n * nb)
    shape = (2, n, size + 16, 384)
    return pl.pallas_call(
        lambda *a: qkv_grad_kernel(n, nb, T, *a),
        grid_spec=pltpu.PrefetchScalarGridSpec(
            num_scalar_prefetch=1,
            grid=(1,),
            in_specs=[
                whole((n, T, D)),
                whole((n, T, 384)),
                whole((n * nb, 1, 384)),
                pl.BlockSpec(memory_space=pl.ANY),
            ],
            out_specs=[whole(shape), whole(shape)],
            scratch_shapes=[pltpu.VMEM((384, D), F32)],
        ),
        out_shape=[jax.ShapeDtypeStruct(shape, BF16)] * 2,
        compiler_params=params(),
        cost_estimate=cost(3),
        name="qkv_grad",
    )(sc, h, dm, aux, after)


def scatter_rows(cap, slots, kaug, values):
    feature = kaug[:, 128:256].astype(F32)
    code = (feature[:, 16:17] * cap + feature[:, 17:18]).astype(jnp.int32)
    pick = jnp.where(code == iota((feature.shape[0], slots), 1), 1.0, 0.0).astype(BF16)
    return dot_nn(pick, values)


def input_grad_kernel(n, T, cap, sc, dm, w_qkv, hidden, d_ret, kaug, gain, out, full):
    for k in range(n):
        for part in range(3):
            full[:, part * D + k * 128 : part * D + (k + 1) * 128] = dm[
                k, :, part * 128 : (part + 1) * 128
            ]
    u = dot_nt(full[...], w_qkv[...])
    vhat, inv_std = normed_rows(hidden[...].astype(F32))
    scaled = u * gain[...]
    first = jnp.mean(scaled, axis=-1, keepdims=True)
    second = jnp.mean(scaled * vhat, axis=-1, keepdims=True)
    d_one = scatter_rows(cap, d_ret.shape[0], kaug[...], d_ret[...])
    out[...] = (d_one + inv_std * (scaled - first - vhat * second)).astype(BF16)


def input_grad_call(n, T, cap, sc, dm, w_qkv, hidden, d_ret, kaug, gain):
    slots = d_ret.shape[0]
    return pl.pallas_call(
        lambda *a: input_grad_kernel(n, T, cap, *a),
        grid_spec=pltpu.PrefetchScalarGridSpec(
            num_scalar_prefetch=1,
            grid=(1,),
            in_specs=[
                whole((n, T, 384)),
                whole((D, 3 * D)),
                whole((T, D)),
                whole((slots, D)),
                pl.BlockSpec((T, 256), lambda i, sc: (sc[n], 0)),
                whole((1, D)),
            ],
            out_specs=whole((T, D)),
            scratch_shapes=[pltpu.VMEM((T, 3 * D), BF16)],
        ),
        out_shape=jax.ShapeDtypeStruct((T, D), BF16),
        compiler_params=params(),
        cost_estimate=SMALL,
        name="input_grad",
    )(sc, dm, w_qkv, hidden, d_ret, kaug, gain)


def output_kernel(cap, sc, ret, kaug, out):
    out[...] = scatter_rows(cap, ret.shape[0], kaug[...], ret[...]).astype(BF16)


def output_call(n, T, cap, sc, ret, kaug):
    return pl.pallas_call(
        lambda *a: output_kernel(cap, *a),
        grid_spec=pltpu.PrefetchScalarGridSpec(
            num_scalar_prefetch=1,
            grid=(1,),
            in_specs=[
                whole(ret.shape),
                pl.BlockSpec((T, 256), lambda i, sc: (sc[n], 0)),
            ],
            out_specs=whole((T, D)),
        ),
        out_shape=jax.ShapeDtypeStruct((T, D), BF16),
        compiler_params=params(),
        cost_estimate=SMALL,
        name="output_rows",
    )(sc, ret, kaug)


def final_kernel(n, nb, sc, got, w_rows, gb, gw, gains, biases, qvb, outb, gwo, s_rows, w_full):
    size = D // (n * nb)
    me, me_b = sc[n], sc[n + 1]
    smalls = jnp.zeros((1, 384), F32)
    s_rows[...] = jnp.zeros_like(s_rows)
    for k in range(n):
        tile = got[k, 0 : size + 16, :].astype(F32)
        for part in range(3):
            cols = slice(part * D + k * 128, part * D + (k + 1) * 128)
            w_full[:, cols] = tile[0:size, part * 128 : (part + 1) * 128]
            s_rows[0:1, cols] = tile[size : size + 1, part * 128 : (part + 1) * 128]
        smalls = smalls + tile[size + 1 : size + 2, :]
    gw[...] = w_full[...]
    for g in range(-(-D // 384)):
        cols = slice(g * 384, min(D, (g + 1) * 384))
        rows = slice((g + 1) * size + 16, (g + 2) * size + 16)
        total = jnp.zeros((size, 384), F32)
        for k in range(n):
            total = total + got[k, rows, :].astype(F32)
        gwo[:, cols] = total[:, 0 : cols.stop - cols.start]
    weights = w_rows[...].astype(F32)
    high = lax.Precision.HIGHEST
    nt = (((1,), (1,)), ((), ()))
    bias_one = lax.dot_general(s_rows[...], weights, nt, precision=high, preferred_element_type=F32)[0:1]
    both = lax.dot_general(
        jnp.ones((8, 3 * D), F32), weights * w_full[...], nt, precision=high, preferred_element_type=F32
    )[0:1]
    gains[0:1, :] = (both - gb[1:2, :] * bias_one) / gb[0:1, :]
    gains[1:2, :] = smalls[:, 0:size]
    biases[0:1, :] = bias_one
    biases[1:2, :] = smalls[:, size : 2 * size]
    outb[...] = smalls[:, 2 * size : 3 * size]
    own = got[me, size : size + 16, :].astype(F32)[0:1]
    for row, first in ((0, 0), (1, 256)):
        value = jnp.zeros((1, size), F32)
        for c in range(nb):
            value = jnp.where(me_b == c, own[:, first + c * size : first + (c + 1) * size], value)
        qvb[row : row + 1, :] = value


def final_call(n, nb, sc, got, w_qkv, gb):
    size = D // (n * nb)
    shapes = [(size, 3 * D), (2, size), (2, size), (2, size), (1, size), (size, D)]
    return pl.pallas_call(
        lambda *a: final_kernel(n, nb, *a),
        grid_spec=pltpu.PrefetchScalarGridSpec(
            num_scalar_prefetch=1,
            grid=(1,),
            in_specs=[
                whole(got.shape),
                pl.BlockSpec((size, 3 * D), lambda i, sc: (nb * sc[n] + sc[n + 1], 0)),
                whole((2, size)),
            ],
            out_specs=[whole(s) for s in shapes],
            scratch_shapes=[pltpu.VMEM((8, 3 * D), F32), pltpu.VMEM((size, 3 * D), F32)],
        ),
        out_shape=[jax.ShapeDtypeStruct(s, F32) for s in shapes],
        compiler_params=params(),
        cost_estimate=cost(3),
        name="final_rows",
    )(sc, got, w_qkv, gb)


def exchange(values, axis, bit):
    size = lax.axis_size(axis)
    return lax.ppermute(values, axis, [(i, i ^ bit) for i in range(size)])


def arrival_tables(n, ring):
    place = [ring.index(i) for i in range(n)]
    order = [[0]] + [[-o, o] for o in range(1, n // 2)] + [[n // 2]]
    sources, tiles, counts = [], [], None
    for i in range(n):
        blocks = [[ring[(place[i] + o) % n] for o in step] for step in order]
        arrived, listed, sizes = [], [], []
        for at, step in enumerate(blocks):
            arrived += step
            if at == 0:
                continue
            new = arrived if at == 1 else step
            diag = [(q, q) for q in sorted(new)]
            pairs = [
                (q, k)
                for k in range(n)
                for q in range(k + 1, n)
                if q in arrived and k in arrived and (q in new or k in new)
            ]
            listed.append([x for t in diag + pairs for x in t])
            sizes.append((len(diag), len(pairs)))
        sources.append([b for step in blocks for b in step])
        tiles.append(listed)
        counts = counts or sizes
    return np.array(sources, np.int32), tiles, counts


def reduce_cores(keep, send, after=None):
    got = exchange(send, "batch", 1)
    if after is not None:
        got = gate(got, after)
    return [(keep[y].astype(F32) + got[y].astype(F32)).astype(BF16) for y in range(2)]


def gate(value, *after):
    def nothing(*refs):
        del refs

    anywhere = pl.BlockSpec(memory_space=pl.ANY)
    return pl.pallas_call(
        nothing,
        in_specs=[anywhere] * (1 + len(after)),
        out_specs=anywhere,
        out_shape=jax.ShapeDtypeStruct(value.shape, value.dtype),
        input_output_aliases={0: 0},
        name="gate",
    )(value, *after)


def local_by_heads(
    hidden_in,
    out_grad,
    norm_gain_pair,
    norm_bias_pair,
    w_qkv,
    qv_bias,
    w_out,
    out_bias,
    w_in_exp,
    b_in_exp,
    w_out_exp,
    b_out_exp,
    expert_ids,
    doc_lengths,
    pad_mask,
):
    T = hidden_in.shape[1]
    n, nb = lax.axis_size("seq"), lax.axis_size("batch")
    experts = EXP_DEV * n
    cap = max(2, 3 * T // (2 * experts))
    s, b = lax.axis_index("seq"), lax.axis_index("batch")
    ring = [*range(0, n, 2), *range(n - 1, 0, -2)]
    sources, tiles, counts = arrival_tables(n, ring)

    every = [(i, i) for i in range(n)] + [(q, k) for k in range(n) for q in range(k + 1, n)]
    every = np.array(every, np.int32).reshape(-1)
    table = [
        np.concatenate([sources[i], [i, 0]] + tiles[i] + [every]).astype(np.int32) for i in range(n)
    ]
    firsts = n + 2 + np.cumsum([0] + [2 * (d + p) for d, p in counts])
    row = lax.dynamic_index_in_dim(jnp.asarray(np.stack(table)), s, 0, keepdims=False)
    sc = jnp.where(jnp.arange(row.shape[0]) == n + 1, b.astype(jnp.int32), row)
    hidden = hidden_in[0]
    ids = expert_ids[0, :, 0]
    codes = jnp.concatenate([ids, pad_mask[0], jnp.zeros((D - 2 * T,), jnp.int32)]).astype(BF16)
    codes = jnp.where(jnp.arange(16)[:, None] == 0, codes[None, :], jnp.zeros((), BF16))
    payload = jnp.concatenate([hidden, codes], axis=0)

    count = doc_lengths.shape[1]
    at = jnp.arange(128)
    ends = jnp.sum(
        jnp.where(jnp.arange(count)[:, None] <= at[None, :], doc_lengths[0][:, None], 0), axis=0
    )
    starts = jnp.sum(
        jnp.where(jnp.arange(count)[:, None] < at[None, :], doc_lengths[0][:, None], 0), axis=0
    )
    docs = jnp.stack([starts, ends]).astype(F32)
    gain_rows = [norm_gain_pair[i : i + 1] for i in range(2)]
    bias_rows = [norm_bias_pair[i : i + 1] for i in range(2)]

    ahead = [(ring[i], ring[(i + 1) % n]) for i in range(n)]
    back = [(ring[i], ring[i - 1]) for i in range(n)]
    split = -(-payload.shape[0] // 32) * 16
    size = D // (n * nb)
    own = (s * nb + b) * size
    gb = jnp.stack(
        [
            lax.dynamic_slice_in_dim(norm_gain_pair[0], own, size, 0),
            lax.dynamic_slice_in_dim(norm_bias_pair[0], own, size, 0),
        ]
    )
    held, block = None, 0
    left = right = payload
    waiting = [[payload]]
    sent_grads = dispatch_call(cap, experts * cap, [], ids[None], out_grad[0])
    for step in range(1, n // 2 + 1):
        last = step == n // 2
        if last:
            left, right = left[:split], right[split:]
        left, right = lax.ppermute(left, "seq", ahead), lax.ppermute(right, "seq", back)
        if last:
            waiting.append([left, right])
        else:
            left = gate(left, right, *(held or ())[6:7])
            right = gate(right, left)
            waiting += [[left], [right]]
        if last:
            sent_grads = gate(sent_grads, left, right, held[6])
        diags, pairs = counts[step - 1]
        held = ring_call(
            n, T, cap, block, int(firsts[step - 1]), diags, pairs, sc, waiting, held, last,
            w_qkv, qv_bias, gain_rows[0], bias_rows[0], docs, [sent_grads, gb] if last else [],
        )
        block += len(waiting)
        waiting = []
    h_one, sel, qa, ka = held[:4]
    *att_out, o, lse = held[9:]
    sel = sel.reshape(EXP_DEV * n * cap, D)

    sent_grads = sent_grads.reshape(n, EXP_DEV * cap, D)
    grads = lax.all_to_all(sent_grads, "seq", split_axis=0, concat_axis=0, tiled=True)
    grads = grads.reshape(n, EXP_DEV, cap, D).transpose(1, 0, 2, 3).reshape(experts * cap, D)
    g_y = exchange(grads, "batch", 2)
    g_parts = [grads, exchange(grads, "batch", 1), g_y, exchange(g_y, "batch", 1)]

    def by_seq(rows):
        return lax.all_to_all(rows, "seq", split_axis=0, concat_axis=0, tiled=True)

    att_in = []
    for e in range(EXP_DEV):
        att_in.append(by_seq(gate(att_out[e], att_in[-1]) if e else att_out[e]))
    x_two, x_one, att_b = [], [], []
    for e in range(EXP_DEV):
        rows, one, att_rows = owner_fwd_call(
            n, e, att_in[e], w_out, sel, out_bias[None], gain_rows[1], bias_rows[1]
        )
        x_two.append(rows)
        x_one.append(one)
        att_b.append(att_rows)
    x_core = [exchange(rows, "batch", 1) for rows in x_two]
    x_y = [exchange(rows, "batch", 2) for rows in x_two]
    x_parts, hidden_act, dpre, grad_b_in, sums, from_y = [], [], [], [], [], []
    d_one_b, small, datt, outs = [], [], [], []
    to_add = []
    after = [x_one[-1]]
    terms = None

    def turn_back(e):
        datt_out, rows, totals = owner_bwd_call(
            n, e, sums[e][0], from_y[e], x_one[e], grads, gain_rows[1], w_out, after
        )
        datt.append(by_seq(gate(datt_out, datt[-1]) if e else datt_out))
        d_one_b.append(rows)
        small.append(totals)
        return datt_out

    for e in range(EXP_DEV):
        if e:
            x_y[e] = gate(x_y[e], terms[0])
        x_parts.append([x_two[e], x_core[e], x_y[e], exchange(x_y[e], "batch", 1)])
        act, dact, *terms, grad_b = expert_call(
            e, sc, x_parts[e], g_parts, w_in_exp, b_in_exp, w_out_exp, after
        )
        hidden_act.append(act)
        dpre.append(dact)
        grad_b_in.append(grad_b[0])
        if e == 0:
            to_add.append(expert_out_call(nb, e, act, w_out_exp, []))
            filler = to_add[e][0]
        else:
            after = [terms[0]]
            turn_back(e - 1)
            filler = d_one_b[-1]
        sums.append(reduce_cores(*terms, after=filler))
        from_y.append(exchange(sums[e][1], "batch", 2))
        after = [sums[e][0]]
    for i in range(1, EXP_DEV):
        to_add.append(expert_out_call(nb, i, hidden_act[i], w_out_exp, after))
    after = [to_add[-1][0]]
    datt_out = turn_back(EXP_DEV - 1)
    outs = [reduce_cores(*to_add[i], after=datt_out) for i in range(EXP_DEV)]
    from_y = [exchange(both[1], "batch", 2) for both in outs]

    size = D // (n * nb)
    home = []
    for e in range(EXP_DEV):
        expert_rows = (
            outs[e][0].astype(F32) + from_y[e].astype(F32) + b_out_exp[e][None, :]
        ).astype(BF16)
        home.append((x_one[e] + expert_rows.astype(F32)).astype(BF16))
    home = [rows.reshape(n, cap, D) for rows in d_one_b + home]
    home = jnp.concatenate(home, axis=1)
    returned = by_seq(home)
    at = EXP_DEV * cap
    d_ret = returned[:, :at].reshape(experts * cap, D)
    dm = attn_bwd_call(
        n, T, cap, int(firsts[-1]), n, n * (n - 1) // 2, sc, qa, ka, lse, o, datt, [home]
    )
    w_out_terms = w_out_grad_call(n, nb, sc, att_b, d_one_b, [dm])
    aux = sum(small)[:3].reshape(3, n * nb, size).transpose(1, 0, 2).reshape(n * nb, 1, 3 * size)
    aux = jnp.pad(aux, ((0, 0), (0, 0), (0, 384 - 3 * size)))
    keep_w, send_w = qkv_grad_call(n, nb, T, sc, h_one, dm, aux, dm)
    dm_own = by_seq(gate(dm, keep_w, w_out_terms[0], returned))
    both = reduce_cores(keep_w, gate(send_w, returned))
    w_y = exchange(both[1], "batch", 2)
    w_out_both = reduce_cores(w_out_terms[0], gate(w_out_terms[1], both[0]))
    w_out_y = exchange(w_out_both[1], "batch", 2)
    weights = None
    for e in range(EXP_DEV):
        weights = expert_grad_call(
            e, sc, x_parts[e], g_parts, hidden_act[e], dpre[e], weights, [w_out_both[0]]
        )
    grad_w_in, grad_w_out_exp, grad_b_out = weights
    w_out_y = gate(w_out_y, grad_b_out)
    dm_own = gate(dm_own, w_y, w_out_y)
    w_y = gate(w_y, dm_own)
    w_sum = (both[0].astype(F32) + w_y.astype(F32)).astype(BF16)
    summed = (w_out_both[0].astype(F32) + w_out_y.astype(F32)).astype(BF16)
    w_got = by_seq(jnp.concatenate([w_sum, summed], axis=1))
    out_ret = gate(returned[:, at : 2 * at].reshape(experts * cap, D), dm_own)
    output = output_call(n, T, cap, sc, out_ret, ka)
    gw_qkv, g_gains, g_biases, g_qvb, g_outb, grad_w_out = final_call(n, nb, sc, w_got, w_qkv, gb)
    input_grad = input_grad_call(n, T, cap, sc, dm_own, w_qkv, hidden, d_ret, ka, gain_rows[0])
    return (
        output[None],
        input_grad[None],
        g_gains,
        g_biases,
        gw_qkv,
        g_qvb,
        grad_w_out,
        g_outb[0],
        grad_w_in,
        jnp.concatenate(grad_b_in, axis=0),
        grad_w_out_exp,
        grad_b_out[:, 0],
    )


def solution(mesh):
    n, nb = mesh.shape["seq"], mesh.shape["batch"]
    by_heads = HEADS * HEAD_DIM == 128 * n and nb == 4
    return jax.shard_map(
        local_by_heads if by_heads else local,
        mesh=mesh,
        in_specs=(
            P("batch", "seq", None),
            P("batch", "seq", None),
            P(),
            P(),
            P(),
            P(),
            P(),
            P(),
            P("seq", None, "batch"),
            P("seq", "batch"),
            P("seq", "batch", None),
            P("seq", None),
            P("batch", "seq", None),
            P("batch", None),
            P("batch", "seq"),
        ),
        out_specs=(
            P("batch", "seq", None),
            P("batch", "seq", None),
            P(None, ("seq", "batch")),
            P(None, ("seq", "batch")),
            P(("seq", "batch"), None),
            P(None, ("seq", "batch")),
            P(("seq", "batch"), None),
            P(("seq", "batch")),
            P("seq", None, "batch"),
            P("seq", "batch"),
            P("seq", "batch", None),
            P("seq", None),
        ),
        check_vma=False,
    )
```

```python
import math

import jax
import jax.numpy as jnp
import numpy as np
from jax import lax
from jax.experimental import pallas as pl
from jax.experimental.pallas import tpu as pltpu
from jax.sharding import PartitionSpec as P

D = 1024
HEADS = 16
HEAD_DIM = 64
EXP_DEV = 2


EPS = 1e-05
NEG = -1e30
BIG = 1e30
F32 = jnp.float32
BF16 = jnp.bfloat16
VMEM_LIMIT = 60 * 1024 * 1024


def dot_nn(a, b):
    return lax.dot_general(a, b, (((1,), (0,)), ((), ())), preferred_element_type=F32)


def dot_nt(a, b):
    return lax.dot_general(a, b, (((1,), (1,)), ((), ())), preferred_element_type=F32)


def dot_tn(a, b):
    return lax.dot_general(a, b, (((0,), (0,)), ((), ())), preferred_element_type=F32)


def normed_rows(values):
    centre = values - jnp.mean(values, axis=-1, keepdims=True)
    spread = jnp.mean(centre * centre, axis=-1, keepdims=True)
    inv_std = lax.rsqrt(spread + EPS)
    return centre * inv_std, inv_std


def whole(shape):
    return pl.BlockSpec(shape, lambda *_: (0,) * len(shape))


def params(**more):
    return pltpu.CompilerParams(vmem_limit_bytes=VMEM_LIMIT, **more)


def iota(shape, axis):
    return lax.broadcasted_iota(jnp.int32, shape, axis)


def running_sums(values):
    upto = jnp.arange(values.shape[0])[:, None] >= jnp.arange(values.shape[0])[None, :]
    return jnp.sum(jnp.where(upto, values[None, :], 0), axis=1)


def layer_normalize(values, gain, shift):
    centre = values - jnp.mean(values, axis=-1, keepdims=True)
    spread = jnp.mean(centre * centre, axis=-1, keepdims=True)
    inv_std = lax.rsqrt(spread + EPS)
    normed = centre * inv_std
    return (normed * gain + shift, normed, inv_std)


def norm_backward_pass(grads, normed, inv_std, gain):
    scaled = grads * gain
    first_mean = jnp.mean(scaled, axis=-1, keepdims=True)
    second_mean = jnp.mean(scaled * normed, axis=-1, keepdims=True)
    return (
        inv_std * (scaled - first_mean - normed * second_mean),
        jnp.sum(grads * normed, axis=0),
        jnp.sum(grads, axis=0),
    )


def doc_of(positions, doc_ends):
    return jnp.sum((positions[:, None] >= doc_ends[None, :]).astype(jnp.int32), axis=1)


def allowed_pairs(q_pos, q_doc, k_pos, k_doc, k_pad):
    same_doc = q_doc[:, None] == k_doc[None, :]
    before = k_pos[None, :] <= q_pos[:, None]
    usable = (k_pad[None, :] == 1) | (k_pos[None, :] == q_pos[:, None])
    return same_doc & before & usable


def over_blocks(step_fn, totals, arrays, first_row):
    row_count = arrays[0].shape[0]
    block_rows = math.gcd(row_count, 512)

    def advance(current, block_index):
        pieces = tuple(
            (
                lax.dynamic_slice_in_dim(member, block_index * block_rows, block_rows, 0)
                for member in arrays
            )
        )
        return (step_fn(current, pieces, first_row + block_index * block_rows), None)

    result, _ = lax.scan(advance, totals, jnp.arange(row_count // block_rows, dtype=jnp.int32))
    return result


def key_grads(
    query_h, dout_h, lse_rows, delta_rows, q_pos, q_doc, key_h, value_h, k_pos, k_doc, k_pad
):
    allowed = allowed_pairs(q_pos, q_doc, k_pos, k_doc, k_pad)
    scores = jnp.einsum("qhd,khd->hqk", query_h, key_h, preferred_element_type=jnp.float32)
    probs = jnp.where(allowed[None], jnp.exp(scores - lse_rows.T[:, :, None]), 0.0)
    dprobs = jnp.einsum("qhd,khd->hqk", dout_h, value_h, preferred_element_type=jnp.float32)
    dscores = (probs * (dprobs - delta_rows.T[:, :, None])).astype(jnp.bfloat16)
    grad_keys = jnp.einsum("hqk,qhd->khd", dscores, query_h, preferred_element_type=jnp.float32)
    grad_values = jnp.einsum(
        "hqk,qhd->khd", probs.astype(jnp.bfloat16), dout_h, preferred_element_type=jnp.float32
    )
    return (grad_keys, grad_values)


def gelu_exact(values):
    return jax.nn.gelu(values, approximate=False)


def local(
    hidden_in,
    out_grad,
    norm_gain_pair,
    norm_bias_pair,
    w_qkv,
    qv_bias,
    w_out,
    out_bias,
    w_in_exp,
    b_in_exp,
    w_out_exp,
    b_out_exp,
    expert_ids,
    doc_lengths,
    pad_mask,
):
    tok_rows = hidden_in.shape[1]
    seq_count = lax.axis_size("seq")
    experts_all = EXP_DEV * seq_count
    capacity = max(2, 3 * tok_rows // (2 * experts_all))
    scale = HEAD_DIM ** (-0.5)
    input_tokens = hidden_in[0].astype(jnp.float32)
    first_normalized, first_centred_scaled, first_inverse_deviation = layer_normalize(
        input_tokens, norm_gain_pair[0], norm_bias_pair[0]
    )
    h_one = first_normalized.astype(jnp.bfloat16)
    mixed = jnp.dot(h_one, w_qkv, preferred_element_type=jnp.float32)
    queries = ((mixed[:, :D] + qv_bias[0]) * scale).astype(jnp.bfloat16)
    keys_vals = jnp.concatenate(
        [mixed[:, D : 2 * D], mixed[:, 2 * D :] + qv_bias[1][None, :]], axis=1
    ).astype(jnp.bfloat16)
    query_h = queries.reshape(tok_rows, HEADS, HEAD_DIM)
    q_pos = lax.axis_index("seq") * tok_rows + jnp.arange(tok_rows, dtype=jnp.int32)
    doc_ends = running_sums(doc_lengths[0])
    q_doc = doc_of(q_pos, doc_ends)
    key_pad = pad_mask[0]

    def split_keys(pieces, first_row):
        block_kv, block_pad = pieces
        row_count = block_kv.shape[0]
        key_h = block_kv[:, :D].reshape(row_count, HEADS, HEAD_DIM)
        value_h = block_kv[:, D:].reshape(row_count, HEADS, HEAD_DIM)
        k_pos = first_row + jnp.arange(row_count, dtype=jnp.int32)
        allowed = allowed_pairs(q_pos, q_doc, k_pos, doc_of(k_pos, doc_ends), block_pad)
        scores = jnp.einsum("thd,khd->htk", query_h, key_h, preferred_element_type=jnp.float32)
        return (key_h, value_h, allowed, jnp.where(allowed[None], scores, NEG))

    def stats_step(current, pieces, first_row):
        _, _, allowed, scores = split_keys(pieces, first_row)
        top_now, mass_now = current
        new_top = jnp.maximum(top_now, jnp.max(scores, axis=-1))
        weights = jnp.where(allowed[None], jnp.exp(scores - new_top[:, :, None]), 0.0)
        return (new_top, mass_now * jnp.exp(top_now - new_top) + jnp.sum(weights, axis=-1))

    def output_step(current, pieces, first_row):
        _, value_h, allowed, scores = split_keys(pieces, first_row)
        probs = jnp.where(allowed[None], jnp.exp(scores - log_mass[:, :, None]), 0.0).astype(
            jnp.bfloat16
        )
        return current + jnp.einsum(
            "htk,khd->thd", probs, value_h, preferred_element_type=jnp.float32
        )

    def dquery_step(current, pieces, first_row):
        key_h, value_h, allowed, scores = split_keys(pieces, first_row)
        probs = jnp.where(allowed[None], jnp.exp(scores - log_mass[:, :, None]), 0.0)
        dprobs = jnp.einsum("thd,khd->htk", dout_h, value_h, preferred_element_type=jnp.float32)
        dscores = (probs * (dprobs - delta[:, :, None])).astype(jnp.bfloat16)
        return current + jnp.einsum(
            "htk,khd->thd", dscores, key_h, preferred_element_type=jnp.float32
        )

    head_zeros = jnp.zeros((tok_rows, HEADS, HEAD_DIM), jnp.float32)
    init_stats = (
        jnp.full((HEADS, tok_rows), NEG, jnp.float32),
        jnp.zeros((HEADS, tok_rows), jnp.float32),
    )
    all_kv, all_pad = (
        lax.all_gather(keys_vals, "seq", axis=0, tiled=True),
        lax.all_gather(key_pad, "seq", axis=0, tiled=True),
    )

    def run_keys(step_fn, totals):
        return over_blocks(step_fn, totals, (all_kv, all_pad), 0)

    top_all, mass_all = run_keys(stats_step, init_stats)
    log_mass = top_all + jnp.log(mass_all)
    attended = run_keys(output_step, head_zeros)
    attended_b = attended.reshape(tok_rows, D).astype(jnp.bfloat16)
    branch = jnp.dot(attended_b, w_out, preferred_element_type=jnp.float32) + out_bias
    first_residual_input = input_tokens + branch
    second_normalized, second_centred_scaled, second_inverse_deviation = layer_normalize(
        first_residual_input, norm_gain_pair[1], norm_bias_pair[1]
    )
    x_two = second_normalized.astype(jnp.bfloat16)
    token_ids = expert_ids[0, :, 0]
    earlier = jnp.arange(tok_rows)[None, :] < jnp.arange(tok_rows)[:, None]
    ranks = jnp.sum(((token_ids[:, None] == token_ids[None, :]) & earlier).astype(jnp.int32), axis=1)
    target = token_ids * capacity + ranks
    dispatch = (
        jnp.arange(experts_all * capacity, dtype=jnp.int32)[:, None] == target[None, :]
    ).astype(jnp.bfloat16)
    sent_rows = (
        jnp.dot(dispatch, x_two, preferred_element_type=jnp.float32)
        .astype(jnp.bfloat16)
        .reshape(seq_count, EXP_DEV, capacity, D)
    )
    rows_all = lax.all_gather(
        lax.all_to_all(sent_rows, "seq", split_axis=0, concat_axis=0, tiled=True),
        "batch",
        axis=0,
        tiled=True,
    )
    pre_act = (
        jnp.einsum("recd,edf->recf", rows_all, w_in_exp, preferred_element_type=jnp.float32)
        + b_in_exp[None, :, None, :]
    )
    hidden = gelu_exact(pre_act).astype(jnp.bfloat16)
    part_sums = jnp.einsum("recf,efd->recd", hidden, w_out_exp, preferred_element_type=jnp.float32)
    summed = lax.psum_scatter(
        part_sums.astype(jnp.bfloat16), "batch", scatter_dimension=0, tiled=True
    ).astype(jnp.float32)
    produced = (summed + b_out_exp[None, :, None, :]).astype(jnp.bfloat16)
    returned = lax.all_to_all(produced, "seq", split_axis=0, concat_axis=0, tiled=True)
    expert_rows = jnp.einsum(
        "st,sd->td",
        dispatch,
        returned.reshape(experts_all * capacity, D),
        preferred_element_type=jnp.float32,
    )
    output = (first_residual_input + expert_rows).astype(jnp.bfloat16)
    dout = out_grad[0].astype(jnp.float32)
    sent_grads = (
        jnp.dot(dispatch, out_grad[0], preferred_element_type=jnp.float32)
        .astype(jnp.bfloat16)
        .reshape(seq_count, EXP_DEV, capacity, D)
    )
    arrived_rows, arrived_grads = (
        lax.all_to_all(sent_rows, "seq", split_axis=0, concat_axis=0, tiled=True),
        lax.all_to_all(sent_grads, "seq", split_axis=0, concat_axis=0, tiled=True),
    )
    rows_all, grads_all = (
        lax.all_gather(arrived_rows, "batch", axis=0, tiled=True),
        lax.all_gather(arrived_grads, "batch", axis=0, tiled=True),
    )
    pre_act = (
        jnp.einsum("recd,edf->recf", rows_all, w_in_exp, preferred_element_type=jnp.float32)
        + b_in_exp[None, :, None, :]
    )
    hidden_f, gelu_back = jax.vjp(gelu_exact, pre_act)
    hidden_b = hidden_f.astype(jnp.bfloat16)
    dhidden = jnp.einsum(
        "recd,efd->recf", grads_all, w_out_exp, preferred_element_type=jnp.float32
    ).astype(jnp.bfloat16)
    dpre = gelu_back(dhidden.astype(jnp.float32))[0].astype(jnp.bfloat16)
    grad_w_out_exp = jnp.einsum(
        "recf,recd->efd", hidden_b, grads_all, preferred_element_type=jnp.float32
    )
    grad_b_out_exp = jnp.sum(grads_all, axis=(0, 2), dtype=jnp.float32)
    grad_w_in_exp = jnp.einsum("recd,recf->edf", rows_all, dpre, preferred_element_type=jnp.float32)
    grad_b_in_exp = jnp.sum(dpre, axis=(0, 2), dtype=jnp.float32)
    drows = jnp.einsum("recf,edf->recd", dpre, w_in_exp, preferred_element_type=jnp.float32)
    drows_sum = lax.psum_scatter(
        drows.astype(jnp.bfloat16), "batch", scatter_dimension=0, tiled=True
    )
    drows_home = lax.all_to_all(drows_sum, "seq", split_axis=0, concat_axis=0, tiled=True)
    second_residual_gradient = jnp.einsum(
        "st,sd->td",
        dispatch,
        drows_home.reshape(experts_all * capacity, D),
        preferred_element_type=jnp.float32,
    )
    second_norm_gradient, second_gain_gradient, second_shift_gradient = norm_backward_pass(
        second_residual_gradient, second_centred_scaled, second_inverse_deviation, norm_gain_pair[1]
    )
    d_one = dout + second_norm_gradient
    d_one_b = d_one.astype(jnp.bfloat16)
    grad_w_out = jnp.einsum("td,te->de", attended_b, d_one_b, preferred_element_type=jnp.float32)
    grad_out_bias = jnp.sum(d_one, axis=0)
    dout_b = jnp.einsum("te,de->td", d_one_b, w_out, preferred_element_type=jnp.float32).astype(
        jnp.bfloat16
    )
    dout_h = dout_b.reshape(tok_rows, HEADS, HEAD_DIM)
    delta = jnp.einsum("thd,thd->ht", dout_h.astype(jnp.float32), attended)
    dquery = run_keys(dquery_step, head_zeros)
    lse_rows = log_mass.T
    delta_rows = delta.T
    block_rows = math.gcd(tok_rows * lax.axis_size("seq"), 512)

    def one_block(block_index):
        first_key = block_index * block_rows
        block_kv = lax.dynamic_slice_in_dim(all_kv, first_key, block_rows, 0)
        block_pad = lax.dynamic_slice_in_dim(all_pad, first_key, block_rows, 0)
        k_pos = first_key + jnp.arange(block_rows, dtype=jnp.int32)
        grad_k, grad_v = key_grads(
            query_h,
            dout_h,
            lse_rows,
            delta_rows,
            q_pos,
            q_doc,
            block_kv[:, :D].reshape(block_rows, HEADS, HEAD_DIM),
            block_kv[:, D:].reshape(block_rows, HEADS, HEAD_DIM),
            k_pos,
            doc_of(k_pos, doc_ends),
            block_pad,
        )
        return jnp.concatenate(
            [grad_k.reshape(block_rows, D), grad_v.reshape(block_rows, D)], axis=1
        )

    blocks = lax.map(
        one_block, jnp.arange(tok_rows * lax.axis_size("seq") // block_rows, dtype=jnp.int32)
    )
    key_terms = lax.psum_scatter(
        blocks.reshape(tok_rows * lax.axis_size("seq"), 2 * D).astype(jnp.bfloat16),
        "seq",
        scatter_dimension=0,
        tiled=True,
    )
    dq_b = dquery.reshape(tok_rows, D).astype(jnp.bfloat16)
    dmixed = jnp.concatenate([dq_b * scale, key_terms], axis=1)
    grad_w_qkv = jnp.einsum("td,te->de", h_one, dmixed, preferred_element_type=jnp.float32)
    first_hidden_gradient = jnp.einsum(
        "te,de->td", dmixed, w_qkv, preferred_element_type=jnp.float32
    )
    first_norm_gradient, first_gain_gradient, first_shift_gradient = norm_backward_pass(
        first_hidden_gradient, first_centred_scaled, first_inverse_deviation, norm_gain_pair[0]
    )
    input_grad = (d_one + first_norm_gradient).astype(jnp.bfloat16)
    grad_q_bias = jnp.sum(dmixed[:, :D], axis=0, dtype=jnp.float32)
    grad_v_bias = jnp.sum(key_terms[:, D:], axis=0, dtype=jnp.float32)
    small_grads = jnp.stack(
        [
            first_gain_gradient,
            second_gain_gradient,
            first_shift_gradient,
            second_shift_gradient,
            grad_q_bias,
            grad_v_bias,
            grad_out_bias,
        ]
    )
    shared_qkv, shared_out, shared_small = (
        lax.psum_scatter(grad_w_qkv, ("seq", "batch"), scatter_dimension=0, tiled=True),
        lax.psum_scatter(grad_w_out, ("seq", "batch"), scatter_dimension=0, tiled=True),
        lax.psum_scatter(small_grads, ("seq", "batch"), scatter_dimension=1, tiled=True),
    )
    return (
        output[None],
        input_grad[None],
        shared_small[0:2],
        shared_small[2:4],
        shared_qkv,
        shared_small[4:6],
        shared_out,
        shared_small[6],
        grad_w_in_exp,
        grad_b_in_exp,
        grad_w_out_exp,
        grad_b_out_exp,
    )


MICROSECOND = 1 << 30


def cost(us):
    return pl.CostEstimate(flops=us * MICROSECOND, bytes_accessed=1 << 20, transcendentals=0)


MICROSECOND = 1 << 30


def cost(us):
    return pl.CostEstimate(flops=us * MICROSECOND, bytes_accessed=1 << 20, transcendentals=0)


SMALL = pl.CostEstimate(flops=1, bytes_accessed=1, transcendentals=0)
HALVES = [slice(h * HEAD_DIM, (h + 1) * HEAD_DIM) for h in range(2)]


def block_rows(i, T):
    return pl.ds(pl.multiple_of(i * T, T), T)


def diag_parts(T, key_rows):
    lane = iota((T, 256), 1)
    values = key_rows.astype(F32)
    unpadded = jnp.where(lane == 136, 0.0, values).astype(BF16)
    k_at, q_at = iota((T, T), 0), iota((T, T), 1)
    padded = values[:, 136:137] > 0.5
    allowed = ((k_at < q_at) & jnp.logical_not(padded)) | (k_at == q_at)
    return unpadded, allowed


def ring_kernel(n, T, cap, block, parts, at_tile, diags, pairs, first, last, extra, sc, *refs):
    refs = list(refs)

    def take(count):
        got = refs[:count]
        del refs[:count]
        return got

    count = len(parts)
    chunks = [take(p) for p in parts]
    wq, wk, wv, qvb, gain, bias, docs = take(7)
    old = [] if first else take(9)
    take(extra)
    outs = take(9)
    results = take(EXP_DEV + 2) if last else None
    h_out, sel_out, qa_out, ka_out, vt_out, code_out = outs[:6]
    h_s, sel_s, qa, ka, vt, code, top, mass, acc, w, in_sems, out_sems = take(12)
    me = sc[n]
    loads = [
        pltpu.make_async_copy(ref, to, in_sems.at[i])
        for i, (ref, to) in enumerate(zip(old[2:], (qa, ka, vt, code, top, mass, acc)))
    ]
    for load in loads:
        load.start()
    w[:, 0:128] = wq[...]
    w[:, 128:256] = wk[...]
    w[:, 256:384] = wv[...]
    payloads = []
    for c in range(count):
        rows = [ref[...] for ref in chunks[c]]
        rows = rows[0] if len(rows) == 1 else jnp.concatenate(rows, axis=0)
        payloads.append(rows)
        vhat, _ = normed_rows(rows[0:T].astype(F32))
        h_s[c] = (vhat * gain[...] + bias[...]).astype(BF16)
    for load in loads:
        load.wait()
    stores = []

    def send(ref, to):
        store = pltpu.make_async_copy(ref, to, out_sems.at[len(stores)])
        store.start()
        stores.append(store)

    for c in range(count):
        src = sc[block + c]
        rows = block_rows(src, T)
        mixed = dot_nn(h_s[c], w[...])
        q = ((mixed[:, 0:128] + qvb[0:1, :]) * (HEAD_DIM**-0.5)).astype(BF16).astype(F32)
        v = (mixed[:, 256:384] + qvb[1:2, :]).astype(BF16)
        codes = payloads[c][T : T + 16].astype(F32)
        id_row = codes[0:1, 0:T]
        pad_row = codes[0:1, T : 2 * T]
        id_col = jnp.transpose(jnp.broadcast_to(id_row, (128, T)))
        pad_col = jnp.transpose(jnp.broadcast_to(pad_row, (128, T)))
        same = jnp.where(
            (id_col[:, 0:1] == id_row) & (iota((T, T), 0) < iota((T, T), 1)), 1.0, 0.0
        )
        rank_row = jnp.sum(same, axis=0, keepdims=True)
        rank_col = jnp.transpose(jnp.broadcast_to(rank_row, (128, T)))
        lane = iota((T, 128), 1)
        pos = (iota((T, 128), 0) + src * T).astype(F32)
        doc = jnp.where((pos >= docs[0:1, :]) & (pos < docs[1:2, :]), 1.0, 0.0)
        aug = jnp.where(lane < 8, doc, 0.0)
        aug = jnp.where(lane == 8, 1.0 - pad_col, aug)
        aug = jnp.where(lane == 16, id_col, aug)
        aug = jnp.where(lane == 17, rank_col, aug)
        masked = jnp.where(lane < 8, (doc - 1.0) * BIG, jnp.where(lane == 8, -BIG, 0.0)).astype(BF16)
        for h in range(2):
            mine = (lane < HEAD_DIM) == (h == 0)
            qa[h, rows, 0:128] = jnp.where(mine, q, 0.0).astype(BF16)
            qa[h, rows, 128:256] = masked
        ka[rows, 0:128] = mixed[:, 128:256].astype(BF16)
        ka[rows, 128:256] = aug.astype(BF16)
        ka[rows, 256:384] = v
        vt[src] = jnp.transpose(v.astype(F32)).astype(BF16)
        slot = (id_row * cap + rank_row).astype(jnp.int32)
        half = lax.rem(src, 2) * cap
        code[src] = (id_row * (2 * cap) + rank_row).astype(jnp.int32) + half
        pick = jnp.where(
            slot == iota((EXP_DEV * cap, T), 0) + me * (EXP_DEV * cap), 1.0, 0.0
        ).astype(BF16)
        chosen = dot_nn(pick, payloads[c][0:T])
        for e in range(EXP_DEV):
            sel_s[c, e] = chosen[e * cap : (e + 1) * cap]
            send(sel_s.at[c, e], sel_out.at[e, src])
        send(h_s.at[c], h_out.at[src])
        for h in range(2):
            send(qa.at[h, rows], qa_out.at[h, rows])
        send(ka.at[rows], ka_out.at[rows])
        if not last:
            send(vt.at[src], vt_out.at[src])
            send(code.at[src], code_out.at[src])

    def one_diag(r, carry):
        i = sc[at_tile + 2 * r]
        rows = block_rows(i, T)
        kd, allowed = diag_parts(T, ka[rows, 0:256])
        for h in range(2):
            s = jnp.where(allowed, dot_nt(kd, qa[h, rows, :]), NEG)
            best = jnp.max(s, axis=0, keepdims=True)
            p = jnp.exp(s - best)
            top[h, i] = best
            mass[h, i] = jnp.sum(p, axis=0, keepdims=True)
            acc[i, HALVES[h], :] = dot_nn(vt[i, HALVES[h], :], p.astype(BF16))
        return carry

    lax.fori_loop(0, diags, one_diag, 0)

    def pair_tile(at):
        i, j = sc[at_tile + 2 * at], sc[at_tile + 2 * at + 1]
        rows, cols = block_rows(i, T), block_rows(j, T)
        old_top = [top[h, i] for h in range(2)]
        old_mass = [mass[h, i] for h in range(2)]
        old_acc = [acc[i, HALVES[h], :] for h in range(2)]
        s = [dot_nt(ka[cols, 0:256], qa[h, rows, :]) for h in range(2)]
        best = [jnp.maximum(old_top[h], jnp.max(s[h], axis=0, keepdims=True)) for h in range(2)]
        p = [jnp.exp(s[h] - best[h]) for h in range(2)]
        more = [dot_nn(vt[j, HALVES[h], :], p[h].astype(BF16)) for h in range(2)]
        for h in range(2):
            fade = jnp.exp(old_top[h] - best[h])
            top[h, i] = best[h]
            mass[h, i] = old_mass[h] * fade + jnp.sum(p[h], axis=0, keepdims=True)
            acc[i, HALVES[h], :] = old_acc[h] * fade + more[h]

    def two_pairs(r, carry):
        pair_tile(diags + 2 * r)
        pair_tile(diags + 2 * r + 1)
        return carry

    lax.fori_loop(0, pairs // 2, two_pairs, 0)
    if pairs % 2:
        pair_tile(diags + pairs - 1)
    if not last:
        for ref, to in zip((top, mass, acc), outs[6:]):
            send(ref, to)
    else:
        *att_out, o_out, lse_out = results

        def finish(i, carry):
            rows = block_rows(i, T)
            scaled = []
            for h in range(2):
                lse_out[h, i] = top[h, i] + jnp.log(mass[h, i])
                scaled.append(acc[i, HALVES[h], :] / mass[h, i])
            o_out[rows, :] = jnp.transpose(jnp.concatenate(scaled, axis=0))
            return carry

        lax.fori_loop(0, n, finish, 0)
        slots = n * EXP_DEV * 2 * cap

        def pair(p, carry):
            codes = jnp.concatenate([code[2 * p], code[2 * p + 1]], axis=1)
            pick = jnp.where(codes == iota((slots, 2 * T), 0), 1.0, 0.0).astype(BF16)
            chosen = dot_nn(pick, o_out[block_rows(p, 2 * T), :].astype(BF16)).astype(BF16)
            for k in range(n):
                for e in range(EXP_DEV):
                    at = (k * EXP_DEV + e) * 2 * cap
                    to = pl.multiple_of(p * 2 * cap, 16)
                    att_out[e][k, pl.ds(to, 2 * cap), :] = chosen[at : at + 2 * cap]
            return carry

        lax.fori_loop(0, n // 2, pair, 0)
    for store in stores:
        store.wait()


def ring_call(
    n, T, cap, block, at_tile, diags, pairs, sc, chunks, held, last, w_qkv, qv_bias, gain, bias, docs, after
):
    row = n * T
    shapes = [
        ((n, T, D), BF16),
        ((EXP_DEV, n, cap, D), F32),
        ((2, row, 256), BF16),
        ((row, 384), BF16),
        ((n, 128, T), BF16),
        ((n, 1, T), jnp.int32),
        ((2, n, 1, T), F32),
        ((2, n, 1, T), F32),
        ((n, 128, T), F32),
    ]
    anywhere = pl.BlockSpec(memory_space=pl.ANY)
    operands = [part for chunk in chunks for part in chunk]
    in_specs = [whole(part.shape) for part in operands] + [
        pl.BlockSpec((D, 128), lambda i, sc: (0, sc[n])),
        pl.BlockSpec((D, 128), lambda i, sc: (0, n + sc[n])),
        pl.BlockSpec((D, 128), lambda i, sc: (0, 2 * n + sc[n])),
        pl.BlockSpec((2, 128), lambda i, sc: (0, sc[n])),
        whole((1, D)),
        whole((1, D)),
        whole((2, 128)),
    ]
    aliases = {}
    first = held is None
    if not first:
        aliases = {1 + len(in_specs) + i: i for i in range(len(shapes))}
        in_specs = in_specs + [anywhere] * len(shapes)
    in_specs = in_specs + [anywhere] * len(after)
    out_specs = [anywhere] * len(shapes)
    results = []
    if last:
        results = [((n, n * cap, 128), BF16)] * EXP_DEV
        results = results + [((row, 128), F32), ((2, n, 1, T), F32)]
        out_specs = out_specs + [whole(s) for s, _ in results]
    count = len(chunks)
    parts = [len(chunk) for chunk in chunks]
    return pl.pallas_call(
        lambda *a: ring_kernel(
            n, T, cap, block, parts, at_tile, diags, pairs, first, last, len(after), *a
        ),
        grid_spec=pltpu.PrefetchScalarGridSpec(
            num_scalar_prefetch=1,
            grid=(1,),
            in_specs=in_specs,
            out_specs=out_specs,
            scratch_shapes=[
                pltpu.VMEM((count, T, D), BF16),
                pltpu.VMEM((count, EXP_DEV, cap, D), F32),
            ]
            + [pltpu.VMEM(s, t) for s, t in shapes[2:]]
            + [
                pltpu.VMEM((D, 384), BF16),
                pltpu.SemaphoreType.DMA((7,)),
                pltpu.SemaphoreType.DMA((8 * count + 3,)),
            ],
        ),
        out_shape=[jax.ShapeDtypeStruct(s, t) for s, t in shapes + results],
        input_output_aliases=aliases,
        compiler_params=params(),
        cost_estimate=cost(10),
        name="ring_step",
    )(sc, *operands, w_qkv, w_qkv, w_qkv, qv_bias, gain, bias, docs, *(held or ()), *after)


def attn_bwd_kernel(
    n, T, cap, at_tile, diags, pairs, tiles, qa, ka, lse, o_ref, *refs
):
    datt = refs[:EXP_DEV]
    dm_out, do, delta, kh, dqa, dka, dva = refs[-7:]
    slots = n * EXP_DEV * 2 * cap

    def pair(p, carry):
        rows = block_rows(p, 2 * T)
        feature = ka[rows, 128:256].astype(F32)
        half = jnp.where(iota((2 * T, 1), 0) >= T, float(cap), 0.0)
        code = (feature[:, 16:17] * (2 * cap) + feature[:, 17:18] + half).astype(jnp.int32)
        pick = jnp.where(code == iota((2 * T, slots), 1), 1.0, 0.0).astype(BF16)
        parts = []
        for k in range(n):
            for e in range(EXP_DEV):
                at = pl.multiple_of(p * 2 * cap, 16)
                parts.append(datt[e][k, pl.ds(at, 2 * cap), :])
        got = dot_nn(pick, jnp.concatenate(parts, axis=0))
        lane = iota((2 * T, 128), 1)
        keys = ka[rows, 0:128].astype(F32)
        for h in range(2):
            mine = (lane < HEAD_DIM) == (h == 0)
            do[h, rows, :] = jnp.where(mine, got, 0.0).astype(BF16)
            kh[h, rows, :] = jnp.where(mine, keys, 0.0).astype(BF16)
        prod = jnp.transpose(got * o_ref[rows, :])
        for h in range(2):
            total = jnp.sum(prod[HALVES[h], :], axis=0, keepdims=True)
            delta[h, 2 * p] = total[:, 0:T]
            delta[h, 2 * p + 1] = total[:, T : 2 * T]
        return carry

    lax.fori_loop(0, n // 2, pair, 0)

    def tile(i, j, key_rows, mask):
        rows, cols = block_rows(i, T), block_rows(j, T)
        ps, dss = [], []
        for h in range(2):
            s = dot_nt(key_rows, qa[h, rows, :])
            dp = dot_nt(ka[cols, 256:384], do[h, rows, :])
            if mask is not None:
                s = jnp.where(mask, s, NEG)
            p = jnp.exp(s - lse[h, i])
            dss.append((p * (dp - delta[h, i])).astype(BF16))
            ps.append(p.astype(BF16))
        dv = dot_nn(
            jnp.concatenate(ps, axis=1), jnp.concatenate([do[0, rows, :], do[1, rows, :]], axis=0)
        )
        dk = dot_nn(
            jnp.concatenate(dss, axis=1),
            jnp.concatenate([qa[0, rows, 0:128], qa[1, rows, 0:128]], axis=0),
        )
        dq = dot_tn(
            jnp.concatenate(dss, axis=0), jnp.concatenate([kh[0, cols, :], kh[1, cols, :]], axis=0)
        )
        return dq, dk, dv

    def diag_tile(j, carry):
        kd, allowed = diag_parts(T, ka[block_rows(j, T), 0:256])
        dqa[j], dka[j], dva[j] = tile(j, j, kd, allowed)
        return carry

    lax.fori_loop(0, n, diag_tile, 0)

    def pair_tile(at):
        i, j = tiles[at_tile + 2 * at], tiles[at_tile + 2 * at + 1]
        dq, dk, dv = tile(i, j, ka[block_rows(j, T), 0:256], None)
        dqa[i] += dq
        dka[j] += dk
        dva[j] += dv

    width = next(w for w in (4, 2, 1) if pairs % w == 0)

    def some_pairs(r, carry):
        for w in range(width):
            pair_tile(diags + width * r + w)
        return carry

    lax.fori_loop(0, pairs // width, some_pairs, 0)

    def finish(i, carry):
        dq = dqa[i].astype(BF16).astype(F32)
        dm_out[i, :, 0:128] = (dq * (HEAD_DIM**-0.5)).astype(BF16)
        dm_out[i, :, 128:256] = dka[i].astype(BF16)
        dm_out[i, :, 256:384] = dva[i].astype(BF16)
        return carry

    lax.fori_loop(0, n, finish, 0)


def attn_bwd_call(n, T, cap, at_tile, diags, pairs, tiles, qa, ka, lse, o, datt, after):
    row = n * T
    vmem = pl.BlockSpec(memory_space=pltpu.VMEM)
    return pl.pallas_call(
        lambda *a: attn_bwd_kernel(n, T, cap, at_tile, diags, pairs, *a),
        out_shape=jax.ShapeDtypeStruct((n, T, 384), BF16),
        in_specs=[pl.BlockSpec(memory_space=pltpu.SMEM)]
        + [vmem] * (4 + EXP_DEV)
        + [pl.BlockSpec(memory_space=pl.ANY)] * len(after),
        out_specs=vmem,
        scratch_shapes=[
            pltpu.VMEM((2, row, 128), BF16),
            pltpu.VMEM((2, n, 1, T), F32),
            pltpu.VMEM((2, row, 128), BF16),
            pltpu.VMEM((n, T, 128), F32),
            pltpu.VMEM((n, T, 128), F32),
            pltpu.VMEM((n, T, 128), F32),
        ],
        compiler_params=params(),
        cost_estimate=cost(28),
        name="attn_bwd",
    )(tiles, qa, ka, lse, o, *datt, *after)


def dispatch_kernel(cap, slots, ids, grads, *refs):
    out = refs[-1]
    id_row = ids[...].astype(F32)
    T = id_row.shape[1]
    id_col = jnp.transpose(jnp.broadcast_to(id_row, (128, T)))[:, 0:1]
    same = jnp.where((id_col == id_row) & (iota((T, T), 0) < iota((T, T), 1)), 1.0, 0.0)
    rank = jnp.sum(same, axis=0, keepdims=True)
    slot = (id_row * cap + rank).astype(jnp.int32)
    pick = jnp.where(slot == iota((slots, T), 0), 1.0, 0.0).astype(BF16)
    out[...] = dot_nn(pick, grads[...]).astype(BF16)


def dispatch_call(cap, slots, after, ids, grads):
    vmem = pl.BlockSpec(memory_space=pltpu.VMEM)
    return pl.pallas_call(
        lambda *a: dispatch_kernel(cap, slots, *a),
        out_shape=jax.ShapeDtypeStruct((slots, D), BF16),
        in_specs=[vmem, vmem] + [pl.BlockSpec(memory_space=pl.ANY)] * len(after),
        out_specs=vmem,
        compiler_params=params(),
        cost_estimate=cost(3),
        name="dispatch",
    )(ids, grads, *after)


def owner_fwd_kernel(n, att_in, w_out, sel, out_bias, gain, bias, x_two, x_one, att_b):
    for k in range(n):
        att_b[:, k * 128 : (k + 1) * 128] = att_in[k]
    branch = dot_nn(att_b[...], w_out[...]) + out_bias[...]
    x = sel[...] + branch
    x_one[...] = x
    vhat, _ = normed_rows(x)
    x_two[...] = (vhat * gain[...] + bias[...]).astype(BF16)


def owner_fwd_call(n, e, att_in, w_out, sel, out_bias, gain, bias):
    slots = sel.shape[0] // EXP_DEV
    rows = pl.BlockSpec((slots, D), lambda i: (e, 0))
    mine = whole((slots, D))
    return pl.pallas_call(
        lambda *a: owner_fwd_kernel(n, *a),
        grid=(1,),
        in_specs=[
            whole((n, slots, 128)),
            whole((D, D)),
            rows,
            whole((1, D)),
            whole((1, D)),
            whole((1, D)),
        ],
        out_specs=[mine, mine, mine],
        out_shape=[
            jax.ShapeDtypeStruct((slots, D), BF16),
            jax.ShapeDtypeStruct((slots, D), F32),
            jax.ShapeDtypeStruct((slots, D), BF16),
        ],
        compiler_params=params(),
        cost_estimate=cost(3),
        name="owner_fwd",
    )(att_in, w_out, sel, out_bias, gain, bias)


def owner_bwd_kernel(n, part_a, part_b, x_one, og, gain, w_out, *refs):
    datt, d_one_b, small = refs[-3:]
    u = (part_a[...].astype(F32) + part_b[...].astype(F32)).astype(BF16).astype(F32)
    vhat, inv_std = normed_rows(x_one[...])
    scaled = u * gain[...]
    first = jnp.mean(scaled, axis=-1, keepdims=True)
    second = jnp.mean(scaled * vhat, axis=-1, keepdims=True)
    d_one = og[...].astype(F32) + inv_std * (scaled - first - vhat * second)
    d_b = d_one.astype(BF16)
    d_one_b[...] = d_b
    back = dot_nt(d_b, w_out[...]).astype(BF16)
    for k in range(n):
        datt[k] = back[:, k * 128 : (k + 1) * 128]
    small[0:1, :] = jnp.sum(u * vhat, axis=0, keepdims=True)
    small[1:2, :] = jnp.sum(u, axis=0, keepdims=True)
    small[2:3, :] = jnp.sum(d_one, axis=0, keepdims=True)


def owner_bwd_call(n, e, part_a, part_b, x_one, og, gain, w_out, after):
    slots = x_one.shape[0]
    mine = whole((slots, D))
    in_specs = [
        mine,
        mine,
        mine,
        pl.BlockSpec((slots, D), lambda i: (e, 0)),
        whole((1, D)),
        whole((D, D)),
    ]
    return pl.pallas_call(
        lambda *a: owner_bwd_kernel(n, *a),
        grid=(1,),
        in_specs=in_specs + [pl.BlockSpec(memory_space=pl.ANY)] * len(after),
        out_specs=[
            whole((n, slots, 128)),
            mine,
            whole((8, D)),
        ],
        out_shape=[
            jax.ShapeDtypeStruct((n, slots, 128), BF16),
            jax.ShapeDtypeStruct((slots, D), BF16),
            jax.ShapeDtypeStruct((8, D), F32),
        ],
        compiler_params=params(),
        cost_estimate=cost(4),
        name="owner_bwd",
    )(part_a, part_b, x_one, og, gain, w_out, *after)


def gelu_parts(u):
    cdf = 0.5 * (1.0 + lax.erf(u * (0.5**0.5)))
    return cdf, cdf + u * jnp.exp(-0.5 * u * u) * ((2.0 * math.pi) ** -0.5)


ROW_ORDER = (1, 3, 0, 2)


def expert_kernel(e, nb, rows, ff, width, extra, *refs):
    x_parts, g_parts = refs[:nb], refs[nb : 2 * nb]
    w_in, b_in, w_out = refs[2 * nb : 2 * nb + 3]
    hidden_out, dpre_out, keep, send, grad_b = refs[2 * nb + 3 + extra : 2 * nb + 8 + extra]
    xs, gs, w1, w2, hidden, dpre, part, sems = refs[2 * nb + 8 + extra :]
    copies = []

    def copy(ref, to):
        made = pltpu.make_async_copy(ref, to, sems.at[len(copies)])
        made.start()
        copies.append(made)

    for at, k in enumerate(ROW_ORDER):
        copy(x_parts[k], xs.at[pl.ds(at * rows, rows)])
    copy(w_in.at[e], w1)
    for at, k in enumerate(ROW_ORDER):
        copy(g_parts[k].at[pl.ds(e * rows, rows)], gs.at[pl.ds(at * rows, rows)])
    copy(w_out.at[e], w2)
    for c in copies[: nb + 1]:
        c.wait()
    ready = len(copies)
    for f in range(ff // width):
        cols = slice(f * width, (f + 1) * width)
        pre = dot_nn(xs[...], w1[:, cols]) + b_in[e : e + 1, cols]
        if f == 0:
            for c in copies[nb + 1 : ready]:
                c.wait()
        dhidden = dot_nt(gs[...], w2[cols, :]).astype(BF16).astype(F32)
        cdf, slope = gelu_parts(pre)
        hidden[:, cols] = (pre * cdf).astype(BF16)
        value = (dhidden * slope).astype(BF16)
        dpre[:, cols] = value
        grad_b[0, :, cols] = jnp.sum(value.astype(F32), axis=0, keepdims=True)
    copy(hidden, hidden_out)
    copy(dpre, dpre_out)
    for half, to in enumerate((send, keep)):
        at = slice(2 * half * rows, 2 * (half + 1) * rows)
        value = dot_nt(dpre[at, :], w1[...]).astype(BF16)
        for y in range(2):
            part[2 * half + y] = value[y * rows : (y + 1) * rows]
            copy(part.at[2 * half + y], to.at[y])
    for c in copies[ready:]:
        c.wait()


def expert_call(e, sc, x_parts, g_parts, w_in, b_in, w_out, after):
    del sc
    nb = len(x_parts)
    rows = x_parts[0].shape[0]
    ff = w_in.shape[2]
    anywhere = pl.BlockSpec(memory_space=pl.ANY)
    return pl.pallas_call(
        lambda *a: expert_kernel(e, nb, rows, ff, min(256, ff), len(after), *a),
        in_specs=[anywhere] * (2 * nb + 1)
        + [pl.BlockSpec(memory_space=pltpu.VMEM), anywhere]
        + [anywhere] * len(after),
        out_specs=[anywhere] * 4 + [pl.BlockSpec(memory_space=pltpu.VMEM)],
        scratch_shapes=[
            pltpu.VMEM((nb * rows, D), BF16),
            pltpu.VMEM((nb * rows, D), BF16),
            pltpu.VMEM((D, ff), BF16),
            pltpu.VMEM((ff, D), BF16),
            pltpu.VMEM((nb * rows, ff), BF16),
            pltpu.VMEM((nb * rows, ff), BF16),
            pltpu.VMEM((nb, rows, D), BF16),
            pltpu.SemaphoreType.DMA((3 * nb + 4,)),
        ],
        out_shape=[
            jax.ShapeDtypeStruct((nb * rows, ff), BF16),
            jax.ShapeDtypeStruct((nb * rows, ff), BF16),
            jax.ShapeDtypeStruct((2, rows, D), BF16),
            jax.ShapeDtypeStruct((2, rows, D), BF16),
            jax.ShapeDtypeStruct((1, 1, ff), F32),
        ],
        compiler_params=params(),
        cost_estimate=cost(10),
        name="expert_main",
    )(*x_parts, *g_parts, w_in, b_in, w_out, *after)


def expert_out_kernel(rows, hidden, w_out, *refs):
    keep, send = refs[-2:]
    total = dot_nn(hidden[...], w_out[0]).astype(BF16)
    for y in range(2):
        send[y] = total[y * rows : (y + 1) * rows, :]
        keep[y] = total[(2 + y) * rows : (3 + y) * rows, :]


def expert_out_call(nb, e, hidden, w_out, after):
    rows = hidden.shape[0] // nb
    ff = hidden.shape[1]
    return pl.pallas_call(
        lambda *a: expert_out_kernel(rows, *a),
        grid=(1,),
        in_specs=[whole(hidden.shape), pl.BlockSpec((1, ff, D), lambda i: (e, 0, 0))]
        + [pl.BlockSpec(memory_space=pl.ANY)] * len(after),
        out_specs=[whole((2, rows, D))] * 2,
        out_shape=[jax.ShapeDtypeStruct((2, rows, D), BF16)] * 2,
        compiler_params=params(),
        cost_estimate=cost(4),
        name="expert_out",
    )(hidden, w_out, *after)


def expert_grad_kernel(nb, rows, sc, *refs):
    x_parts, g_parts = refs[:nb], refs[nb : 2 * nb]
    hidden, dpre = refs[2 * nb : 2 * nb + 2]
    grad_in, grad_out, grad_b, xs, gs = refs[-5:]

    @pl.when(pl.program_id(0) == 0)
    def _():
        sums = []
        for at, k in enumerate(ROW_ORDER):
            xs[at * rows : (at + 1) * rows, :] = x_parts[k][...]
            gs[at * rows : (at + 1) * rows, :] = g_parts[k][...]
        for k in range(nb):
            sums.append(jnp.sum(g_parts[k][...].astype(F32), axis=0, keepdims=True))
        grad_b[0] = (sums[0] + sums[1]) + (sums[2] + sums[3])

    grad_in[0] = dot_tn(xs[...], dpre[...])
    grad_out[0] = dot_tn(hidden[...], gs[...])


def expert_grad_call(e, sc, x_parts, g_parts, hidden, dpre, held, after):
    nb = len(x_parts)
    rows = x_parts[0].shape[0]
    ff = hidden.shape[1]
    width = min(256, ff)
    g_specs = [pl.BlockSpec((rows, D), lambda f, sc: (e, 0))] * nb
    act = pl.BlockSpec((nb * rows, width), lambda f, sc: (0, f))
    in_specs = [whole((rows, D))] * nb + g_specs + [act, act]
    more = [] if held is None else list(held)
    aliases = {1 + len(in_specs) + i: i for i in range(len(more))}
    more += after
    return pl.pallas_call(
        lambda *a: expert_grad_kernel(nb, rows, *a),
        grid_spec=pltpu.PrefetchScalarGridSpec(
            num_scalar_prefetch=1,
            grid=(ff // width,),
            in_specs=in_specs + [pl.BlockSpec(memory_space=pl.ANY)] * len(more),
            out_specs=[
                pl.BlockSpec((1, D, width), lambda f, sc: (e, 0, f)),
                pl.BlockSpec((1, width, D), lambda f, sc: (e, f, 0)),
                pl.BlockSpec((1, 1, D), lambda f, sc: (e, 0, 0)),
            ],
            scratch_shapes=[pltpu.VMEM((nb * rows, D), BF16)] * 2,
        ),
        out_shape=[
            jax.ShapeDtypeStruct((EXP_DEV, D, ff), F32),
            jax.ShapeDtypeStruct((EXP_DEV, ff, D), F32),
            jax.ShapeDtypeStruct((EXP_DEV, 1, D), F32),
        ],
        input_output_aliases=aliases,
        compiler_params=params(),
        cost_estimate=SMALL,
        name="expert_grads",
    )(sc, *x_parts, *g_parts, hidden, dpre, *more)


def w_out_grad_kernel(n, nb, sc, *refs):
    keep, send = refs[-2:]
    total = dot_tn(refs[0][...], refs[EXP_DEV][...])
    for e in range(1, EXP_DEV):
        total = total + dot_tn(refs[e][...], refs[EXP_DEV + e][...])
    size = D // (n * nb)
    core = lax.rem(sc[n + 1], 2)
    chip = lax.div(sc[n + 1], 2)
    for r in range(n):
        for y in range(nb // 2):
            first = (r * nb + 2 * y) * size
            place = y ^ chip
            for g in range(-(-D // 384)):
                cols = slice(g * 384, min(D, (g + 1) * 384))
                width = cols.stop - cols.start
                pair = [total[first + c * size : first + (c + 1) * size, cols] for c in range(2)]
                rows = slice(g * size, (g + 1) * size)
                keep[place, r, rows, 0:width] = jnp.where(core == 0, pair[0], pair[1]).astype(BF16)
                send[place, r, rows, 0:width] = jnp.where(core == 0, pair[1], pair[0]).astype(BF16)
                if width < 384:
                    keep[place, r, rows, width:384] = jnp.zeros((size, 384 - width), BF16)
                    send[place, r, rows, width:384] = jnp.zeros((size, 384 - width), BF16)


def w_out_grad_call(n, nb, sc, att_b, d_one_b, after):
    size = D // (n * nb)
    shape = (nb // 2, n, -(-D // 384) * size, 384)
    return pl.pallas_call(
        lambda *a: w_out_grad_kernel(n, nb, *a[: 1 + 2 * EXP_DEV], *a[-2:]),
        grid_spec=pltpu.PrefetchScalarGridSpec(
            num_scalar_prefetch=1,
            grid=(1,),
            in_specs=[whole(att_b[0].shape)] * (2 * EXP_DEV)
            + [pl.BlockSpec(memory_space=pl.ANY)] * len(after),
            out_specs=[whole(shape)] * 2,
        ),
        out_shape=[jax.ShapeDtypeStruct(shape, BF16)] * 2,
        compiler_params=params(),
        cost_estimate=cost(4),
        name="w_out_grad",
    )(sc, *att_b, *d_one_b, *after)


def qkv_grad_kernel(n, nb, T, sc, h, dm, aux, after, keep, send, total):
    me_b = sc[n + 1]

    def add(c, carry):
        total[...] += dot_tn(dm[c], h[c])
        return carry

    total[...] = jnp.zeros_like(total)
    lax.fori_loop(0, n, add, 0)
    col_sum = jnp.zeros((1, 384), F32)
    for r in range(n):
        col_sum = col_sum + jnp.sum(dm[r].astype(F32), axis=0, keepdims=True)
    width = D // n
    size = width // nb
    top = iota((16, 384), 0)
    for r in range(n):
        part = jnp.transpose(total[:, r * width : (r + 1) * width])
        for k in range(nb):
            bb = me_b ^ k
            rows = jnp.zeros((size, 384), F32)
            for c in range(nb):
                rows = jnp.where(bb == c, part[c * size : (c + 1) * size, :], rows)
            extra = jnp.where(
                top == 0, col_sum, jnp.where(top == 1, aux[r * nb + bb], 0.0)
            )
            to = keep if k % 2 == 0 else send
            to[k // 2, r, 0:size, :] = rows.astype(BF16)
            to[k // 2, r, size : size + 16, :] = extra.astype(BF16)


def qkv_grad_call(n, nb, T, sc, h, dm, aux, after):
    size = D // (n * nb)
    shape = (2, n, size + 16, 384)
    return pl.pallas_call(
        lambda *a: qkv_grad_kernel(n, nb, T, *a),
        grid_spec=pltpu.PrefetchScalarGridSpec(
            num_scalar_prefetch=1,
            grid=(1,),
            in_specs=[
                whole((n, T, D)),
                whole((n, T, 384)),
                whole((n * nb, 1, 384)),
                pl.BlockSpec(memory_space=pl.ANY),
            ],
            out_specs=[whole(shape), whole(shape)],
            scratch_shapes=[pltpu.VMEM((384, D), F32)],
        ),
        out_shape=[jax.ShapeDtypeStruct(shape, BF16)] * 2,
        compiler_params=params(),
        cost_estimate=cost(3),
        name="qkv_grad",
    )(sc, h, dm, aux, after)


def scatter_rows(cap, slots, kaug, values):
    feature = kaug[:, 128:256].astype(F32)
    code = (feature[:, 16:17] * cap + feature[:, 17:18]).astype(jnp.int32)
    pick = jnp.where(code == iota((feature.shape[0], slots), 1), 1.0, 0.0).astype(BF16)
    return dot_nn(pick, values)


def input_grad_kernel(n, T, cap, sc, dm, w_qkv, hidden, d_ret, kaug, gain, out, full):
    for k in range(n):
        for part in range(3):
            full[:, part * D + k * 128 : part * D + (k + 1) * 128] = dm[
                k, :, part * 128 : (part + 1) * 128
            ]
    u = dot_nt(full[...], w_qkv[...])
    vhat, inv_std = normed_rows(hidden[...].astype(F32))
    scaled = u * gain[...]
    first = jnp.mean(scaled, axis=-1, keepdims=True)
    second = jnp.mean(scaled * vhat, axis=-1, keepdims=True)
    d_one = scatter_rows(cap, d_ret.shape[0], kaug[...], d_ret[...])
    out[...] = (d_one + inv_std * (scaled - first - vhat * second)).astype(BF16)


def input_grad_call(n, T, cap, sc, dm, w_qkv, hidden, d_ret, kaug, gain):
    slots = d_ret.shape[0]
    return pl.pallas_call(
        lambda *a: input_grad_kernel(n, T, cap, *a),
        grid_spec=pltpu.PrefetchScalarGridSpec(
            num_scalar_prefetch=1,
            grid=(1,),
            in_specs=[
                whole((n, T, 384)),
                whole((D, 3 * D)),
                whole((T, D)),
                whole((slots, D)),
                pl.BlockSpec((T, 256), lambda i, sc: (sc[n], 0)),
                whole((1, D)),
            ],
            out_specs=whole((T, D)),
            scratch_shapes=[pltpu.VMEM((T, 3 * D), BF16)],
        ),
        out_shape=jax.ShapeDtypeStruct((T, D), BF16),
        compiler_params=params(),
        cost_estimate=SMALL,
        name="input_grad",
    )(sc, dm, w_qkv, hidden, d_ret, kaug, gain)


def output_kernel(cap, sc, ret, kaug, out):
    out[...] = scatter_rows(cap, ret.shape[0], kaug[...], ret[...]).astype(BF16)


def output_call(n, T, cap, sc, ret, kaug):
    return pl.pallas_call(
        lambda *a: output_kernel(cap, *a),
        grid_spec=pltpu.PrefetchScalarGridSpec(
            num_scalar_prefetch=1,
            grid=(1,),
            in_specs=[
                whole(ret.shape),
                pl.BlockSpec((T, 256), lambda i, sc: (sc[n], 0)),
            ],
            out_specs=whole((T, D)),
        ),
        out_shape=jax.ShapeDtypeStruct((T, D), BF16),
        compiler_params=params(),
        cost_estimate=SMALL,
        name="output_rows",
    )(sc, ret, kaug)


def final_kernel(n, nb, sc, got, w_rows, gb, gw, gains, biases, qvb, outb, gwo, s_rows, w_full):
    size = D // (n * nb)
    me, me_b = sc[n], sc[n + 1]
    smalls = jnp.zeros((1, 384), F32)
    s_rows[...] = jnp.zeros_like(s_rows)
    for k in range(n):
        tile = got[k, 0 : size + 16, :].astype(F32)
        for part in range(3):
            cols = slice(part * D + k * 128, part * D + (k + 1) * 128)
            w_full[:, cols] = tile[0:size, part * 128 : (part + 1) * 128]
            s_rows[0:1, cols] = tile[size : size + 1, part * 128 : (part + 1) * 128]
        smalls = smalls + tile[size + 1 : size + 2, :]
    gw[...] = w_full[...]
    for g in range(-(-D // 384)):
        cols = slice(g * 384, min(D, (g + 1) * 384))
        rows = slice((g + 1) * size + 16, (g + 2) * size + 16)
        total = jnp.zeros((size, 384), F32)
        for k in range(n):
            total = total + got[k, rows, :].astype(F32)
        gwo[:, cols] = total[:, 0 : cols.stop - cols.start]
    weights = w_rows[...].astype(F32)
    high = lax.Precision.HIGHEST
    nt = (((1,), (1,)), ((), ()))
    bias_one = lax.dot_general(s_rows[...], weights, nt, precision=high, preferred_element_type=F32)[0:1]
    both = lax.dot_general(
        jnp.ones((8, 3 * D), F32), weights * w_full[...], nt, precision=high, preferred_element_type=F32
    )[0:1]
    gains[0:1, :] = (both - gb[1:2, :] * bias_one) / gb[0:1, :]
    gains[1:2, :] = smalls[:, 0:size]
    biases[0:1, :] = bias_one
    biases[1:2, :] = smalls[:, size : 2 * size]
    outb[...] = smalls[:, 2 * size : 3 * size]
    own = got[me, size : size + 16, :].astype(F32)[0:1]
    for row, first in ((0, 0), (1, 256)):
        value = jnp.zeros((1, size), F32)
        for c in range(nb):
            value = jnp.where(me_b == c, own[:, first + c * size : first + (c + 1) * size], value)
        qvb[row : row + 1, :] = value


def final_call(n, nb, sc, got, w_qkv, gb):
    size = D // (n * nb)
    shapes = [(size, 3 * D), (2, size), (2, size), (2, size), (1, size), (size, D)]
    return pl.pallas_call(
        lambda *a: final_kernel(n, nb, *a),
        grid_spec=pltpu.PrefetchScalarGridSpec(
            num_scalar_prefetch=1,
            grid=(1,),
            in_specs=[
                whole(got.shape),
                pl.BlockSpec((size, 3 * D), lambda i, sc: (nb * sc[n] + sc[n + 1], 0)),
                whole((2, size)),
            ],
            out_specs=[whole(s) for s in shapes],
            scratch_shapes=[pltpu.VMEM((8, 3 * D), F32), pltpu.VMEM((size, 3 * D), F32)],
        ),
        out_shape=[jax.ShapeDtypeStruct(s, F32) for s in shapes],
        compiler_params=params(),
        cost_estimate=cost(3),
        name="final_rows",
    )(sc, got, w_qkv, gb)


def exchange(values, axis, bit):
    size = lax.axis_size(axis)
    return lax.ppermute(values, axis, [(i, i ^ bit) for i in range(size)])


def arrival_tables(n, ring):
    place = [ring.index(i) for i in range(n)]
    order = [[0]] + [[-o, o] for o in range(1, n // 2)] + [[n // 2]]
    sources, tiles, counts = [], [], None
    for i in range(n):
        blocks = [[ring[(place[i] + o) % n] for o in step] for step in order]
        arrived, listed, sizes = [], [], []
        for at, step in enumerate(blocks):
            arrived += step
            if at == 0:
                continue
            new = arrived if at == 1 else step
            diag = [(q, q) for q in sorted(new)]
            pairs = [
                (q, k)
                for k in range(n)
                for q in range(k + 1, n)
                if q in arrived and k in arrived and (q in new or k in new)
            ]
            listed.append([x for t in diag + pairs for x in t])
            sizes.append((len(diag), len(pairs)))
        sources.append([b for step in blocks for b in step])
        tiles.append(listed)
        counts = counts or sizes
    return np.array(sources, np.int32), tiles, counts


def reduce_cores(keep, send, after=None):
    got = exchange(send, "batch", 1)
    if after is not None:
        got = gate(got, after)
    return [(keep[y].astype(F32) + got[y].astype(F32)).astype(BF16) for y in range(2)]


def gate(value, *after):
    def nothing(*refs):
        del refs

    anywhere = pl.BlockSpec(memory_space=pl.ANY)
    return pl.pallas_call(
        nothing,
        in_specs=[anywhere] * (1 + len(after)),
        out_specs=anywhere,
        out_shape=jax.ShapeDtypeStruct(value.shape, value.dtype),
        input_output_aliases={0: 0},
        name="gate",
    )(value, *after)


def local_by_heads(
    hidden_in,
    out_grad,
    norm_gain_pair,
    norm_bias_pair,
    w_qkv,
    qv_bias,
    w_out,
    out_bias,
    w_in_exp,
    b_in_exp,
    w_out_exp,
    b_out_exp,
    expert_ids,
    doc_lengths,
    pad_mask,
):
    T = hidden_in.shape[1]
    n, nb = lax.axis_size("seq"), lax.axis_size("batch")
    experts = EXP_DEV * n
    cap = max(2, 3 * T // (2 * experts))
    s, b = lax.axis_index("seq"), lax.axis_index("batch")
    ring = [*range(0, n, 2), *range(n - 1, 0, -2)]
    sources, tiles, counts = arrival_tables(n, ring)

    every = [(i, i) for i in range(n)] + [(q, k) for k in range(n) for q in range(k + 1, n)]
    every = np.array(every, np.int32).reshape(-1)
    table = [
        np.concatenate([sources[i], [i, 0]] + tiles[i] + [every]).astype(np.int32) for i in range(n)
    ]
    firsts = n + 2 + np.cumsum([0] + [2 * (d + p) for d, p in counts])
    row = lax.dynamic_index_in_dim(jnp.asarray(np.stack(table)), s, 0, keepdims=False)
    sc = jnp.where(jnp.arange(row.shape[0]) == n + 1, b.astype(jnp.int32), row)
    hidden = hidden_in[0]
    ids = expert_ids[0, :, 0]
    codes = jnp.concatenate([ids, pad_mask[0], jnp.zeros((D - 2 * T,), jnp.int32)]).astype(BF16)
    codes = jnp.where(jnp.arange(16)[:, None] == 0, codes[None, :], jnp.zeros((), BF16))
    payload = jnp.concatenate([hidden, codes], axis=0)

    count = doc_lengths.shape[1]
    at = jnp.arange(128)
    ends = jnp.sum(
        jnp.where(jnp.arange(count)[:, None] <= at[None, :], doc_lengths[0][:, None], 0), axis=0
    )
    starts = jnp.sum(
        jnp.where(jnp.arange(count)[:, None] < at[None, :], doc_lengths[0][:, None], 0), axis=0
    )
    docs = jnp.stack([starts, ends]).astype(F32)
    gain_rows = [norm_gain_pair[i : i + 1] for i in range(2)]
    bias_rows = [norm_bias_pair[i : i + 1] for i in range(2)]

    ahead = [(ring[i], ring[(i + 1) % n]) for i in range(n)]
    back = [(ring[i], ring[i - 1]) for i in range(n)]
    split = -(-payload.shape[0] // 32) * 16
    size = D // (n * nb)
    own = (s * nb + b) * size
    gb = jnp.stack(
        [
            lax.dynamic_slice_in_dim(norm_gain_pair[0], own, size, 0),
            lax.dynamic_slice_in_dim(norm_bias_pair[0], own, size, 0),
        ]
    )
    held, block = None, 0
    left = right = payload
    waiting = [[payload]]
    sent_grads = dispatch_call(cap, experts * cap, [], ids[None], out_grad[0])
    for step in range(1, n // 2 + 1):
        last = step == n // 2
        if last:
            left, right = left[:split], right[split:]
        left, right = lax.ppermute(left, "seq", ahead), lax.ppermute(right, "seq", back)
        if last:
            waiting.append([left, right])
        else:
            left = gate(left, right, *(held or ())[6:7])
            right = gate(right, left)
            waiting += [[left], [right]]
        if last:
            sent_grads = gate(sent_grads, left, right, held[6])
        diags, pairs = counts[step - 1]
        held = ring_call(
            n, T, cap, block, int(firsts[step - 1]), diags, pairs, sc, waiting, held, last,
            w_qkv, qv_bias, gain_rows[0], bias_rows[0], docs, [sent_grads, gb] if last else [],
        )
        block += len(waiting)
        waiting = []
    h_one, sel, qa, ka = held[:4]
    *att_out, o, lse = held[9:]
    sel = sel.reshape(EXP_DEV * n * cap, D)

    sent_grads = sent_grads.reshape(n, EXP_DEV * cap, D)
    grads = lax.all_to_all(sent_grads, "seq", split_axis=0, concat_axis=0, tiled=True)
    grads = grads.reshape(n, EXP_DEV, cap, D).transpose(1, 0, 2, 3).reshape(experts * cap, D)
    g_y = exchange(grads, "batch", 2)
    g_parts = [grads, exchange(grads, "batch", 1), g_y, exchange(g_y, "batch", 1)]

    def by_seq(rows):
        return lax.all_to_all(rows, "seq", split_axis=0, concat_axis=0, tiled=True)

    att_in = []
    for e in range(EXP_DEV):
        att_in.append(by_seq(gate(att_out[e], att_in[-1]) if e else att_out[e]))
    x_two, x_one, att_b = [], [], []
    for e in range(EXP_DEV):
        rows, one, att_rows = owner_fwd_call(
            n, e, att_in[e], w_out, sel, out_bias[None], gain_rows[1], bias_rows[1]
        )
        x_two.append(rows)
        x_one.append(one)
        att_b.append(att_rows)
    x_core = [exchange(rows, "batch", 1) for rows in x_two]
    x_y = [exchange(rows, "batch", 2) for rows in x_two]
    x_parts, hidden_act, dpre, grad_b_in, sums, from_y = [], [], [], [], [], []
    d_one_b, small, datt, outs = [], [], [], []
    to_add = []
    after = [x_one[-1]]
    terms = None

    def turn_back(e):
        datt_out, rows, totals = owner_bwd_call(
            n, e, sums[e][0], from_y[e], x_one[e], grads, gain_rows[1], w_out, after
        )
        datt.append(by_seq(gate(datt_out, datt[-1]) if e else datt_out))
        d_one_b.append(rows)
        small.append(totals)
        return datt_out

    for e in range(EXP_DEV):
        if e:
            x_y[e] = gate(x_y[e], terms[0])
        x_parts.append([x_two[e], x_core[e], x_y[e], exchange(x_y[e], "batch", 1)])
        act, dact, *terms, grad_b = expert_call(
            e, sc, x_parts[e], g_parts, w_in_exp, b_in_exp, w_out_exp, after
        )
        hidden_act.append(act)
        dpre.append(dact)
        grad_b_in.append(grad_b[0])
        if e == 0:
            to_add.append(expert_out_call(nb, e, act, w_out_exp, []))
            filler = to_add[e][0]
        else:
            after = [terms[0]]
            turn_back(e - 1)
            filler = d_one_b[-1]
        sums.append(reduce_cores(*terms, after=filler))
        from_y.append(exchange(sums[e][1], "batch", 2))
        after = [sums[e][0]]
    for i in range(1, EXP_DEV):
        to_add.append(expert_out_call(nb, i, hidden_act[i], w_out_exp, after))
    after = [to_add[-1][0]]
    datt_out = turn_back(EXP_DEV - 1)
    outs = [reduce_cores(*to_add[i], after=datt_out) for i in range(EXP_DEV)]
    from_y = [exchange(both[1], "batch", 2) for both in outs]

    size = D // (n * nb)
    home = []
    for e in range(EXP_DEV):
        expert_rows = (
            outs[e][0].astype(F32) + from_y[e].astype(F32) + b_out_exp[e][None, :]
        ).astype(BF16)
        home.append((x_one[e] + expert_rows.astype(F32)).astype(BF16))
    home = [rows.reshape(n, cap, D) for rows in d_one_b + home]
    home = jnp.concatenate(home, axis=1)
    returned = by_seq(home)
    at = EXP_DEV * cap
    dm = attn_bwd_call(
        n, T, cap, int(firsts[-1]), n, n * (n - 1) // 2, sc, qa, ka, lse, o, datt, [home]
    )
    w_out_terms = w_out_grad_call(n, nb, sc, att_b, d_one_b, [dm])
    aux = sum(small)[:3].reshape(3, n * nb, size).transpose(1, 0, 2).reshape(n * nb, 1, 3 * size)
    aux = jnp.pad(aux, ((0, 0), (0, 0), (0, 384 - 3 * size)))
    keep_w, send_w = qkv_grad_call(n, nb, T, sc, h_one, dm, aux, dm)
    returned = gate(returned, keep_w, w_out_terms[0])
    d_ret = returned[:, :at].reshape(experts * cap, D)
    dm_own = by_seq(gate(dm, returned))
    both = reduce_cores(keep_w, gate(send_w, returned))
    w_y = exchange(both[1], "batch", 2)
    w_out_both = reduce_cores(w_out_terms[0], gate(w_out_terms[1], both[0]))
    w_out_y = exchange(w_out_both[1], "batch", 2)
    weights = None
    for e in range(EXP_DEV):
        weights = expert_grad_call(
            e, sc, x_parts[e], g_parts, hidden_act[e], dpre[e], weights, [w_out_both[0]]
        )
    grad_w_in, grad_w_out_exp, grad_b_out = weights
    w_out_y = gate(w_out_y, grad_b_out)
    w_y = gate(w_y, grad_b_out)
    w_sum = (both[0].astype(F32) + w_y.astype(F32)).astype(BF16)
    summed = (w_out_both[0].astype(F32) + w_out_y.astype(F32)).astype(BF16)
    last_rows = jnp.concatenate([w_sum, summed], axis=1)
    dm_own = gate(dm_own, last_rows)
    w_got = by_seq(gate(last_rows, dm_own))
    out_ret = gate(returned[:, at : 2 * at].reshape(experts * cap, D), dm_own)
    output = output_call(n, T, cap, sc, out_ret, ka)
    gw_qkv, g_gains, g_biases, g_qvb, g_outb, grad_w_out = final_call(n, nb, sc, w_got, w_qkv, gb)
    input_grad = input_grad_call(n, T, cap, sc, dm_own, w_qkv, hidden, d_ret, ka, gain_rows[0])
    return (
        output[None],
        input_grad[None],
        g_gains,
        g_biases,
        gw_qkv,
        g_qvb,
        grad_w_out,
        g_outb[0],
        grad_w_in,
        jnp.concatenate(grad_b_in, axis=0),
        grad_w_out_exp,
        grad_b_out[:, 0],
    )


def solution(mesh):
    n, nb = mesh.shape["seq"], mesh.shape["batch"]
    by_heads = HEADS * HEAD_DIM == 128 * n and nb == 4
    return jax.shard_map(
        local_by_heads if by_heads else local,
        mesh=mesh,
        in_specs=(
            P("batch", "seq", None),
            P("batch", "seq", None),
            P(),
            P(),
            P(),
            P(),
            P(),
            P(),
            P("seq", None, "batch"),
            P("seq", "batch"),
            P("seq", "batch", None),
            P("seq", None),
            P("batch", "seq", None),
            P("batch", None),
            P("batch", "seq"),
        ),
        out_specs=(
            P("batch", "seq", None),
            P("batch", "seq", None),
            P(None, ("seq", "batch")),
            P(None, ("seq", "batch")),
            P(("seq", "batch"), None),
            P(None, ("seq", "batch")),
            P(("seq", "batch"), None),
            P(("seq", "batch")),
            P("seq", None, "batch"),
            P("seq", "batch"),
            P("seq", "batch", None),
            P("seq", None),
        ),
        check_vma=False,
    )
```

```python
import math

import jax
import jax.numpy as jnp
import numpy as np
from jax import lax
from jax.experimental import pallas as pl
from jax.experimental.pallas import tpu as pltpu
from jax.sharding import PartitionSpec as P

D = 1024
HEADS = 16
HEAD_DIM = 64
EXP_DEV = 2


EPS = 1e-05
NEG = -1e30
BIG = 1e30
F32 = jnp.float32
BF16 = jnp.bfloat16
VMEM_LIMIT = 60 * 1024 * 1024


def dot_nn(a, b):
    return lax.dot_general(a, b, (((1,), (0,)), ((), ())), preferred_element_type=F32)


def dot_nt(a, b):
    return lax.dot_general(a, b, (((1,), (1,)), ((), ())), preferred_element_type=F32)


def dot_tn(a, b):
    return lax.dot_general(a, b, (((0,), (0,)), ((), ())), preferred_element_type=F32)


def normed_rows(values):
    centre = values - jnp.mean(values, axis=-1, keepdims=True)
    spread = jnp.mean(centre * centre, axis=-1, keepdims=True)
    inv_std = lax.rsqrt(spread + EPS)
    return centre * inv_std, inv_std


def whole(shape):
    return pl.BlockSpec(shape, lambda *_: (0,) * len(shape))


def params(**more):
    return pltpu.CompilerParams(vmem_limit_bytes=VMEM_LIMIT, **more)


def iota(shape, axis):
    return lax.broadcasted_iota(jnp.int32, shape, axis)


def running_sums(values):
    upto = jnp.arange(values.shape[0])[:, None] >= jnp.arange(values.shape[0])[None, :]
    return jnp.sum(jnp.where(upto, values[None, :], 0), axis=1)


def layer_normalize(values, gain, shift):
    centre = values - jnp.mean(values, axis=-1, keepdims=True)
    spread = jnp.mean(centre * centre, axis=-1, keepdims=True)
    inv_std = lax.rsqrt(spread + EPS)
    normed = centre * inv_std
    return (normed * gain + shift, normed, inv_std)


def norm_backward_pass(grads, normed, inv_std, gain):
    scaled = grads * gain
    first_mean = jnp.mean(scaled, axis=-1, keepdims=True)
    second_mean = jnp.mean(scaled * normed, axis=-1, keepdims=True)
    return (
        inv_std * (scaled - first_mean - normed * second_mean),
        jnp.sum(grads * normed, axis=0),
        jnp.sum(grads, axis=0),
    )


def doc_of(positions, doc_ends):
    return jnp.sum((positions[:, None] >= doc_ends[None, :]).astype(jnp.int32), axis=1)


def allowed_pairs(q_pos, q_doc, k_pos, k_doc, k_pad):
    same_doc = q_doc[:, None] == k_doc[None, :]
    before = k_pos[None, :] <= q_pos[:, None]
    usable = (k_pad[None, :] == 1) | (k_pos[None, :] == q_pos[:, None])
    return same_doc & before & usable


def over_blocks(step_fn, totals, arrays, first_row):
    row_count = arrays[0].shape[0]
    block_rows = math.gcd(row_count, 512)

    def advance(current, block_index):
        pieces = tuple(
            (
                lax.dynamic_slice_in_dim(member, block_index * block_rows, block_rows, 0)
                for member in arrays
            )
        )
        return (step_fn(current, pieces, first_row + block_index * block_rows), None)

    result, _ = lax.scan(advance, totals, jnp.arange(row_count // block_rows, dtype=jnp.int32))
    return result


def key_grads(
    query_h, dout_h, lse_rows, delta_rows, q_pos, q_doc, key_h, value_h, k_pos, k_doc, k_pad
):
    allowed = allowed_pairs(q_pos, q_doc, k_pos, k_doc, k_pad)
    scores = jnp.einsum("qhd,khd->hqk", query_h, key_h, preferred_element_type=jnp.float32)
    probs = jnp.where(allowed[None], jnp.exp(scores - lse_rows.T[:, :, None]), 0.0)
    dprobs = jnp.einsum("qhd,khd->hqk", dout_h, value_h, preferred_element_type=jnp.float32)
    dscores = (probs * (dprobs - delta_rows.T[:, :, None])).astype(jnp.bfloat16)
    grad_keys = jnp.einsum("hqk,qhd->khd", dscores, query_h, preferred_element_type=jnp.float32)
    grad_values = jnp.einsum(
        "hqk,qhd->khd", probs.astype(jnp.bfloat16), dout_h, preferred_element_type=jnp.float32
    )
    return (grad_keys, grad_values)


def gelu_exact(values):
    return jax.nn.gelu(values, approximate=False)


def local(
    hidden_in,
    out_grad,
    norm_gain_pair,
    norm_bias_pair,
    w_qkv,
    qv_bias,
    w_out,
    out_bias,
    w_in_exp,
    b_in_exp,
    w_out_exp,
    b_out_exp,
    expert_ids,
    doc_lengths,
    pad_mask,
):
    tok_rows = hidden_in.shape[1]
    seq_count = lax.axis_size("seq")
    experts_all = EXP_DEV * seq_count
    capacity = max(2, 3 * tok_rows // (2 * experts_all))
    scale = HEAD_DIM ** (-0.5)
    input_tokens = hidden_in[0].astype(jnp.float32)
    first_normalized, first_centred_scaled, first_inverse_deviation = layer_normalize(
        input_tokens, norm_gain_pair[0], norm_bias_pair[0]
    )
    h_one = first_normalized.astype(jnp.bfloat16)
    mixed = jnp.dot(h_one, w_qkv, preferred_element_type=jnp.float32)
    queries = ((mixed[:, :D] + qv_bias[0]) * scale).astype(jnp.bfloat16)
    keys_vals = jnp.concatenate(
        [mixed[:, D : 2 * D], mixed[:, 2 * D :] + qv_bias[1][None, :]], axis=1
    ).astype(jnp.bfloat16)
    query_h = queries.reshape(tok_rows, HEADS, HEAD_DIM)
    q_pos = lax.axis_index("seq") * tok_rows + jnp.arange(tok_rows, dtype=jnp.int32)
    doc_ends = running_sums(doc_lengths[0])
    q_doc = doc_of(q_pos, doc_ends)
    key_pad = pad_mask[0]

    def split_keys(pieces, first_row):
        block_kv, block_pad = pieces
        row_count = block_kv.shape[0]
        key_h = block_kv[:, :D].reshape(row_count, HEADS, HEAD_DIM)
        value_h = block_kv[:, D:].reshape(row_count, HEADS, HEAD_DIM)
        k_pos = first_row + jnp.arange(row_count, dtype=jnp.int32)
        allowed = allowed_pairs(q_pos, q_doc, k_pos, doc_of(k_pos, doc_ends), block_pad)
        scores = jnp.einsum("thd,khd->htk", query_h, key_h, preferred_element_type=jnp.float32)
        return (key_h, value_h, allowed, jnp.where(allowed[None], scores, NEG))

    def stats_step(current, pieces, first_row):
        _, _, allowed, scores = split_keys(pieces, first_row)
        top_now, mass_now = current
        new_top = jnp.maximum(top_now, jnp.max(scores, axis=-1))
        weights = jnp.where(allowed[None], jnp.exp(scores - new_top[:, :, None]), 0.0)
        return (new_top, mass_now * jnp.exp(top_now - new_top) + jnp.sum(weights, axis=-1))

    def output_step(current, pieces, first_row):
        _, value_h, allowed, scores = split_keys(pieces, first_row)
        probs = jnp.where(allowed[None], jnp.exp(scores - log_mass[:, :, None]), 0.0).astype(
            jnp.bfloat16
        )
        return current + jnp.einsum(
            "htk,khd->thd", probs, value_h, preferred_element_type=jnp.float32
        )

    def dquery_step(current, pieces, first_row):
        key_h, value_h, allowed, scores = split_keys(pieces, first_row)
        probs = jnp.where(allowed[None], jnp.exp(scores - log_mass[:, :, None]), 0.0)
        dprobs = jnp.einsum("thd,khd->htk", dout_h, value_h, preferred_element_type=jnp.float32)
        dscores = (probs * (dprobs - delta[:, :, None])).astype(jnp.bfloat16)
        return current + jnp.einsum(
            "htk,khd->thd", dscores, key_h, preferred_element_type=jnp.float32
        )

    head_zeros = jnp.zeros((tok_rows, HEADS, HEAD_DIM), jnp.float32)
    init_stats = (
        jnp.full((HEADS, tok_rows), NEG, jnp.float32),
        jnp.zeros((HEADS, tok_rows), jnp.float32),
    )
    all_kv, all_pad = (
        lax.all_gather(keys_vals, "seq", axis=0, tiled=True),
        lax.all_gather(key_pad, "seq", axis=0, tiled=True),
    )

    def run_keys(step_fn, totals):
        return over_blocks(step_fn, totals, (all_kv, all_pad), 0)

    top_all, mass_all = run_keys(stats_step, init_stats)
    log_mass = top_all + jnp.log(mass_all)
    attended = run_keys(output_step, head_zeros)
    attended_b = attended.reshape(tok_rows, D).astype(jnp.bfloat16)
    branch = jnp.dot(attended_b, w_out, preferred_element_type=jnp.float32) + out_bias
    first_residual_input = input_tokens + branch
    second_normalized, second_centred_scaled, second_inverse_deviation = layer_normalize(
        first_residual_input, norm_gain_pair[1], norm_bias_pair[1]
    )
    x_two = second_normalized.astype(jnp.bfloat16)
    token_ids = expert_ids[0, :, 0]
    earlier = jnp.arange(tok_rows)[None, :] < jnp.arange(tok_rows)[:, None]
    ranks = jnp.sum(((token_ids[:, None] == token_ids[None, :]) & earlier).astype(jnp.int32), axis=1)
    target = token_ids * capacity + ranks
    dispatch = (
        jnp.arange(experts_all * capacity, dtype=jnp.int32)[:, None] == target[None, :]
    ).astype(jnp.bfloat16)
    sent_rows = (
        jnp.dot(dispatch, x_two, preferred_element_type=jnp.float32)
        .astype(jnp.bfloat16)
        .reshape(seq_count, EXP_DEV, capacity, D)
    )
    rows_all = lax.all_gather(
        lax.all_to_all(sent_rows, "seq", split_axis=0, concat_axis=0, tiled=True),
        "batch",
        axis=0,
        tiled=True,
    )
    pre_act = (
        jnp.einsum("recd,edf->recf", rows_all, w_in_exp, preferred_element_type=jnp.float32)
        + b_in_exp[None, :, None, :]
    )
    hidden = gelu_exact(pre_act).astype(jnp.bfloat16)
    part_sums = jnp.einsum("recf,efd->recd", hidden, w_out_exp, preferred_element_type=jnp.float32)
    summed = lax.psum_scatter(
        part_sums.astype(jnp.bfloat16), "batch", scatter_dimension=0, tiled=True
    ).astype(jnp.float32)
    produced = (summed + b_out_exp[None, :, None, :]).astype(jnp.bfloat16)
    returned = lax.all_to_all(produced, "seq", split_axis=0, concat_axis=0, tiled=True)
    expert_rows = jnp.einsum(
        "st,sd->td",
        dispatch,
        returned.reshape(experts_all * capacity, D),
        preferred_element_type=jnp.float32,
    )
    output = (first_residual_input + expert_rows).astype(jnp.bfloat16)
    dout = out_grad[0].astype(jnp.float32)
    sent_grads = (
        jnp.dot(dispatch, out_grad[0], preferred_element_type=jnp.float32)
        .astype(jnp.bfloat16)
        .reshape(seq_count, EXP_DEV, capacity, D)
    )
    arrived_rows, arrived_grads = (
        lax.all_to_all(sent_rows, "seq", split_axis=0, concat_axis=0, tiled=True),
        lax.all_to_all(sent_grads, "seq", split_axis=0, concat_axis=0, tiled=True),
    )
    rows_all, grads_all = (
        lax.all_gather(arrived_rows, "batch", axis=0, tiled=True),
        lax.all_gather(arrived_grads, "batch", axis=0, tiled=True),
    )
    pre_act = (
        jnp.einsum("recd,edf->recf", rows_all, w_in_exp, preferred_element_type=jnp.float32)
        + b_in_exp[None, :, None, :]
    )
    hidden_f, gelu_back = jax.vjp(gelu_exact, pre_act)
    hidden_b = hidden_f.astype(jnp.bfloat16)
    dhidden = jnp.einsum(
        "recd,efd->recf", grads_all, w_out_exp, preferred_element_type=jnp.float32
    ).astype(jnp.bfloat16)
    dpre = gelu_back(dhidden.astype(jnp.float32))[0].astype(jnp.bfloat16)
    grad_w_out_exp = jnp.einsum(
        "recf,recd->efd", hidden_b, grads_all, preferred_element_type=jnp.float32
    )
    grad_b_out_exp = jnp.sum(grads_all, axis=(0, 2), dtype=jnp.float32)
    grad_w_in_exp = jnp.einsum("recd,recf->edf", rows_all, dpre, preferred_element_type=jnp.float32)
    grad_b_in_exp = jnp.sum(dpre, axis=(0, 2), dtype=jnp.float32)
    drows = jnp.einsum("recf,edf->recd", dpre, w_in_exp, preferred_element_type=jnp.float32)
    drows_sum = lax.psum_scatter(
        drows.astype(jnp.bfloat16), "batch", scatter_dimension=0, tiled=True
    )
    drows_home = lax.all_to_all(drows_sum, "seq", split_axis=0, concat_axis=0, tiled=True)
    second_residual_gradient = jnp.einsum(
        "st,sd->td",
        dispatch,
        drows_home.reshape(experts_all * capacity, D),
        preferred_element_type=jnp.float32,
    )
    second_norm_gradient, second_gain_gradient, second_shift_gradient = norm_backward_pass(
        second_residual_gradient, second_centred_scaled, second_inverse_deviation, norm_gain_pair[1]
    )
    d_one = dout + second_norm_gradient
    d_one_b = d_one.astype(jnp.bfloat16)
    grad_w_out = jnp.einsum("td,te->de", attended_b, d_one_b, preferred_element_type=jnp.float32)
    grad_out_bias = jnp.sum(d_one, axis=0)
    dout_b = jnp.einsum("te,de->td", d_one_b, w_out, preferred_element_type=jnp.float32).astype(
        jnp.bfloat16
    )
    dout_h = dout_b.reshape(tok_rows, HEADS, HEAD_DIM)
    delta = jnp.einsum("thd,thd->ht", dout_h.astype(jnp.float32), attended)
    dquery = run_keys(dquery_step, head_zeros)
    lse_rows = log_mass.T
    delta_rows = delta.T
    block_rows = math.gcd(tok_rows * lax.axis_size("seq"), 512)

    def one_block(block_index):
        first_key = block_index * block_rows
        block_kv = lax.dynamic_slice_in_dim(all_kv, first_key, block_rows, 0)
        block_pad = lax.dynamic_slice_in_dim(all_pad, first_key, block_rows, 0)
        k_pos = first_key + jnp.arange(block_rows, dtype=jnp.int32)
        grad_k, grad_v = key_grads(
            query_h,
            dout_h,
            lse_rows,
            delta_rows,
            q_pos,
            q_doc,
            block_kv[:, :D].reshape(block_rows, HEADS, HEAD_DIM),
            block_kv[:, D:].reshape(block_rows, HEADS, HEAD_DIM),
            k_pos,
            doc_of(k_pos, doc_ends),
            block_pad,
        )
        return jnp.concatenate(
            [grad_k.reshape(block_rows, D), grad_v.reshape(block_rows, D)], axis=1
        )

    blocks = lax.map(
        one_block, jnp.arange(tok_rows * lax.axis_size("seq") // block_rows, dtype=jnp.int32)
    )
    key_terms = lax.psum_scatter(
        blocks.reshape(tok_rows * lax.axis_size("seq"), 2 * D).astype(jnp.bfloat16),
        "seq",
        scatter_dimension=0,
        tiled=True,
    )
    dq_b = dquery.reshape(tok_rows, D).astype(jnp.bfloat16)
    dmixed = jnp.concatenate([dq_b * scale, key_terms], axis=1)
    grad_w_qkv = jnp.einsum("td,te->de", h_one, dmixed, preferred_element_type=jnp.float32)
    first_hidden_gradient = jnp.einsum(
        "te,de->td", dmixed, w_qkv, preferred_element_type=jnp.float32
    )
    first_norm_gradient, first_gain_gradient, first_shift_gradient = norm_backward_pass(
        first_hidden_gradient, first_centred_scaled, first_inverse_deviation, norm_gain_pair[0]
    )
    input_grad = (d_one + first_norm_gradient).astype(jnp.bfloat16)
    grad_q_bias = jnp.sum(dmixed[:, :D], axis=0, dtype=jnp.float32)
    grad_v_bias = jnp.sum(key_terms[:, D:], axis=0, dtype=jnp.float32)
    small_grads = jnp.stack(
        [
            first_gain_gradient,
            second_gain_gradient,
            first_shift_gradient,
            second_shift_gradient,
            grad_q_bias,
            grad_v_bias,
            grad_out_bias,
        ]
    )
    shared_qkv, shared_out, shared_small = (
        lax.psum_scatter(grad_w_qkv, ("seq", "batch"), scatter_dimension=0, tiled=True),
        lax.psum_scatter(grad_w_out, ("seq", "batch"), scatter_dimension=0, tiled=True),
        lax.psum_scatter(small_grads, ("seq", "batch"), scatter_dimension=1, tiled=True),
    )
    return (
        output[None],
        input_grad[None],
        shared_small[0:2],
        shared_small[2:4],
        shared_qkv,
        shared_small[4:6],
        shared_out,
        shared_small[6],
        grad_w_in_exp,
        grad_b_in_exp,
        grad_w_out_exp,
        grad_b_out_exp,
    )


MICROSECOND = 1 << 30


def cost(us):
    return pl.CostEstimate(flops=us * MICROSECOND, bytes_accessed=1 << 20, transcendentals=0)


MICROSECOND = 1 << 30


def cost(us):
    return pl.CostEstimate(flops=us * MICROSECOND, bytes_accessed=1 << 20, transcendentals=0)


SMALL = pl.CostEstimate(flops=1, bytes_accessed=1, transcendentals=0)
HALVES = [slice(h * HEAD_DIM, (h + 1) * HEAD_DIM) for h in range(2)]


def block_rows(i, T):
    return pl.ds(pl.multiple_of(i * T, T), T)


def diag_parts(T, key_rows):
    lane = iota((T, 256), 1)
    values = key_rows.astype(F32)
    unpadded = jnp.where(lane == 136, 0.0, values).astype(BF16)
    k_at, q_at = iota((T, T), 0), iota((T, T), 1)
    padded = values[:, 136:137] > 0.5
    allowed = ((k_at < q_at) & jnp.logical_not(padded)) | (k_at == q_at)
    return unpadded, allowed


def ring_kernel(n, T, cap, block, parts, at_tile, diags, pairs, first, last, extra, sc, *refs):
    refs = list(refs)

    def take(count):
        got = refs[:count]
        del refs[:count]
        return got

    count = len(parts)
    chunks = [take(p) for p in parts]
    wq, wk, wv, qvb, gain, bias, docs = take(7)
    old = [] if first else take(9)
    take(extra)
    outs = take(9)
    results = take(EXP_DEV + 2) if last else None
    h_out, sel_out, qa_out, ka_out, vt_out, code_out = outs[:6]
    h_s, sel_s, qa, ka, vt, code, top, mass, acc, w, in_sems, out_sems = take(12)
    me = sc[n]
    loads = [
        pltpu.make_async_copy(ref, to, in_sems.at[i])
        for i, (ref, to) in enumerate(zip(old[2:], (qa, ka, vt, code, top, mass, acc)))
    ]
    for load in loads:
        load.start()
    w[:, 0:128] = wq[...]
    w[:, 128:256] = wk[...]
    w[:, 256:384] = wv[...]
    payloads = []
    for c in range(count):
        rows = [ref[...] for ref in chunks[c]]
        rows = rows[0] if len(rows) == 1 else jnp.concatenate(rows, axis=0)
        payloads.append(rows)
        vhat, _ = normed_rows(rows[0:T].astype(F32))
        h_s[c] = (vhat * gain[...] + bias[...]).astype(BF16)
    for load in loads:
        load.wait()
    stores = []

    def send(ref, to):
        store = pltpu.make_async_copy(ref, to, out_sems.at[len(stores)])
        store.start()
        stores.append(store)

    for c in range(count):
        src = sc[block + c]
        rows = block_rows(src, T)
        mixed = dot_nn(h_s[c], w[...])
        q = ((mixed[:, 0:128] + qvb[0:1, :]) * (HEAD_DIM**-0.5)).astype(BF16).astype(F32)
        v = (mixed[:, 256:384] + qvb[1:2, :]).astype(BF16)
        codes = payloads[c][T : T + 16].astype(F32)
        id_row = codes[0:1, 0:T]
        pad_row = codes[0:1, T : 2 * T]
        id_col = jnp.transpose(jnp.broadcast_to(id_row, (128, T)))
        pad_col = jnp.transpose(jnp.broadcast_to(pad_row, (128, T)))
        same = jnp.where(
            (id_col[:, 0:1] == id_row) & (iota((T, T), 0) < iota((T, T), 1)), 1.0, 0.0
        )
        rank_row = jnp.sum(same, axis=0, keepdims=True)
        rank_col = jnp.transpose(jnp.broadcast_to(rank_row, (128, T)))
        lane = iota((T, 128), 1)
        pos = (iota((T, 128), 0) + src * T).astype(F32)
        doc = jnp.where((pos >= docs[0:1, :]) & (pos < docs[1:2, :]), 1.0, 0.0)
        aug = jnp.where(lane < 8, doc, 0.0)
        aug = jnp.where(lane == 8, 1.0 - pad_col, aug)
        aug = jnp.where(lane == 16, id_col, aug)
        aug = jnp.where(lane == 17, rank_col, aug)
        masked = jnp.where(lane < 8, (doc - 1.0) * BIG, jnp.where(lane == 8, -BIG, 0.0)).astype(BF16)
        for h in range(2):
            mine = (lane < HEAD_DIM) == (h == 0)
            qa[h, rows, 0:128] = jnp.where(mine, q, 0.0).astype(BF16)
            qa[h, rows, 128:256] = masked
        ka[rows, 0:128] = mixed[:, 128:256].astype(BF16)
        ka[rows, 128:256] = aug.astype(BF16)
        ka[rows, 256:384] = v
        vt[src] = jnp.transpose(v.astype(F32)).astype(BF16)
        slot = (id_row * cap + rank_row).astype(jnp.int32)
        half = lax.rem(src, 2) * cap
        code[src] = (id_row * (2 * cap) + rank_row).astype(jnp.int32) + half
        pick = jnp.where(
            slot == iota((EXP_DEV * cap, T), 0) + me * (EXP_DEV * cap), 1.0, 0.0
        ).astype(BF16)
        chosen = dot_nn(pick, payloads[c][0:T])
        for e in range(EXP_DEV):
            sel_s[c, e] = chosen[e * cap : (e + 1) * cap]
            send(sel_s.at[c, e], sel_out.at[e, src])
        send(h_s.at[c], h_out.at[src])
        for h in range(2):
            send(qa.at[h, rows], qa_out.at[h, rows])
        send(ka.at[rows], ka_out.at[rows])
        if not last:
            send(vt.at[src], vt_out.at[src])
            send(code.at[src], code_out.at[src])

    def one_diag(r, carry):
        i = sc[at_tile + 2 * r]
        rows = block_rows(i, T)
        kd, allowed = diag_parts(T, ka[rows, 0:256])
        for h in range(2):
            s = jnp.where(allowed, dot_nt(kd, qa[h, rows, :]), NEG)
            best = jnp.max(s, axis=0, keepdims=True)
            p = jnp.exp(s - best)
            top[h, i] = best
            mass[h, i] = jnp.sum(p, axis=0, keepdims=True)
            acc[i, HALVES[h], :] = dot_nn(vt[i, HALVES[h], :], p.astype(BF16))
        return carry

    lax.fori_loop(0, diags, one_diag, 0)

    def pair_tile(at):
        i, j = sc[at_tile + 2 * at], sc[at_tile + 2 * at + 1]
        rows, cols = block_rows(i, T), block_rows(j, T)
        old_top = [top[h, i] for h in range(2)]
        old_mass = [mass[h, i] for h in range(2)]
        old_acc = [acc[i, HALVES[h], :] for h in range(2)]
        s = [dot_nt(ka[cols, 0:256], qa[h, rows, :]) for h in range(2)]
        best = [jnp.maximum(old_top[h], jnp.max(s[h], axis=0, keepdims=True)) for h in range(2)]
        p = [jnp.exp(s[h] - best[h]) for h in range(2)]
        more = [dot_nn(vt[j, HALVES[h], :], p[h].astype(BF16)) for h in range(2)]
        for h in range(2):
            fade = jnp.exp(old_top[h] - best[h])
            top[h, i] = best[h]
            mass[h, i] = old_mass[h] * fade + jnp.sum(p[h], axis=0, keepdims=True)
            acc[i, HALVES[h], :] = old_acc[h] * fade + more[h]

    def two_pairs(r, carry):
        pair_tile(diags + 2 * r)
        pair_tile(diags + 2 * r + 1)
        return carry

    lax.fori_loop(0, pairs // 2, two_pairs, 0)
    if pairs % 2:
        pair_tile(diags + pairs - 1)
    if not last:
        for ref, to in zip((top, mass, acc), outs[6:]):
            send(ref, to)
    else:
        *att_out, o_out, lse_out = results

        def finish(i, carry):
            rows = block_rows(i, T)
            scaled = []
            for h in range(2):
                lse_out[h, i] = top[h, i] + jnp.log(mass[h, i])
                scaled.append(acc[i, HALVES[h], :] / mass[h, i])
            o_out[rows, :] = jnp.transpose(jnp.concatenate(scaled, axis=0))
            return carry

        lax.fori_loop(0, n, finish, 0)
        slots = n * EXP_DEV * 2 * cap

        def pair(p, carry):
            codes = jnp.concatenate([code[2 * p], code[2 * p + 1]], axis=1)
            pick = jnp.where(codes == iota((slots, 2 * T), 0), 1.0, 0.0).astype(BF16)
            chosen = dot_nn(pick, o_out[block_rows(p, 2 * T), :].astype(BF16)).astype(BF16)
            for k in range(n):
                for e in range(EXP_DEV):
                    at = (k * EXP_DEV + e) * 2 * cap
                    to = pl.multiple_of(p * 2 * cap, 16)
                    att_out[e][k, pl.ds(to, 2 * cap), :] = chosen[at : at + 2 * cap]
            return carry

        lax.fori_loop(0, n // 2, pair, 0)
    for store in stores:
        store.wait()


def ring_call(
    n, T, cap, block, at_tile, diags, pairs, sc, chunks, held, last, w_qkv, qv_bias, gain, bias, docs, after
):
    row = n * T
    shapes = [
        ((n, T, D), BF16),
        ((EXP_DEV, n, cap, D), F32),
        ((2, row, 256), BF16),
        ((row, 384), BF16),
        ((n, 128, T), BF16),
        ((n, 1, T), jnp.int32),
        ((2, n, 1, T), F32),
        ((2, n, 1, T), F32),
        ((n, 128, T), F32),
    ]
    anywhere = pl.BlockSpec(memory_space=pl.ANY)
    operands = [part for chunk in chunks for part in chunk]
    in_specs = [whole(part.shape) for part in operands] + [
        pl.BlockSpec((D, 128), lambda i, sc: (0, sc[n])),
        pl.BlockSpec((D, 128), lambda i, sc: (0, n + sc[n])),
        pl.BlockSpec((D, 128), lambda i, sc: (0, 2 * n + sc[n])),
        pl.BlockSpec((2, 128), lambda i, sc: (0, sc[n])),
        whole((1, D)),
        whole((1, D)),
        whole((2, 128)),
    ]
    aliases = {}
    first = held is None
    if not first:
        aliases = {1 + len(in_specs) + i: i for i in range(len(shapes))}
        in_specs = in_specs + [anywhere] * len(shapes)
    in_specs = in_specs + [anywhere] * len(after)
    out_specs = [anywhere] * len(shapes)
    results = []
    if last:
        results = [((n, n * cap, 128), BF16)] * EXP_DEV
        results = results + [((row, 128), F32), ((2, n, 1, T), F32)]
        out_specs = out_specs + [whole(s) for s, _ in results]
    count = len(chunks)
    parts = [len(chunk) for chunk in chunks]
    return pl.pallas_call(
        lambda *a: ring_kernel(
            n, T, cap, block, parts, at_tile, diags, pairs, first, last, len(after), *a
        ),
        grid_spec=pltpu.PrefetchScalarGridSpec(
            num_scalar_prefetch=1,
            grid=(1,),
            in_specs=in_specs,
            out_specs=out_specs,
            scratch_shapes=[
                pltpu.VMEM((count, T, D), BF16),
                pltpu.VMEM((count, EXP_DEV, cap, D), F32),
            ]
            + [pltpu.VMEM(s, t) for s, t in shapes[2:]]
            + [
                pltpu.VMEM((D, 384), BF16),
                pltpu.SemaphoreType.DMA((7,)),
                pltpu.SemaphoreType.DMA((8 * count + 3,)),
            ],
        ),
        out_shape=[jax.ShapeDtypeStruct(s, t) for s, t in shapes + results],
        input_output_aliases=aliases,
        compiler_params=params(),
        cost_estimate=cost(10),
        name="ring_step",
    )(sc, *operands, w_qkv, w_qkv, w_qkv, qv_bias, gain, bias, docs, *(held or ()), *after)


def attn_bwd_kernel(
    n, T, cap, at_tile, diags, pairs, tiles, qa, ka, lse, o_ref, *refs
):
    datt = refs[:EXP_DEV]
    dm_out, do, delta, kh, dqa, dka, dva = refs[-7:]
    slots = n * EXP_DEV * 2 * cap

    def pair(p, carry):
        rows = block_rows(p, 2 * T)
        feature = ka[rows, 128:256].astype(F32)
        half = jnp.where(iota((2 * T, 1), 0) >= T, float(cap), 0.0)
        code = (feature[:, 16:17] * (2 * cap) + feature[:, 17:18] + half).astype(jnp.int32)
        pick = jnp.where(code == iota((2 * T, slots), 1), 1.0, 0.0).astype(BF16)
        parts = []
        for k in range(n):
            for e in range(EXP_DEV):
                at = pl.multiple_of(p * 2 * cap, 16)
                parts.append(datt[e][k, pl.ds(at, 2 * cap), :])
        got = dot_nn(pick, jnp.concatenate(parts, axis=0))
        lane = iota((2 * T, 128), 1)
        keys = ka[rows, 0:128].astype(F32)
        for h in range(2):
            mine = (lane < HEAD_DIM) == (h == 0)
            do[h, rows, :] = jnp.where(mine, got, 0.0).astype(BF16)
            kh[h, rows, :] = jnp.where(mine, keys, 0.0).astype(BF16)
        prod = jnp.transpose(got * o_ref[rows, :])
        for h in range(2):
            total = jnp.sum(prod[HALVES[h], :], axis=0, keepdims=True)
            delta[h, 2 * p] = total[:, 0:T]
            delta[h, 2 * p + 1] = total[:, T : 2 * T]
        return carry

    lax.fori_loop(0, n // 2, pair, 0)

    def tile(i, j, key_rows, mask):
        rows, cols = block_rows(i, T), block_rows(j, T)
        ps, dss = [], []
        for h in range(2):
            s = dot_nt(key_rows, qa[h, rows, :])
            dp = dot_nt(ka[cols, 256:384], do[h, rows, :])
            if mask is not None:
                s = jnp.where(mask, s, NEG)
            p = jnp.exp(s - lse[h, i])
            dss.append((p * (dp - delta[h, i])).astype(BF16))
            ps.append(p.astype(BF16))
        dv = dot_nn(
            jnp.concatenate(ps, axis=1), jnp.concatenate([do[0, rows, :], do[1, rows, :]], axis=0)
        )
        dk = dot_nn(
            jnp.concatenate(dss, axis=1),
            jnp.concatenate([qa[0, rows, 0:128], qa[1, rows, 0:128]], axis=0),
        )
        dq = dot_tn(
            jnp.concatenate(dss, axis=0), jnp.concatenate([kh[0, cols, :], kh[1, cols, :]], axis=0)
        )
        return dq, dk, dv

    def diag_tile(j, carry):
        kd, allowed = diag_parts(T, ka[block_rows(j, T), 0:256])
        dqa[j], dka[j], dva[j] = tile(j, j, kd, allowed)
        return carry

    lax.fori_loop(0, n, diag_tile, 0)

    def pair_tile(at):
        i, j = tiles[at_tile + 2 * at], tiles[at_tile + 2 * at + 1]
        dq, dk, dv = tile(i, j, ka[block_rows(j, T), 0:256], None)
        dqa[i] += dq
        dka[j] += dk
        dva[j] += dv

    width = next(w for w in (4, 2, 1) if pairs % w == 0)

    def some_pairs(r, carry):
        for w in range(width):
            pair_tile(diags + width * r + w)
        return carry

    lax.fori_loop(0, pairs // width, some_pairs, 0)

    def finish(i, carry):
        dq = dqa[i].astype(BF16).astype(F32)
        dm_out[i, :, 0:128] = (dq * (HEAD_DIM**-0.5)).astype(BF16)
        dm_out[i, :, 128:256] = dka[i].astype(BF16)
        dm_out[i, :, 256:384] = dva[i].astype(BF16)
        return carry

    lax.fori_loop(0, n, finish, 0)


def attn_bwd_call(n, T, cap, at_tile, diags, pairs, tiles, qa, ka, lse, o, datt, after):
    row = n * T
    vmem = pl.BlockSpec(memory_space=pltpu.VMEM)
    return pl.pallas_call(
        lambda *a: attn_bwd_kernel(n, T, cap, at_tile, diags, pairs, *a),
        out_shape=jax.ShapeDtypeStruct((n, T, 384), BF16),
        in_specs=[pl.BlockSpec(memory_space=pltpu.SMEM)]
        + [vmem] * (4 + EXP_DEV)
        + [pl.BlockSpec(memory_space=pl.ANY)] * len(after),
        out_specs=vmem,
        scratch_shapes=[
            pltpu.VMEM((2, row, 128), BF16),
            pltpu.VMEM((2, n, 1, T), F32),
            pltpu.VMEM((2, row, 128), BF16),
            pltpu.VMEM((n, T, 128), F32),
            pltpu.VMEM((n, T, 128), F32),
            pltpu.VMEM((n, T, 128), F32),
        ],
        compiler_params=params(),
        cost_estimate=cost(28),
        name="attn_bwd",
    )(tiles, qa, ka, lse, o, *datt, *after)


def dispatch_kernel(cap, slots, ids, grads, *refs):
    out = refs[-1]
    id_row = ids[...].astype(F32)
    T = id_row.shape[1]
    id_col = jnp.transpose(jnp.broadcast_to(id_row, (128, T)))[:, 0:1]
    same = jnp.where((id_col == id_row) & (iota((T, T), 0) < iota((T, T), 1)), 1.0, 0.0)
    rank = jnp.sum(same, axis=0, keepdims=True)
    slot = (id_row * cap + rank).astype(jnp.int32)
    pick = jnp.where(slot == iota((slots, T), 0), 1.0, 0.0).astype(BF16)
    out[...] = dot_nn(pick, grads[...]).astype(BF16)


def dispatch_call(cap, slots, after, ids, grads):
    vmem = pl.BlockSpec(memory_space=pltpu.VMEM)
    return pl.pallas_call(
        lambda *a: dispatch_kernel(cap, slots, *a),
        out_shape=jax.ShapeDtypeStruct((slots, D), BF16),
        in_specs=[vmem, vmem] + [pl.BlockSpec(memory_space=pl.ANY)] * len(after),
        out_specs=vmem,
        compiler_params=params(),
        cost_estimate=cost(3),
        name="dispatch",
    )(ids, grads, *after)


def owner_fwd_kernel(n, att_in, w_out, sel, out_bias, gain, bias, x_two, x_one, att_b):
    for k in range(n):
        att_b[:, k * 128 : (k + 1) * 128] = att_in[k]
    branch = dot_nn(att_b[...], w_out[...]) + out_bias[...]
    x = sel[...] + branch
    x_one[...] = x
    vhat, _ = normed_rows(x)
    x_two[...] = (vhat * gain[...] + bias[...]).astype(BF16)


def owner_fwd_call(n, e, att_in, w_out, sel, out_bias, gain, bias):
    slots = sel.shape[0] // EXP_DEV
    rows = pl.BlockSpec((slots, D), lambda i: (e, 0))
    mine = whole((slots, D))
    return pl.pallas_call(
        lambda *a: owner_fwd_kernel(n, *a),
        grid=(1,),
        in_specs=[
            whole((n, slots, 128)),
            whole((D, D)),
            rows,
            whole((1, D)),
            whole((1, D)),
            whole((1, D)),
        ],
        out_specs=[mine, mine, mine],
        out_shape=[
            jax.ShapeDtypeStruct((slots, D), BF16),
            jax.ShapeDtypeStruct((slots, D), F32),
            jax.ShapeDtypeStruct((slots, D), BF16),
        ],
        compiler_params=params(),
        cost_estimate=cost(3),
        name="owner_fwd",
    )(att_in, w_out, sel, out_bias, gain, bias)


def owner_bwd_kernel(n, part_a, part_b, x_one, og, gain, w_out, *refs):
    datt, d_one_b, small = refs[-3:]
    u = (part_a[...].astype(F32) + part_b[...].astype(F32)).astype(BF16).astype(F32)
    vhat, inv_std = normed_rows(x_one[...])
    scaled = u * gain[...]
    first = jnp.mean(scaled, axis=-1, keepdims=True)
    second = jnp.mean(scaled * vhat, axis=-1, keepdims=True)
    d_one = og[...].astype(F32) + inv_std * (scaled - first - vhat * second)
    d_b = d_one.astype(BF16)
    d_one_b[...] = d_b
    back = dot_nt(d_b, w_out[...]).astype(BF16)
    for k in range(n):
        datt[k] = back[:, k * 128 : (k + 1) * 128]
    small[0:1, :] = jnp.sum(u * vhat, axis=0, keepdims=True)
    small[1:2, :] = jnp.sum(u, axis=0, keepdims=True)
    small[2:3, :] = jnp.sum(d_one, axis=0, keepdims=True)


def owner_bwd_call(n, e, part_a, part_b, x_one, og, gain, w_out, after):
    slots = x_one.shape[0]
    mine = whole((slots, D))
    in_specs = [
        mine,
        mine,
        mine,
        pl.BlockSpec((slots, D), lambda i: (e, 0)),
        whole((1, D)),
        whole((D, D)),
    ]
    return pl.pallas_call(
        lambda *a: owner_bwd_kernel(n, *a),
        grid=(1,),
        in_specs=in_specs + [pl.BlockSpec(memory_space=pl.ANY)] * len(after),
        out_specs=[
            whole((n, slots, 128)),
            mine,
            whole((8, D)),
        ],
        out_shape=[
            jax.ShapeDtypeStruct((n, slots, 128), BF16),
            jax.ShapeDtypeStruct((slots, D), BF16),
            jax.ShapeDtypeStruct((8, D), F32),
        ],
        compiler_params=params(),
        cost_estimate=cost(4),
        name="owner_bwd",
    )(part_a, part_b, x_one, og, gain, w_out, *after)


def gelu_parts(u):
    cdf = 0.5 * (1.0 + lax.erf(u * (0.5**0.5)))
    return cdf, cdf + u * jnp.exp(-0.5 * u * u) * ((2.0 * math.pi) ** -0.5)


ROW_ORDER = (1, 3, 0, 2)


def expert_kernel(e, nb, rows, ff, width, extra, *refs):
    x_parts, g_parts = refs[:nb], refs[nb : 2 * nb]
    w_in, b_in, w_out = refs[2 * nb : 2 * nb + 3]
    hidden_out, dpre_out, keep, send, grad_b = refs[2 * nb + 3 + extra : 2 * nb + 8 + extra]
    xs, gs, w1, w2, hidden, dpre, part, sems = refs[2 * nb + 8 + extra :]
    copies = []

    def copy(ref, to):
        made = pltpu.make_async_copy(ref, to, sems.at[len(copies)])
        made.start()
        copies.append(made)

    for at, k in enumerate(ROW_ORDER):
        copy(x_parts[k], xs.at[pl.ds(at * rows, rows)])
    copy(w_in.at[e], w1)
    for at, k in enumerate(ROW_ORDER):
        copy(g_parts[k].at[pl.ds(e * rows, rows)], gs.at[pl.ds(at * rows, rows)])
    copy(w_out.at[e], w2)
    for c in copies[: nb + 1]:
        c.wait()
    ready = len(copies)
    for f in range(ff // width):
        cols = slice(f * width, (f + 1) * width)
        pre = dot_nn(xs[...], w1[:, cols]) + b_in[e : e + 1, cols]
        if f == 0:
            for c in copies[nb + 1 : ready]:
                c.wait()
        dhidden = dot_nt(gs[...], w2[cols, :]).astype(BF16).astype(F32)
        cdf, slope = gelu_parts(pre)
        hidden[:, cols] = (pre * cdf).astype(BF16)
        value = (dhidden * slope).astype(BF16)
        dpre[:, cols] = value
        grad_b[0, :, cols] = jnp.sum(value.astype(F32), axis=0, keepdims=True)
    copy(hidden, hidden_out)
    copy(dpre, dpre_out)
    for half, to in enumerate((send, keep)):
        at = slice(2 * half * rows, 2 * (half + 1) * rows)
        value = dot_nt(dpre[at, :], w1[...]).astype(BF16)
        for y in range(2):
            part[2 * half + y] = value[y * rows : (y + 1) * rows]
            copy(part.at[2 * half + y], to.at[y])
    for c in copies[ready:]:
        c.wait()


def expert_call(e, sc, x_parts, g_parts, w_in, b_in, w_out, after):
    del sc
    nb = len(x_parts)
    rows = x_parts[0].shape[0]
    ff = w_in.shape[2]
    anywhere = pl.BlockSpec(memory_space=pl.ANY)
    return pl.pallas_call(
        lambda *a: expert_kernel(e, nb, rows, ff, min(256, ff), len(after), *a),
        in_specs=[anywhere] * (2 * nb + 1)
        + [pl.BlockSpec(memory_space=pltpu.VMEM), anywhere]
        + [anywhere] * len(after),
        out_specs=[anywhere] * 4 + [pl.BlockSpec(memory_space=pltpu.VMEM)],
        scratch_shapes=[
            pltpu.VMEM((nb * rows, D), BF16),
            pltpu.VMEM((nb * rows, D), BF16),
            pltpu.VMEM((D, ff), BF16),
            pltpu.VMEM((ff, D), BF16),
            pltpu.VMEM((nb * rows, ff), BF16),
            pltpu.VMEM((nb * rows, ff), BF16),
            pltpu.VMEM((nb, rows, D), BF16),
            pltpu.SemaphoreType.DMA((3 * nb + 4,)),
        ],
        out_shape=[
            jax.ShapeDtypeStruct((nb * rows, ff), BF16),
            jax.ShapeDtypeStruct((nb * rows, ff), BF16),
            jax.ShapeDtypeStruct((2, rows, D), BF16),
            jax.ShapeDtypeStruct((2, rows, D), BF16),
            jax.ShapeDtypeStruct((1, 1, ff), F32),
        ],
        compiler_params=params(),
        cost_estimate=cost(10),
        name="expert_main",
    )(*x_parts, *g_parts, w_in, b_in, w_out, *after)


def expert_out_kernel(rows, hidden, w_out, *refs):
    keep, send = refs[-2:]
    total = dot_nn(hidden[...], w_out[0]).astype(BF16)
    for y in range(2):
        send[y] = total[y * rows : (y + 1) * rows, :]
        keep[y] = total[(2 + y) * rows : (3 + y) * rows, :]


def expert_out_call(nb, e, hidden, w_out, after):
    rows = hidden.shape[0] // nb
    ff = hidden.shape[1]
    return pl.pallas_call(
        lambda *a: expert_out_kernel(rows, *a),
        grid=(1,),
        in_specs=[whole(hidden.shape), pl.BlockSpec((1, ff, D), lambda i: (e, 0, 0))]
        + [pl.BlockSpec(memory_space=pl.ANY)] * len(after),
        out_specs=[whole((2, rows, D))] * 2,
        out_shape=[jax.ShapeDtypeStruct((2, rows, D), BF16)] * 2,
        compiler_params=params(),
        cost_estimate=cost(4),
        name="expert_out",
    )(hidden, w_out, *after)


def expert_grad_kernel(nb, rows, sc, *refs):
    x_parts, g_parts = refs[:nb], refs[nb : 2 * nb]
    hidden, dpre = refs[2 * nb : 2 * nb + 2]
    grad_in, grad_out, grad_b, xs, gs = refs[-5:]

    @pl.when(pl.program_id(0) == 0)
    def _():
        sums = []
        for at, k in enumerate(ROW_ORDER):
            xs[at * rows : (at + 1) * rows, :] = x_parts[k][...]
            gs[at * rows : (at + 1) * rows, :] = g_parts[k][...]
        for k in range(nb):
            sums.append(jnp.sum(g_parts[k][...].astype(F32), axis=0, keepdims=True))
        grad_b[0] = (sums[0] + sums[1]) + (sums[2] + sums[3])

    grad_in[0] = dot_tn(xs[...], dpre[...])
    grad_out[0] = dot_tn(hidden[...], gs[...])


def expert_grad_call(e, sc, x_parts, g_parts, hidden, dpre, held, after):
    nb = len(x_parts)
    rows = x_parts[0].shape[0]
    ff = hidden.shape[1]
    width = min(256, ff)
    g_specs = [pl.BlockSpec((rows, D), lambda f, sc: (e, 0))] * nb
    act = pl.BlockSpec((nb * rows, width), lambda f, sc: (0, f))
    in_specs = [whole((rows, D))] * nb + g_specs + [act, act]
    more = [] if held is None else list(held)
    aliases = {1 + len(in_specs) + i: i for i in range(len(more))}
    more += after
    return pl.pallas_call(
        lambda *a: expert_grad_kernel(nb, rows, *a),
        grid_spec=pltpu.PrefetchScalarGridSpec(
            num_scalar_prefetch=1,
            grid=(ff // width,),
            in_specs=in_specs + [pl.BlockSpec(memory_space=pl.ANY)] * len(more),
            out_specs=[
                pl.BlockSpec((1, D, width), lambda f, sc: (e, 0, f)),
                pl.BlockSpec((1, width, D), lambda f, sc: (e, f, 0)),
                pl.BlockSpec((1, 1, D), lambda f, sc: (e, 0, 0)),
            ],
            scratch_shapes=[pltpu.VMEM((nb * rows, D), BF16)] * 2,
        ),
        out_shape=[
            jax.ShapeDtypeStruct((EXP_DEV, D, ff), F32),
            jax.ShapeDtypeStruct((EXP_DEV, ff, D), F32),
            jax.ShapeDtypeStruct((EXP_DEV, 1, D), F32),
        ],
        input_output_aliases=aliases,
        compiler_params=params(),
        cost_estimate=SMALL,
        name="expert_grads",
    )(sc, *x_parts, *g_parts, hidden, dpre, *more)


def w_out_grad_kernel(n, nb, sc, *refs):
    keep, send = refs[-2:]
    total = dot_tn(refs[0][...], refs[EXP_DEV][...])
    for e in range(1, EXP_DEV):
        total = total + dot_tn(refs[e][...], refs[EXP_DEV + e][...])
    size = D // (n * nb)
    core = lax.rem(sc[n + 1], 2)
    chip = lax.div(sc[n + 1], 2)
    for r in range(n):
        for y in range(nb // 2):
            first = (r * nb + 2 * y) * size
            place = y ^ chip
            for g in range(-(-D // 384)):
                cols = slice(g * 384, min(D, (g + 1) * 384))
                width = cols.stop - cols.start
                pair = [total[first + c * size : first + (c + 1) * size, cols] for c in range(2)]
                rows = slice(g * size, (g + 1) * size)
                keep[place, r, rows, 0:width] = jnp.where(core == 0, pair[0], pair[1]).astype(BF16)
                send[place, r, rows, 0:width] = jnp.where(core == 0, pair[1], pair[0]).astype(BF16)
                if width < 384:
                    keep[place, r, rows, width:384] = jnp.zeros((size, 384 - width), BF16)
                    send[place, r, rows, width:384] = jnp.zeros((size, 384 - width), BF16)


def w_out_grad_call(n, nb, sc, att_b, d_one_b, after):
    size = D // (n * nb)
    shape = (nb // 2, n, -(-D // 384) * size, 384)
    return pl.pallas_call(
        lambda *a: w_out_grad_kernel(n, nb, *a[: 1 + 2 * EXP_DEV], *a[-2:]),
        grid_spec=pltpu.PrefetchScalarGridSpec(
            num_scalar_prefetch=1,
            grid=(1,),
            in_specs=[whole(att_b[0].shape)] * (2 * EXP_DEV)
            + [pl.BlockSpec(memory_space=pl.ANY)] * len(after),
            out_specs=[whole(shape)] * 2,
        ),
        out_shape=[jax.ShapeDtypeStruct(shape, BF16)] * 2,
        compiler_params=params(),
        cost_estimate=cost(4),
        name="w_out_grad",
    )(sc, *att_b, *d_one_b, *after)


def qkv_grad_kernel(n, nb, T, sc, h, dm, aux, after, keep, send, total):
    me_b = sc[n + 1]

    def add(c, carry):
        total[...] += dot_tn(dm[c], h[c])
        return carry

    total[...] = jnp.zeros_like(total)
    lax.fori_loop(0, n, add, 0)
    col_sum = jnp.zeros((1, 384), F32)
    for r in range(n):
        col_sum = col_sum + jnp.sum(dm[r].astype(F32), axis=0, keepdims=True)
    width = D // n
    size = width // nb
    top = iota((16, 384), 0)
    for r in range(n):
        part = jnp.transpose(total[:, r * width : (r + 1) * width])
        for k in range(nb):
            bb = me_b ^ k
            rows = jnp.zeros((size, 384), F32)
            for c in range(nb):
                rows = jnp.where(bb == c, part[c * size : (c + 1) * size, :], rows)
            extra = jnp.where(
                top == 0, col_sum, jnp.where(top == 1, aux[r * nb + bb], 0.0)
            )
            to = keep if k % 2 == 0 else send
            to[k // 2, r, 0:size, :] = rows.astype(BF16)
            to[k // 2, r, size : size + 16, :] = extra.astype(BF16)


def qkv_grad_call(n, nb, T, sc, h, dm, aux, after):
    size = D // (n * nb)
    shape = (2, n, size + 16, 384)
    return pl.pallas_call(
        lambda *a: qkv_grad_kernel(n, nb, T, *a),
        grid_spec=pltpu.PrefetchScalarGridSpec(
            num_scalar_prefetch=1,
            grid=(1,),
            in_specs=[
                whole((n, T, D)),
                whole((n, T, 384)),
                whole((n * nb, 1, 384)),
                pl.BlockSpec(memory_space=pl.ANY),
            ],
            out_specs=[whole(shape), whole(shape)],
            scratch_shapes=[pltpu.VMEM((384, D), F32)],
        ),
        out_shape=[jax.ShapeDtypeStruct(shape, BF16)] * 2,
        compiler_params=params(),
        cost_estimate=cost(3),
        name="qkv_grad",
    )(sc, h, dm, aux, after)


def scatter_rows(cap, slots, kaug, values):
    feature = kaug[:, 128:256].astype(F32)
    code = (feature[:, 16:17] * cap + feature[:, 17:18]).astype(jnp.int32)
    pick = jnp.where(code == iota((feature.shape[0], slots), 1), 1.0, 0.0).astype(BF16)
    return dot_nn(pick, values)


def input_grad_kernel(n, T, cap, sc, dm, w_qkv, hidden, d_ret, kaug, gain, out, full):
    for k in range(n):
        for part in range(3):
            full[:, part * D + k * 128 : part * D + (k + 1) * 128] = dm[
                k, :, part * 128 : (part + 1) * 128
            ]
    u = dot_nt(full[...], w_qkv[...])
    vhat, inv_std = normed_rows(hidden[...].astype(F32))
    scaled = u * gain[...]
    first = jnp.mean(scaled, axis=-1, keepdims=True)
    second = jnp.mean(scaled * vhat, axis=-1, keepdims=True)
    d_one = scatter_rows(cap, d_ret.shape[0], kaug[...], d_ret[...])
    out[...] = (d_one + inv_std * (scaled - first - vhat * second)).astype(BF16)


def input_grad_call(n, T, cap, sc, dm, w_qkv, hidden, d_ret, kaug, gain):
    slots = d_ret.shape[0]
    return pl.pallas_call(
        lambda *a: input_grad_kernel(n, T, cap, *a),
        grid_spec=pltpu.PrefetchScalarGridSpec(
            num_scalar_prefetch=1,
            grid=(1,),
            in_specs=[
                whole((n, T, 384)),
                whole((D, 3 * D)),
                whole((T, D)),
                whole((slots, D)),
                pl.BlockSpec((T, 256), lambda i, sc: (sc[n], 0)),
                whole((1, D)),
            ],
            out_specs=whole((T, D)),
            scratch_shapes=[pltpu.VMEM((T, 3 * D), BF16)],
        ),
        out_shape=jax.ShapeDtypeStruct((T, D), BF16),
        compiler_params=params(),
        cost_estimate=SMALL,
        name="input_grad",
    )(sc, dm, w_qkv, hidden, d_ret, kaug, gain)


def output_kernel(cap, sc, ret, kaug, out):
    out[...] = scatter_rows(cap, ret.shape[0], kaug[...], ret[...]).astype(BF16)


def output_call(n, T, cap, sc, ret, kaug):
    return pl.pallas_call(
        lambda *a: output_kernel(cap, *a),
        grid_spec=pltpu.PrefetchScalarGridSpec(
            num_scalar_prefetch=1,
            grid=(1,),
            in_specs=[
                whole(ret.shape),
                pl.BlockSpec((T, 256), lambda i, sc: (sc[n], 0)),
            ],
            out_specs=whole((T, D)),
        ),
        out_shape=jax.ShapeDtypeStruct((T, D), BF16),
        compiler_params=params(),
        cost_estimate=SMALL,
        name="output_rows",
    )(sc, ret, kaug)


def final_kernel(n, nb, sc, got, w_rows, gb, gw, gains, biases, qvb, outb, gwo, s_rows, w_full):
    size = D // (n * nb)
    me, me_b = sc[n], sc[n + 1]
    smalls = jnp.zeros((1, 384), F32)
    s_rows[...] = jnp.zeros_like(s_rows)
    for k in range(n):
        tile = got[k, 0 : size + 16, :].astype(F32)
        for part in range(3):
            cols = slice(part * D + k * 128, part * D + (k + 1) * 128)
            w_full[:, cols] = tile[0:size, part * 128 : (part + 1) * 128]
            s_rows[0:1, cols] = tile[size : size + 1, part * 128 : (part + 1) * 128]
        smalls = smalls + tile[size + 1 : size + 2, :]
    gw[...] = w_full[...]
    for g in range(-(-D // 384)):
        cols = slice(g * 384, min(D, (g + 1) * 384))
        rows = slice((g + 1) * size + 16, (g + 2) * size + 16)
        total = jnp.zeros((size, 384), F32)
        for k in range(n):
            total = total + got[k, rows, :].astype(F32)
        gwo[:, cols] = total[:, 0 : cols.stop - cols.start]
    weights = w_rows[...].astype(F32)
    high = lax.Precision.HIGHEST
    nt = (((1,), (1,)), ((), ()))
    bias_one = lax.dot_general(s_rows[...], weights, nt, precision=high, preferred_element_type=F32)[0:1]
    both = lax.dot_general(
        jnp.ones((8, 3 * D), F32), weights * w_full[...], nt, precision=high, preferred_element_type=F32
    )[0:1]
    gains[0:1, :] = (both - gb[1:2, :] * bias_one) / gb[0:1, :]
    gains[1:2, :] = smalls[:, 0:size]
    biases[0:1, :] = bias_one
    biases[1:2, :] = smalls[:, size : 2 * size]
    outb[...] = smalls[:, 2 * size : 3 * size]
    own = got[me, size : size + 16, :].astype(F32)[0:1]
    for row, first in ((0, 0), (1, 256)):
        value = jnp.zeros((1, size), F32)
        for c in range(nb):
            value = jnp.where(me_b == c, own[:, first + c * size : first + (c + 1) * size], value)
        qvb[row : row + 1, :] = value


def final_call(n, nb, sc, got, w_qkv, gb):
    size = D // (n * nb)
    shapes = [(size, 3 * D), (2, size), (2, size), (2, size), (1, size), (size, D)]
    return pl.pallas_call(
        lambda *a: final_kernel(n, nb, *a),
        grid_spec=pltpu.PrefetchScalarGridSpec(
            num_scalar_prefetch=1,
            grid=(1,),
            in_specs=[
                whole(got.shape),
                pl.BlockSpec((size, 3 * D), lambda i, sc: (nb * sc[n] + sc[n + 1], 0)),
                whole((2, size)),
            ],
            out_specs=[whole(s) for s in shapes],
            scratch_shapes=[pltpu.VMEM((8, 3 * D), F32), pltpu.VMEM((size, 3 * D), F32)],
        ),
        out_shape=[jax.ShapeDtypeStruct(s, F32) for s in shapes],
        compiler_params=params(),
        cost_estimate=cost(3),
        name="final_rows",
    )(sc, got, w_qkv, gb)


def exchange(values, axis, bit):
    size = lax.axis_size(axis)
    return lax.ppermute(values, axis, [(i, i ^ bit) for i in range(size)])


def arrival_tables(n, ring):
    place = [ring.index(i) for i in range(n)]
    order = [[0]] + [[-o, o] for o in range(1, n // 2)] + [[n // 2]]
    sources, tiles, counts = [], [], None
    for i in range(n):
        blocks = [[ring[(place[i] + o) % n] for o in step] for step in order]
        arrived, listed, sizes = [], [], []
        for at, step in enumerate(blocks):
            arrived += step
            if at == 0:
                continue
            new = arrived if at == 1 else step
            diag = [(q, q) for q in sorted(new)]
            pairs = [
                (q, k)
                for k in range(n)
                for q in range(k + 1, n)
                if q in arrived and k in arrived and (q in new or k in new)
            ]
            listed.append([x for t in diag + pairs for x in t])
            sizes.append((len(diag), len(pairs)))
        sources.append([b for step in blocks for b in step])
        tiles.append(listed)
        counts = counts or sizes
    return np.array(sources, np.int32), tiles, counts


def reduce_cores(keep, send, after=None):
    got = exchange(send, "batch", 1)
    if after is not None:
        got = gate(got, after)
    return [(keep[y].astype(F32) + got[y].astype(F32)).astype(BF16) for y in range(2)]


def gate(value, *after):
    def nothing(*refs):
        del refs

    anywhere = pl.BlockSpec(memory_space=pl.ANY)
    return pl.pallas_call(
        nothing,
        in_specs=[anywhere] * (1 + len(after)),
        out_specs=anywhere,
        out_shape=jax.ShapeDtypeStruct(value.shape, value.dtype),
        input_output_aliases={0: 0},
        name="gate",
    )(value, *after)


def local_by_heads(
    hidden_in,
    out_grad,
    norm_gain_pair,
    norm_bias_pair,
    w_qkv,
    qv_bias,
    w_out,
    out_bias,
    w_in_exp,
    b_in_exp,
    w_out_exp,
    b_out_exp,
    expert_ids,
    doc_lengths,
    pad_mask,
):
    T = hidden_in.shape[1]
    n, nb = lax.axis_size("seq"), lax.axis_size("batch")
    experts = EXP_DEV * n
    cap = max(2, 3 * T // (2 * experts))
    s, b = lax.axis_index("seq"), lax.axis_index("batch")
    ring = [*range(0, n, 2), *range(n - 1, 0, -2)]
    sources, tiles, counts = arrival_tables(n, ring)

    every = [(i, i) for i in range(n)] + [(q, k) for k in range(n) for q in range(k + 1, n)]
    every = np.array(every, np.int32).reshape(-1)
    table = [
        np.concatenate([sources[i], [i, 0]] + tiles[i] + [every]).astype(np.int32) for i in range(n)
    ]
    firsts = n + 2 + np.cumsum([0] + [2 * (d + p) for d, p in counts])
    row = lax.dynamic_index_in_dim(jnp.asarray(np.stack(table)), s, 0, keepdims=False)
    sc = jnp.where(jnp.arange(row.shape[0]) == n + 1, b.astype(jnp.int32), row)
    hidden = hidden_in[0]
    ids = expert_ids[0, :, 0]
    codes = jnp.concatenate([ids, pad_mask[0], jnp.zeros((D - 2 * T,), jnp.int32)]).astype(BF16)
    codes = jnp.where(jnp.arange(16)[:, None] == 0, codes[None, :], jnp.zeros((), BF16))
    payload = jnp.concatenate([hidden, codes], axis=0)

    count = doc_lengths.shape[1]
    at = jnp.arange(128)
    ends = jnp.sum(
        jnp.where(jnp.arange(count)[:, None] <= at[None, :], doc_lengths[0][:, None], 0), axis=0
    )
    starts = jnp.sum(
        jnp.where(jnp.arange(count)[:, None] < at[None, :], doc_lengths[0][:, None], 0), axis=0
    )
    docs = jnp.stack([starts, ends]).astype(F32)
    gain_rows = [norm_gain_pair[i : i + 1] for i in range(2)]
    bias_rows = [norm_bias_pair[i : i + 1] for i in range(2)]

    ahead = [(ring[i], ring[(i + 1) % n]) for i in range(n)]
    back = [(ring[i], ring[i - 1]) for i in range(n)]
    split = -(-payload.shape[0] // 32) * 16
    size = D // (n * nb)
    own = (s * nb + b) * size
    gb = jnp.stack(
        [
            lax.dynamic_slice_in_dim(norm_gain_pair[0], own, size, 0),
            lax.dynamic_slice_in_dim(norm_bias_pair[0], own, size, 0),
        ]
    )
    held, block = None, 0
    left = right = payload
    waiting = [[payload]]
    sent_grads = dispatch_call(cap, experts * cap, [], ids[None], out_grad[0])
    for step in range(1, n // 2 + 1):
        last = step == n // 2
        if last:
            left, right = left[:split], right[split:]
        left, right = lax.ppermute(left, "seq", ahead), lax.ppermute(right, "seq", back)
        if last:
            waiting.append([left, right])
        else:
            left = gate(left, right, *(held or ())[6:7])
            right = gate(right, left)
            waiting += [[left], [right]]
        if step == n // 2 - 1:
            sent_grads = gate(sent_grads, right)
            sent_grads = sent_grads.reshape(n, EXP_DEV * cap, D)
            grads = lax.all_to_all(sent_grads, "seq", split_axis=0, concat_axis=0, tiled=True)
            grads = grads.reshape(n, EXP_DEV, cap, D).transpose(1, 0, 2, 3).reshape(experts * cap, D)
        diags, pairs = counts[step - 1]
        held = ring_call(
            n, T, cap, block, int(firsts[step - 1]), diags, pairs, sc, waiting, held, last,
            w_qkv, qv_bias, gain_rows[0], bias_rows[0], docs,
            [grads] if last else [gb] if step == 1 else [],
        )
        block += len(waiting)
        waiting = []
    h_one, sel, qa, ka = held[:4]
    *att_out, o, lse = held[9:]
    sel = sel.reshape(EXP_DEV * n * cap, D)

    g_y = exchange(grads, "batch", 2)
    g_parts = [grads, exchange(grads, "batch", 1), g_y, exchange(g_y, "batch", 1)]

    def by_seq(rows):
        return lax.all_to_all(rows, "seq", split_axis=0, concat_axis=0, tiled=True)

    att_in = []
    for e in range(EXP_DEV):
        att_in.append(by_seq(gate(att_out[e], att_in[-1]) if e else att_out[e]))
    x_two, x_one, att_b = [], [], []
    for e in range(EXP_DEV):
        rows, one, att_rows = owner_fwd_call(
            n, e, att_in[e], w_out, sel, out_bias[None], gain_rows[1], bias_rows[1]
        )
        x_two.append(rows)
        x_one.append(one)
        att_b.append(att_rows)
    x_core = [exchange(rows, "batch", 1) for rows in x_two]
    x_y = [exchange(rows, "batch", 2) for rows in x_two]
    x_parts, hidden_act, dpre, grad_b_in, sums, from_y = [], [], [], [], [], []
    d_one_b, small, datt, outs = [], [], [], []
    to_add = []
    after = [x_one[-1]]
    terms = None

    def turn_back(e):
        datt_out, rows, totals = owner_bwd_call(
            n, e, sums[e][0], from_y[e], x_one[e], grads, gain_rows[1], w_out, after
        )
        datt.append(by_seq(gate(datt_out, datt[-1]) if e else datt_out))
        d_one_b.append(rows)
        small.append(totals)
        return datt_out

    for e in range(EXP_DEV):
        if e:
            x_y[e] = gate(x_y[e], terms[0])
        x_parts.append([x_two[e], x_core[e], x_y[e], exchange(x_y[e], "batch", 1)])
        act, dact, *terms, grad_b = expert_call(
            e, sc, x_parts[e], g_parts, w_in_exp, b_in_exp, w_out_exp, after
        )
        hidden_act.append(act)
        dpre.append(dact)
        grad_b_in.append(grad_b[0])
        if e == 0:
            to_add.append(expert_out_call(nb, e, act, w_out_exp, []))
            filler = to_add[e][0]
        else:
            after = [terms[0]]
            turn_back(e - 1)
            filler = d_one_b[-1]
        sums.append(reduce_cores(*terms, after=filler))
        from_y.append(exchange(sums[e][1], "batch", 2))
        after = [sums[e][0]]
    for i in range(1, EXP_DEV):
        to_add.append(expert_out_call(nb, i, hidden_act[i], w_out_exp, after))
    after = [to_add[-1][0]]
    datt_out = turn_back(EXP_DEV - 1)
    outs = [reduce_cores(*to_add[i], after=datt_out) for i in range(EXP_DEV)]
    from_y = [exchange(both[1], "batch", 2) for both in outs]

    size = D // (n * nb)
    home = []
    for e in range(EXP_DEV):
        expert_rows = (
            outs[e][0].astype(F32) + from_y[e].astype(F32) + b_out_exp[e][None, :]
        ).astype(BF16)
        home.append((x_one[e] + expert_rows.astype(F32)).astype(BF16))
    home = [rows.reshape(n, cap, D) for rows in d_one_b + home]
    home = jnp.concatenate(home, axis=1)
    returned = by_seq(home)
    at = EXP_DEV * cap
    dm = attn_bwd_call(
        n, T, cap, int(firsts[-1]), n, n * (n - 1) // 2, sc, qa, ka, lse, o, datt, [home]
    )
    w_out_terms = w_out_grad_call(n, nb, sc, att_b, d_one_b, [dm])
    aux = sum(small)[:3].reshape(3, n * nb, size).transpose(1, 0, 2).reshape(n * nb, 1, 3 * size)
    aux = jnp.pad(aux, ((0, 0), (0, 0), (0, 384 - 3 * size)))
    keep_w, send_w = qkv_grad_call(n, nb, T, sc, h_one, dm, aux, dm)
    returned = gate(returned, keep_w, w_out_terms[0])
    d_ret = returned[:, :at].reshape(experts * cap, D)
    dm_own = by_seq(gate(dm, returned))
    both = reduce_cores(keep_w, gate(send_w, returned))
    w_y = exchange(both[1], "batch", 2)
    w_out_both = reduce_cores(w_out_terms[0], gate(w_out_terms[1], both[0]))
    w_out_y = exchange(w_out_both[1], "batch", 2)
    weights = None
    for e in range(EXP_DEV):
        weights = expert_grad_call(
            e, sc, x_parts[e], g_parts, hidden_act[e], dpre[e], weights, [w_out_both[0]]
        )
    grad_w_in, grad_w_out_exp, grad_b_out = weights
    w_out_y = gate(w_out_y, grad_b_out)
    w_y = gate(w_y, grad_b_out)
    w_sum = (both[0].astype(F32) + w_y.astype(F32)).astype(BF16)
    summed = (w_out_both[0].astype(F32) + w_out_y.astype(F32)).astype(BF16)
    last_rows = jnp.concatenate([w_sum, summed], axis=1)
    dm_own = gate(dm_own, last_rows)
    w_got = by_seq(gate(last_rows, dm_own))
    out_ret = gate(returned[:, at : 2 * at].reshape(experts * cap, D), dm_own)
    output = output_call(n, T, cap, sc, out_ret, ka)
    gw_qkv, g_gains, g_biases, g_qvb, g_outb, grad_w_out = final_call(n, nb, sc, w_got, w_qkv, gb)
    input_grad = input_grad_call(n, T, cap, sc, dm_own, w_qkv, hidden, d_ret, ka, gain_rows[0])
    return (
        output[None],
        input_grad[None],
        g_gains,
        g_biases,
        gw_qkv,
        g_qvb,
        grad_w_out,
        g_outb[0],
        grad_w_in,
        jnp.concatenate(grad_b_in, axis=0),
        grad_w_out_exp,
        grad_b_out[:, 0],
    )


def solution(mesh):
    n, nb = mesh.shape["seq"], mesh.shape["batch"]
    by_heads = HEADS * HEAD_DIM == 128 * n and nb == 4
    return jax.shard_map(
        local_by_heads if by_heads else local,
        mesh=mesh,
        in_specs=(
            P("batch", "seq", None),
            P("batch", "seq", None),
            P(),
            P(),
            P(),
            P(),
            P(),
            P(),
            P("seq", None, "batch"),
            P("seq", "batch"),
            P("seq", "batch", None),
            P("seq", None),
            P("batch", "seq", None),
            P("batch", None),
            P("batch", "seq"),
        ),
        out_specs=(
            P("batch", "seq", None),
            P("batch", "seq", None),
            P(None, ("seq", "batch")),
            P(None, ("seq", "batch")),
            P(("seq", "batch"), None),
            P(None, ("seq", "batch")),
            P(("seq", "batch"), None),
            P(("seq", "batch")),
            P("seq", None, "batch"),
            P("seq", "batch"),
            P("seq", "batch", None),
            P("seq", None),
        ),
        check_vma=False,
    )
```

```python
import math

import jax
import jax.numpy as jnp
import numpy as np
from jax import lax
from jax.experimental import pallas as pl
from jax.experimental.pallas import tpu as pltpu
from jax.sharding import PartitionSpec as P

D = 1024
HEADS = 16
HEAD_DIM = 64
EXP_DEV = 2


EPS = 1e-05
NEG = -1e30
BIG = 1e30
F32 = jnp.float32
BF16 = jnp.bfloat16
VMEM_LIMIT = 60 * 1024 * 1024


def dot_nn(a, b):
    return lax.dot_general(a, b, (((1,), (0,)), ((), ())), preferred_element_type=F32)


def dot_nt(a, b):
    return lax.dot_general(a, b, (((1,), (1,)), ((), ())), preferred_element_type=F32)


def dot_tn(a, b):
    return lax.dot_general(a, b, (((0,), (0,)), ((), ())), preferred_element_type=F32)


def normed_rows(values):
    centre = values - jnp.mean(values, axis=-1, keepdims=True)
    spread = jnp.mean(centre * centre, axis=-1, keepdims=True)
    inv_std = lax.rsqrt(spread + EPS)
    return centre * inv_std, inv_std


def whole(shape):
    return pl.BlockSpec(shape, lambda *_: (0,) * len(shape))


def params(**more):
    return pltpu.CompilerParams(vmem_limit_bytes=VMEM_LIMIT, **more)


def iota(shape, axis):
    return lax.broadcasted_iota(jnp.int32, shape, axis)


def running_sums(values):
    upto = jnp.arange(values.shape[0])[:, None] >= jnp.arange(values.shape[0])[None, :]
    return jnp.sum(jnp.where(upto, values[None, :], 0), axis=1)


def layer_normalize(values, gain, shift):
    centre = values - jnp.mean(values, axis=-1, keepdims=True)
    spread = jnp.mean(centre * centre, axis=-1, keepdims=True)
    inv_std = lax.rsqrt(spread + EPS)
    normed = centre * inv_std
    return (normed * gain + shift, normed, inv_std)


def norm_backward_pass(grads, normed, inv_std, gain):
    scaled = grads * gain
    first_mean = jnp.mean(scaled, axis=-1, keepdims=True)
    second_mean = jnp.mean(scaled * normed, axis=-1, keepdims=True)
    return (
        inv_std * (scaled - first_mean - normed * second_mean),
        jnp.sum(grads * normed, axis=0),
        jnp.sum(grads, axis=0),
    )


def doc_of(positions, doc_ends):
    return jnp.sum((positions[:, None] >= doc_ends[None, :]).astype(jnp.int32), axis=1)


def allowed_pairs(q_pos, q_doc, k_pos, k_doc, k_pad):
    same_doc = q_doc[:, None] == k_doc[None, :]
    before = k_pos[None, :] <= q_pos[:, None]
    usable = (k_pad[None, :] == 1) | (k_pos[None, :] == q_pos[:, None])
    return same_doc & before & usable


def over_blocks(step_fn, totals, arrays, first_row):
    row_count = arrays[0].shape[0]
    block_rows = math.gcd(row_count, 512)

    def advance(current, block_index):
        pieces = tuple(
            (
                lax.dynamic_slice_in_dim(member, block_index * block_rows, block_rows, 0)
                for member in arrays
            )
        )
        return (step_fn(current, pieces, first_row + block_index * block_rows), None)

    result, _ = lax.scan(advance, totals, jnp.arange(row_count // block_rows, dtype=jnp.int32))
    return result


def key_grads(
    query_h, dout_h, lse_rows, delta_rows, q_pos, q_doc, key_h, value_h, k_pos, k_doc, k_pad
):
    allowed = allowed_pairs(q_pos, q_doc, k_pos, k_doc, k_pad)
    scores = jnp.einsum("qhd,khd->hqk", query_h, key_h, preferred_element_type=jnp.float32)
    probs = jnp.where(allowed[None], jnp.exp(scores - lse_rows.T[:, :, None]), 0.0)
    dprobs = jnp.einsum("qhd,khd->hqk", dout_h, value_h, preferred_element_type=jnp.float32)
    dscores = (probs * (dprobs - delta_rows.T[:, :, None])).astype(jnp.bfloat16)
    grad_keys = jnp.einsum("hqk,qhd->khd", dscores, query_h, preferred_element_type=jnp.float32)
    grad_values = jnp.einsum(
        "hqk,qhd->khd", probs.astype(jnp.bfloat16), dout_h, preferred_element_type=jnp.float32
    )
    return (grad_keys, grad_values)


def gelu_exact(values):
    return jax.nn.gelu(values, approximate=False)


def local(
    hidden_in,
    out_grad,
    norm_gain_pair,
    norm_bias_pair,
    w_qkv,
    qv_bias,
    w_out,
    out_bias,
    w_in_exp,
    b_in_exp,
    w_out_exp,
    b_out_exp,
    expert_ids,
    doc_lengths,
    pad_mask,
):
    tok_rows = hidden_in.shape[1]
    seq_count = lax.axis_size("seq")
    experts_all = EXP_DEV * seq_count
    capacity = max(2, 3 * tok_rows // (2 * experts_all))
    scale = HEAD_DIM ** (-0.5)
    input_tokens = hidden_in[0].astype(jnp.float32)
    first_normalized, first_centred_scaled, first_inverse_deviation = layer_normalize(
        input_tokens, norm_gain_pair[0], norm_bias_pair[0]
    )
    h_one = first_normalized.astype(jnp.bfloat16)
    mixed = jnp.dot(h_one, w_qkv, preferred_element_type=jnp.float32)
    queries = ((mixed[:, :D] + qv_bias[0]) * scale).astype(jnp.bfloat16)
    keys_vals = jnp.concatenate(
        [mixed[:, D : 2 * D], mixed[:, 2 * D :] + qv_bias[1][None, :]], axis=1
    ).astype(jnp.bfloat16)
    query_h = queries.reshape(tok_rows, HEADS, HEAD_DIM)
    q_pos = lax.axis_index("seq") * tok_rows + jnp.arange(tok_rows, dtype=jnp.int32)
    doc_ends = running_sums(doc_lengths[0])
    q_doc = doc_of(q_pos, doc_ends)
    key_pad = pad_mask[0]

    def split_keys(pieces, first_row):
        block_kv, block_pad = pieces
        row_count = block_kv.shape[0]
        key_h = block_kv[:, :D].reshape(row_count, HEADS, HEAD_DIM)
        value_h = block_kv[:, D:].reshape(row_count, HEADS, HEAD_DIM)
        k_pos = first_row + jnp.arange(row_count, dtype=jnp.int32)
        allowed = allowed_pairs(q_pos, q_doc, k_pos, doc_of(k_pos, doc_ends), block_pad)
        scores = jnp.einsum("thd,khd->htk", query_h, key_h, preferred_element_type=jnp.float32)
        return (key_h, value_h, allowed, jnp.where(allowed[None], scores, NEG))

    def stats_step(current, pieces, first_row):
        _, _, allowed, scores = split_keys(pieces, first_row)
        top_now, mass_now = current
        new_top = jnp.maximum(top_now, jnp.max(scores, axis=-1))
        weights = jnp.where(allowed[None], jnp.exp(scores - new_top[:, :, None]), 0.0)
        return (new_top, mass_now * jnp.exp(top_now - new_top) + jnp.sum(weights, axis=-1))

    def output_step(current, pieces, first_row):
        _, value_h, allowed, scores = split_keys(pieces, first_row)
        probs = jnp.where(allowed[None], jnp.exp(scores - log_mass[:, :, None]), 0.0).astype(
            jnp.bfloat16
        )
        return current + jnp.einsum(
            "htk,khd->thd", probs, value_h, preferred_element_type=jnp.float32
        )

    def dquery_step(current, pieces, first_row):
        key_h, value_h, allowed, scores = split_keys(pieces, first_row)
        probs = jnp.where(allowed[None], jnp.exp(scores - log_mass[:, :, None]), 0.0)
        dprobs = jnp.einsum("thd,khd->htk", dout_h, value_h, preferred_element_type=jnp.float32)
        dscores = (probs * (dprobs - delta[:, :, None])).astype(jnp.bfloat16)
        return current + jnp.einsum(
            "htk,khd->thd", dscores, key_h, preferred_element_type=jnp.float32
        )

    head_zeros = jnp.zeros((tok_rows, HEADS, HEAD_DIM), jnp.float32)
    init_stats = (
        jnp.full((HEADS, tok_rows), NEG, jnp.float32),
        jnp.zeros((HEADS, tok_rows), jnp.float32),
    )
    all_kv, all_pad = (
        lax.all_gather(keys_vals, "seq", axis=0, tiled=True),
        lax.all_gather(key_pad, "seq", axis=0, tiled=True),
    )

    def run_keys(step_fn, totals):
        return over_blocks(step_fn, totals, (all_kv, all_pad), 0)

    top_all, mass_all = run_keys(stats_step, init_stats)
    log_mass = top_all + jnp.log(mass_all)
    attended = run_keys(output_step, head_zeros)
    attended_b = attended.reshape(tok_rows, D).astype(jnp.bfloat16)
    branch = jnp.dot(attended_b, w_out, preferred_element_type=jnp.float32) + out_bias
    first_residual_input = input_tokens + branch
    second_normalized, second_centred_scaled, second_inverse_deviation = layer_normalize(
        first_residual_input, norm_gain_pair[1], norm_bias_pair[1]
    )
    x_two = second_normalized.astype(jnp.bfloat16)
    token_ids = expert_ids[0, :, 0]
    earlier = jnp.arange(tok_rows)[None, :] < jnp.arange(tok_rows)[:, None]
    ranks = jnp.sum(((token_ids[:, None] == token_ids[None, :]) & earlier).astype(jnp.int32), axis=1)
    target = token_ids * capacity + ranks
    dispatch = (
        jnp.arange(experts_all * capacity, dtype=jnp.int32)[:, None] == target[None, :]
    ).astype(jnp.bfloat16)
    sent_rows = (
        jnp.dot(dispatch, x_two, preferred_element_type=jnp.float32)
        .astype(jnp.bfloat16)
        .reshape(seq_count, EXP_DEV, capacity, D)
    )
    rows_all = lax.all_gather(
        lax.all_to_all(sent_rows, "seq", split_axis=0, concat_axis=0, tiled=True),
        "batch",
        axis=0,
        tiled=True,
    )
    pre_act = (
        jnp.einsum("recd,edf->recf", rows_all, w_in_exp, preferred_element_type=jnp.float32)
        + b_in_exp[None, :, None, :]
    )
    hidden = gelu_exact(pre_act).astype(jnp.bfloat16)
    part_sums = jnp.einsum("recf,efd->recd", hidden, w_out_exp, preferred_element_type=jnp.float32)
    summed = lax.psum_scatter(
        part_sums.astype(jnp.bfloat16), "batch", scatter_dimension=0, tiled=True
    ).astype(jnp.float32)
    produced = (summed + b_out_exp[None, :, None, :]).astype(jnp.bfloat16)
    returned = lax.all_to_all(produced, "seq", split_axis=0, concat_axis=0, tiled=True)
    expert_rows = jnp.einsum(
        "st,sd->td",
        dispatch,
        returned.reshape(experts_all * capacity, D),
        preferred_element_type=jnp.float32,
    )
    output = (first_residual_input + expert_rows).astype(jnp.bfloat16)
    dout = out_grad[0].astype(jnp.float32)
    sent_grads = (
        jnp.dot(dispatch, out_grad[0], preferred_element_type=jnp.float32)
        .astype(jnp.bfloat16)
        .reshape(seq_count, EXP_DEV, capacity, D)
    )
    arrived_rows, arrived_grads = (
        lax.all_to_all(sent_rows, "seq", split_axis=0, concat_axis=0, tiled=True),
        lax.all_to_all(sent_grads, "seq", split_axis=0, concat_axis=0, tiled=True),
    )
    rows_all, grads_all = (
        lax.all_gather(arrived_rows, "batch", axis=0, tiled=True),
        lax.all_gather(arrived_grads, "batch", axis=0, tiled=True),
    )
    pre_act = (
        jnp.einsum("recd,edf->recf", rows_all, w_in_exp, preferred_element_type=jnp.float32)
        + b_in_exp[None, :, None, :]
    )
    hidden_f, gelu_back = jax.vjp(gelu_exact, pre_act)
    hidden_b = hidden_f.astype(jnp.bfloat16)
    dhidden = jnp.einsum(
        "recd,efd->recf", grads_all, w_out_exp, preferred_element_type=jnp.float32
    ).astype(jnp.bfloat16)
    dpre = gelu_back(dhidden.astype(jnp.float32))[0].astype(jnp.bfloat16)
    grad_w_out_exp = jnp.einsum(
        "recf,recd->efd", hidden_b, grads_all, preferred_element_type=jnp.float32
    )
    grad_b_out_exp = jnp.sum(grads_all, axis=(0, 2), dtype=jnp.float32)
    grad_w_in_exp = jnp.einsum("recd,recf->edf", rows_all, dpre, preferred_element_type=jnp.float32)
    grad_b_in_exp = jnp.sum(dpre, axis=(0, 2), dtype=jnp.float32)
    drows = jnp.einsum("recf,edf->recd", dpre, w_in_exp, preferred_element_type=jnp.float32)
    drows_sum = lax.psum_scatter(
        drows.astype(jnp.bfloat16), "batch", scatter_dimension=0, tiled=True
    )
    drows_home = lax.all_to_all(drows_sum, "seq", split_axis=0, concat_axis=0, tiled=True)
    second_residual_gradient = jnp.einsum(
        "st,sd->td",
        dispatch,
        drows_home.reshape(experts_all * capacity, D),
        preferred_element_type=jnp.float32,
    )
    second_norm_gradient, second_gain_gradient, second_shift_gradient = norm_backward_pass(
        second_residual_gradient, second_centred_scaled, second_inverse_deviation, norm_gain_pair[1]
    )
    d_one = dout + second_norm_gradient
    d_one_b = d_one.astype(jnp.bfloat16)
    grad_w_out = jnp.einsum("td,te->de", attended_b, d_one_b, preferred_element_type=jnp.float32)
    grad_out_bias = jnp.sum(d_one, axis=0)
    dout_b = jnp.einsum("te,de->td", d_one_b, w_out, preferred_element_type=jnp.float32).astype(
        jnp.bfloat16
    )
    dout_h = dout_b.reshape(tok_rows, HEADS, HEAD_DIM)
    delta = jnp.einsum("thd,thd->ht", dout_h.astype(jnp.float32), attended)
    dquery = run_keys(dquery_step, head_zeros)
    lse_rows = log_mass.T
    delta_rows = delta.T
    block_rows = math.gcd(tok_rows * lax.axis_size("seq"), 512)

    def one_block(block_index):
        first_key = block_index * block_rows
        block_kv = lax.dynamic_slice_in_dim(all_kv, first_key, block_rows, 0)
        block_pad = lax.dynamic_slice_in_dim(all_pad, first_key, block_rows, 0)
        k_pos = first_key + jnp.arange(block_rows, dtype=jnp.int32)
        grad_k, grad_v = key_grads(
            query_h,
            dout_h,
            lse_rows,
            delta_rows,
            q_pos,
            q_doc,
            block_kv[:, :D].reshape(block_rows, HEADS, HEAD_DIM),
            block_kv[:, D:].reshape(block_rows, HEADS, HEAD_DIM),
            k_pos,
            doc_of(k_pos, doc_ends),
            block_pad,
        )
        return jnp.concatenate(
            [grad_k.reshape(block_rows, D), grad_v.reshape(block_rows, D)], axis=1
        )

    blocks = lax.map(
        one_block, jnp.arange(tok_rows * lax.axis_size("seq") // block_rows, dtype=jnp.int32)
    )
    key_terms = lax.psum_scatter(
        blocks.reshape(tok_rows * lax.axis_size("seq"), 2 * D).astype(jnp.bfloat16),
        "seq",
        scatter_dimension=0,
        tiled=True,
    )
    dq_b = dquery.reshape(tok_rows, D).astype(jnp.bfloat16)
    dmixed = jnp.concatenate([dq_b * scale, key_terms], axis=1)
    grad_w_qkv = jnp.einsum("td,te->de", h_one, dmixed, preferred_element_type=jnp.float32)
    first_hidden_gradient = jnp.einsum(
        "te,de->td", dmixed, w_qkv, preferred_element_type=jnp.float32
    )
    first_norm_gradient, first_gain_gradient, first_shift_gradient = norm_backward_pass(
        first_hidden_gradient, first_centred_scaled, first_inverse_deviation, norm_gain_pair[0]
    )
    input_grad = (d_one + first_norm_gradient).astype(jnp.bfloat16)
    grad_q_bias = jnp.sum(dmixed[:, :D], axis=0, dtype=jnp.float32)
    grad_v_bias = jnp.sum(key_terms[:, D:], axis=0, dtype=jnp.float32)
    small_grads = jnp.stack(
        [
            first_gain_gradient,
            second_gain_gradient,
            first_shift_gradient,
            second_shift_gradient,
            grad_q_bias,
            grad_v_bias,
            grad_out_bias,
        ]
    )
    shared_qkv, shared_out, shared_small = (
        lax.psum_scatter(grad_w_qkv, ("seq", "batch"), scatter_dimension=0, tiled=True),
        lax.psum_scatter(grad_w_out, ("seq", "batch"), scatter_dimension=0, tiled=True),
        lax.psum_scatter(small_grads, ("seq", "batch"), scatter_dimension=1, tiled=True),
    )
    return (
        output[None],
        input_grad[None],
        shared_small[0:2],
        shared_small[2:4],
        shared_qkv,
        shared_small[4:6],
        shared_out,
        shared_small[6],
        grad_w_in_exp,
        grad_b_in_exp,
        grad_w_out_exp,
        grad_b_out_exp,
    )


MICROSECOND = 1 << 30


def cost(us):
    return pl.CostEstimate(flops=us * MICROSECOND, bytes_accessed=1 << 20, transcendentals=0)


MICROSECOND = 1 << 30


def cost(us):
    return pl.CostEstimate(flops=us * MICROSECOND, bytes_accessed=1 << 20, transcendentals=0)


SMALL = pl.CostEstimate(flops=1, bytes_accessed=1, transcendentals=0)
HALVES = [slice(h * HEAD_DIM, (h + 1) * HEAD_DIM) for h in range(2)]


def block_rows(i, T):
    return pl.ds(pl.multiple_of(i * T, T), T)


def diag_parts(T, key_rows):
    lane = iota((T, 256), 1)
    values = key_rows.astype(F32)
    unpadded = jnp.where(lane == 136, 0.0, values).astype(BF16)
    k_at, q_at = iota((T, T), 0), iota((T, T), 1)
    padded = values[:, 136:137] > 0.5
    allowed = ((k_at < q_at) & jnp.logical_not(padded)) | (k_at == q_at)
    return unpadded, allowed


def ring_kernel(n, T, cap, block, parts, at_tile, diags, pairs, first, last, extra, sc, *refs):
    refs = list(refs)

    def take(count):
        got = refs[:count]
        del refs[:count]
        return got

    count = len(parts)
    chunks = [take(p) for p in parts]
    wq, wk, wv, qvb, gain, bias, docs = take(7)
    old = [] if first else take(9)
    take(extra)
    outs = take(9)
    results = take(EXP_DEV + 2) if last else None
    h_out, sel_out, qa_out, ka_out, vt_out, code_out = outs[:6]
    h_s, sel_s, qa, ka, vt, code, top, mass, acc, w, in_sems, out_sems = take(12)
    me = sc[n]
    loads = []

    def load(ref, to, needed=None):
        made = pltpu.make_async_copy(ref, to, in_sems.at[len(loads)])
        loads.append((made, needed))
        if needed is None:
            made.start()
        else:
            pl.when(needed)(made.start)

    if not first:
        for ref, to in zip(old[5:], (code, top, mass, acc)):
            load(ref, to)
        if not last:
            for ref, to in zip(old[2:5], (qa, ka, vt)):
                load(ref, to)
        else:
            new = sc[block]
            for i in range(n):
                rows = pl.ds(i * T, T)
                load(old[2].at[:, rows], qa.at[:, rows], i > new)
                load(old[3].at[rows], ka.at[rows], i < new)
                load(old[4].at[i], vt.at[i], i < new)
    w[:, 0:128] = wq[...]
    w[:, 128:256] = wk[...]
    w[:, 256:384] = wv[...]
    payloads = []
    for c in range(count):
        rows = [ref[...] for ref in chunks[c]]
        rows = rows[0] if len(rows) == 1 else jnp.concatenate(rows, axis=0)
        payloads.append(rows)
        vhat, _ = normed_rows(rows[0:T].astype(F32))
        h_s[c] = (vhat * gain[...] + bias[...]).astype(BF16)
    for made, needed in loads:
        if needed is None:
            made.wait()
        else:
            pl.when(needed)(made.wait)
    stores = []

    def send(ref, to):
        store = pltpu.make_async_copy(ref, to, out_sems.at[len(stores)])
        store.start()
        stores.append(store)

    for c in range(count):
        src = sc[block + c]
        rows = block_rows(src, T)
        mixed = dot_nn(h_s[c], w[...])
        q = ((mixed[:, 0:128] + qvb[0:1, :]) * (HEAD_DIM**-0.5)).astype(BF16).astype(F32)
        v = (mixed[:, 256:384] + qvb[1:2, :]).astype(BF16)
        codes = payloads[c][T : T + 16].astype(F32)
        id_row = codes[0:1, 0:T]
        pad_row = codes[0:1, T : 2 * T]
        id_col = jnp.transpose(jnp.broadcast_to(id_row, (128, T)))
        pad_col = jnp.transpose(jnp.broadcast_to(pad_row, (128, T)))
        same = jnp.where(
            (id_col[:, 0:1] == id_row) & (iota((T, T), 0) < iota((T, T), 1)), 1.0, 0.0
        )
        rank_row = jnp.sum(same, axis=0, keepdims=True)
        rank_col = jnp.transpose(jnp.broadcast_to(rank_row, (128, T)))
        lane = iota((T, 128), 1)
        pos = (iota((T, 128), 0) + src * T).astype(F32)
        doc = jnp.where((pos >= docs[0:1, :]) & (pos < docs[1:2, :]), 1.0, 0.0)
        aug = jnp.where(lane < 8, doc, 0.0)
        aug = jnp.where(lane == 8, 1.0 - pad_col, aug)
        aug = jnp.where(lane == 16, id_col, aug)
        aug = jnp.where(lane == 17, rank_col, aug)
        masked = jnp.where(lane < 8, (doc - 1.0) * BIG, jnp.where(lane == 8, -BIG, 0.0)).astype(BF16)
        for h in range(2):
            mine = (lane < HEAD_DIM) == (h == 0)
            qa[h, rows, 0:128] = jnp.where(mine, q, 0.0).astype(BF16)
            qa[h, rows, 128:256] = masked
        ka[rows, 0:128] = mixed[:, 128:256].astype(BF16)
        ka[rows, 128:256] = aug.astype(BF16)
        ka[rows, 256:384] = v
        vt[src] = jnp.transpose(v.astype(F32)).astype(BF16)
        slot = (id_row * cap + rank_row).astype(jnp.int32)
        half = lax.rem(src, 2) * cap
        code[src] = (id_row * (2 * cap) + rank_row).astype(jnp.int32) + half
        pick = jnp.where(
            slot == iota((EXP_DEV * cap, T), 0) + me * (EXP_DEV * cap), 1.0, 0.0
        ).astype(BF16)
        chosen = dot_nn(pick, payloads[c][0:T])
        for e in range(EXP_DEV):
            sel_s[c, e] = chosen[e * cap : (e + 1) * cap]
            send(sel_s.at[c, e], sel_out.at[e, src])
        send(h_s.at[c], h_out.at[src])
        for h in range(2):
            send(qa.at[h, rows], qa_out.at[h, rows])
        send(ka.at[rows], ka_out.at[rows])
        if not last:
            send(vt.at[src], vt_out.at[src])
            send(code.at[src], code_out.at[src])

    def one_diag(r, carry):
        i = sc[at_tile + 2 * r]
        rows = block_rows(i, T)
        kd, allowed = diag_parts(T, ka[rows, 0:256])
        for h in range(2):
            s = jnp.where(allowed, dot_nt(kd, qa[h, rows, :]), NEG)
            best = jnp.max(s, axis=0, keepdims=True)
            p = jnp.exp(s - best)
            top[h, i] = best
            mass[h, i] = jnp.sum(p, axis=0, keepdims=True)
            acc[i, HALVES[h], :] = dot_nn(vt[i, HALVES[h], :], p.astype(BF16))
        return carry

    lax.fori_loop(0, diags, one_diag, 0)

    def pair_tile(at):
        i, j = sc[at_tile + 2 * at], sc[at_tile + 2 * at + 1]
        rows, cols = block_rows(i, T), block_rows(j, T)
        old_top = [top[h, i] for h in range(2)]
        old_mass = [mass[h, i] for h in range(2)]
        old_acc = [acc[i, HALVES[h], :] for h in range(2)]
        s = [dot_nt(ka[cols, 0:256], qa[h, rows, :]) for h in range(2)]
        best = [jnp.maximum(old_top[h], jnp.max(s[h], axis=0, keepdims=True)) for h in range(2)]
        p = [jnp.exp(s[h] - best[h]) for h in range(2)]
        more = [dot_nn(vt[j, HALVES[h], :], p[h].astype(BF16)) for h in range(2)]
        for h in range(2):
            fade = jnp.exp(old_top[h] - best[h])
            top[h, i] = best[h]
            mass[h, i] = old_mass[h] * fade + jnp.sum(p[h], axis=0, keepdims=True)
            acc[i, HALVES[h], :] = old_acc[h] * fade + more[h]

    def two_pairs(r, carry):
        pair_tile(diags + 2 * r)
        pair_tile(diags + 2 * r + 1)
        return carry

    lax.fori_loop(0, pairs // 2, two_pairs, 0)
    if pairs % 2:
        pair_tile(diags + pairs - 1)
    if not last:
        for ref, to in zip((top, mass, acc), outs[6:]):
            send(ref, to)
    else:
        *att_out, o_out, lse_out = results

        def finish(i, carry):
            rows = block_rows(i, T)
            scaled = []
            for h in range(2):
                lse_out[h, i] = top[h, i] + jnp.log(mass[h, i])
                scaled.append(acc[i, HALVES[h], :] / mass[h, i])
            o_out[rows, :] = jnp.transpose(jnp.concatenate(scaled, axis=0))
            return carry

        lax.fori_loop(0, n, finish, 0)
        slots = n * EXP_DEV * 2 * cap

        def pair(p, carry):
            codes = jnp.concatenate([code[2 * p], code[2 * p + 1]], axis=1)
            pick = jnp.where(codes == iota((slots, 2 * T), 0), 1.0, 0.0).astype(BF16)
            chosen = dot_nn(pick, o_out[block_rows(p, 2 * T), :].astype(BF16)).astype(BF16)
            for k in range(n):
                for e in range(EXP_DEV):
                    at = (k * EXP_DEV + e) * 2 * cap
                    to = pl.multiple_of(p * 2 * cap, 16)
                    att_out[e][k, pl.ds(to, 2 * cap), :] = chosen[at : at + 2 * cap]
            return carry

        lax.fori_loop(0, n // 2, pair, 0)
    for store in stores:
        store.wait()


def ring_call(
    n, T, cap, block, at_tile, diags, pairs, sc, chunks, held, last, w_qkv, qv_bias, gain, bias, docs, after
):
    row = n * T
    shapes = [
        ((n, T, D), BF16),
        ((EXP_DEV, n, cap, D), F32),
        ((2, row, 256), BF16),
        ((row, 384), BF16),
        ((n, 128, T), BF16),
        ((n, 1, T), jnp.int32),
        ((2, n, 1, T), F32),
        ((2, n, 1, T), F32),
        ((n, 128, T), F32),
    ]
    anywhere = pl.BlockSpec(memory_space=pl.ANY)
    operands = [part for chunk in chunks for part in chunk]
    in_specs = [whole(part.shape) for part in operands] + [
        pl.BlockSpec((D, 128), lambda i, sc: (0, sc[n])),
        pl.BlockSpec((D, 128), lambda i, sc: (0, n + sc[n])),
        pl.BlockSpec((D, 128), lambda i, sc: (0, 2 * n + sc[n])),
        pl.BlockSpec((2, 128), lambda i, sc: (0, sc[n])),
        whole((1, D)),
        whole((1, D)),
        whole((2, 128)),
    ]
    aliases = {}
    first = held is None
    if not first:
        aliases = {1 + len(in_specs) + i: i for i in range(len(shapes))}
        in_specs = in_specs + [anywhere] * len(shapes)
    in_specs = in_specs + [anywhere] * len(after)
    out_specs = [anywhere] * len(shapes)
    results = []
    if last:
        results = [((n, n * cap, 128), BF16)] * EXP_DEV
        results = results + [((row, 128), F32), ((2, n, 1, T), F32)]
        out_specs = out_specs + [whole(s) for s, _ in results]
    count = len(chunks)
    parts = [len(chunk) for chunk in chunks]
    return pl.pallas_call(
        lambda *a: ring_kernel(
            n, T, cap, block, parts, at_tile, diags, pairs, first, last, len(after), *a
        ),
        grid_spec=pltpu.PrefetchScalarGridSpec(
            num_scalar_prefetch=1,
            grid=(1,),
            in_specs=in_specs,
            out_specs=out_specs,
            scratch_shapes=[
                pltpu.VMEM((count, T, D), BF16),
                pltpu.VMEM((count, EXP_DEV, cap, D), F32),
            ]
            + [pltpu.VMEM(s, t) for s, t in shapes[2:]]
            + [
                pltpu.VMEM((D, 384), BF16),
                pltpu.SemaphoreType.DMA((4 + 3 * n,)),
                pltpu.SemaphoreType.DMA((8 * count + 3,)),
            ],
        ),
        out_shape=[jax.ShapeDtypeStruct(s, t) for s, t in shapes + results],
        input_output_aliases=aliases,
        compiler_params=params(),
        cost_estimate=cost(10),
        name="ring_step",
    )(sc, *operands, w_qkv, w_qkv, w_qkv, qv_bias, gain, bias, docs, *(held or ()), *after)


def attn_bwd_kernel(
    n, T, cap, at_tile, diags, pairs, tiles, qa, ka, lse, o_ref, *refs
):
    datt = refs[:EXP_DEV]
    dm_out, do, delta, kh, dqa, dka, dva = refs[-7:]
    slots = n * EXP_DEV * 2 * cap

    def pair(p, carry):
        rows = block_rows(p, 2 * T)
        feature = ka[rows, 128:256].astype(F32)
        half = jnp.where(iota((2 * T, 1), 0) >= T, float(cap), 0.0)
        code = (feature[:, 16:17] * (2 * cap) + feature[:, 17:18] + half).astype(jnp.int32)
        pick = jnp.where(code == iota((2 * T, slots), 1), 1.0, 0.0).astype(BF16)
        parts = []
        for k in range(n):
            for e in range(EXP_DEV):
                at = pl.multiple_of(p * 2 * cap, 16)
                parts.append(datt[e][k, pl.ds(at, 2 * cap), :])
        got = dot_nn(pick, jnp.concatenate(parts, axis=0))
        lane = iota((2 * T, 128), 1)
        keys = ka[rows, 0:128].astype(F32)
        for h in range(2):
            mine = (lane < HEAD_DIM) == (h == 0)
            do[h, rows, :] = jnp.where(mine, got, 0.0).astype(BF16)
            kh[h, rows, :] = jnp.where(mine, keys, 0.0).astype(BF16)
        prod = jnp.transpose(got * o_ref[rows, :])
        for h in range(2):
            total = jnp.sum(prod[HALVES[h], :], axis=0, keepdims=True)
            delta[h, 2 * p] = total[:, 0:T]
            delta[h, 2 * p + 1] = total[:, T : 2 * T]
        return carry

    lax.fori_loop(0, n // 2, pair, 0)

    def tile(i, j, key_rows, mask):
        rows, cols = block_rows(i, T), block_rows(j, T)
        ps, dss = [], []
        for h in range(2):
            s = dot_nt(key_rows, qa[h, rows, :])
            dp = dot_nt(ka[cols, 256:384], do[h, rows, :])
            if mask is not None:
                s = jnp.where(mask, s, NEG)
            p = jnp.exp(s - lse[h, i])
            dss.append((p * (dp - delta[h, i])).astype(BF16))
            ps.append(p.astype(BF16))
        dv = dot_nn(
            jnp.concatenate(ps, axis=1), jnp.concatenate([do[0, rows, :], do[1, rows, :]], axis=0)
        )
        dk = dot_nn(
            jnp.concatenate(dss, axis=1),
            jnp.concatenate([qa[0, rows, 0:128], qa[1, rows, 0:128]], axis=0),
        )
        dq = dot_tn(
            jnp.concatenate(dss, axis=0), jnp.concatenate([kh[0, cols, :], kh[1, cols, :]], axis=0)
        )
        return dq, dk, dv

    def diag_tile(j, carry):
        kd, allowed = diag_parts(T, ka[block_rows(j, T), 0:256])
        dqa[j], dka[j], dva[j] = tile(j, j, kd, allowed)
        return carry

    lax.fori_loop(0, n, diag_tile, 0)

    def pair_tile(at):
        i, j = tiles[at_tile + 2 * at], tiles[at_tile + 2 * at + 1]
        dq, dk, dv = tile(i, j, ka[block_rows(j, T), 0:256], None)
        dqa[i] += dq
        dka[j] += dk
        dva[j] += dv

    width = next(w for w in (4, 2, 1) if pairs % w == 0)

    def some_pairs(r, carry):
        for w in range(width):
            pair_tile(diags + width * r + w)
        return carry

    lax.fori_loop(0, pairs // width, some_pairs, 0)

    def finish(i, carry):
        dq = dqa[i].astype(BF16).astype(F32)
        dm_out[i, :, 0:128] = (dq * (HEAD_DIM**-0.5)).astype(BF16)
        dm_out[i, :, 128:256] = dka[i].astype(BF16)
        dm_out[i, :, 256:384] = dva[i].astype(BF16)
        return carry

    lax.fori_loop(0, n, finish, 0)


def attn_bwd_call(n, T, cap, at_tile, diags, pairs, tiles, qa, ka, lse, o, datt, after):
    row = n * T
    vmem = pl.BlockSpec(memory_space=pltpu.VMEM)
    return pl.pallas_call(
        lambda *a: attn_bwd_kernel(n, T, cap, at_tile, diags, pairs, *a),
        out_shape=jax.ShapeDtypeStruct((n, T, 384), BF16),
        in_specs=[pl.BlockSpec(memory_space=pltpu.SMEM)]
        + [vmem] * (4 + EXP_DEV)
        + [pl.BlockSpec(memory_space=pl.ANY)] * len(after),
        out_specs=vmem,
        scratch_shapes=[
            pltpu.VMEM((2, row, 128), BF16),
            pltpu.VMEM((2, n, 1, T), F32),
            pltpu.VMEM((2, row, 128), BF16),
            pltpu.VMEM((n, T, 128), F32),
            pltpu.VMEM((n, T, 128), F32),
            pltpu.VMEM((n, T, 128), F32),
        ],
        compiler_params=params(),
        cost_estimate=cost(28),
        name="attn_bwd",
    )(tiles, qa, ka, lse, o, *datt, *after)


def dispatch_kernel(cap, slots, ids, grads, *refs):
    out = refs[-1]
    id_row = ids[...].astype(F32)
    T = id_row.shape[1]
    id_col = jnp.transpose(jnp.broadcast_to(id_row, (128, T)))[:, 0:1]
    same = jnp.where((id_col == id_row) & (iota((T, T), 0) < iota((T, T), 1)), 1.0, 0.0)
    rank = jnp.sum(same, axis=0, keepdims=True)
    slot = (id_row * cap + rank).astype(jnp.int32)
    pick = jnp.where(slot == iota((slots, T), 0), 1.0, 0.0).astype(BF16)
    out[...] = dot_nn(pick, grads[...]).astype(BF16)


def dispatch_call(cap, slots, after, ids, grads):
    vmem = pl.BlockSpec(memory_space=pltpu.VMEM)
    return pl.pallas_call(
        lambda *a: dispatch_kernel(cap, slots, *a),
        out_shape=jax.ShapeDtypeStruct((slots, D), BF16),
        in_specs=[vmem, vmem] + [pl.BlockSpec(memory_space=pl.ANY)] * len(after),
        out_specs=vmem,
        compiler_params=params(),
        cost_estimate=cost(3),
        name="dispatch",
    )(ids, grads, *after)


def owner_fwd_kernel(n, att_in, w_out, sel, out_bias, gain, bias, x_two, x_one, att_b):
    for k in range(n):
        att_b[:, k * 128 : (k + 1) * 128] = att_in[k]
    branch = dot_nn(att_b[...], w_out[...]) + out_bias[...]
    x = sel[...] + branch
    x_one[...] = x
    vhat, _ = normed_rows(x)
    x_two[...] = (vhat * gain[...] + bias[...]).astype(BF16)


def owner_fwd_call(n, e, att_in, w_out, sel, out_bias, gain, bias):
    slots = sel.shape[0] // EXP_DEV
    rows = pl.BlockSpec((slots, D), lambda i: (e, 0))
    mine = whole((slots, D))
    return pl.pallas_call(
        lambda *a: owner_fwd_kernel(n, *a),
        grid=(1,),
        in_specs=[
            whole((n, slots, 128)),
            whole((D, D)),
            rows,
            whole((1, D)),
            whole((1, D)),
            whole((1, D)),
        ],
        out_specs=[mine, mine, mine],
        out_shape=[
            jax.ShapeDtypeStruct((slots, D), BF16),
            jax.ShapeDtypeStruct((slots, D), F32),
            jax.ShapeDtypeStruct((slots, D), BF16),
        ],
        compiler_params=params(),
        cost_estimate=cost(3),
        name="owner_fwd",
    )(att_in, w_out, sel, out_bias, gain, bias)


def owner_bwd_kernel(n, part_a, part_b, x_one, og, gain, w_out, *refs):
    datt, d_one_b, small = refs[-3:]
    u = (part_a[...].astype(F32) + part_b[...].astype(F32)).astype(BF16).astype(F32)
    vhat, inv_std = normed_rows(x_one[...])
    scaled = u * gain[...]
    first = jnp.mean(scaled, axis=-1, keepdims=True)
    second = jnp.mean(scaled * vhat, axis=-1, keepdims=True)
    d_one = og[...].astype(F32) + inv_std * (scaled - first - vhat * second)
    d_b = d_one.astype(BF16)
    d_one_b[...] = d_b
    back = dot_nt(d_b, w_out[...]).astype(BF16)
    for k in range(n):
        datt[k] = back[:, k * 128 : (k + 1) * 128]
    small[0:1, :] = jnp.sum(u * vhat, axis=0, keepdims=True)
    small[1:2, :] = jnp.sum(u, axis=0, keepdims=True)
    small[2:3, :] = jnp.sum(d_one, axis=0, keepdims=True)


def owner_bwd_call(n, e, part_a, part_b, x_one, og, gain, w_out, after):
    slots = x_one.shape[0]
    mine = whole((slots, D))
    in_specs = [
        mine,
        mine,
        mine,
        pl.BlockSpec((slots, D), lambda i: (e, 0)),
        whole((1, D)),
        whole((D, D)),
    ]
    return pl.pallas_call(
        lambda *a: owner_bwd_kernel(n, *a),
        grid=(1,),
        in_specs=in_specs + [pl.BlockSpec(memory_space=pl.ANY)] * len(after),
        out_specs=[
            whole((n, slots, 128)),
            mine,
            whole((8, D)),
        ],
        out_shape=[
            jax.ShapeDtypeStruct((n, slots, 128), BF16),
            jax.ShapeDtypeStruct((slots, D), BF16),
            jax.ShapeDtypeStruct((8, D), F32),
        ],
        compiler_params=params(),
        cost_estimate=cost(4),
        name="owner_bwd",
    )(part_a, part_b, x_one, og, gain, w_out, *after)


def gelu_parts(u):
    cdf = 0.5 * (1.0 + lax.erf(u * (0.5**0.5)))
    return cdf, cdf + u * jnp.exp(-0.5 * u * u) * ((2.0 * math.pi) ** -0.5)


ROW_ORDER = (1, 3, 0, 2)


def expert_kernel(e, nb, rows, ff, width, extra, *refs):
    x_parts, g_parts = refs[:nb], refs[nb : 2 * nb]
    w_in, b_in, w_out = refs[2 * nb : 2 * nb + 3]
    hidden_out, dpre_out, keep, send, grad_b = refs[2 * nb + 3 + extra : 2 * nb + 8 + extra]
    xs, gs, w1, w2, hidden, dpre, part, sems = refs[2 * nb + 8 + extra :]
    copies = []

    def copy(ref, to):
        made = pltpu.make_async_copy(ref, to, sems.at[len(copies)])
        made.start()
        copies.append(made)

    for at, k in enumerate(ROW_ORDER):
        copy(x_parts[k], xs.at[pl.ds(at * rows, rows)])
    copy(w_in.at[e], w1)
    for at, k in enumerate(ROW_ORDER):
        copy(g_parts[k].at[pl.ds(e * rows, rows)], gs.at[pl.ds(at * rows, rows)])
    copy(w_out.at[e], w2)
    for c in copies[: nb + 1]:
        c.wait()
    ready = len(copies)
    for f in range(ff // width):
        cols = slice(f * width, (f + 1) * width)
        pre = dot_nn(xs[...], w1[:, cols]) + b_in[e : e + 1, cols]
        if f == 0:
            for c in copies[nb + 1 : ready]:
                c.wait()
        dhidden = dot_nt(gs[...], w2[cols, :]).astype(BF16).astype(F32)
        cdf, slope = gelu_parts(pre)
        hidden[:, cols] = (pre * cdf).astype(BF16)
        value = (dhidden * slope).astype(BF16)
        dpre[:, cols] = value
        grad_b[0, :, cols] = jnp.sum(value.astype(F32), axis=0, keepdims=True)
    copy(hidden, hidden_out)
    copy(dpre, dpre_out)
    for half, to in enumerate((send, keep)):
        at = slice(2 * half * rows, 2 * (half + 1) * rows)
        value = dot_nt(dpre[at, :], w1[...]).astype(BF16)
        for y in range(2):
            part[2 * half + y] = value[y * rows : (y + 1) * rows]
            copy(part.at[2 * half + y], to.at[y])
    for c in copies[ready:]:
        c.wait()


def expert_call(e, sc, x_parts, g_parts, w_in, b_in, w_out, after):
    del sc
    nb = len(x_parts)
    rows = x_parts[0].shape[0]
    ff = w_in.shape[2]
    anywhere = pl.BlockSpec(memory_space=pl.ANY)
    return pl.pallas_call(
        lambda *a: expert_kernel(e, nb, rows, ff, min(512, ff), len(after), *a),
        in_specs=[anywhere] * (2 * nb + 1)
        + [pl.BlockSpec(memory_space=pltpu.VMEM), anywhere]
        + [anywhere] * len(after),
        out_specs=[anywhere] * 4 + [pl.BlockSpec(memory_space=pltpu.VMEM)],
        scratch_shapes=[
            pltpu.VMEM((nb * rows, D), BF16),
            pltpu.VMEM((nb * rows, D), BF16),
            pltpu.VMEM((D, ff), BF16),
            pltpu.VMEM((ff, D), BF16),
            pltpu.VMEM((nb * rows, ff), BF16),
            pltpu.VMEM((nb * rows, ff), BF16),
            pltpu.VMEM((nb, rows, D), BF16),
            pltpu.SemaphoreType.DMA((3 * nb + 4,)),
        ],
        out_shape=[
            jax.ShapeDtypeStruct((nb * rows, ff), BF16),
            jax.ShapeDtypeStruct((nb * rows, ff), BF16),
            jax.ShapeDtypeStruct((2, rows, D), BF16),
            jax.ShapeDtypeStruct((2, rows, D), BF16),
            jax.ShapeDtypeStruct((1, 1, ff), F32),
        ],
        compiler_params=params(),
        cost_estimate=cost(10),
        name="expert_main",
    )(*x_parts, *g_parts, w_in, b_in, w_out, *after)


def expert_out_kernel(rows, hidden, w_out, *refs):
    keep, send = refs[-2:]
    total = dot_nn(hidden[...], w_out[0]).astype(BF16)
    for y in range(2):
        send[y] = total[y * rows : (y + 1) * rows, :]
        keep[y] = total[(2 + y) * rows : (3 + y) * rows, :]


def expert_out_call(nb, e, hidden, w_out, after):
    rows = hidden.shape[0] // nb
    ff = hidden.shape[1]
    return pl.pallas_call(
        lambda *a: expert_out_kernel(rows, *a),
        grid=(1,),
        in_specs=[whole(hidden.shape), pl.BlockSpec((1, ff, D), lambda i: (e, 0, 0))]
        + [pl.BlockSpec(memory_space=pl.ANY)] * len(after),
        out_specs=[whole((2, rows, D))] * 2,
        out_shape=[jax.ShapeDtypeStruct((2, rows, D), BF16)] * 2,
        compiler_params=params(),
        cost_estimate=cost(4),
        name="expert_out",
    )(hidden, w_out, *after)


def expert_grad_kernel(nb, rows, sc, *refs):
    x_parts, g_parts = refs[:nb], refs[nb : 2 * nb]
    hidden, dpre = refs[2 * nb : 2 * nb + 2]
    grad_in, grad_out, grad_b, xs, gs = refs[-5:]

    @pl.when(pl.program_id(0) == 0)
    def _():
        sums = []
        for at, k in enumerate(ROW_ORDER):
            xs[at * rows : (at + 1) * rows, :] = x_parts[k][...]
            gs[at * rows : (at + 1) * rows, :] = g_parts[k][...]
        for k in range(nb):
            sums.append(jnp.sum(g_parts[k][...].astype(F32), axis=0, keepdims=True))
        grad_b[0] = (sums[0] + sums[1]) + (sums[2] + sums[3])

    grad_in[0] = dot_tn(xs[...], dpre[...])
    grad_out[0] = dot_tn(hidden[...], gs[...])


def expert_grad_call(e, sc, x_parts, g_parts, hidden, dpre, held, after):
    nb = len(x_parts)
    rows = x_parts[0].shape[0]
    ff = hidden.shape[1]
    width = min(256, ff)
    g_specs = [pl.BlockSpec((rows, D), lambda f, sc: (e, 0))] * nb
    act = pl.BlockSpec((nb * rows, width), lambda f, sc: (0, f))
    in_specs = [whole((rows, D))] * nb + g_specs + [act, act]
    more = [] if held is None else list(held)
    aliases = {1 + len(in_specs) + i: i for i in range(len(more))}
    more += after
    return pl.pallas_call(
        lambda *a: expert_grad_kernel(nb, rows, *a),
        grid_spec=pltpu.PrefetchScalarGridSpec(
            num_scalar_prefetch=1,
            grid=(ff // width,),
            in_specs=in_specs + [pl.BlockSpec(memory_space=pl.ANY)] * len(more),
            out_specs=[
                pl.BlockSpec((1, D, width), lambda f, sc: (e, 0, f)),
                pl.BlockSpec((1, width, D), lambda f, sc: (e, f, 0)),
                pl.BlockSpec((1, 1, D), lambda f, sc: (e, 0, 0)),
            ],
            scratch_shapes=[pltpu.VMEM((nb * rows, D), BF16)] * 2,
        ),
        out_shape=[
            jax.ShapeDtypeStruct((EXP_DEV, D, ff), F32),
            jax.ShapeDtypeStruct((EXP_DEV, ff, D), F32),
            jax.ShapeDtypeStruct((EXP_DEV, 1, D), F32),
        ],
        input_output_aliases=aliases,
        compiler_params=params(),
        cost_estimate=SMALL,
        name="expert_grads",
    )(sc, *x_parts, *g_parts, hidden, dpre, *more)


def w_out_grad_kernel(n, nb, sc, *refs):
    keep, send = refs[-2:]
    total = dot_tn(refs[0][...], refs[EXP_DEV][...])
    for e in range(1, EXP_DEV):
        total = total + dot_tn(refs[e][...], refs[EXP_DEV + e][...])
    size = D // (n * nb)
    core = lax.rem(sc[n + 1], 2)
    chip = lax.div(sc[n + 1], 2)
    for r in range(n):
        for y in range(nb // 2):
            first = (r * nb + 2 * y) * size
            place = y ^ chip
            for g in range(-(-D // 384)):
                cols = slice(g * 384, min(D, (g + 1) * 384))
                width = cols.stop - cols.start
                pair = [total[first + c * size : first + (c + 1) * size, cols] for c in range(2)]
                rows = slice(g * size, (g + 1) * size)
                keep[place, r, rows, 0:width] = jnp.where(core == 0, pair[0], pair[1]).astype(BF16)
                send[place, r, rows, 0:width] = jnp.where(core == 0, pair[1], pair[0]).astype(BF16)
                if width < 384:
                    keep[place, r, rows, width:384] = jnp.zeros((size, 384 - width), BF16)
                    send[place, r, rows, width:384] = jnp.zeros((size, 384 - width), BF16)


def w_out_grad_call(n, nb, sc, att_b, d_one_b, after):
    size = D // (n * nb)
    shape = (nb // 2, n, -(-D // 384) * size, 384)
    return pl.pallas_call(
        lambda *a: w_out_grad_kernel(n, nb, *a[: 1 + 2 * EXP_DEV], *a[-2:]),
        grid_spec=pltpu.PrefetchScalarGridSpec(
            num_scalar_prefetch=1,
            grid=(1,),
            in_specs=[whole(att_b[0].shape)] * (2 * EXP_DEV)
            + [pl.BlockSpec(memory_space=pl.ANY)] * len(after),
            out_specs=[whole(shape)] * 2,
        ),
        out_shape=[jax.ShapeDtypeStruct(shape, BF16)] * 2,
        compiler_params=params(),
        cost_estimate=cost(4),
        name="w_out_grad",
    )(sc, *att_b, *d_one_b, *after)


def qkv_grad_kernel(n, nb, T, sc, h, dm, aux, after, keep, send, total):
    me_b = sc[n + 1]

    def add(c, carry):
        total[...] += dot_tn(dm[c], h[c])
        return carry

    total[...] = jnp.zeros_like(total)
    lax.fori_loop(0, n, add, 0)
    col_sum = jnp.zeros((1, 384), F32)
    for r in range(n):
        col_sum = col_sum + jnp.sum(dm[r].astype(F32), axis=0, keepdims=True)
    width = D // n
    size = width // nb
    top = iota((16, 384), 0)
    for r in range(n):
        part = jnp.transpose(total[:, r * width : (r + 1) * width])
        for k in range(nb):
            bb = me_b ^ k
            rows = jnp.zeros((size, 384), F32)
            for c in range(nb):
                rows = jnp.where(bb == c, part[c * size : (c + 1) * size, :], rows)
            extra = jnp.where(
                top == 0, col_sum, jnp.where(top == 1, aux[r * nb + bb], 0.0)
            )
            to = keep if k % 2 == 0 else send
            to[k // 2, r, 0:size, :] = rows.astype(BF16)
            to[k // 2, r, size : size + 16, :] = extra.astype(BF16)


def qkv_grad_call(n, nb, T, sc, h, dm, aux, after):
    size = D // (n * nb)
    shape = (2, n, size + 16, 384)
    return pl.pallas_call(
        lambda *a: qkv_grad_kernel(n, nb, T, *a),
        grid_spec=pltpu.PrefetchScalarGridSpec(
            num_scalar_prefetch=1,
            grid=(1,),
            in_specs=[
                whole((n, T, D)),
                whole((n, T, 384)),
                whole((n * nb, 1, 384)),
                pl.BlockSpec(memory_space=pl.ANY),
            ],
            out_specs=[whole(shape), whole(shape)],
            scratch_shapes=[pltpu.VMEM((384, D), F32)],
        ),
        out_shape=[jax.ShapeDtypeStruct(shape, BF16)] * 2,
        compiler_params=params(),
        cost_estimate=cost(3),
        name="qkv_grad",
    )(sc, h, dm, aux, after)


def scatter_rows(cap, slots, kaug, values):
    feature = kaug[:, 128:256].astype(F32)
    code = (feature[:, 16:17] * cap + feature[:, 17:18]).astype(jnp.int32)
    pick = jnp.where(code == iota((feature.shape[0], slots), 1), 1.0, 0.0).astype(BF16)
    return dot_nn(pick, values)


def input_grad_kernel(n, T, cap, sc, dm, w_qkv, hidden, d_ret, kaug, gain, out, full):
    for k in range(n):
        for part in range(3):
            full[:, part * D + k * 128 : part * D + (k + 1) * 128] = dm[
                k, :, part * 128 : (part + 1) * 128
            ]
    u = dot_nt(full[...], w_qkv[...])
    vhat, inv_std = normed_rows(hidden[...].astype(F32))
    scaled = u * gain[...]
    first = jnp.mean(scaled, axis=-1, keepdims=True)
    second = jnp.mean(scaled * vhat, axis=-1, keepdims=True)
    d_one = scatter_rows(cap, d_ret.shape[0], kaug[...], d_ret[...])
    out[...] = (d_one + inv_std * (scaled - first - vhat * second)).astype(BF16)


def input_grad_call(n, T, cap, sc, dm, w_qkv, hidden, d_ret, kaug, gain):
    slots = d_ret.shape[0]
    return pl.pallas_call(
        lambda *a: input_grad_kernel(n, T, cap, *a),
        grid_spec=pltpu.PrefetchScalarGridSpec(
            num_scalar_prefetch=1,
            grid=(1,),
            in_specs=[
                whole((n, T, 384)),
                whole((D, 3 * D)),
                whole((T, D)),
                whole((slots, D)),
                pl.BlockSpec((T, 256), lambda i, sc: (sc[n], 0)),
                whole((1, D)),
            ],
            out_specs=whole((T, D)),
            scratch_shapes=[pltpu.VMEM((T, 3 * D), BF16)],
        ),
        out_shape=jax.ShapeDtypeStruct((T, D), BF16),
        compiler_params=params(),
        cost_estimate=SMALL,
        name="input_grad",
    )(sc, dm, w_qkv, hidden, d_ret, kaug, gain)


def output_kernel(cap, sc, ret, kaug, out):
    out[...] = scatter_rows(cap, ret.shape[0], kaug[...], ret[...]).astype(BF16)


def output_call(n, T, cap, sc, ret, kaug):
    return pl.pallas_call(
        lambda *a: output_kernel(cap, *a),
        grid_spec=pltpu.PrefetchScalarGridSpec(
            num_scalar_prefetch=1,
            grid=(1,),
            in_specs=[
                whole(ret.shape),
                pl.BlockSpec((T, 256), lambda i, sc: (sc[n], 0)),
            ],
            out_specs=whole((T, D)),
        ),
        out_shape=jax.ShapeDtypeStruct((T, D), BF16),
        compiler_params=params(),
        cost_estimate=SMALL,
        name="output_rows",
    )(sc, ret, kaug)


def final_kernel(n, nb, sc, got, w_rows, gb, gw, gains, biases, qvb, outb, gwo, s_rows, w_full):
    size = D // (n * nb)
    me, me_b = sc[n], sc[n + 1]
    smalls = jnp.zeros((1, 384), F32)
    s_rows[...] = jnp.zeros_like(s_rows)
    for k in range(n):
        tile = got[k, 0 : size + 16, :].astype(F32)
        for part in range(3):
            cols = slice(part * D + k * 128, part * D + (k + 1) * 128)
            w_full[:, cols] = tile[0:size, part * 128 : (part + 1) * 128]
            s_rows[0:1, cols] = tile[size : size + 1, part * 128 : (part + 1) * 128]
        smalls = smalls + tile[size + 1 : size + 2, :]
    gw[...] = w_full[...]
    for g in range(-(-D // 384)):
        cols = slice(g * 384, min(D, (g + 1) * 384))
        rows = slice((g + 1) * size + 16, (g + 2) * size + 16)
        total = jnp.zeros((size, 384), F32)
        for k in range(n):
            total = total + got[k, rows, :].astype(F32)
        gwo[:, cols] = total[:, 0 : cols.stop - cols.start]
    weights = w_rows[...].astype(F32)
    high = lax.Precision.HIGHEST
    nt = (((1,), (1,)), ((), ()))
    bias_one = lax.dot_general(s_rows[...], weights, nt, precision=high, preferred_element_type=F32)[0:1]
    both = lax.dot_general(
        jnp.ones((8, 3 * D), F32), weights * w_full[...], nt, precision=high, preferred_element_type=F32
    )[0:1]
    gains[0:1, :] = (both - gb[1:2, :] * bias_one) / gb[0:1, :]
    gains[1:2, :] = smalls[:, 0:size]
    biases[0:1, :] = bias_one
    biases[1:2, :] = smalls[:, size : 2 * size]
    outb[...] = smalls[:, 2 * size : 3 * size]
    own = got[me, size : size + 16, :].astype(F32)[0:1]
    for row, first in ((0, 0), (1, 256)):
        value = jnp.zeros((1, size), F32)
        for c in range(nb):
            value = jnp.where(me_b == c, own[:, first + c * size : first + (c + 1) * size], value)
        qvb[row : row + 1, :] = value


def final_call(n, nb, sc, got, w_qkv, gb):
    size = D // (n * nb)
    shapes = [(size, 3 * D), (2, size), (2, size), (2, size), (1, size), (size, D)]
    return pl.pallas_call(
        lambda *a: final_kernel(n, nb, *a),
        grid_spec=pltpu.PrefetchScalarGridSpec(
            num_scalar_prefetch=1,
            grid=(1,),
            in_specs=[
                whole(got.shape),
                pl.BlockSpec((size, 3 * D), lambda i, sc: (nb * sc[n] + sc[n + 1], 0)),
                whole((2, size)),
            ],
            out_specs=[whole(s) for s in shapes],
            scratch_shapes=[pltpu.VMEM((8, 3 * D), F32), pltpu.VMEM((size, 3 * D), F32)],
        ),
        out_shape=[jax.ShapeDtypeStruct(s, F32) for s in shapes],
        compiler_params=params(),
        cost_estimate=cost(3),
        name="final_rows",
    )(sc, got, w_qkv, gb)


def exchange(values, axis, bit):
    size = lax.axis_size(axis)
    return lax.ppermute(values, axis, [(i, i ^ bit) for i in range(size)])


def arrival_tables(n, ring):
    place = [ring.index(i) for i in range(n)]
    order = [[0]] + [[-o, o] for o in range(1, n // 2)] + [[n // 2]]
    sources, tiles, counts = [], [], None
    for i in range(n):
        blocks = [[ring[(place[i] + o) % n] for o in step] for step in order]
        arrived, listed, sizes = [], [], []
        for at, step in enumerate(blocks):
            arrived += step
            if at == 0:
                continue
            new = arrived if at == 1 else step
            diag = [(q, q) for q in sorted(new)]
            pairs = [
                (q, k)
                for k in range(n)
                for q in range(k + 1, n)
                if q in arrived and k in arrived and (q in new or k in new)
            ]
            listed.append([x for t in diag + pairs for x in t])
            sizes.append((len(diag), len(pairs)))
        sources.append([b for step in blocks for b in step])
        tiles.append(listed)
        counts = counts or sizes
    return np.array(sources, np.int32), tiles, counts


def reduce_cores(keep, send, after=None):
    got = exchange(send, "batch", 1)
    if after is not None:
        got = gate(got, after)
    return [(keep[y].astype(F32) + got[y].astype(F32)).astype(BF16) for y in range(2)]


def gate(value, *after):
    def nothing(*refs):
        del refs

    anywhere = pl.BlockSpec(memory_space=pl.ANY)
    return pl.pallas_call(
        nothing,
        in_specs=[anywhere] * (1 + len(after)),
        out_specs=anywhere,
        out_shape=jax.ShapeDtypeStruct(value.shape, value.dtype),
        input_output_aliases={0: 0},
        name="gate",
    )(value, *after)


def local_by_heads(
    hidden_in,
    out_grad,
    norm_gain_pair,
    norm_bias_pair,
    w_qkv,
    qv_bias,
    w_out,
    out_bias,
    w_in_exp,
    b_in_exp,
    w_out_exp,
    b_out_exp,
    expert_ids,
    doc_lengths,
    pad_mask,
):
    T = hidden_in.shape[1]
    n, nb = lax.axis_size("seq"), lax.axis_size("batch")
    experts = EXP_DEV * n
    cap = max(2, 3 * T // (2 * experts))
    s, b = lax.axis_index("seq"), lax.axis_index("batch")
    ring = [*range(0, n, 2), *range(n - 1, 0, -2)]
    sources, tiles, counts = arrival_tables(n, ring)

    every = [(i, i) for i in range(n)] + [(q, k) for k in range(n) for q in range(k + 1, n)]
    every = np.array(every, np.int32).reshape(-1)
    table = [
        np.concatenate([sources[i], [i, 0]] + tiles[i] + [every]).astype(np.int32) for i in range(n)
    ]
    firsts = n + 2 + np.cumsum([0] + [2 * (d + p) for d, p in counts])
    row = lax.dynamic_index_in_dim(jnp.asarray(np.stack(table)), s, 0, keepdims=False)
    sc = jnp.where(jnp.arange(row.shape[0]) == n + 1, b.astype(jnp.int32), row)
    hidden = hidden_in[0]
    ids = expert_ids[0, :, 0]
    codes = jnp.concatenate([ids, pad_mask[0], jnp.zeros((D - 2 * T,), jnp.int32)]).astype(BF16)
    codes = jnp.where(jnp.arange(16)[:, None] == 0, codes[None, :], jnp.zeros((), BF16))
    payload = jnp.concatenate([hidden, codes], axis=0)

    count = doc_lengths.shape[1]
    at = jnp.arange(128)
    ends = jnp.sum(
        jnp.where(jnp.arange(count)[:, None] <= at[None, :], doc_lengths[0][:, None], 0), axis=0
    )
    starts = jnp.sum(
        jnp.where(jnp.arange(count)[:, None] < at[None, :], doc_lengths[0][:, None], 0), axis=0
    )
    docs = jnp.stack([starts, ends]).astype(F32)
    gain_rows = [norm_gain_pair[i : i + 1] for i in range(2)]
    bias_rows = [norm_bias_pair[i : i + 1] for i in range(2)]

    ahead = [(ring[i], ring[(i + 1) % n]) for i in range(n)]
    back = [(ring[i], ring[i - 1]) for i in range(n)]
    split = -(-payload.shape[0] // 32) * 16
    size = D // (n * nb)
    own = (s * nb + b) * size
    gb = jnp.stack(
        [
            lax.dynamic_slice_in_dim(norm_gain_pair[0], own, size, 0),
            lax.dynamic_slice_in_dim(norm_bias_pair[0], own, size, 0),
        ]
    )
    held, block = None, 0
    left = right = payload
    waiting = [[payload]]
    sent_grads = dispatch_call(cap, experts * cap, [], ids[None], out_grad[0])
    for step in range(1, n // 2 + 1):
        last = step == n // 2
        if last:
            left, right = left[:split], right[split:]
        left, right = lax.ppermute(left, "seq", ahead), lax.ppermute(right, "seq", back)
        if last:
            waiting.append([left, right])
        else:
            left = gate(left, right, *(held or ())[6:7])
            right = gate(right, left)
            waiting += [[left], [right]]
        if step == n // 2 - 1:
            sent_grads = gate(sent_grads, right)
            sent_grads = sent_grads.reshape(n, EXP_DEV * cap, D)
            grads = lax.all_to_all(sent_grads, "seq", split_axis=0, concat_axis=0, tiled=True)
            grads = grads.reshape(n, EXP_DEV, cap, D).transpose(1, 0, 2, 3).reshape(experts * cap, D)
        diags, pairs = counts[step - 1]
        held = ring_call(
            n, T, cap, block, int(firsts[step - 1]), diags, pairs, sc, waiting, held, last,
            w_qkv, qv_bias, gain_rows[0], bias_rows[0], docs,
            [grads] if last else [gb] if step == 1 else [],
        )
        block += len(waiting)
        waiting = []
    h_one, sel, qa, ka = held[:4]
    *att_out, o, lse = held[9:]
    sel = sel.reshape(EXP_DEV * n * cap, D)

    g_y = exchange(grads, "batch", 2)
    g_parts = [grads, exchange(grads, "batch", 1), g_y, exchange(g_y, "batch", 1)]

    def by_seq(rows):
        return lax.all_to_all(rows, "seq", split_axis=0, concat_axis=0, tiled=True)

    att_in = []
    for e in range(EXP_DEV):
        att_in.append(by_seq(gate(att_out[e], att_in[-1]) if e else att_out[e]))
    x_two, x_one, att_b = [], [], []
    for e in range(EXP_DEV):
        rows, one, att_rows = owner_fwd_call(
            n, e, att_in[e], w_out, sel, out_bias[None], gain_rows[1], bias_rows[1]
        )
        x_two.append(rows)
        x_one.append(one)
        att_b.append(att_rows)
    x_core = [exchange(rows, "batch", 1) for rows in x_two]
    x_y = [exchange(rows, "batch", 2) for rows in x_two]
    x_parts, hidden_act, dpre, grad_b_in, sums, from_y = [], [], [], [], [], []
    d_one_b, small, datt, outs = [], [], [], []
    to_add = []
    after = [x_one[-1]]
    terms = None

    def turn_back(e):
        datt_out, rows, totals = owner_bwd_call(
            n, e, sums[e][0], from_y[e], x_one[e], grads, gain_rows[1], w_out, after
        )
        datt.append(by_seq(gate(datt_out, datt[-1]) if e else datt_out))
        d_one_b.append(rows)
        small.append(totals)
        return datt_out

    for e in range(EXP_DEV):
        if e:
            x_y[e] = gate(x_y[e], terms[0])
        x_parts.append([x_two[e], x_core[e], x_y[e], exchange(x_y[e], "batch", 1)])
        act, dact, *terms, grad_b = expert_call(
            e, sc, x_parts[e], g_parts, w_in_exp, b_in_exp, w_out_exp, after
        )
        hidden_act.append(act)
        dpre.append(dact)
        grad_b_in.append(grad_b[0])
        if e == 0:
            to_add.append(expert_out_call(nb, e, act, w_out_exp, []))
            filler = to_add[e][0]
        else:
            after = [terms[0]]
            turn_back(e - 1)
            filler = d_one_b[-1]
        sums.append(reduce_cores(*terms, after=filler))
        from_y.append(exchange(sums[e][1], "batch", 2))
        after = [sums[e][0]]
    for i in range(1, EXP_DEV):
        to_add.append(expert_out_call(nb, i, hidden_act[i], w_out_exp, after))
    after = [to_add[-1][0]]
    datt_out = turn_back(EXP_DEV - 1)
    outs = [reduce_cores(*to_add[i], after=datt_out) for i in range(EXP_DEV)]
    from_y = [exchange(both[1], "batch", 2) for both in outs]

    size = D // (n * nb)
    home = []
    for e in range(EXP_DEV):
        expert_rows = (
            outs[e][0].astype(F32) + from_y[e].astype(F32) + b_out_exp[e][None, :]
        ).astype(BF16)
        home.append((x_one[e] + expert_rows.astype(F32)).astype(BF16))
    home = [rows.reshape(n, cap, D) for rows in d_one_b + home]
    home = jnp.concatenate(home, axis=1)
    returned = by_seq(home)
    at = EXP_DEV * cap
    dm = attn_bwd_call(
        n, T, cap, int(firsts[-1]), n, n * (n - 1) // 2, sc, qa, ka, lse, o, datt, [home]
    )
    w_out_terms = w_out_grad_call(n, nb, sc, att_b, d_one_b, [dm])
    aux = sum(small)[:3].reshape(3, n * nb, size).transpose(1, 0, 2).reshape(n * nb, 1, 3 * size)
    aux = jnp.pad(aux, ((0, 0), (0, 0), (0, 384 - 3 * size)))
    keep_w, send_w = qkv_grad_call(n, nb, T, sc, h_one, dm, aux, dm)
    returned = gate(returned, keep_w, w_out_terms[0])
    d_ret = returned[:, :at].reshape(experts * cap, D)
    dm_own = by_seq(gate(dm, returned))
    both = reduce_cores(keep_w, gate(send_w, returned))
    w_y = exchange(both[1], "batch", 2)
    w_out_both = reduce_cores(w_out_terms[0], gate(w_out_terms[1], both[0]))
    w_out_y = exchange(w_out_both[1], "batch", 2)
    weights = None
    for e in range(EXP_DEV):
        weights = expert_grad_call(
            e, sc, x_parts[e], g_parts, hidden_act[e], dpre[e], weights, [w_out_both[0]]
        )
    grad_w_in, grad_w_out_exp, grad_b_out = weights
    w_out_y = gate(w_out_y, grad_b_out)
    w_y = gate(w_y, grad_b_out)
    w_sum = (both[0].astype(F32) + w_y.astype(F32)).astype(BF16)
    summed = (w_out_both[0].astype(F32) + w_out_y.astype(F32)).astype(BF16)
    last_rows = jnp.concatenate([w_sum, summed], axis=1)
    dm_own = gate(dm_own, last_rows)
    w_got = by_seq(gate(last_rows, dm_own))
    out_ret = gate(returned[:, at : 2 * at].reshape(experts * cap, D), dm_own)
    output = output_call(n, T, cap, sc, out_ret, ka)
    gw_qkv, g_gains, g_biases, g_qvb, g_outb, grad_w_out = final_call(n, nb, sc, w_got, w_qkv, gb)
    input_grad = input_grad_call(n, T, cap, sc, dm_own, w_qkv, hidden, d_ret, ka, gain_rows[0])
    return (
        output[None],
        input_grad[None],
        g_gains,
        g_biases,
        gw_qkv,
        g_qvb,
        grad_w_out,
        g_outb[0],
        grad_w_in,
        jnp.concatenate(grad_b_in, axis=0),
        grad_w_out_exp,
        grad_b_out[:, 0],
    )


def solution(mesh):
    n, nb = mesh.shape["seq"], mesh.shape["batch"]
    by_heads = HEADS * HEAD_DIM == 128 * n and nb == 4
    return jax.shard_map(
        local_by_heads if by_heads else local,
        mesh=mesh,
        in_specs=(
            P("batch", "seq", None),
            P("batch", "seq", None),
            P(),
            P(),
            P(),
            P(),
            P(),
            P(),
            P("seq", None, "batch"),
            P("seq", "batch"),
            P("seq", "batch", None),
            P("seq", None),
            P("batch", "seq", None),
            P("batch", None),
            P("batch", "seq"),
        ),
        out_specs=(
            P("batch", "seq", None),
            P("batch", "seq", None),
            P(None, ("seq", "batch")),
            P(None, ("seq", "batch")),
            P(("seq", "batch"), None),
            P(None, ("seq", "batch")),
            P(("seq", "batch"), None),
            P(("seq", "batch")),
            P("seq", None, "batch"),
            P("seq", "batch"),
            P("seq", "batch", None),
            P("seq", None),
        ),
        check_vma=False,
    )
```
